32 devices in a mesh: seq: 16 (over z, y, x), tp: 2 (over core).
Axes of the slice: x: 2, y: 2, z: 4, core: 2. Of those that a mesh axis runs over, the one named last changes fastest.
Arguments:
- residual_in: bfloat16 [2048, 1536], P('seq'), may hold values from -6 to 6
- query_rows: bfloat16 [2048, 2048], P('seq', 'tp'), may hold values from -6 to 6
- rotated_key_rows: bfloat16 [2048, 256], P('seq', 'tp'), may hold values from -6 to 6
- value_row_matrix: bfloat16 [2048, 256], P('seq', 'tp'), may hold values from -6 to 6
- learned_sink_scores: float32 [32], P('tp'), may hold values from 0 to 6
- w_out: bfloat16 [2048, 1536], P('tp'), may hold values from -1 to 1
- norm_gain: float32 [1536], replicated, may hold values from 0.1 to 1.9
- expert_ids: int32 [2048, 4], P('seq'), may hold values from 0 to 15, all different within a row; in each aligned block of 128 rows (0 to 127, 128 to 255, ...) at most 64 rows name the same one
- route_weights: float32 [2048, 4], P('seq'), may hold values from 0.1 to 1
- w_gate: bfloat16 [16, 1536, 1536], P('seq', None, 'tp'), may hold values from -0.15625 to 0.15625
- w_up: bfloat16 [16, 1536, 1536], P('seq', None, 'tp'), may hold values from -0.15625 to 0.15625
- w_down: bfloat16 [16, 1536, 1536], P('seq', 'tp'), may hold values from -0.15625 to 0.15625
Outputs:
- layer_out: bfloat16 [2048, 1536], P('seq', 'tp')
The draws below stay inside these ranges and needn't reach their ends.
Inputs may be any that keep to these rules, and one draw needn't show every extreme that they name: `expert_ids`: in the rows of one device (aligned blocks of 128 rows) no expert is named by more than 64 rows, and each row names 4 different experts.
All inputs are finite; a program needn't handle non-finite values.
Results may differ from the reference program's by a relative error of at most 0.014.
Values may be sent and summed in bfloat16 or wider, within the bound.
No kernel may reach another device: no remote copies, remote signals or barrier semaphores. Data moves between devices by JAX's collectives and lax.ppermute only.
A program may use at most 64 MiB of HBM per device.

```python
import math
import jax
import jax.numpy as jnp
import numpy as np
from jax import lax

D = 1536
FF = 1536
QUERY_HEADS = 32
KEY_VALUE_HEADS = 4
HEAD_SIZE = 64
WINDOW_LENGTH = 128
TOPK = 4
TOK_DEV = 128
EXPERTS = 16
CAP = 64
SEQUENCE_TOKENS = 2048
N_SEQ = 16


def drawn_pair(key):
    key_query = jax.random.fold_in(key, 101)
    random_key_seed = jax.random.fold_in(key, 202)
    queries = jnp.clip(jax.random.normal(key_query, (SEQUENCE_TOKENS, QUERY_HEADS * HEAD_SIZE), jnp.float32), -4.5, 4.5)
    sampled_keys = jnp.clip(jax.random.normal(random_key_seed, (SEQUENCE_TOKENS, KEY_VALUE_HEADS * HEAD_SIZE), jnp.float32), -4.5, 4.5)
    return (queries, sampled_keys)


def draw_query_rows(key, part):
    queries, sampled_keys = drawn_pair(key)
    return queries.astype(jnp.bfloat16)


def draw_rotated_key_rows(key, part):
    queries, sampled_keys = drawn_pair(key)
    return sampled_keys.astype(jnp.bfloat16)


def level_of(own_key, shape, split, least, top_value):
    loudness = 1.0
    for axis_at, parts in split:
        draws = jax.random.uniform(jax.random.fold_in(jax.random.fold_in(own_key, 6), axis_at), (parts,), jnp.float32, least / len(split), top_value / len(split))
        loudness = loudness * jnp.repeat(jnp.exp(draws), shape[axis_at] // parts).reshape((-1,) + (1,) * (len(shape) - 1 - axis_at))
    return loudness


def routed_block(stream_key, own, number, rows, count, top, bound, slope):
    sequence = jax.random.permutation(stream_key, count)
    crowded, common = load_shares(count, rows * top, bound, slope, True), load_shares(count, rows * top, bound, slope, False)
    places = jnp.arange(count)

    def named(lengths, rotation):
        used = int((lengths > 0).sum())
        fixed = max(1, used // 4)
        passed = fixed + (places - fixed + rotation * (used - fixed)) % max(1, count - fixed)
        return jnp.zeros((count,), jnp.int32).at[sequence[jnp.where(places < fixed, places, passed)]].set(jnp.asarray(lengths, jnp.int32))

    lengths = jnp.where(number % 4 == 0, named(crowded, number // 4), named(common, number - number // 4 - 1))
    mixed = jax.random.permutation(jax.random.fold_in(own, 3), count)
    giver, sink = mixed[0:count // 2 * 2:2], mixed[1:count // 2 * 2:2]
    slack = jnp.minimum(lengths[giver] - 1, bound - lengths[sink]) // 2
    slack = jnp.where((giver == sequence[0]) | (sink == sequence[0]) | (lengths[sink] == 0), 0, jnp.maximum(slack, 0))
    passed = jax.random.randint(jax.random.fold_in(own, 4), (count // 2,), 0, 1 << 20) % (slack + 1)
    lengths = lengths.at[giver].add(-passed).at[sink].add(passed)
    labels = jnp.searchsorted(jnp.cumsum(lengths), jnp.arange(rows * top), side="right").astype(jnp.int32)
    table = labels.reshape(top, rows).T
    table = table[jax.random.permutation(jax.random.fold_in(own, 1), rows)]
    rotation = jax.random.randint(jax.random.fold_in(own, 2), (rows, 1), 0, top)
    return jnp.take_along_axis(table, (jnp.arange(top)[None, :] + rotation) % top, axis=1)


def load_shares(number_of, total, most, skew, full):
    weights = [(1 << 20) // math.isqrt(grade ** skew) + 1 for grade in range(1, number_of + 1)]
    largest = most if full else min(most, max(-(-total // number_of), total * weights[0] // sum(weights)))
    least = 1 if total - largest >= number_of - 1 else 0
    given, rest = [largest] + [least] * (number_of - 1), total - largest - least * (number_of - 1)
    while rest > 0:
        movable = [i for i in range(1, number_of) if given[i] < largest] or [i for i in range(1, number_of) if given[i] < most]
        mass, remaining = sum([weights[i] for i in movable]), rest
        for i in movable:
            more = min(most - given[i], max(1, remaining * weights[i] // mass), rest)
            given[i] = given[i] + more
            rest = rest - more
    return np.array(given)


def scatter_about(key, dims, spread, limit, split=(), held_as=jnp.bfloat16):
    level = level_of(key, dims, split, -0.22, 0.18) if split else 1.0
    entries = jax.random.normal(key, dims, jnp.float32) * spread * level
    return jnp.minimum(jnp.maximum(entries, -limit), limit).astype(held_as)


def setup_inputs(seed: int = 0) -> dict:
    key_list = jax.random.split(jax.random.key(seed), 13)
    residual_in = scatter_about(key_list[0], (SEQUENCE_TOKENS, D), 1.0, 6.0, ((0, 16),))
    query_rows = draw_query_rows(jax.random.fold_in(key_list[12], 71), 0)
    rotated_key_rows = draw_rotated_key_rows(jax.random.fold_in(key_list[12], 71), 0)
    value_row_matrix = scatter_about(key_list[3], (SEQUENCE_TOKENS, KEY_VALUE_HEADS * HEAD_SIZE), 1.0, 6.0, ((0, 16), (1, 2)))
    learned_sink_scores = jnp.clip(6.0 * jax.random.uniform(key_list[4], (QUERY_HEADS,), jnp.float32) ** level_of(key_list[4], (QUERY_HEADS,), ((0, 2),), -0.2, 0.2), 0.0, 6.0)
    w_out = scatter_about(key_list[5], (QUERY_HEADS * HEAD_SIZE, D), (QUERY_HEADS * HEAD_SIZE // 64) ** -0.5, 1.0, ((0, 2),))
    norm_gain = jnp.clip(1.0 + 0.18 * jax.random.normal(key_list[6], (D,), jnp.float32), 0.1, 1.9)
    expert_ids_keys = jax.random.split(jax.random.fold_in(key_list[7], 1), SEQUENCE_TOKENS // TOK_DEV)
    expert_ids_turns = jax.random.permutation(jax.random.fold_in(key_list[7], 3), SEQUENCE_TOKENS // TOK_DEV)
    expert_ids = jax.vmap(lambda own, number: routed_block(jax.random.fold_in(key_list[7], 2), own, number, TOK_DEV, EXPERTS, TOPK, CAP, 2))(expert_ids_keys, expert_ids_turns).reshape((SEQUENCE_TOKENS, TOPK))
    route_weights = jnp.clip(0.1 + 0.9 * jax.random.uniform(key_list[8], (SEQUENCE_TOKENS, TOPK), jnp.float32) ** level_of(key_list[8], (SEQUENCE_TOKENS, TOPK), ((0, 16),), -0.2, 0.2), 0.1, 1.0)
    w_gate = scatter_about(key_list[9], (EXPERTS, D, FF), D ** -0.5, 0.15625, ((0, 16), (2, 2)))
    w_up = scatter_about(key_list[10], (EXPERTS, D, FF), D ** -0.5, 0.15625, ((0, 16), (2, 2)))
    w_down = scatter_about(key_list[11], (EXPERTS, FF, D), FF ** -0.5, 0.15625, ((0, 16), (1, 2)))
    return {"residual_in": residual_in, "query_rows": query_rows, "rotated_key_rows": rotated_key_rows, "value_row_matrix": value_row_matrix, "learned_sink_scores": learned_sink_scores, "w_out": w_out, "norm_gain": norm_gain, "expert_ids": expert_ids, "route_weights": route_weights, "w_gate": w_gate, "w_up": w_up, "w_down": w_down}


neg_large = -1e+30
epsilon = 1e-05

def attention_block(block_index, query_rows, keys_padded, values_padded, learned_sink_scores):
    group_width = QUERY_HEADS // KEY_VALUE_HEADS
    start = block_index * WINDOW_LENGTH
    query_tile_block = lax.dynamic_slice_in_dim(query_rows, start, WINDOW_LENGTH, 0).astype(jnp.float32)
    key_tile_block = lax.dynamic_slice_in_dim(keys_padded, start, 2 * WINDOW_LENGTH, 0).astype(jnp.float32)
    value_tile_block = lax.dynamic_slice_in_dim(values_padded, start, 2 * WINDOW_LENGTH, 0).astype(jnp.float32)
    query_head_split = query_tile_block.reshape(WINDOW_LENGTH, KEY_VALUE_HEADS, group_width, HEAD_SIZE)
    key_head_split = key_tile_block.reshape(2 * WINDOW_LENGTH, KEY_VALUE_HEADS, HEAD_SIZE)
    value_head_split = value_tile_block.reshape(2 * WINDOW_LENGTH, KEY_VALUE_HEADS, HEAD_SIZE)
    scores = jnp.einsum('tkgd,skd->kgts', query_head_split, key_head_split) * HEAD_SIZE ** (-0.5)
    query_pos = start + jnp.arange(WINDOW_LENGTH, dtype=jnp.int32)
    key_pos = start - WINDOW_LENGTH + jnp.arange(2 * WINDOW_LENGTH, dtype=jnp.int32)
    distance = query_pos[:, None] - key_pos[None, :]
    allowed = (distance >= 0) & (distance < WINDOW_LENGTH) & (key_pos[None, :] >= 0)
    scores = jnp.where(allowed[None, None], scores, neg_large)
    head_sink_score = learned_sink_scores.reshape(KEY_VALUE_HEADS, group_width)[:, :, None]
    row_top = jnp.maximum(lax.optimization_barrier(jnp.max(scores, axis=-1)), head_sink_score)
    exp_terms = jnp.exp(scores - row_top[..., None])
    denom_sum = lax.optimization_barrier(jnp.sum(exp_terms, axis=-1)) + jnp.exp(head_sink_score - row_top)
    prob_bf = (exp_terms / denom_sum[..., None]).astype(jnp.bfloat16)
    head_out = jnp.einsum('kgts,skd->tkgd', prob_bf.astype(jnp.float32), value_head_split)
    return head_out.astype(jnp.bfloat16).reshape(WINDOW_LENGTH, QUERY_HEADS * HEAD_SIZE)

def reference(residual_in, query_rows, rotated_key_rows, value_row_matrix, learned_sink_scores, w_out, norm_gain, expert_ids, route_weights, w_gate, w_up, w_down):
    leading_zero_rows = jnp.zeros((WINDOW_LENGTH, KEY_VALUE_HEADS * HEAD_SIZE), rotated_key_rows.dtype)
    keys_padded = jnp.concatenate([leading_zero_rows, rotated_key_rows], axis=0)
    values_padded = jnp.concatenate([leading_zero_rows, value_row_matrix], axis=0)

    def one_block(block_index):
        return attention_block(block_index, query_rows, keys_padded, values_padded, learned_sink_scores)
    attended = lax.map(one_block, jnp.arange(SEQUENCE_TOKENS // WINDOW_LENGTH, dtype=jnp.int32))
    attended = attended.reshape(SEQUENCE_TOKENS, QUERY_HEADS * HEAD_SIZE)
    projected = jnp.dot(attended, w_out, preferred_element_type=jnp.float32)
    residual = (residual_in.astype(jnp.float32) + projected).astype(jnp.bfloat16)
    residual_float = residual.astype(jnp.float32)
    mean_square = lax.optimization_barrier(jnp.mean(residual_float * residual_float, axis=1))
    normed = (residual_float * lax.rsqrt(mean_square + epsilon)[:, None] * norm_gain).astype(jnp.bfloat16)
    pair_count = SEQUENCE_TOKENS * TOPK
    per_expert = N_SEQ * CAP
    block_ids = expert_ids.reshape(N_SEQ, TOK_DEV * TOPK)
    onehot = (block_ids[:, :, None] == jnp.arange(EXPERTS, dtype=jnp.int32)[None, None, :]).astype(jnp.int32)
    slot_index = lax.optimization_barrier(jnp.sum((jnp.cumsum(onehot, axis=1) - onehot) * onehot, axis=2))
    device_index = jnp.arange(N_SEQ, dtype=jnp.int32)[:, None]
    place = (block_ids * per_expert + device_index * CAP + slot_index).reshape(-1).astype(jnp.int32)
    slot_table = jnp.full((EXPERTS * per_expert,), pair_count, jnp.int32)
    slot_table = slot_table.at[place].set(jnp.arange(pair_count, dtype=jnp.int32))
    slot_table = slot_table.reshape(EXPERTS, per_expert)
    rows_padded = jnp.concatenate([normed, jnp.zeros((1, D), jnp.bfloat16)], axis=0)

    def expert_apply(operands):
        table_row, gate_mat, up_mat, down_mat = operands
        token_idx = jnp.minimum(table_row // TOPK, SEQUENCE_TOKENS)
        chosen = rows_padded[token_idx]
        gate_act = jnp.dot(chosen, gate_mat, preferred_element_type=jnp.float32)
        up_act = jnp.dot(chosen, up_mat, preferred_element_type=jnp.float32)
        hidden = (jax.nn.silu(gate_act) * up_act).astype(jnp.bfloat16)
        return jnp.dot(hidden, down_mat, preferred_element_type=jnp.float32)
    expert_out = lax.map(expert_apply, (slot_table, w_gate, w_up, w_down))
    picked = expert_out.reshape(EXPERTS * per_expert, D)[place].reshape(SEQUENCE_TOKENS, TOPK, D)
    combined = lax.optimization_barrier(jnp.sum(picked * route_weights[:, :, None], axis=1))
    return (residual_float + combined).astype(jnp.bfloat16)
```

```python
import jax
import jax.numpy as jnp
from jax import lax
from jax.sharding import PartitionSpec as P

HEAD_SIZE = 64
WINDOW_LENGTH = 128


neg_large = -1e30
epsilon = 1e-05


def passed_along(block, axis, distance):
    devices = range(lax.axis_size(axis))
    route = [(i - distance, i) for i in devices if i - distance in devices]
    return lax.ppermute(block, axis, route)


def local(
    residual_in,
    query_rows,
    rotated_key_rows,
    value_row_matrix,
    learned_sink_scores,
    w_out,
    norm_gain,
    expert_ids,
    route_weights,
    w_gate,
    w_up,
    w_down,
):
    tok_dev, model_width = residual_in.shape
    seq_count = lax.axis_size("seq")
    tp_count = lax.axis_size("tp")
    exp_dev = w_gate.shape[0]
    experts = exp_dev * seq_count
    capacity = max(2, 8 * tok_dev // experts)
    half_width = model_width // tp_count
    tp_index = lax.axis_index("tp")
    kv_heads = rotated_key_rows.shape[1] // HEAD_SIZE
    q_heads = query_rows.shape[1] // HEAD_SIZE
    group_width = q_heads // kv_heads
    top_count = expert_ids.shape[1]
    tails = jnp.stack([rotated_key_rows, value_row_matrix])
    earlier = passed_along(tails, "seq", 1)
    keys_all = jnp.concatenate([earlier[0], rotated_key_rows], axis=0)
    values_all = jnp.concatenate([earlier[1], value_row_matrix], axis=0)
    offset = lax.axis_index("seq") * tok_dev
    query_pos = offset + jnp.arange(tok_dev, dtype=jnp.int32)
    key_pos = offset - WINDOW_LENGTH + jnp.arange(WINDOW_LENGTH + tok_dev, dtype=jnp.int32)
    distance = query_pos[:, None] - key_pos[None, :]
    allowed = (distance >= 0) & (distance < WINDOW_LENGTH) & (key_pos[None, :] >= 0)
    query_head_split = query_rows.reshape(tok_dev, kv_heads, group_width, HEAD_SIZE)
    key_head_split = keys_all.reshape(WINDOW_LENGTH + tok_dev, kv_heads, HEAD_SIZE)
    value_head_split = values_all.reshape(WINDOW_LENGTH + tok_dev, kv_heads, HEAD_SIZE)
    scores = jnp.einsum(
        "tkgd,skd->kgts", query_head_split, key_head_split, preferred_element_type=jnp.float32
    ) * HEAD_SIZE ** (-0.5)
    scores = jnp.where(allowed[None, None], scores, neg_large)
    head_sink_score = learned_sink_scores.reshape(kv_heads, group_width)[:, :, None]
    row_top = jnp.maximum(jnp.max(scores, axis=-1), head_sink_score)
    exp_terms = jnp.exp(scores - row_top[..., None])
    denom_sum = jnp.sum(exp_terms, axis=-1) + jnp.exp(head_sink_score - row_top)
    prob_bf = (exp_terms / denom_sum[..., None]).astype(jnp.bfloat16)
    head_out = jnp.einsum(
        "kgts,skd->tkgd", prob_bf, value_head_split, preferred_element_type=jnp.float32
    )
    head_out = head_out.astype(jnp.bfloat16).reshape(tok_dev, q_heads * HEAD_SIZE)
    proj_part = jnp.dot(head_out, w_out, preferred_element_type=jnp.float32)
    notes = jnp.concatenate([expert_ids.astype(jnp.float32), route_weights], axis=1)
    notes = lax.all_gather(notes, "seq", axis=0, tiled=True)
    chosen = notes[:, :top_count] == lax.axis_index("seq").astype(jnp.float32)
    share = jnp.sum(jnp.where(chosen, notes[:, top_count:], 0.0), axis=1)
    flat_ids = expert_ids.reshape(-1)
    onehot = (flat_ids[:, None] == jnp.arange(experts, dtype=jnp.int32)[None, :]).astype(jnp.int32)
    slot_index = jnp.sum((jnp.cumsum(onehot, axis=0) - onehot) * onehot, axis=1)
    target_row = flat_ids * capacity + slot_index
    source_row = jnp.arange(tok_dev * top_count, dtype=jnp.int32) // top_count
    full_sum = lax.psum(proj_part.astype(jnp.bfloat16), "tp").astype(jnp.float32)
    whole = (residual_in.astype(jnp.float32) + full_sum).astype(jnp.bfloat16)
    whole_float = whole.astype(jnp.float32)
    mean_square = jnp.mean(whole_float * whole_float, axis=1)
    normed = (whole_float * lax.rsqrt(mean_square + epsilon)[:, None] * norm_gain).astype(
        jnp.bfloat16
    )
    residual = lax.dynamic_slice_in_dim(whole, tp_index * half_width, half_width, 1)
    if seq_count * tok_dev <= 2 * experts * capacity and exp_dev == 1:
        half = lax.dynamic_slice_in_dim(normed, tp_index * half_width, half_width, 1)
        gathered = lax.all_gather(half, "seq", axis=0, tiled=True)
        rows = lax.all_gather(gathered, "tp", axis=1, tiled=True)
        gate_act = jnp.dot(rows, w_gate[0], preferred_element_type=jnp.float32)
        up_act = jnp.dot(rows, w_up[0], preferred_element_type=jnp.float32)
        hidden = (jax.nn.silu(gate_act) * up_act).astype(jnp.bfloat16)
        partial_value = jnp.dot(hidden, w_down[0], preferred_element_type=jnp.float32)
        partial_value = (partial_value * share[:, None]).astype(jnp.bfloat16)
        partial_value = lax.psum_scatter(partial_value, "tp", scatter_dimension=1, tiled=True)
        combined = lax.psum_scatter(partial_value, "seq", scatter_dimension=0, tiled=True)
        return (residual.astype(jnp.float32) + combined.astype(jnp.float32)).astype(jnp.bfloat16)
    outgoing = jnp.zeros((experts * capacity, model_width), jnp.bfloat16)
    outgoing = outgoing.at[target_row].set(normed[source_row])
    arrived = lax.all_to_all(
        outgoing.reshape(seq_count, exp_dev, capacity, model_width),
        "seq",
        split_axis=0,
        concat_axis=0,
        tiled=True,
    )
    gate_act = jnp.einsum("sejd,edf->sejf", arrived, w_gate, preferred_element_type=jnp.float32)
    up_act = jnp.einsum("sejd,edf->sejf", arrived, w_up, preferred_element_type=jnp.float32)
    hidden = (jax.nn.silu(gate_act) * up_act).astype(jnp.bfloat16)
    partial_value = jnp.einsum("sejf,efd->sejd", hidden, w_down, preferred_element_type=jnp.float32)
    share_sum = lax.psum_scatter(
        partial_value.astype(jnp.bfloat16), "tp", scatter_dimension=3, tiled=True
    ).astype(jnp.float32)
    returned = lax.all_to_all(
        share_sum.astype(jnp.bfloat16), "seq", split_axis=0, concat_axis=0, tiled=True
    ).astype(share_sum.dtype)
    out_width = returned.shape[3]
    picked = returned.reshape(experts * capacity, out_width)[target_row]
    picked = picked.reshape(tok_dev, top_count, out_width)
    combined = jnp.sum(picked * route_weights[:, :, None], axis=1)
    return (residual.astype(jnp.float32) + combined).astype(jnp.bfloat16)


def solution(mesh):
    placed = (
        P("seq", None),
        P("seq", "tp"),
        P("seq", "tp"),
        P("seq", "tp"),
        P("tp"),
        P("tp", None),
        P(),
        P("seq", None),
        P("seq", None),
        P("seq", None, "tp"),
        P("seq", None, "tp"),
        P("seq", "tp", None),
    )
    return jax.shard_map(
        local, mesh=mesh, in_specs=placed, out_specs=P("seq", "tp"), check_vma=False
    )
```

```python
import functools

import jax
import jax.numpy as jnp
from jax import lax
from jax.experimental import pallas as pl
from jax.experimental.pallas import tpu as pltpu
from jax.sharding import PartitionSpec as P

HEAD_SIZE = 64
WINDOW_LENGTH = 128
LANES = 128
MIB = 1024 * 1024

neg_large = -1e30
epsilon = 1e-05

VMEM = pl.BlockSpec(memory_space=pltpu.VMEM)
SMEM = pl.BlockSpec(memory_space=pltpu.SMEM)
ANY = pl.BlockSpec(memory_space=pl.ANY)


def passed_along(block, axis, distance):
    devices = range(lax.axis_size(axis))
    route = [(i - distance, i) for i in devices if i - distance in devices]
    return lax.ppermute(block, axis, route)


def swapped(block, axis):
    count = lax.axis_size(axis)
    return lax.ppermute(block, axis, [(i, count - 1 - i) for i in range(count)])


def shape_of(dims, dtype=jnp.bfloat16):
    return jax.ShapeDtypeStruct(dims, dtype)


def cost(flops, moved, transcendentals=0):
    return pl.CostEstimate(flops=flops, bytes_accessed=moved, transcendentals=transcendentals)


def iota(dims, dimension):
    return lax.broadcasted_iota(jnp.int32, dims, dimension)


def place_kernel(experts, part_rows, parts, ids_ref, ids_across_ref, down_ref, across_ref):
    tokens, top_count = ids_ref.shape
    ids, ids_across = ids_ref[...], ids_across_ref[...]
    square = (tokens, tokens)

    def placed(slot, expert):
        part = sum([(slot >= float(k * part_rows)).astype(jnp.float32) for k in range(1, parts)], 0.0)
        return expert * part_rows + slot + part * ((experts - 1) * part_rows)

    names = iota((tokens, experts), 1)
    hits = [ids[:, c : c + 1] == names for c in range(top_count)]
    named = sum([hit.astype(jnp.float32) for hit in hits]).astype(jnp.bfloat16)
    earlier = (iota(square, 1) < iota(square, 0)).astype(jnp.bfloat16)
    slots = jnp.dot(earlier, named, preferred_element_type=jnp.float32)
    rows = placed(slots, names.astype(jnp.float32))
    columns = [jnp.sum(jnp.where(hit, rows, 0.0), axis=1, keepdims=True) for hit in hits]
    down_ref[...] = jnp.concatenate(columns, axis=1).astype(jnp.int32)

    names = iota((experts, tokens), 0)
    hits = [ids_across[c : c + 1, :] == names for c in range(top_count)]
    named = sum([hit.astype(jnp.float32) for hit in hits]).astype(jnp.bfloat16)
    earlier = (iota(square, 0) < iota(square, 1)).astype(jnp.bfloat16)
    slots = jnp.dot(named, earlier, preferred_element_type=jnp.float32)
    rows = placed(slots, names.astype(jnp.float32))
    lines = [jnp.sum(jnp.where(hit, rows, 0.0), axis=0, keepdims=True) for hit in hits]
    across_ref[...] = jnp.concatenate(lines, axis=0).astype(jnp.int32)


def places(expert_ids, experts, part_rows, parts):
    tokens, top_count = expert_ids.shape
    return pl.pallas_call(
        functools.partial(place_kernel, experts, part_rows, parts),
        out_shape=(
            shape_of((tokens, top_count), jnp.int32),
            shape_of((top_count, tokens), jnp.int32),
        ),
        in_specs=[VMEM, VMEM],
        out_specs=(VMEM, VMEM),
        cost_estimate=cost(8 * tokens * tokens * experts, 16 * tokens * top_count),
        name="places",
    )(expert_ids, expert_ids.T)


def attention_kernel(
    first_ref, sink_ref, q_ref, k_ref, v_ref, k_before_ref, v_before_ref, w_hbm, out_ref, w_ref, att_ref, sem
):
    tokens, width = q_ref.shape
    kv_heads = k_ref.shape[1] // HEAD_SIZE
    pairs = width // LANES // kv_heads
    load = pltpu.make_async_copy(w_hbm, w_ref, sem)
    load.start()
    rows = pairs * tokens
    lane = iota((tokens, LANES), 1)
    low = lane < HEAD_SIZE

    def doubled(block, head):
        wide = block.astype(jnp.float32)
        turned = pltpu.roll(wide, HEAD_SIZE, 1)
        first, second = (wide, turned) if head == 0 else (turned, wide)
        return [
            jnp.where(low, first, 0.0).astype(jnp.bfloat16),
            jnp.where(low, 0.0, second).astype(jnp.bfloat16),
        ]

    token = jnp.bitwise_and(iota((rows, 2 * tokens), 0), tokens - 1)
    key = jnp.bitwise_and(iota((rows, 2 * tokens), 1), tokens - 1)
    own = key <= token
    usable = first_ref[0] == 0
    k, v, k_before, v_before = k_ref[...], v_ref[...], k_before_ref[...], v_before_ref[...]
    contract = (((1,), (1,)), ((), ()))
    for head in range(kv_heads):
        q = jnp.concatenate(
            [q_ref[:, (head * pairs + j) * LANES : (head * pairs + j + 1) * LANES] for j in range(pairs)], axis=0
        )
        keys = jnp.concatenate(doubled(k, head), axis=0)
        keys_before = jnp.concatenate(doubled(k_before, head), axis=0)
        values = jnp.concatenate(doubled(v, head) + doubled(v_before, head), axis=0)
        near = lax.dot_general(q, keys, contract, preferred_element_type=jnp.float32)
        far = lax.dot_general(q, keys_before, contract, preferred_element_type=jnp.float32)
        far = jnp.where(usable, far * HEAD_SIZE**-0.5, neg_large)
        scores = jnp.where(own, near * HEAD_SIZE**-0.5, far)
        kept_own, kept_before = [], []
        for side in range(2):
            part = scores[:, side * tokens : (side + 1) * tokens]
            sink = jnp.concatenate(
                [jnp.full((tokens, 1), sink_ref[2 * (head * pairs + j) + side], jnp.float32) for j in range(pairs)],
                axis=0,
            )
            top = jnp.maximum(jnp.max(part, axis=1, keepdims=True), sink)
            terms = jnp.exp(part - top)
            total = jnp.sum(terms, axis=1, keepdims=True) + jnp.exp(sink - top)
            prob = terms * (1.0 / total)
            mine = own[:, :tokens]
            kept_own.append(jnp.where(mine, prob, 0.0).astype(jnp.bfloat16))
            kept_before.append(jnp.where(mine, 0.0, prob).astype(jnp.bfloat16))
        probs = jnp.concatenate(kept_own + kept_before, axis=1)
        found = jnp.dot(probs, values, preferred_element_type=jnp.float32).astype(jnp.bfloat16)
        for j in range(pairs):
            at = (head * pairs + j) * LANES
            att_ref[:, at : at + LANES] = found[j * tokens : (j + 1) * tokens]
    load.wait()
    step = 2 * LANES
    for at in range(0, out_ref.shape[1], step):
        out_ref[:, at : at + step] = jnp.dot(
            att_ref[...], w_ref[:, at : at + step], preferred_element_type=jnp.float32
        ).astype(jnp.bfloat16)


def attention(first, sinks, q, k, v, k_before, v_before, w_out):
    tokens = q.shape[0]
    return pl.pallas_call(
        attention_kernel,
        out_shape=shape_of((tokens, w_out.shape[1])),
        in_specs=[SMEM, SMEM, VMEM, VMEM, VMEM, VMEM, VMEM, ANY],
        out_specs=VMEM,
        scratch_shapes=[
            pltpu.VMEM(w_out.shape, jnp.bfloat16),
            pltpu.VMEM(q.shape, jnp.bfloat16),
            pltpu.SemaphoreType.DMA,
        ],
        compiler_params=pltpu.CompilerParams(vmem_limit_bytes=24 * MIB),
        cost_estimate=cost(2 * tokens * w_out.size * 2, 2 * w_out.size, tokens * tokens * q.shape[1] // HEAD_SIZE),
        name="attention",
    )(first, sinks, q, k, v, k_before, v_before, w_out)


def norm_kernel(side_ref, residual_ref, near_ref, far_ref, gain_ref, across_ref, *refs):
    *out_refs, kept_ref, whole_ref, normed_ref = refs
    tokens, half = kept_ref.shape
    top_count = across_ref.shape[0]
    added = near_ref[...].astype(jnp.float32) + far_ref[...].astype(jnp.float32)
    whole = (residual_ref[...].astype(jnp.float32) + added).astype(jnp.bfloat16)
    whole_ref[...] = whole
    wide = whole.astype(jnp.float32)
    mean_square = jnp.mean(wide * wide, axis=1, keepdims=True)
    normed_ref[...] = (wide * lax.rsqrt(mean_square + epsilon) * gain_ref[...]).astype(jnp.bfloat16)
    columns = pl.ds(pl.multiple_of(side_ref[0] * half, LANES), half)
    kept_ref[...] = whole_ref[:, columns]
    normed = normed_ref[:, columns]
    base = 0
    for out_ref in out_refs:
        rows = out_ref.shape[0]
        step = min(rows, 256)
        for at in range(0, rows, step):
            row = iota((step, tokens), 0) + (base + at)
            taken = across_ref[0:1, :] == row
            for c in range(1, top_count):
                taken = taken | (across_ref[c : c + 1, :] == row)
            taken = jnp.where(taken, 1.0, 0.0).astype(jnp.bfloat16)
            out_ref[at : at + step, :] = jnp.dot(
                taken, normed, preferred_element_type=jnp.float32
            ).astype(jnp.bfloat16)
        base += rows


def norm_and_pack(side, residual_in, near, far, gain, across, half, part_total, parts):
    tokens, width = residual_in.shape
    return pl.pallas_call(
        norm_kernel,
        out_shape=tuple([shape_of((part_total, half))] * parts + [shape_of((tokens, half))]),
        in_specs=[SMEM, VMEM, VMEM, VMEM, VMEM, VMEM],
        out_specs=tuple([VMEM] * (parts + 1)),
        scratch_shapes=[pltpu.VMEM((tokens, width), jnp.bfloat16)] * 2,
        compiler_params=pltpu.CompilerParams(vmem_limit_bytes=24 * MIB),
        cost_estimate=cost(2 * part_total * parts * tokens * half, 2 * part_total * parts * half),
        name="norm_and_pack",
    )(side, residual_in, near, far, gain.reshape(1, width), across)


def expert_kernel(
    side_ref, near_ref, far_ref, gate_hbm, up_hbm, down_hbm, kept_ref, sent_ref, x_ref, gate_ref, up_ref, down_ref,
    hidden_ref, y_ref, gate_sem, up_sem, down_sem,
):
    rows, half = near_ref.shape
    hidden_width = gate_ref.shape[1]
    side = side_ref[0]
    step = 2 * LANES
    tile = min(rows, 256)
    gate_loads, up_loads = [], []
    for i in range(hidden_width // step):
        columns = pl.ds(i * step, step)
        gate_loads.append(pltpu.make_async_copy(gate_hbm.at[0, :, columns], gate_ref.at[:, columns], gate_sem.at[i]))
        up_loads.append(pltpu.make_async_copy(up_hbm.at[0, :, columns], up_ref.at[:, columns], up_sem.at[i]))
    down_load = pltpu.make_async_copy(down_hbm.at[0], down_ref, down_sem)
    for load in [load for pair in zip(gate_loads, up_loads) for load in pair] + [down_load]:
        load.start()
    mine = pl.ds(pl.multiple_of(side * half, LANES), half)
    other = pl.ds(pl.multiple_of((1 - side) * half, LANES), half)
    x_ref[:, mine] = near_ref[...]
    x_ref[:, other] = far_ref[...]
    for i in range(hidden_width // step):
        gate_loads[i].wait()
        up_loads[i].wait()
        for at in range(0, rows, tile):
            x = x_ref[at : at + tile, :]
            gate = jnp.dot(x, gate_ref[:, i * step : (i + 1) * step], preferred_element_type=jnp.float32)
            up = jnp.dot(x, up_ref[:, i * step : (i + 1) * step], preferred_element_type=jnp.float32)
            hidden = gate / (1.0 + jnp.exp(-gate)) * up
            hidden_ref[at : at + tile, i * step : (i + 1) * step] = hidden.astype(jnp.bfloat16)
    down_load.wait()
    for at in range(0, rows, tile):
        hidden = hidden_ref[at : at + tile, :]
        for i in range(2 * half // step):
            y_ref[at : at + tile, i * step : (i + 1) * step] = jnp.dot(
                hidden, down_ref[:, i * step : (i + 1) * step], preferred_element_type=jnp.float32
            ).astype(jnp.bfloat16)
    kept_ref[...] = y_ref[:, mine]
    sent_ref[...] = y_ref[:, other]


def expert_layer(side, near, far, w_gate, w_up, w_down):
    rows, half = near.shape
    _, width, hidden_width = w_gate.shape
    tiles = hidden_width // (2 * LANES)
    return pl.pallas_call(
        expert_kernel,
        out_shape=(shape_of((rows, half)), shape_of((rows, half))),
        in_specs=[SMEM, VMEM, VMEM, ANY, ANY, ANY],
        out_specs=(VMEM, VMEM),
        scratch_shapes=[
            pltpu.VMEM((rows, width), jnp.bfloat16),
            pltpu.VMEM((width, hidden_width), jnp.bfloat16),
            pltpu.VMEM((width, hidden_width), jnp.bfloat16),
            pltpu.VMEM((hidden_width, width), jnp.bfloat16),
            pltpu.VMEM((rows, hidden_width), jnp.bfloat16),
            pltpu.VMEM((rows, width), jnp.bfloat16),
            pltpu.SemaphoreType.DMA((tiles,)),
            pltpu.SemaphoreType.DMA((tiles,)),
            pltpu.SemaphoreType.DMA,
        ],
        compiler_params=pltpu.CompilerParams(vmem_limit_bytes=32 * MIB),
        cost_estimate=cost(6 * rows * width * hidden_width, 6 * width * hidden_width, rows * hidden_width),
        name="expert_layer",
    )(side, near, far, w_gate, w_up, w_down)


def combine_kernel(down_ref, weights_ref, kept_ref, *refs):
    *part_refs, out_ref = refs
    tokens, top_count = down_ref.shape
    total = kept_ref[...].astype(jnp.float32)
    base = 0
    for part_ref in part_refs:
        rows = part_ref.shape[0]
        row = iota((tokens, rows), 1) + base
        share = jnp.zeros((tokens, rows), jnp.float32)
        for c in range(top_count):
            share = jnp.where(down_ref[:, c : c + 1] == row, weights_ref[:, c : c + 1], share)
        coarse = share.astype(jnp.bfloat16)
        fine = (share - coarse.astype(jnp.float32)).astype(jnp.bfloat16)
        total += jnp.dot(coarse, part_ref[...], preferred_element_type=jnp.float32)
        total += jnp.dot(fine, part_ref[...], preferred_element_type=jnp.float32)
        base += rows
    out_ref[...] = total.astype(jnp.bfloat16)


def combine(down, weights, kept, returned):
    tokens, half = kept.shape
    rows = sum(part.shape[0] for part in returned)
    return pl.pallas_call(
        combine_kernel,
        out_shape=shape_of((tokens, half)),
        in_specs=[VMEM] * (3 + len(returned)),
        out_specs=VMEM,
        compiler_params=pltpu.CompilerParams(vmem_limit_bytes=24 * MIB),
        cost_estimate=cost(4 * rows * tokens * half, 2 * rows * half),
        name="combine",
    )(down, weights, kept, *returned)


def local(
    residual_in,
    query_rows,
    rotated_key_rows,
    value_row_matrix,
    learned_sink_scores,
    w_out,
    norm_gain,
    expert_ids,
    route_weights,
    w_gate,
    w_up,
    w_down,
):
    tok_dev, model_width = residual_in.shape
    seq_count = lax.axis_size("seq")
    experts = w_gate.shape[0] * seq_count
    capacity = max(2, 8 * tok_dev // experts)
    parts = PARTS if capacity // PARTS >= 16 else 1
    part_rows = capacity // parts
    part_total = experts * part_rows
    half = model_width // lax.axis_size("tp")
    side = lax.axis_index("tp").astype(jnp.int32).reshape(1)
    first = (lax.axis_index("seq") == 0).astype(jnp.int32).reshape(1)

    k_before = passed_along(rotated_key_rows, "seq", 1)
    v_before = passed_along(value_row_matrix, "seq", 1)
    down, across = places(expert_ids, experts, part_rows, parts)
    near = attention(
        first, learned_sink_scores, query_rows, rotated_key_rows, value_row_matrix, k_before, v_before, w_out
    )
    far = swapped(near, "tp")
    *outgoing, kept = norm_and_pack(
        side, residual_in, near, far, norm_gain, across, half, part_total, parts
    )

    def exchanged(block):
        block = block.reshape(seq_count, part_total // seq_count, half)
        block = lax.all_to_all(block, "seq", split_axis=0, concat_axis=0, tiled=True)
        return block.reshape(part_total, half)

    returned = []
    for block in outgoing:
        arrived = exchanged(block)
        other = swapped(arrived, "tp")
        mine, theirs = expert_layer(side, arrived, other, w_gate, w_up, w_down)
        summed = mine.astype(jnp.float32) + swapped(theirs, "tp").astype(jnp.float32)
        returned.append(exchanged(summed.astype(jnp.bfloat16)))
    return combine(down, route_weights, kept, returned)


PARTS = 1


def solution(mesh):
    placed = (
        P("seq", None),
        P("seq", "tp"),
        P("seq", "tp"),
        P("seq", "tp"),
        P("tp"),
        P("tp", None),
        P(),
        P("seq", None),
        P("seq", None),
        P("seq", None, "tp"),
        P("seq", None, "tp"),
        P("seq", "tp", None),
    )
    return jax.shard_map(
        local, mesh=mesh, in_specs=placed, out_specs=P("seq", "tp"), check_vma=False
    )
```

```python
import functools

import jax
import jax.numpy as jnp
from jax import lax
from jax.experimental import pallas as pl
from jax.experimental.pallas import tpu as pltpu
from jax.sharding import PartitionSpec as P

HEAD_SIZE = 64
WINDOW_LENGTH = 128
LANES = 128
MIB = 1024 * 1024

neg_large = -1e30
epsilon = 1e-05

VMEM = pl.BlockSpec(memory_space=pltpu.VMEM)
SMEM = pl.BlockSpec(memory_space=pltpu.SMEM)
ANY = pl.BlockSpec(memory_space=pl.ANY)


def passed_along(block, axis, distance):
    devices = range(lax.axis_size(axis))
    route = [(i - distance, i) for i in devices if i - distance in devices]
    return lax.ppermute(block, axis, route)


def swapped(block, axis):
    count = lax.axis_size(axis)
    return lax.ppermute(block, axis, [(i, count - 1 - i) for i in range(count)])


def shape_of(dims, dtype=jnp.bfloat16):
    return jax.ShapeDtypeStruct(dims, dtype)


def cost(flops, moved, transcendentals=0):
    return pl.CostEstimate(flops=flops, bytes_accessed=moved, transcendentals=transcendentals)


def iota(dims, dimension):
    return lax.broadcasted_iota(jnp.int32, dims, dimension)


def place_kernel(experts, part_rows, parts, ids_ref, ids_across_ref, down_ref, across_ref):
    tokens, top_count = ids_ref.shape
    ids, ids_across = ids_ref[...], ids_across_ref[...]
    square = (tokens, tokens)

    def placed(slot, expert):
        part = sum([(slot >= float(k * part_rows)).astype(jnp.float32) for k in range(1, parts)], 0.0)
        return expert * part_rows + slot + part * ((experts - 1) * part_rows)

    names = iota((tokens, experts), 1)
    hits = [ids[:, c : c + 1] == names for c in range(top_count)]
    named = sum([hit.astype(jnp.float32) for hit in hits]).astype(jnp.bfloat16)
    earlier = (iota(square, 1) < iota(square, 0)).astype(jnp.bfloat16)
    slots = jnp.dot(earlier, named, preferred_element_type=jnp.float32)
    rows = placed(slots, names.astype(jnp.float32))
    columns = [jnp.sum(jnp.where(hit, rows, 0.0), axis=1, keepdims=True) for hit in hits]
    down_ref[...] = jnp.concatenate(columns, axis=1).astype(jnp.int32)

    names = iota((experts, tokens), 0)
    hits = [ids_across[c : c + 1, :] == names for c in range(top_count)]
    named = sum([hit.astype(jnp.float32) for hit in hits]).astype(jnp.bfloat16)
    earlier = (iota(square, 0) < iota(square, 1)).astype(jnp.bfloat16)
    slots = jnp.dot(named, earlier, preferred_element_type=jnp.float32)
    rows = placed(slots, names.astype(jnp.float32))
    lines = [jnp.sum(jnp.where(hit, rows, 0.0), axis=0, keepdims=True) for hit in hits]
    across_ref[...] = jnp.concatenate(lines, axis=0).astype(jnp.int32)


def places(expert_ids, experts, part_rows, parts):
    tokens, top_count = expert_ids.shape
    return pl.pallas_call(
        functools.partial(place_kernel, experts, part_rows, parts),
        out_shape=(
            shape_of((tokens, top_count), jnp.int32),
            shape_of((top_count, tokens), jnp.int32),
        ),
        in_specs=[VMEM, VMEM],
        out_specs=(VMEM, VMEM),
        cost_estimate=cost(8 * tokens * tokens * experts, 16 * tokens * top_count),
        name="places",
    )(expert_ids, expert_ids.T)


def attention_kernel(
    first_ref, sink_ref, q_ref, k_ref, v_ref, k_before_ref, v_before_ref, w_hbm, out_ref, w_ref, att_ref, sem
):
    tokens, width = q_ref.shape
    kv_heads = k_ref.shape[1] // HEAD_SIZE
    pairs = width // LANES // kv_heads
    load = pltpu.make_async_copy(w_hbm, w_ref, sem)
    load.start()
    rows = pairs * tokens
    lane = iota((tokens, LANES), 1)
    low = lane < HEAD_SIZE

    def doubled(block, head):
        wide = block.astype(jnp.float32)
        turned = pltpu.roll(wide, HEAD_SIZE, 1)
        first, second = (wide, turned) if head == 0 else (turned, wide)
        return [
            jnp.where(low, first, 0.0).astype(jnp.bfloat16),
            jnp.where(low, 0.0, second).astype(jnp.bfloat16),
        ]

    token = jnp.bitwise_and(iota((rows, 2 * tokens), 0), tokens - 1)
    key = jnp.bitwise_and(iota((rows, 2 * tokens), 1), tokens - 1)
    own = key <= token
    usable = first_ref[0] == 0
    k, v, k_before, v_before = k_ref[...], v_ref[...], k_before_ref[...], v_before_ref[...]
    contract = (((1,), (1,)), ((), ()))
    for head in range(kv_heads):
        q = jnp.concatenate(
            [q_ref[:, (head * pairs + j) * LANES : (head * pairs + j + 1) * LANES] for j in range(pairs)], axis=0
        )
        keys = jnp.concatenate(doubled(k, head), axis=0)
        keys_before = jnp.concatenate(doubled(k_before, head), axis=0)
        values = jnp.concatenate(doubled(v, head) + doubled(v_before, head), axis=0)
        near = lax.dot_general(q, keys, contract, preferred_element_type=jnp.float32)
        far = lax.dot_general(q, keys_before, contract, preferred_element_type=jnp.float32)
        far = jnp.where(usable, far * HEAD_SIZE**-0.5, neg_large)
        scores = jnp.where(own, near * HEAD_SIZE**-0.5, far)
        kept_own, kept_before = [], []
        for side in range(2):
            part = scores[:, side * tokens : (side + 1) * tokens]
            sink = jnp.concatenate(
                [jnp.full((tokens, 1), sink_ref[2 * (head * pairs + j) + side], jnp.float32) for j in range(pairs)],
                axis=0,
            )
            top = jnp.maximum(jnp.max(part, axis=1, keepdims=True), sink)
            terms = jnp.exp(part - top)
            total = jnp.sum(terms, axis=1, keepdims=True) + jnp.exp(sink - top)
            prob = terms * (1.0 / total)
            mine = own[:, :tokens]
            kept_own.append(jnp.where(mine, prob, 0.0).astype(jnp.bfloat16))
            kept_before.append(jnp.where(mine, 0.0, prob).astype(jnp.bfloat16))
        probs = jnp.concatenate(kept_own + kept_before, axis=1)
        found = jnp.dot(probs, values, preferred_element_type=jnp.float32).astype(jnp.bfloat16)
        for j in range(pairs):
            at = (head * pairs + j) * LANES
            att_ref[:, at : at + LANES] = found[j * tokens : (j + 1) * tokens]
    load.wait()
    step = 2 * LANES
    for at in range(0, out_ref.shape[1], step):
        out_ref[:, at : at + step] = jnp.dot(
            att_ref[...], w_ref[:, at : at + step], preferred_element_type=jnp.float32
        ).astype(jnp.bfloat16)


def attention(first, sinks, q, k, v, k_before, v_before, w_out):
    tokens = q.shape[0]
    return pl.pallas_call(
        attention_kernel,
        out_shape=shape_of((tokens, w_out.shape[1])),
        in_specs=[SMEM, SMEM, VMEM, VMEM, VMEM, VMEM, VMEM, ANY],
        out_specs=VMEM,
        scratch_shapes=[
            pltpu.VMEM(w_out.shape, jnp.bfloat16),
            pltpu.VMEM(q.shape, jnp.bfloat16),
            pltpu.SemaphoreType.DMA,
        ],
        compiler_params=pltpu.CompilerParams(vmem_limit_bytes=24 * MIB),
        cost_estimate=cost(2 * tokens * w_out.size * 2, 2 * w_out.size, tokens * tokens * q.shape[1] // HEAD_SIZE),
        name="attention",
    )(first, sinks, q, k, v, k_before, v_before, w_out)


def norm_kernel(side_ref, residual_ref, near_ref, far_ref, gain_ref, across_ref, *refs):
    *out_refs, kept_ref, whole_ref, normed_ref = refs
    tokens, half = kept_ref.shape
    top_count = across_ref.shape[0]
    added = near_ref[...].astype(jnp.float32) + far_ref[...].astype(jnp.float32)
    whole = (residual_ref[...].astype(jnp.float32) + added).astype(jnp.bfloat16)
    whole_ref[...] = whole
    wide = whole.astype(jnp.float32)
    mean_square = jnp.mean(wide * wide, axis=1, keepdims=True)
    normed_ref[...] = (wide * lax.rsqrt(mean_square + epsilon) * gain_ref[...]).astype(jnp.bfloat16)
    columns = pl.ds(pl.multiple_of(side_ref[0] * half, LANES), half)
    kept_ref[...] = whole_ref[:, columns]
    normed = normed_ref[:, columns]
    base = 0
    for out_ref in out_refs:
        rows = out_ref.shape[0]
        step = min(rows, 256)
        for at in range(0, rows, step):
            row = iota((step, tokens), 0) + (base + at)
            taken = across_ref[0:1, :] == row
            for c in range(1, top_count):
                taken = taken | (across_ref[c : c + 1, :] == row)
            taken = jnp.where(taken, 1.0, 0.0).astype(jnp.bfloat16)
            out_ref[at : at + step, :] = jnp.dot(
                taken, normed, preferred_element_type=jnp.float32
            ).astype(jnp.bfloat16)
        base += rows


def norm_and_pack(side, residual_in, near, far, gain, across, half, part_total, parts):
    tokens, width = residual_in.shape
    return pl.pallas_call(
        norm_kernel,
        out_shape=tuple([shape_of((part_total, half))] * parts + [shape_of((tokens, half))]),
        in_specs=[SMEM, VMEM, VMEM, VMEM, VMEM, VMEM],
        out_specs=tuple([VMEM] * (parts + 1)),
        scratch_shapes=[pltpu.VMEM((tokens, width), jnp.bfloat16)] * 2,
        compiler_params=pltpu.CompilerParams(vmem_limit_bytes=24 * MIB),
        cost_estimate=cost(2 * part_total * parts * tokens * half, 2 * part_total * parts * half),
        name="norm_and_pack",
    )(side, residual_in, near, far, gain.reshape(1, width), across)


def expert_kernel(
    side_ref, near_ref, far_ref, gate_hbm, up_hbm, down_hbm, kept_ref, sent_ref, x_ref, gate_ref, up_ref, down_ref,
    hidden_ref, y_ref, gate_sem, up_sem, down_sem,
):
    rows, half = near_ref.shape
    hidden_width = gate_ref.shape[1]
    side = side_ref[0]
    step = 2 * LANES
    tile = min(rows, 256)
    gate_loads, up_loads = [], []
    for i in range(hidden_width // step):
        columns = pl.ds(i * step, step)
        gate_loads.append(pltpu.make_async_copy(gate_hbm.at[0, :, columns], gate_ref.at[:, columns], gate_sem.at[i]))
        up_loads.append(pltpu.make_async_copy(up_hbm.at[0, :, columns], up_ref.at[:, columns], up_sem.at[i]))
    down_load = pltpu.make_async_copy(down_hbm.at[0], down_ref, down_sem)
    for load in [load for pair in zip(gate_loads, up_loads) for load in pair] + [down_load]:
        load.start()
    mine = pl.ds(pl.multiple_of(side * half, LANES), half)
    other = pl.ds(pl.multiple_of((1 - side) * half, LANES), half)
    x_ref[:, mine] = near_ref[...]
    x_ref[:, other] = far_ref[...]
    for i in range(hidden_width // step):
        gate_loads[i].wait()
        up_loads[i].wait()
        for at in range(0, rows, tile):
            x = x_ref[at : at + tile, :]
            gate = jnp.dot(x, gate_ref[:, i * step : (i + 1) * step], preferred_element_type=jnp.float32)
            up = jnp.dot(x, up_ref[:, i * step : (i + 1) * step], preferred_element_type=jnp.float32)
            hidden = gate / (1.0 + jnp.exp(-gate)) * up
            hidden_ref[at : at + tile, i * step : (i + 1) * step] = hidden.astype(jnp.bfloat16)
    down_load.wait()
    for at in range(0, rows, tile):
        hidden = hidden_ref[at : at + tile, :]
        for i in range(2 * half // step):
            y_ref[at : at + tile, i * step : (i + 1) * step] = jnp.dot(
                hidden, down_ref[:, i * step : (i + 1) * step], preferred_element_type=jnp.float32
            ).astype(jnp.bfloat16)
    kept_ref[...] = y_ref[:, mine]
    sent_ref[...] = y_ref[:, other]


def expert_layer(side, near, far, w_gate, w_up, w_down):
    rows, half = near.shape
    _, width, hidden_width = w_gate.shape
    tiles = hidden_width // (2 * LANES)
    return pl.pallas_call(
        expert_kernel,
        out_shape=(shape_of((rows, half)), shape_of((rows, half))),
        in_specs=[SMEM, VMEM, VMEM, ANY, ANY, ANY],
        out_specs=(VMEM, VMEM),
        scratch_shapes=[
            pltpu.VMEM((rows, width), jnp.bfloat16),
            pltpu.VMEM((width, hidden_width), jnp.bfloat16),
            pltpu.VMEM((width, hidden_width), jnp.bfloat16),
            pltpu.VMEM((hidden_width, width), jnp.bfloat16),
            pltpu.VMEM((rows, hidden_width), jnp.bfloat16),
            pltpu.VMEM((rows, width), jnp.bfloat16),
            pltpu.SemaphoreType.DMA((tiles,)),
            pltpu.SemaphoreType.DMA((tiles,)),
            pltpu.SemaphoreType.DMA,
        ],
        compiler_params=pltpu.CompilerParams(vmem_limit_bytes=32 * MIB),
        cost_estimate=cost(6 * rows * width * hidden_width, 6 * width * hidden_width, rows * hidden_width),
        name="expert_layer",
    )(side, near, far, w_gate, w_up, w_down)


def combine_kernel(down_ref, weights_ref, kept_ref, *refs):
    *part_refs, out_ref = refs
    tokens, top_count = down_ref.shape
    total = kept_ref[...].astype(jnp.float32)
    base = 0
    for part_ref in part_refs:
        rows = part_ref.shape[0]
        row = iota((tokens, rows), 1) + base
        share = jnp.zeros((tokens, rows), jnp.float32)
        for c in range(top_count):
            share = jnp.where(down_ref[:, c : c + 1] == row, weights_ref[:, c : c + 1], share)
        coarse = share.astype(jnp.bfloat16)
        fine = (share - coarse.astype(jnp.float32)).astype(jnp.bfloat16)
        total += jnp.dot(coarse, part_ref[...], preferred_element_type=jnp.float32)
        total += jnp.dot(fine, part_ref[...], preferred_element_type=jnp.float32)
        base += rows
    out_ref[...] = total.astype(jnp.bfloat16)


def combine(down, weights, kept, returned):
    tokens, half = kept.shape
    rows = sum(part.shape[0] for part in returned)
    return pl.pallas_call(
        combine_kernel,
        out_shape=shape_of((tokens, half)),
        in_specs=[VMEM] * (3 + len(returned)),
        out_specs=VMEM,
        compiler_params=pltpu.CompilerParams(vmem_limit_bytes=24 * MIB),
        cost_estimate=cost(4 * rows * tokens * half, 2 * rows * half),
        name="combine",
    )(down, weights, kept, *returned)


def local(
    residual_in,
    query_rows,
    rotated_key_rows,
    value_row_matrix,
    learned_sink_scores,
    w_out,
    norm_gain,
    expert_ids,
    route_weights,
    w_gate,
    w_up,
    w_down,
):
    tok_dev, model_width = residual_in.shape
    seq_count = lax.axis_size("seq")
    experts = w_gate.shape[0] * seq_count
    capacity = max(2, 8 * tok_dev // experts)
    parts = PARTS if capacity // PARTS >= 16 else 1
    part_rows = capacity // parts
    part_total = experts * part_rows
    half = model_width // lax.axis_size("tp")
    side = lax.axis_index("tp").astype(jnp.int32).reshape(1)
    first = (lax.axis_index("seq") == 0).astype(jnp.int32).reshape(1)

    k_before = passed_along(rotated_key_rows, "seq", 1)
    v_before = passed_along(value_row_matrix, "seq", 1)
    down, across = places(expert_ids, experts, part_rows, parts)
    near = attention(
        first, learned_sink_scores, query_rows, rotated_key_rows, value_row_matrix, k_before, v_before, w_out
    )
    far = swapped(near, "tp")
    *outgoing, kept = norm_and_pack(
        side, residual_in, near, far, norm_gain, across, half, part_total, parts
    )

    def exchanged(block):
        block = block.reshape(seq_count, part_total // seq_count, half)
        block = lax.all_to_all(block, "seq", split_axis=0, concat_axis=0, tiled=True)
        return block.reshape(part_total, half)

    returned = []
    for block in outgoing:
        arrived = exchanged(block)
        other = swapped(arrived, "tp")
        mine, theirs = expert_layer(side, arrived, other, w_gate, w_up, w_down)
        summed = mine.astype(jnp.float32) + swapped(theirs, "tp").astype(jnp.float32)
        returned.append(exchanged(summed.astype(jnp.bfloat16)))
    return combine(down, route_weights, kept, returned)


PARTS = 2


def solution(mesh):
    placed = (
        P("seq", None),
        P("seq", "tp"),
        P("seq", "tp"),
        P("seq", "tp"),
        P("tp"),
        P("tp", None),
        P(),
        P("seq", None),
        P("seq", None),
        P("seq", None, "tp"),
        P("seq", None, "tp"),
        P("seq", "tp", None),
    )
    return jax.shard_map(
        local, mesh=mesh, in_specs=placed, out_specs=P("seq", "tp"), check_vma=False
    )
```

```python
import functools

import jax
import jax.numpy as jnp
from jax import lax
from jax.experimental import pallas as pl
from jax.experimental.pallas import tpu as pltpu
from jax.sharding import PartitionSpec as P

HEAD_SIZE = 64
WINDOW_LENGTH = 128
LANES = 128
MIB = 1024 * 1024

neg_large = -1e30
epsilon = 1e-05

VMEM = pl.BlockSpec(memory_space=pltpu.VMEM)
SMEM = pl.BlockSpec(memory_space=pltpu.SMEM)
HBM = pl.BlockSpec(memory_space=pltpu.HBM)


def passed_along(block, axis, distance):
    devices = range(lax.axis_size(axis))
    route = [(i - distance, i) for i in devices if i - distance in devices]
    return lax.ppermute(block, axis, route)


def swapped(block, axis):
    count = lax.axis_size(axis)
    return lax.ppermute(block, axis, [(i, count - 1 - i) for i in range(count)])


def shape_of(dims, dtype=jnp.bfloat16):
    return jax.ShapeDtypeStruct(dims, dtype)


def cost(flops, moved, transcendentals=0):
    return pl.CostEstimate(flops=flops, bytes_accessed=moved, transcendentals=transcendentals)


def iota(dims, dimension):
    return lax.broadcasted_iota(jnp.int32, dims, dimension)


def place_kernel(experts, side_rows, sides, ids_ref, *out_refs):
    top_count, tokens = ids_ref.shape
    ids = ids_ref[...]
    names = iota((experts, tokens), 0)
    hits = [ids[c : c + 1, :] == names for c in range(top_count)]
    named = sum([hit.astype(jnp.float32) for hit in hits]).astype(jnp.bfloat16)
    square = (tokens, tokens)
    earlier = (iota(square, 0) < iota(square, 1)).astype(jnp.bfloat16)
    slot = jnp.dot(named, earlier, preferred_element_type=jnp.float32)
    part = sum([(slot >= float(k * side_rows)).astype(jnp.float32) for k in range(1, sides)], 0.0)
    rows = names.astype(jnp.float32) * side_rows + slot + part * ((experts - 1) * side_rows)
    lines = [jnp.sum(jnp.where(hit, rows, 0.0), axis=0, keepdims=True) for hit in hits]
    found = jnp.concatenate(lines, axis=0).astype(jnp.int32)
    for out_ref in out_refs:
        out_ref[...] = found


def places(ids, experts, side_rows, sides):
    top_count, tokens = ids.shape
    return pl.pallas_call(
        functools.partial(place_kernel, experts, side_rows, sides),
        out_shape=(shape_of(ids.shape, jnp.int32), shape_of(ids.shape, jnp.int32)),
        in_specs=[VMEM],
        out_specs=(VMEM, VMEM),
        cost_estimate=cost(4 * tokens * tokens * experts, 16 * tokens * top_count),
        name="places",
    )(ids)


def attention_kernel(
    first_ref, sink_ref, q_hbm, k_hbm, v_hbm, before_ref, w_hbm, out_ref, q_ref, k_ref, v_ref, w_ref, att_ref, sems
):
    tokens, width = q_ref.shape
    kv_heads = k_ref.shape[1] // HEAD_SIZE
    pairs = width // LANES // kv_heads
    moves = [(q_hbm, q_ref), (k_hbm, k_ref), (v_hbm, v_ref), (w_hbm, w_ref)]
    *loads, w_load = [pltpu.make_async_copy(source, target, sems.at[i]) for i, (source, target) in enumerate(moves)]
    for load in loads + [w_load]:
        load.start()
    for load in loads:
        load.wait()
    rows = pairs * tokens
    lane = iota((tokens, LANES), 1)
    low = lane < HEAD_SIZE

    def doubled(block, head):
        wide = block.astype(jnp.float32)
        turned = pltpu.roll(wide, HEAD_SIZE, 1)
        first, second = (wide, turned) if head == 0 else (turned, wide)
        return [
            jnp.where(low, first, 0.0).astype(jnp.bfloat16),
            jnp.where(low, 0.0, second).astype(jnp.bfloat16),
        ]

    token = jnp.bitwise_and(iota((rows, 2 * tokens), 0), tokens - 1)
    key = jnp.bitwise_and(iota((rows, 2 * tokens), 1), tokens - 1)
    own = key <= token
    usable = first_ref[0] == 0
    k, v = k_ref[...], v_ref[...]
    k_before, v_before = before_ref[:, :LANES], before_ref[:, LANES:]
    contract = (((1,), (1,)), ((), ()))
    for head in range(kv_heads):
        q = jnp.concatenate(
            [q_ref[:, (head * pairs + j) * LANES : (head * pairs + j + 1) * LANES] for j in range(pairs)], axis=0
        )
        keys = jnp.concatenate(doubled(k, head), axis=0)
        keys_before = jnp.concatenate(doubled(k_before, head), axis=0)
        values = jnp.concatenate(doubled(v, head) + doubled(v_before, head), axis=0)
        near = lax.dot_general(q, keys, contract, preferred_element_type=jnp.float32)
        far = lax.dot_general(q, keys_before, contract, preferred_element_type=jnp.float32)
        far = jnp.where(usable, far * HEAD_SIZE**-0.5, neg_large)
        scores = jnp.where(own, near * HEAD_SIZE**-0.5, far)
        kept_own, kept_before = [], []
        for side in range(2):
            part = scores[:, side * tokens : (side + 1) * tokens]
            sink = jnp.concatenate(
                [jnp.full((tokens, 1), sink_ref[2 * (head * pairs + j) + side], jnp.float32) for j in range(pairs)],
                axis=0,
            )
            top = jnp.maximum(jnp.max(part, axis=1, keepdims=True), sink)
            terms = jnp.exp(part - top)
            total = jnp.sum(terms, axis=1, keepdims=True) + jnp.exp(sink - top)
            prob = terms * (1.0 / total)
            mine = own[:, :tokens]
            kept_own.append(jnp.where(mine, prob, 0.0).astype(jnp.bfloat16))
            kept_before.append(jnp.where(mine, 0.0, prob).astype(jnp.bfloat16))
        probs = jnp.concatenate(kept_own + kept_before, axis=1)
        found = jnp.dot(probs, values, preferred_element_type=jnp.float32).astype(jnp.bfloat16)
        for j in range(pairs):
            at = (head * pairs + j) * LANES
            att_ref[:, at : at + LANES] = found[j * tokens : (j + 1) * tokens]
    w_load.wait()
    step = 2 * LANES
    for at in range(0, out_ref.shape[1], step):
        out_ref[:, at : at + step] = jnp.dot(
            att_ref[...], w_ref[:, at : at + step], preferred_element_type=jnp.float32
        ).astype(jnp.bfloat16)


def attention(first, sinks, q, k, v, before, w_out):
    tokens = q.shape[0]
    return pl.pallas_call(
        attention_kernel,
        out_shape=shape_of((tokens, w_out.shape[1])),
        in_specs=[SMEM, SMEM, HBM, HBM, HBM, VMEM, HBM],
        out_specs=VMEM,
        scratch_shapes=[
            pltpu.VMEM(q.shape, jnp.bfloat16),
            pltpu.VMEM(k.shape, jnp.bfloat16),
            pltpu.VMEM(v.shape, jnp.bfloat16),
            pltpu.VMEM(w_out.shape, jnp.bfloat16),
            pltpu.VMEM(q.shape, jnp.bfloat16),
            pltpu.SemaphoreType.DMA((4,)),
        ],
        compiler_params=pltpu.CompilerParams(vmem_limit_bytes=24 * MIB),
        cost_estimate=cost(2 * tokens * w_out.size * 2, 2 * w_out.size, tokens * tokens * q.shape[1] // HEAD_SIZE),
        name="attention",
    )(first, sinks, q, k, v, before, w_out)


def norm_kernel(
    side_ref, residual_hbm, near_ref, far_ref, gain_ref, across_ref, out_ref, kept_ref, residual_ref, whole_ref, sem
):
    load = pltpu.make_async_copy(residual_hbm, residual_ref, sem)
    load.start()
    tokens, half = kept_ref.shape
    top_count = across_ref.shape[0]
    rows = out_ref.shape[0]
    added = near_ref[...].astype(jnp.float32) + far_ref[...].astype(jnp.float32)
    load.wait()
    whole = (residual_ref[...].astype(jnp.float32) + added).astype(jnp.bfloat16)
    whole_ref[...] = whole
    wide = whole.astype(jnp.float32)
    mean_square = jnp.mean(wide * wide, axis=1, keepdims=True)
    normed = (wide * lax.rsqrt(mean_square + epsilon) * gain_ref[...]).astype(jnp.bfloat16)
    kept_ref[...] = whole_ref[:, pl.ds(pl.multiple_of(side_ref[0] * half, LANES), half)]
    base = side_ref[0] * rows
    step = min(rows, 256)
    for at in range(0, rows, step):
        row = iota((step, tokens), 0) + (base + at)
        taken = across_ref[0:1, :] == row
        for c in range(1, top_count):
            taken = taken | (across_ref[c : c + 1, :] == row)
        taken = jnp.where(taken, 1.0, 0.0).astype(jnp.bfloat16)
        out_ref[at : at + step, :] = jnp.dot(taken, normed, preferred_element_type=jnp.float32).astype(jnp.bfloat16)


def norm_and_pack(side, residual_in, near, far, gain, across, half, rows):
    tokens, width = residual_in.shape
    return pl.pallas_call(
        norm_kernel,
        out_shape=(shape_of((rows, width)), shape_of((tokens, half))),
        in_specs=[SMEM, HBM, VMEM, VMEM, VMEM, VMEM],
        out_specs=(VMEM, VMEM),
        scratch_shapes=[
            pltpu.VMEM((tokens, width), jnp.bfloat16),
            pltpu.VMEM((tokens, width), jnp.bfloat16),
            pltpu.SemaphoreType.DMA,
        ],
        compiler_params=pltpu.CompilerParams(vmem_limit_bytes=24 * MIB),
        cost_estimate=cost(2 * rows * tokens * width, 2 * rows * width),
        name="norm_and_pack",
    )(side, residual_in, near, far, gain.reshape(1, width), across)


def expert_kernel(
    x_ref, gate_hbm, up_hbm, down_hbm, gate_too_hbm, up_too_hbm, down_too_hbm, y_ref, gate_ref, up_ref, down_ref,
    hidden_ref, gate_sem, up_sem, down_sem,
):
    rows, width = x_ref.shape
    share = gate_hbm.shape[2]
    step = 2 * LANES
    tile = min(rows, 256)
    loads = []
    for i in range(2 * share // step):
        gate, up, at = (gate_hbm, up_hbm, i * step) if i * step < share else (gate_too_hbm, up_too_hbm, i * step - share)
        source, target = pl.ds(at, step), pl.ds(i * step, step)
        loads.append(pltpu.make_async_copy(gate.at[0, :, source], gate_ref.at[:, target], gate_sem.at[i]))
        loads.append(pltpu.make_async_copy(up.at[0, :, source], up_ref.at[:, target], up_sem.at[i]))
    down_loads = [
        pltpu.make_async_copy(down_hbm.at[0], down_ref.at[pl.ds(0, share)], down_sem.at[0]),
        pltpu.make_async_copy(down_too_hbm.at[0], down_ref.at[pl.ds(share, share)], down_sem.at[1]),
    ]
    for load in loads + down_loads:
        load.start()
    for i in range(2 * share // step):
        loads[2 * i].wait()
        loads[2 * i + 1].wait()
        for at in range(0, rows, tile):
            x = x_ref[at : at + tile, :]
            gate = jnp.dot(x, gate_ref[:, i * step : (i + 1) * step], preferred_element_type=jnp.float32)
            up = jnp.dot(x, up_ref[:, i * step : (i + 1) * step], preferred_element_type=jnp.float32)
            hidden = gate / (1.0 + jnp.exp(-gate)) * up
            hidden_ref[at : at + tile, i * step : (i + 1) * step] = hidden.astype(jnp.bfloat16)
    for load in down_loads:
        load.wait()
    for at in range(0, rows, tile):
        hidden = hidden_ref[at : at + tile, :]
        for i in range(width // step):
            y_ref[at : at + tile, i * step : (i + 1) * step] = jnp.dot(
                hidden, down_ref[:, i * step : (i + 1) * step], preferred_element_type=jnp.float32
            ).astype(jnp.bfloat16)


def expert_layer(x, mine, others):
    rows, width = x.shape
    hidden_width = 2 * mine[0].shape[2]
    tiles = hidden_width // (2 * LANES)
    return pl.pallas_call(
        expert_kernel,
        out_shape=shape_of((rows, width)),
        in_specs=[VMEM] + [HBM] * 6,
        out_specs=VMEM,
        scratch_shapes=[
            pltpu.VMEM((width, hidden_width), jnp.bfloat16),
            pltpu.VMEM((width, hidden_width), jnp.bfloat16),
            pltpu.VMEM((hidden_width, width), jnp.bfloat16),
            pltpu.VMEM((rows, hidden_width), jnp.bfloat16),
            pltpu.SemaphoreType.DMA((tiles,)),
            pltpu.SemaphoreType.DMA((tiles,)),
            pltpu.SemaphoreType.DMA((2,)),
        ],
        compiler_params=pltpu.CompilerParams(vmem_limit_bytes=40 * MIB),
        cost_estimate=cost(6 * rows * width * hidden_width, 6 * width * hidden_width, rows * hidden_width),
        name="expert_layer",
    )(x, *mine, *others)


def combine_kernel(side_ref, across_ref, weights_ref, kept_ref, y_ref, mine_ref, sent_ref, total_ref):
    top_count, tokens = across_ref.shape
    half = kept_ref.shape[1]
    rows = y_ref.shape[0]
    base = side_ref[0] * rows
    step = min(rows, 256)
    total_ref[...] = jnp.zeros(total_ref.shape, jnp.float32)
    contract = (((0,), (0,)), ((), ()))
    for at in range(0, rows, step):
        row = iota((step, tokens), 0) + (base + at)
        share = jnp.zeros((step, tokens), jnp.float32)
        for c in range(top_count):
            share = jnp.where(across_ref[c : c + 1, :] == row, weights_ref[c : c + 1, :], share)
        coarse = share.astype(jnp.bfloat16)
        fine = (share - coarse.astype(jnp.float32)).astype(jnp.bfloat16)
        y = y_ref[at : at + step, :]
        total_ref[...] += lax.dot_general(
            coarse, y, contract, preferred_element_type=jnp.float32
        ) + lax.dot_general(fine, y, contract, preferred_element_type=jnp.float32)
    mine = pl.ds(pl.multiple_of(side_ref[0] * half, LANES), half)
    other = pl.ds(pl.multiple_of((1 - side_ref[0]) * half, LANES), half)
    mine_ref[...] = kept_ref[...].astype(jnp.float32) + total_ref[:, mine]
    sent_ref[...] = total_ref[:, other].astype(jnp.bfloat16)


def combine(side, across, weights, kept, y):
    tokens, half = kept.shape
    rows, width = y.shape
    return pl.pallas_call(
        combine_kernel,
        out_shape=(shape_of((tokens, half), jnp.float32), shape_of((tokens, half))),
        in_specs=[SMEM, VMEM, VMEM, VMEM, VMEM],
        out_specs=(VMEM, VMEM),
        scratch_shapes=[pltpu.VMEM((tokens, width), jnp.float32)],
        compiler_params=pltpu.CompilerParams(vmem_limit_bytes=24 * MIB),
        cost_estimate=cost(4 * rows * tokens * width, 2 * rows * width),
        name="combine",
    )(side, across, weights, kept, y)


def local(
    residual_in,
    query_rows,
    rotated_key_rows,
    value_row_matrix,
    learned_sink_scores,
    w_out,
    norm_gain,
    expert_ids,
    route_weights,
    w_gate,
    w_up,
    w_down,
):
    tok_dev, model_width = residual_in.shape
    seq_count = lax.axis_size("seq")
    experts = w_gate.shape[0] * seq_count
    capacity = max(2, 8 * tok_dev // experts)
    sides = lax.axis_size("tp")
    side_rows = capacity // sides
    rows = experts * side_rows
    half = model_width // sides
    side = lax.axis_index("tp").astype(jnp.int32).reshape(1)
    first = (lax.axis_index("seq") == 0).astype(jnp.int32).reshape(1)

    before = passed_along(jnp.concatenate([rotated_key_rows, value_row_matrix], axis=1), "seq", 1)
    weights = (w_gate, w_up, w_down)
    others = [swapped(weight, "tp") for weight in weights]
    across, across_again = places(expert_ids.T, experts, side_rows, sides)
    near = attention(first, learned_sink_scores, query_rows, rotated_key_rows, value_row_matrix, before, w_out)
    far = swapped(near, "tp")
    outgoing, kept = norm_and_pack(side, residual_in, near, far, norm_gain, across, half, rows)

    def exchanged(block):
        block = block.reshape(seq_count, rows // seq_count, model_width)
        block = lax.all_to_all(block, "seq", split_axis=0, concat_axis=0, tiled=True)
        return block.reshape(rows, model_width)

    returned = exchanged(expert_layer(exchanged(outgoing), weights, others))
    mine, sent = combine(side, across_again, route_weights.T, kept, returned)
    return (mine + swapped(sent, "tp").astype(jnp.float32)).astype(jnp.bfloat16)


def solution(mesh):
    placed = (
        P("seq", None),
        P("seq", "tp"),
        P("seq", "tp"),
        P("seq", "tp"),
        P("tp"),
        P("tp", None),
        P(),
        P("seq", None),
        P("seq", None),
        P("seq", None, "tp"),
        P("seq", None, "tp"),
        P("seq", "tp", None),
    )
    return jax.shard_map(
        local, mesh=mesh, in_specs=placed, out_specs=P("seq", "tp"), check_vma=False
    )
```

```python
import functools

import jax
import jax.numpy as jnp
from jax import lax
from jax.experimental import pallas as pl
from jax.experimental.pallas import tpu as pltpu
from jax.sharding import PartitionSpec as P

HEAD_SIZE = 64
WINDOW_LENGTH = 128
LANES = 128
MIB = 1024 * 1024

neg_large = -1e30
epsilon = 1e-05

VMEM = pl.BlockSpec(memory_space=pltpu.VMEM)
SMEM = pl.BlockSpec(memory_space=pltpu.SMEM)
HBM = pl.BlockSpec(memory_space=pltpu.HBM)


def passed_along(block, axis, distance):
    devices = range(lax.axis_size(axis))
    route = [(i - distance, i) for i in devices if i - distance in devices]
    return lax.ppermute(block, axis, route)


def swapped(block, axis):
    count = lax.axis_size(axis)
    return lax.ppermute(block, axis, [(i, count - 1 - i) for i in range(count)])


def swapped_halves(block, axis):
    count = lax.axis_size(axis)
    return lax.ppermute(block, axis, [(i, (i + count // 2) % count) for i in range(count)])


def shape_of(dims, dtype=jnp.bfloat16):
    return jax.ShapeDtypeStruct(dims, dtype)


def cost(flops, moved, transcendentals=0):
    return pl.CostEstimate(flops=flops, bytes_accessed=moved, transcendentals=transcendentals)


def iota(dims, dimension):
    return lax.broadcasted_iota(jnp.int32, dims, dimension)


def rows_of(ids, experts, side_rows, base, side):
    top_count, tokens = ids.shape
    names = iota((experts, tokens), 0).astype(jnp.float32)
    hits = [ids[c : c + 1, :] == names for c in range(top_count)]
    named = sum([hit.astype(jnp.float32) for hit in hits]).astype(jnp.bfloat16)
    square = (tokens, tokens)
    earlier = (iota(square, 0) < iota(square, 1)).astype(jnp.bfloat16)
    slot = jnp.dot(named, earlier, preferred_element_type=jnp.float32) - (side * side_rows).astype(jnp.float32)
    expert = names - base.astype(jnp.float32)
    here = (slot >= 0.0) & (slot < side_rows) & (expert >= 0.0) & (expert < experts // 2)
    rows = jnp.where(here, expert * side_rows + slot, -1.0)
    lines = [jnp.sum(jnp.where(hit, rows, 0.0), axis=0, keepdims=True) for hit in hits]
    return jnp.concatenate(lines, axis=0).astype(jnp.int32)


def place_kernel(experts, side_rows, where_ref, notes_ref, notes_peer_ref, own_ref, peer_ref):
    top_count = own_ref.shape[0]
    base, side = where_ref[0], where_ref[1]
    own_ref[...] = rows_of(notes_ref[:top_count, :], experts, side_rows, base, side)
    peer_ref[...] = rows_of(notes_peer_ref[:top_count, :], experts, side_rows, base, side)


def places(where, notes, notes_peer, experts, side_rows):
    top_count, tokens = notes.shape[0] // 2, notes.shape[1]
    return pl.pallas_call(
        functools.partial(place_kernel, experts, side_rows),
        out_shape=(shape_of((top_count, tokens), jnp.int32), shape_of((top_count, tokens), jnp.int32)),
        in_specs=[SMEM, VMEM, VMEM],
        out_specs=(VMEM, VMEM),
        cost_estimate=cost(4 * tokens * tokens * experts, 16 * tokens * top_count),
        name="places",
    )(where, notes, notes_peer)


def attention_kernel(
    first_ref, sink_hbm, q_hbm, k_hbm, v_hbm, before_ref, w_hbm, out_ref, sink_ref, q_ref, k_ref, v_ref, w_ref,
    att_ref, sems,
):
    tokens, width = q_ref.shape
    kv_heads = k_ref.shape[1] // HEAD_SIZE
    pairs = width // LANES // kv_heads
    moves = [(sink_hbm, sink_ref), (q_hbm, q_ref), (k_hbm, k_ref), (v_hbm, v_ref), (w_hbm, w_ref)]
    *loads, w_load = [pltpu.make_async_copy(source, target, sems.at[i]) for i, (source, target) in enumerate(moves)]
    for load in loads + [w_load]:
        load.start()
    for load in loads:
        load.wait()
    rows = pairs * tokens
    lane = iota((tokens, LANES), 1)
    low = lane < HEAD_SIZE

    def doubled(block, head):
        wide = block.astype(jnp.float32)
        turned = pltpu.roll(wide, HEAD_SIZE, 1)
        first, second = (wide, turned) if head == 0 else (turned, wide)
        return [
            jnp.where(low, first, 0.0).astype(jnp.bfloat16),
            jnp.where(low, 0.0, second).astype(jnp.bfloat16),
        ]

    token = jnp.bitwise_and(iota((rows, 2 * tokens), 0), tokens - 1)
    key = jnp.bitwise_and(iota((rows, 2 * tokens), 1), tokens - 1)
    own = key <= token
    usable = first_ref[0] == 0
    k, v = k_ref[...], v_ref[...]
    k_before, v_before = before_ref[:, :LANES], before_ref[:, LANES:]
    contract = (((1,), (1,)), ((), ()))
    for head in range(kv_heads):
        q = jnp.concatenate(
            [q_ref[:, (head * pairs + j) * LANES : (head * pairs + j + 1) * LANES] for j in range(pairs)], axis=0
        )
        keys = jnp.concatenate(doubled(k, head), axis=0)
        keys_before = jnp.concatenate(doubled(k_before, head), axis=0)
        values = jnp.concatenate(doubled(v, head) + doubled(v_before, head), axis=0)
        near = lax.dot_general(q, keys, contract, preferred_element_type=jnp.float32)
        far = lax.dot_general(q, keys_before, contract, preferred_element_type=jnp.float32)
        far = jnp.where(usable, far * HEAD_SIZE**-0.5, neg_large)
        scores = jnp.where(own, near * HEAD_SIZE**-0.5, far)
        kept_own, kept_before = [], []
        for side in range(2):
            part = scores[:, side * tokens : (side + 1) * tokens]
            sink = jnp.concatenate(
                [jnp.full((tokens, 1), sink_ref[2 * (head * pairs + j) + side], jnp.float32) for j in range(pairs)],
                axis=0,
            )
            top = jnp.maximum(jnp.max(part, axis=1, keepdims=True), sink)
            terms = jnp.exp(part - top)
            total = jnp.sum(terms, axis=1, keepdims=True) + jnp.exp(sink - top)
            prob = terms * (1.0 / total)
            mine = own[:, :tokens]
            kept_own.append(jnp.where(mine, prob, 0.0).astype(jnp.bfloat16))
            kept_before.append(jnp.where(mine, 0.0, prob).astype(jnp.bfloat16))
        probs = jnp.concatenate(kept_own + kept_before, axis=1)
        found = jnp.dot(probs, values, preferred_element_type=jnp.float32).astype(jnp.bfloat16)
        for j in range(pairs):
            at = (head * pairs + j) * LANES
            att_ref[:, at : at + LANES] = found[j * tokens : (j + 1) * tokens]
    w_load.wait()
    step = 2 * LANES
    for at in range(0, out_ref.shape[1], step):
        out_ref[:, at : at + step] = jnp.dot(
            att_ref[...], w_ref[:, at : at + step], preferred_element_type=jnp.float32
        ).astype(jnp.bfloat16)


def attention(first, sinks, q, k, v, before, w_out):
    tokens = q.shape[0]
    return pl.pallas_call(
        attention_kernel,
        out_shape=shape_of((tokens, w_out.shape[1])),
        in_specs=[SMEM, HBM, HBM, HBM, HBM, VMEM, HBM],
        out_specs=VMEM,
        scratch_shapes=[
            pltpu.SMEM(sinks.shape, jnp.float32),
            pltpu.VMEM(q.shape, jnp.bfloat16),
            pltpu.VMEM(k.shape, jnp.bfloat16),
            pltpu.VMEM(v.shape, jnp.bfloat16),
            pltpu.VMEM(w_out.shape, jnp.bfloat16),
            pltpu.VMEM(q.shape, jnp.bfloat16),
            pltpu.SemaphoreType.DMA((5,)),
        ],
        compiler_params=pltpu.CompilerParams(vmem_limit_bytes=60 * MIB),
        cost_estimate=cost(2 * tokens * w_out.size * 2, 2 * w_out.size, tokens * tokens * q.shape[1] // HEAD_SIZE),
        name="attention",
    )(first, sinks, q, k, v, before, w_out)


def pack(rows_ref, normed, out_ref):
    rows, tokens = out_ref.shape[0], normed.shape[0]
    row = iota((rows, tokens), 0)
    taken = rows_ref[0:1, :] == row
    for c in range(1, rows_ref.shape[0]):
        taken = taken | (rows_ref[c : c + 1, :] == row)
    taken = jnp.where(taken, 1.0, 0.0).astype(jnp.bfloat16)
    out_ref[...] = jnp.dot(taken, normed, preferred_element_type=jnp.float32).astype(jnp.bfloat16)


def norm_kernel(
    where_ref, residual_hbm, near_ref, far_ref, gain_ref, rows_ref, out_ref, sent_ref, kept_ref, residual_ref,
    whole_ref, normed_ref, sem,
):
    load = pltpu.make_async_copy(residual_hbm, residual_ref, sem)
    load.start()
    side = where_ref[1]
    half_tokens, half = sent_ref.shape[0], kept_ref.shape[1]
    added = near_ref[...].astype(jnp.float32) + far_ref[...].astype(jnp.float32)
    load.wait()
    whole = (residual_ref[...].astype(jnp.float32) + added).astype(jnp.bfloat16)
    whole_ref[...] = whole
    wide = whole.astype(jnp.float32)
    mean_square = jnp.mean(wide * wide, axis=1, keepdims=True)
    normed = (wide * lax.rsqrt(mean_square + epsilon) * gain_ref[...]).astype(jnp.bfloat16)
    normed_ref[...] = normed
    kept_ref[...] = whole_ref[:, pl.ds(pl.multiple_of(side * half, LANES), half)]
    sent_ref[...] = normed_ref[pl.ds(pl.multiple_of(side * half_tokens, half_tokens), half_tokens), :]
    pack(rows_ref, normed, out_ref)


def norm_and_pack(where, residual_in, near, far, gain, placed, half, rows):
    tokens, width = residual_in.shape
    return pl.pallas_call(
        norm_kernel,
        out_shape=(shape_of((rows, width)), shape_of((tokens // 2, width)), shape_of((tokens, half))),
        in_specs=[SMEM, HBM, VMEM, VMEM, VMEM, VMEM],
        out_specs=(VMEM, VMEM, VMEM),
        scratch_shapes=[pltpu.VMEM((tokens, width), jnp.bfloat16)] * 3 + [pltpu.SemaphoreType.DMA],
        compiler_params=pltpu.CompilerParams(vmem_limit_bytes=24 * MIB),
        cost_estimate=cost(2 * rows * tokens * width, 2 * rows * width),
        name="norm_and_pack",
    )(where, residual_in, near, far, gain.reshape(1, width), placed)


def peer_kernel(where_ref, mine_ref, other_ref, rows_ref, out_ref, normed_ref):
    side, part = where_ref[1], mine_ref.shape[0]
    normed_ref[pl.ds(pl.multiple_of(side * part, part), part), :] = mine_ref[...]
    normed_ref[pl.ds(pl.multiple_of((1 - side) * part, part), part), :] = other_ref[...]
    pack(rows_ref, normed_ref[...], out_ref)


def pack_peer(where, mine, other, placed, rows):
    part, width = mine.shape
    return pl.pallas_call(
        peer_kernel,
        out_shape=shape_of((rows, width)),
        in_specs=[SMEM, VMEM, VMEM, VMEM],
        out_specs=VMEM,
        scratch_shapes=[pltpu.VMEM((2 * part, width), jnp.bfloat16)],
        compiler_params=pltpu.CompilerParams(vmem_limit_bytes=24 * MIB),
        cost_estimate=cost(4 * rows * part * width, 2 * rows * width),
        name="pack_peer",
    )(where, mine, other, placed)


def expert_kernel(
    x_hbm, gate_hbm, up_hbm, down_hbm, gate_too_hbm, up_too_hbm, down_too_hbm, y_hbm, x_ref, y_ref, gate_ref, up_ref,
    down_ref, hidden_ref, x_sem, y_sem, gate_sem, up_sem, down_sem,
):
    rows, width = x_ref.shape
    x_load = pltpu.make_async_copy(x_hbm, x_ref, x_sem)
    x_load.start()
    share = gate_hbm.shape[2]
    step = 2 * LANES
    tile = min(rows, 256)
    loads = []
    for i in range(2 * share // step):
        gate, up, at = (gate_hbm, up_hbm, i * step) if i * step < share else (gate_too_hbm, up_too_hbm, i * step - share)
        source, target = pl.ds(at, step), pl.ds(i * step, step)
        loads.append(pltpu.make_async_copy(gate.at[0, :, source], gate_ref.at[:, target], gate_sem.at[i]))
        loads.append(pltpu.make_async_copy(up.at[0, :, source], up_ref.at[:, target], up_sem.at[i]))
    down_loads = [
        pltpu.make_async_copy(down_hbm.at[0], down_ref.at[pl.ds(0, share)], down_sem.at[0]),
        pltpu.make_async_copy(down_too_hbm.at[0], down_ref.at[pl.ds(share, share)], down_sem.at[1]),
    ]
    for load in loads + down_loads:
        load.start()
    x_load.wait()
    for i in range(2 * share // step):
        loads[2 * i].wait()
        loads[2 * i + 1].wait()
        for at in range(0, rows, tile):
            x = x_ref[at : at + tile, :]
            gate = jnp.dot(x, gate_ref[:, i * step : (i + 1) * step], preferred_element_type=jnp.float32)
            up = jnp.dot(x, up_ref[:, i * step : (i + 1) * step], preferred_element_type=jnp.float32)
            hidden = gate / (1.0 + jnp.exp(-gate)) * up
            hidden_ref[at : at + tile, i * step : (i + 1) * step] = hidden.astype(jnp.bfloat16)
    for load in down_loads:
        load.wait()
    stores = []
    for i in range(width // step):
        columns = pl.ds(i * step, step)
        for at in range(0, rows, tile):
            y_ref[at : at + tile, i * step : (i + 1) * step] = jnp.dot(
                hidden_ref[at : at + tile, :], down_ref[:, i * step : (i + 1) * step],
                preferred_element_type=jnp.float32,
            ).astype(jnp.bfloat16)
        stores.append(pltpu.make_async_copy(y_ref.at[:, columns], y_hbm.at[:, columns], y_sem.at[i]))
        stores[i].start()
    for store in stores:
        store.wait()


def expert_layer(x, mine, others):
    rows, width = x.shape
    hidden_width = 2 * mine[0].shape[2]
    tiles = hidden_width // (2 * LANES)
    return pl.pallas_call(
        expert_kernel,
        out_shape=shape_of((rows, width)),
        in_specs=[HBM] * 7,
        out_specs=HBM,
        scratch_shapes=[
            pltpu.VMEM((rows, width), jnp.bfloat16),
            pltpu.VMEM((rows, width), jnp.bfloat16),
            pltpu.VMEM((width, hidden_width), jnp.bfloat16),
            pltpu.VMEM((width, hidden_width), jnp.bfloat16),
            pltpu.VMEM((hidden_width, width), jnp.bfloat16),
            pltpu.VMEM((rows, hidden_width), jnp.bfloat16),
            pltpu.SemaphoreType.DMA,
            pltpu.SemaphoreType.DMA((width // (2 * LANES),)),
            pltpu.SemaphoreType.DMA((tiles,)),
            pltpu.SemaphoreType.DMA((tiles,)),
            pltpu.SemaphoreType.DMA((2,)),
        ],
        compiler_params=pltpu.CompilerParams(vmem_limit_bytes=60 * MIB),
        cost_estimate=cost(6 * rows * width * hidden_width, 6 * width * hidden_width, rows * hidden_width),
        name="expert_layer",
    )(x, *mine, *others)


def combine_kernel(where_ref, rows_ref, weights_ref, y_ref, mine_ref, sent_ref, total_ref):
    top_count, tokens = rows_ref.shape
    half = mine_ref.shape[1]
    row = iota((y_ref.shape[0], tokens), 0)
    share = jnp.zeros(row.shape, jnp.float32)
    for c in range(top_count):
        share = jnp.where(rows_ref[c : c + 1, :] == row, weights_ref[c : c + 1, :], share)
    coarse = share.astype(jnp.bfloat16)
    fine = (share - coarse.astype(jnp.float32)).astype(jnp.bfloat16)
    y = y_ref[...]
    contract = (((0,), (0,)), ((), ()))
    total_ref[...] = lax.dot_general(coarse, y, contract, preferred_element_type=jnp.float32)
    total_ref[...] += lax.dot_general(fine, y, contract, preferred_element_type=jnp.float32)
    side = where_ref[1]
    mine_ref[...] = total_ref[:, pl.ds(pl.multiple_of(side * half, LANES), half)]
    sent_ref[...] = total_ref[:, pl.ds(pl.multiple_of((1 - side) * half, LANES), half)].astype(jnp.bfloat16)


def combine(where, placed, weights, y, half):
    tokens = placed.shape[1]
    rows, width = y.shape
    return pl.pallas_call(
        combine_kernel,
        out_shape=(shape_of((tokens, half), jnp.float32), shape_of((tokens, half))),
        in_specs=[SMEM, VMEM, VMEM, VMEM],
        out_specs=(VMEM, VMEM),
        scratch_shapes=[pltpu.VMEM((tokens, width), jnp.float32)],
        compiler_params=pltpu.CompilerParams(vmem_limit_bytes=24 * MIB),
        cost_estimate=cost(4 * rows * tokens * width, 2 * rows * width),
        name="combine",
    )(where, placed, weights, y)


def local(
    residual_in,
    query_rows,
    rotated_key_rows,
    value_row_matrix,
    learned_sink_scores,
    w_out,
    norm_gain,
    expert_ids,
    route_weights,
    w_gate,
    w_up,
    w_down,
):
    tok_dev, model_width = residual_in.shape
    seq_count = lax.axis_size("seq")
    experts = w_gate.shape[0] * seq_count
    top_count = expert_ids.shape[1]
    capacity = max(2, 8 * tok_dev // experts)
    sides = lax.axis_size("tp")
    side_rows = capacity // sides
    group = seq_count // 2
    rows = experts // 2 * side_rows
    half = model_width // sides
    at_seq = lax.axis_index("seq").astype(jnp.int32)
    base = at_seq // group * (experts // 2)
    where = jnp.stack([base, lax.axis_index("tp").astype(jnp.int32)])
    first = (at_seq == 0).astype(jnp.int32).reshape(1)

    before = passed_along(jnp.concatenate([rotated_key_rows, value_row_matrix], axis=1), "seq", 1)
    notes = jnp.concatenate([expert_ids.T.astype(jnp.float32), route_weights.T], axis=0)
    notes_peer = swapped_halves(notes, "seq")
    weights = (w_gate, w_up, w_down)
    others = [swapped(weight, "tp") for weight in weights]
    placed, placed_peer = places(where, notes, notes_peer, experts, side_rows)
    near = attention(first, learned_sink_scores, query_rows, rotated_key_rows, value_row_matrix, before, w_out)
    far = swapped(near, "tp")
    packed, sent, kept = norm_and_pack(where, residual_in, near, far, norm_gain, placed, half, rows)

    def exchanged(block):
        block = block.reshape(group, rows // group, model_width)
        groups = [list(range(group)), list(range(group, seq_count))]
        block = lax.all_to_all(
            block, "seq", split_axis=0, concat_axis=0, axis_index_groups=groups, tiled=True
        )
        return block.reshape(rows, model_width)

    crossed = swapped_halves(sent, "seq")
    arrived = exchanged(packed)
    packed_peer = pack_peer(where, crossed, swapped(crossed, "tp"), placed_peer, rows)
    arrived_peer = exchanged(packed_peer)
    result = expert_layer(arrived, weights, others)
    result_peer = expert_layer(arrived_peer, weights, others)

    returned_peer = exchanged(result_peer)
    returned = exchanged(result)
    mine_peer, sent_peer = combine(where, placed_peer, notes_peer[top_count:], returned_peer, half)
    summed_peer = (mine_peer + swapped(sent_peer, "tp").astype(jnp.float32)).astype(jnp.bfloat16)
    back = swapped_halves(summed_peer, "seq").astype(jnp.float32)
    mine, sent = combine(where, placed, notes[top_count:], returned, half)
    total = mine + swapped(sent, "tp").astype(jnp.float32) + back
    return (kept.astype(jnp.float32) + total).astype(jnp.bfloat16)


def solution(mesh):
    placed = (
        P("seq", None),
        P("seq", "tp"),
        P("seq", "tp"),
        P("seq", "tp"),
        P("tp"),
        P("tp", None),
        P(),
        P("seq", None),
        P("seq", None),
        P("seq", None, "tp"),
        P("seq", None, "tp"),
        P("seq", "tp", None),
    )
    return jax.shard_map(
        local, mesh=mesh, in_specs=placed, out_specs=P("seq", "tp"), check_vma=False
    )
```

```python
import functools

import jax
import jax.numpy as jnp
from jax import lax
from jax.experimental import pallas as pl
from jax.experimental.pallas import tpu as pltpu
from jax.sharding import PartitionSpec as P

HEAD_SIZE = 64
WINDOW_LENGTH = 128
LANES = 128
MIB = 1024 * 1024

neg_large = -1e30
epsilon = 1e-05

VMEM = pl.BlockSpec(memory_space=pltpu.VMEM)
SMEM = pl.BlockSpec(memory_space=pltpu.SMEM)
HBM = pl.BlockSpec(memory_space=pltpu.HBM)


def passed_along(block, axis, distance):
    devices = range(lax.axis_size(axis))
    route = [(i - distance, i) for i in devices if i - distance in devices]
    return lax.ppermute(block, axis, route)


def swapped(block, axis):
    count = lax.axis_size(axis)
    return lax.ppermute(block, axis, [(i, count - 1 - i) for i in range(count)])


def swapped_halves(block, axis):
    count = lax.axis_size(axis)
    return lax.ppermute(block, axis, [(i, (i + count // 2) % count) for i in range(count)])


def shape_of(dims, dtype=jnp.bfloat16):
    return jax.ShapeDtypeStruct(dims, dtype)


def cost(flops, moved, transcendentals=0):
    return pl.CostEstimate(flops=flops, bytes_accessed=moved, transcendentals=transcendentals)


def iota(dims, dimension):
    return lax.broadcasted_iota(jnp.int32, dims, dimension)


def rows_of(ids, experts, side_rows, base, side):
    top_count, tokens = ids.shape
    names = iota((experts, tokens), 0).astype(jnp.float32)
    hits = [ids[c : c + 1, :] == names for c in range(top_count)]
    named = sum([hit.astype(jnp.float32) for hit in hits]).astype(jnp.bfloat16)
    square = (tokens, tokens)
    earlier = (iota(square, 0) < iota(square, 1)).astype(jnp.bfloat16)
    slot = jnp.dot(named, earlier, preferred_element_type=jnp.float32) - (side * side_rows).astype(jnp.float32)
    expert = names - base.astype(jnp.float32)
    here = (slot >= 0.0) & (slot < side_rows) & (expert >= 0.0) & (expert < experts // 2)
    rows = jnp.where(here, expert * side_rows + slot, -1.0)
    lines = [jnp.sum(jnp.where(hit, rows, 0.0), axis=0, keepdims=True) for hit in hits]
    return jnp.concatenate(lines, axis=0).astype(jnp.int32)


def place_kernel(experts, side_rows, base_ref, side_ref, ids_ref, rows_ref):
    rows_ref[...] = rows_of(ids_ref[...].astype(jnp.float32), experts, side_rows, base_ref[0], side_ref[0])


def places(base, side, ids, experts, side_rows):
    top_count, tokens = ids.shape
    return pl.pallas_call(
        functools.partial(place_kernel, experts, side_rows),
        out_shape=shape_of(ids.shape, jnp.int32),
        in_specs=[SMEM, SMEM, VMEM],
        out_specs=VMEM,
        cost_estimate=cost(2 * tokens * tokens * experts, 8 * tokens * top_count),
        name="places",
    )(base, side, ids)


def attention_kernel(
    first_ref, sink_hbm, q_hbm, k_hbm, v_hbm, before_ref, w_hbm, out_ref, sink_ref, q_ref, k_ref, v_ref, w_ref,
    att_ref, sems,
):
    tokens, width = q_ref.shape
    kv_heads = k_ref.shape[1] // HEAD_SIZE
    pairs = width // LANES // kv_heads
    moves = [(sink_hbm, sink_ref), (q_hbm, q_ref), (k_hbm, k_ref), (v_hbm, v_ref), (w_hbm, w_ref)]
    *loads, w_load = [pltpu.make_async_copy(source, target, sems.at[i]) for i, (source, target) in enumerate(moves)]
    for load in loads + [w_load]:
        load.start()
    for load in loads:
        load.wait()
    rows = pairs * tokens
    lane = iota((tokens, LANES), 1)
    low = lane < HEAD_SIZE

    def doubled(block, head):
        wide = block.astype(jnp.float32)
        turned = pltpu.roll(wide, HEAD_SIZE, 1)
        first, second = (wide, turned) if head == 0 else (turned, wide)
        return [
            jnp.where(low, first, 0.0).astype(jnp.bfloat16),
            jnp.where(low, 0.0, second).astype(jnp.bfloat16),
        ]

    token = jnp.bitwise_and(iota((rows, 2 * tokens), 0), tokens - 1)
    key = jnp.bitwise_and(iota((rows, 2 * tokens), 1), tokens - 1)
    own = key <= token
    usable = first_ref[0] == 0
    k, v = k_ref[...], v_ref[...]
    k_before, v_before = before_ref[:, :LANES], before_ref[:, LANES:]
    contract = (((1,), (1,)), ((), ()))
    for head in range(kv_heads):
        q = jnp.concatenate(
            [q_ref[:, (head * pairs + j) * LANES : (head * pairs + j + 1) * LANES] for j in range(pairs)], axis=0
        )
        keys = jnp.concatenate(doubled(k, head), axis=0)
        keys_before = jnp.concatenate(doubled(k_before, head), axis=0)
        values = jnp.concatenate(doubled(v, head) + doubled(v_before, head), axis=0)
        near = lax.dot_general(q, keys, contract, preferred_element_type=jnp.float32)
        far = lax.dot_general(q, keys_before, contract, preferred_element_type=jnp.float32)
        far = jnp.where(usable, far * HEAD_SIZE**-0.5, neg_large)
        scores = jnp.where(own, near * HEAD_SIZE**-0.5, far)
        kept_own, kept_before = [], []
        for side in range(2):
            part = scores[:, side * tokens : (side + 1) * tokens]
            sink = jnp.concatenate(
                [jnp.full((tokens, 1), sink_ref[2 * (head * pairs + j) + side], jnp.float32) for j in range(pairs)],
                axis=0,
            )
            top = jnp.maximum(jnp.max(part, axis=1, keepdims=True), sink)
            terms = jnp.exp(part - top)
            total = jnp.sum(terms, axis=1, keepdims=True) + jnp.exp(sink - top)
            prob = terms * (1.0 / total)
            mine = own[:, :tokens]
            kept_own.append(jnp.where(mine, prob, 0.0).astype(jnp.bfloat16))
            kept_before.append(jnp.where(mine, 0.0, prob).astype(jnp.bfloat16))
        probs = jnp.concatenate(kept_own + kept_before, axis=1)
        found = jnp.dot(probs, values, preferred_element_type=jnp.float32).astype(jnp.bfloat16)
        for j in range(pairs):
            at = (head * pairs + j) * LANES
            att_ref[:, at : at + LANES] = found[j * tokens : (j + 1) * tokens]
    w_load.wait()
    step = 2 * LANES
    for at in range(0, out_ref.shape[1], step):
        out_ref[:, at : at + step] = jnp.dot(
            att_ref[...], w_ref[:, at : at + step], preferred_element_type=jnp.float32
        ).astype(jnp.bfloat16)


def attention(first, sinks, q, k, v, before, w_out):
    tokens = q.shape[0]
    return pl.pallas_call(
        attention_kernel,
        out_shape=shape_of((tokens, w_out.shape[1])),
        in_specs=[SMEM, HBM, HBM, HBM, HBM, VMEM, HBM],
        out_specs=VMEM,
        scratch_shapes=[
            pltpu.SMEM(sinks.shape, jnp.float32),
            pltpu.VMEM(q.shape, jnp.bfloat16),
            pltpu.VMEM(k.shape, jnp.bfloat16),
            pltpu.VMEM(v.shape, jnp.bfloat16),
            pltpu.VMEM(w_out.shape, jnp.bfloat16),
            pltpu.VMEM(q.shape, jnp.bfloat16),
            pltpu.SemaphoreType.DMA((5,)),
        ],
        compiler_params=pltpu.CompilerParams(vmem_limit_bytes=60 * MIB),
        cost_estimate=cost(2 * tokens * w_out.size * 2, 2 * w_out.size, tokens * tokens * q.shape[1] // HEAD_SIZE),
        name="attention",
    )(first, sinks, q, k, v, before, w_out)


def pack(placed, normed, out_ref):
    rows, tokens = out_ref.shape[0], normed.shape[0]
    row = iota((rows, tokens), 0)
    taken = placed[0:1, :] == row
    for c in range(1, placed.shape[0]):
        taken = taken | (placed[c : c + 1, :] == row)
    taken = jnp.where(taken, 1.0, 0.0).astype(jnp.bfloat16)
    out_ref[...] = jnp.dot(taken, normed, preferred_element_type=jnp.float32).astype(jnp.bfloat16)


def noted(ids, weights):
    coarse = weights.astype(jnp.bfloat16).astype(jnp.float32)
    middle = (weights - coarse).astype(jnp.bfloat16).astype(jnp.float32)
    fine = weights - coarse - middle
    used = [ids.astype(jnp.float32), coarse, middle, fine]
    empty = jnp.zeros((LANES - 4 * ids.shape[0], ids.shape[1]), jnp.float32)
    return jnp.concatenate(used + [empty], axis=0).T.astype(jnp.bfloat16)


def norm_kernel(
    side_ref, residual_ref, near_ref, far_ref, gain_ref, rows_ref, ids_ref, weights_ref, out_ref, sent_ref, kept_ref,
    whole_ref, sending_ref,
):
    side = side_ref[0]
    half_tokens, half, width = sent_ref.shape[0], kept_ref.shape[1], whole_ref.shape[1]
    added = near_ref[...].astype(jnp.float32) + far_ref[...].astype(jnp.float32)
    whole = (residual_ref[...].astype(jnp.float32) + added).astype(jnp.bfloat16)
    whole_ref[...] = whole
    wide = whole.astype(jnp.float32)
    mean_square = jnp.mean(wide * wide, axis=1, keepdims=True)
    normed = (wide * lax.rsqrt(mean_square + epsilon) * gain_ref[...]).astype(jnp.bfloat16)
    sending_ref[:, :width] = normed
    sending_ref[:, width:] = noted(ids_ref[...], weights_ref[...])
    kept_ref[...] = whole_ref[:, pl.ds(pl.multiple_of(side * half, LANES), half)]
    sent_ref[...] = sending_ref[pl.ds(pl.multiple_of(side * half_tokens, half_tokens), half_tokens), :]
    pack(rows_ref[...], normed, out_ref)


def norm_and_pack(side, residual_in, near, far, gain, placed, ids, weights, half, rows):
    tokens, width = residual_in.shape
    return pl.pallas_call(
        norm_kernel,
        out_shape=(shape_of((rows, width)), shape_of((tokens // 2, width + LANES)), shape_of((tokens, half))),
        in_specs=[SMEM] + [VMEM] * 7,
        out_specs=(VMEM, VMEM, VMEM),
        scratch_shapes=[pltpu.VMEM((tokens, width), jnp.bfloat16), pltpu.VMEM((tokens, width + LANES), jnp.bfloat16)],
        compiler_params=pltpu.CompilerParams(vmem_limit_bytes=24 * MIB),
        cost_estimate=cost(2 * rows * tokens * width, 2 * rows * width),
        name="norm_and_pack",
    )(side, residual_in, near, far, gain.reshape(1, width), placed, ids, weights)


def peer_kernel(
    experts, side_rows, base_ref, side_ref, mine_ref, other_ref, out_ref, rows_ref, weights_ref, arrived_ref
):
    side, part = side_ref[0], mine_ref.shape[0]
    top_count = rows_ref.shape[0]
    width = out_ref.shape[1]
    arrived_ref[pl.ds(pl.multiple_of(side * part, part), part), :] = mine_ref[...]
    arrived_ref[pl.ds(pl.multiple_of((1 - side) * part, part), part), :] = other_ref[...]
    notes = arrived_ref[:, width:].astype(jnp.float32).T
    weights_ref[...] = sum([notes[k * top_count : (k + 1) * top_count, :] for k in range(2, 4)], notes[top_count : 2 * top_count, :])
    rows = rows_of(notes[:top_count, :], experts, side_rows, base_ref[0], side)
    rows_ref[...] = rows
    pack(rows, arrived_ref[:, :width], out_ref)


def pack_peer(base, side, mine, other, top_count, experts, side_rows, rows):
    part = mine.shape[0]
    width = mine.shape[1] - LANES
    return pl.pallas_call(
        functools.partial(peer_kernel, experts, side_rows),
        out_shape=(
            shape_of((rows, width)),
            shape_of((top_count, 2 * part), jnp.int32),
            shape_of((top_count, 2 * part), jnp.float32),
        ),
        in_specs=[SMEM, SMEM, VMEM, VMEM],
        out_specs=(VMEM, VMEM, VMEM),
        scratch_shapes=[pltpu.VMEM((2 * part, width + LANES), jnp.bfloat16)],
        compiler_params=pltpu.CompilerParams(vmem_limit_bytes=24 * MIB),
        cost_estimate=cost(4 * rows * part * width, 2 * rows * width),
        name="pack_peer",
    )(base, side, mine, other)


def expert_kernel(
    x_hbm, gate_hbm, up_hbm, down_hbm, gate_too_hbm, up_too_hbm, down_too_hbm, y_hbm, x_ref, y_ref, gate_ref, up_ref,
    down_ref, hidden_ref, x_sem, y_sem, gate_sem, up_sem, down_sem,
):
    rows, width = x_ref.shape
    share = gate_hbm.shape[2]
    step = 2 * LANES
    tile = min(rows, 256)

    def loads_of(source, target, sem):
        cut = source.shape[1] // 2
        spans = [pl.ds(k * cut, cut) for k in range(2)]
        return [pltpu.make_async_copy(source.at[0, span], target.at[span], sem.at[k]) for k, span in enumerate(spans)]

    loads = [[pltpu.make_async_copy(x_hbm, x_ref, x_sem)]]
    for k, (gate, up) in enumerate([(gate_hbm, up_hbm), (gate_too_hbm, up_too_hbm)]):
        loads[-1] += loads_of(gate, gate_ref.at[k], gate_sem.at[k]) + loads_of(up, up_ref.at[k], up_sem.at[k])
        loads.append([])
    for k, down in enumerate([down_hbm, down_too_hbm]):
        loads[-1] += loads_of(down, down_ref.at[pl.ds(k * share, share)], down_sem.at[k])
    for load in sum(loads, []):
        load.start()
    for k in range(2):
        for load in loads[k]:
            load.wait()
        for i in range(share // step):
            columns = slice(i * step, (i + 1) * step)
            for at in range(0, rows, tile):
                x = x_ref[at : at + tile, :]
                gate = jnp.dot(x, gate_ref[k, :, columns], preferred_element_type=jnp.float32)
                up = jnp.dot(x, up_ref[k, :, columns], preferred_element_type=jnp.float32)
                hidden = gate / (1.0 + jnp.exp(-gate)) * up
                hidden_ref[at : at + tile, k * share + i * step : k * share + (i + 1) * step] = hidden.astype(
                    jnp.bfloat16
                )
    for load in loads[2]:
        load.wait()
    stores = []
    for i in range(width // step):
        columns = pl.ds(i * step, step)
        for at in range(0, rows, tile):
            y_ref[at : at + tile, i * step : (i + 1) * step] = jnp.dot(
                hidden_ref[at : at + tile, :],
                down_ref[:, i * step : (i + 1) * step],
                preferred_element_type=jnp.float32,
            ).astype(jnp.bfloat16)
        stores.append(pltpu.make_async_copy(y_ref.at[:, columns], y_hbm.at[:, columns], y_sem.at[i]))
        stores[i].start()
    for store in stores:
        store.wait()


def expert_layer(x, mine, others):
    rows, width = x.shape
    share = mine[0].shape[2]
    return pl.pallas_call(
        expert_kernel,
        out_shape=shape_of((rows, width)),
        in_specs=[HBM] * 7,
        out_specs=HBM,
        scratch_shapes=[
            pltpu.VMEM((rows, width), jnp.bfloat16),
            pltpu.VMEM((rows, width), jnp.bfloat16),
            pltpu.VMEM((2, width, share), jnp.bfloat16),
            pltpu.VMEM((2, width, share), jnp.bfloat16),
            pltpu.VMEM((2 * share, width), jnp.bfloat16),
            pltpu.VMEM((rows, 2 * share), jnp.bfloat16),
            pltpu.SemaphoreType.DMA,
            pltpu.SemaphoreType.DMA((width // (2 * LANES),)),
            pltpu.SemaphoreType.DMA((2, 2)),
            pltpu.SemaphoreType.DMA((2, 2)),
            pltpu.SemaphoreType.DMA((2, 2)),
        ],
        compiler_params=pltpu.CompilerParams(vmem_limit_bytes=60 * MIB),
        cost_estimate=cost(12 * rows * width * share, 12 * width * share, 2 * rows * share),
        name="expert_layer",
    )(x, *mine, *others)


def combine_kernel(side_ref, rows_ref, weights_ref, y_ref, *refs):
    *more_refs, mine_ref, sent_ref, total_ref = refs
    top_count, tokens = rows_ref.shape
    half = mine_ref.shape[1]
    row = iota((y_ref.shape[0], tokens), 0)
    share = jnp.zeros(row.shape, jnp.float32)
    for c in range(top_count):
        share = jnp.where(rows_ref[c : c + 1, :] == row, weights_ref[c : c + 1, :], share)
    coarse = share.astype(jnp.bfloat16)
    fine = (share - coarse.astype(jnp.float32)).astype(jnp.bfloat16)
    y = y_ref[...]
    contract = (((0,), (0,)), ((), ()))
    total_ref[...] = lax.dot_general(coarse, y, contract, preferred_element_type=jnp.float32)
    total_ref[...] += lax.dot_general(fine, y, contract, preferred_element_type=jnp.float32)
    side = side_ref[0]
    mine = total_ref[:, pl.ds(pl.multiple_of(side * half, LANES), half)]
    for more_ref in more_refs:
        mine += more_ref[...].astype(jnp.float32)
    mine_ref[...] = mine
    sent_ref[...] = total_ref[:, pl.ds(pl.multiple_of((1 - side) * half, LANES), half)].astype(jnp.bfloat16)


def combine(side, placed, weights, y, half, more=()):
    tokens = placed.shape[1]
    rows, width = y.shape
    return pl.pallas_call(
        combine_kernel,
        out_shape=(shape_of((tokens, half), jnp.float32), shape_of((tokens, half))),
        in_specs=[SMEM] + [VMEM] * (3 + len(more)),
        out_specs=(VMEM, VMEM),
        scratch_shapes=[pltpu.VMEM((tokens, width), jnp.float32)],
        compiler_params=pltpu.CompilerParams(vmem_limit_bytes=24 * MIB),
        cost_estimate=cost(4 * rows * tokens * width, 2 * rows * width),
        name="combine",
    )(side, placed, weights, y, *more)


def local(
    residual_in,
    query_rows,
    rotated_key_rows,
    value_row_matrix,
    learned_sink_scores,
    w_out,
    norm_gain,
    expert_ids,
    route_weights,
    w_gate,
    w_up,
    w_down,
):
    tok_dev, model_width = residual_in.shape
    seq_count = lax.axis_size("seq")
    experts = w_gate.shape[0] * seq_count
    top_count = expert_ids.shape[1]
    capacity = max(2, 8 * tok_dev // experts)
    sides = lax.axis_size("tp")
    side_rows = capacity // sides
    group = seq_count // 2
    rows = experts // 2 * side_rows
    half = model_width // sides
    at_seq = lax.axis_index("seq").astype(jnp.int32)
    base = jnp.where(at_seq < group, 0, experts // 2).astype(jnp.int32).reshape(1)
    side = lax.axis_index("tp").astype(jnp.int32).reshape(1)
    first = (at_seq == 0).astype(jnp.int32).reshape(1)
    ids, route = expert_ids.T, route_weights.T

    before = passed_along(jnp.concatenate([rotated_key_rows, value_row_matrix], axis=1), "seq", 1)
    weights = (w_gate, w_up, w_down)
    others = [swapped(weight, "tp") for weight in weights]
    placed = places(base, side, ids, experts, side_rows)
    near = attention(first, learned_sink_scores, query_rows, rotated_key_rows, value_row_matrix, before, w_out)
    near, *others = lax.optimization_barrier((near, *others))
    far = swapped(near, "tp")
    packed, sent, kept = norm_and_pack(
        side, residual_in, near, far, norm_gain, placed, ids, route, half, rows
    )

    def exchanged(block):
        block = block.reshape(group, rows // group, model_width)
        groups = [list(range(group)), list(range(group, seq_count))]
        block = lax.all_to_all(
            block, "seq", split_axis=0, concat_axis=0, axis_index_groups=groups, tiled=True
        )
        return block.reshape(rows, model_width)

    crossed = swapped_halves(sent, "seq")
    arrived = exchanged(packed)
    crossed, arrived = lax.optimization_barrier((crossed, arrived))
    packed_peer, placed_peer, route_peer = pack_peer(
        base, side, crossed, swapped(crossed, "tp"), top_count, experts, side_rows, rows
    )
    arrived_peer = exchanged(packed_peer)
    result = expert_layer(arrived, weights, others)
    result_peer = expert_layer(arrived_peer, weights, others)

    returned_peer = exchanged(result_peer)
    result, returned_peer = lax.optimization_barrier((result, returned_peer))
    returned = exchanged(result)
    mine_peer, sent_peer = combine(side, placed_peer, route_peer, returned_peer, half)
    summed_peer = (mine_peer + swapped(sent_peer, "tp").astype(jnp.float32)).astype(jnp.bfloat16)
    back = swapped_halves(summed_peer, "seq")
    mine, sent = combine(side, placed, route, returned, half, (kept, back))
    return (mine + swapped(sent, "tp").astype(jnp.float32)).astype(jnp.bfloat16)


def solution(mesh):
    placed = (
        P("seq", None),
        P("seq", "tp"),
        P("seq", "tp"),
        P("seq", "tp"),
        P("tp"),
        P("tp", None),
        P(),
        P("seq", None),
        P("seq", None),
        P("seq", None, "tp"),
        P("seq", None, "tp"),
        P("seq", "tp", None),
    )
    return jax.shard_map(
        local, mesh=mesh, in_specs=placed, out_specs=P("seq", "tp"), check_vma=False
    )
```

```python
import functools

import jax
import jax.numpy as jnp
from jax import lax
from jax.experimental import pallas as pl
from jax.experimental.pallas import tpu as pltpu
from jax.sharding import PartitionSpec as P

HEAD_SIZE = 64
WINDOW_LENGTH = 128
LANES = 128
MIB = 1024 * 1024

neg_large = -1e30
epsilon = 1e-05

VMEM = pl.BlockSpec(memory_space=pltpu.VMEM)
SMEM = pl.BlockSpec(memory_space=pltpu.SMEM)
HBM = pl.BlockSpec(memory_space=pltpu.HBM)


def passed_along(block, axis, distance):
    devices = range(lax.axis_size(axis))
    route = [(i - distance, i) for i in devices if i - distance in devices]
    return lax.ppermute(block, axis, route)


def swapped(block, axis):
    count = lax.axis_size(axis)
    return lax.ppermute(block, axis, [(i, count - 1 - i) for i in range(count)])


def swapped_halves(block, axis):
    count = lax.axis_size(axis)
    return lax.ppermute(block, axis, [(i, (i + count // 2) % count) for i in range(count)])


def shape_of(dims, dtype=jnp.bfloat16):
    return jax.ShapeDtypeStruct(dims, dtype)


def cost(flops, moved, transcendentals=0):
    return pl.CostEstimate(flops=flops, bytes_accessed=moved, transcendentals=transcendentals)


def iota(dims, dimension):
    return lax.broadcasted_iota(jnp.int32, dims, dimension)


def rows_of(ids, experts, side_rows, base, side):
    top_count, tokens = ids.shape
    names = iota((experts, tokens), 0).astype(jnp.float32)
    hits = [ids[c : c + 1, :] == names for c in range(top_count)]
    named = sum([hit.astype(jnp.float32) for hit in hits]).astype(jnp.bfloat16)
    square = (tokens, tokens)
    earlier = (iota(square, 0) < iota(square, 1)).astype(jnp.bfloat16)
    slot = jnp.dot(named, earlier, preferred_element_type=jnp.float32) - (side * side_rows).astype(jnp.float32)
    expert = names - base.astype(jnp.float32)
    here = (slot >= 0.0) & (slot < side_rows) & (expert >= 0.0) & (expert < experts // 2)
    rows = jnp.where(here, expert * side_rows + slot, -1.0)
    lines = [jnp.sum(jnp.where(hit, rows, 0.0), axis=0, keepdims=True) for hit in hits]
    return jnp.concatenate(lines, axis=0).astype(jnp.int32)


def place_kernel(experts, side_rows, base_ref, side_ref, ids_ref, rows_ref):
    rows_ref[...] = rows_of(ids_ref[...].astype(jnp.float32), experts, side_rows, base_ref[0], side_ref[0])


def places(base, side, ids, experts, side_rows):
    top_count, tokens = ids.shape
    return pl.pallas_call(
        functools.partial(place_kernel, experts, side_rows),
        out_shape=shape_of(ids.shape, jnp.int32),
        in_specs=[SMEM, SMEM, VMEM],
        out_specs=VMEM,
        cost_estimate=cost(2 * tokens * tokens * experts, 8 * tokens * top_count),
        name="places",
    )(base, side, ids)


def attention_kernel(first_ref, sink_hbm, q_hbm, kv_ref, before_ref, w_hbm, out_ref, sink_ref, q_ref, w_ref, att_ref, sems):
    tokens, width = q_ref.shape
    kv_heads = kv_ref.shape[1] // (2 * HEAD_SIZE)
    pairs = width // LANES // kv_heads
    moves = [(sink_hbm, sink_ref), (q_hbm, q_ref), (w_hbm, w_ref)]
    *loads, w_load = [pltpu.make_async_copy(source, target, sems.at[i]) for i, (source, target) in enumerate(moves)]
    for load in loads + [w_load]:
        load.start()
    low = iota((tokens, LANES), 1) < HEAD_SIZE

    def doubled(block, head):
        wide = block.astype(jnp.float32)
        turned = pltpu.roll(wide, HEAD_SIZE, 1)
        first, second = (wide, turned) if head == 0 else (turned, wide)
        return [
            jnp.where(low, first, 0.0).astype(jnp.bfloat16),
            jnp.where(low, 0.0, second).astype(jnp.bfloat16),
        ]

    own = iota((tokens, tokens), 1) <= iota((tokens, tokens), 0)
    usable = first_ref[0] == 0
    k, v = kv_ref[:, :LANES], kv_ref[:, LANES:]
    k_before, v_before = before_ref[:, :LANES], before_ref[:, LANES:]
    contract = (((1,), (1,)), ((), ()))
    loaded = False
    for head in range(kv_heads):
        keys = jnp.concatenate(doubled(k, head), axis=0)
        keys_before = jnp.concatenate(doubled(k_before, head), axis=0)
        values = jnp.concatenate(doubled(v, head) + doubled(v_before, head), axis=0)
        if not loaded:
            for load in loads:
                load.wait()
            loaded = True
        for j in range(head * pairs, (head + 1) * pairs):
            q = q_ref[:, j * LANES : (j + 1) * LANES]
            near = lax.dot_general(q, keys, contract, preferred_element_type=jnp.float32)
            far = lax.dot_general(q, keys_before, contract, preferred_element_type=jnp.float32)
            kept_own, kept_before = [], []
            for at in range(2):
                far_part = jnp.where(usable, far[:, at * tokens : (at + 1) * tokens], neg_large)
                part = jnp.where(own, near[:, at * tokens : (at + 1) * tokens], far_part) * HEAD_SIZE**-0.5
                sink = sink_ref[2 * j + at]
                top = jnp.maximum(jnp.max(part, axis=1, keepdims=True), sink)
                terms = jnp.exp(part - top)
                total = jnp.sum(terms, axis=1, keepdims=True) + jnp.exp(sink - top)
                prob = terms * (1.0 / total)
                kept_own.append(jnp.where(own, prob, 0.0).astype(jnp.bfloat16))
                kept_before.append(jnp.where(own, 0.0, prob).astype(jnp.bfloat16))
            probs = jnp.concatenate(kept_own + kept_before, axis=1)
            att_ref[:, j * LANES : (j + 1) * LANES] = jnp.dot(
                probs, values, preferred_element_type=jnp.float32
            ).astype(jnp.bfloat16)
    w_load.wait()
    step = 2 * LANES
    for at in range(0, out_ref.shape[1], step):
        out_ref[:, at : at + step] = jnp.dot(
            att_ref[...], w_ref[:, at : at + step], preferred_element_type=jnp.float32
        ).astype(jnp.bfloat16)


def attention(first, sinks, q, kv, before, w_out):
    tokens = q.shape[0]
    return pl.pallas_call(
        attention_kernel,
        out_shape=shape_of((tokens, w_out.shape[1])),
        in_specs=[SMEM, HBM, HBM, VMEM, VMEM, HBM],
        out_specs=VMEM,
        scratch_shapes=[
            pltpu.SMEM(sinks.shape, jnp.float32),
            pltpu.VMEM(q.shape, jnp.bfloat16),
            pltpu.VMEM(w_out.shape, jnp.bfloat16),
            pltpu.VMEM(q.shape, jnp.bfloat16),
            pltpu.SemaphoreType.DMA((3,)),
        ],
        compiler_params=pltpu.CompilerParams(vmem_limit_bytes=60_580_000),
        cost_estimate=cost(2 * tokens * w_out.size * 2, 2 * w_out.size, tokens * tokens * q.shape[1] // HEAD_SIZE),
        name="attention",
    )(first, sinks, q, kv, before, w_out)


def pack(placed, normed, out_ref):
    rows, tokens = out_ref.shape[0], normed.shape[0]
    row = iota((rows, tokens), 0)
    taken = placed[0:1, :] == row
    for c in range(1, placed.shape[0]):
        taken = taken | (placed[c : c + 1, :] == row)
    taken = jnp.where(taken, 1.0, 0.0).astype(jnp.bfloat16)
    out_ref[...] = jnp.dot(taken, normed, preferred_element_type=jnp.float32).astype(jnp.bfloat16)


def noted(ids, weights):
    coarse = weights.astype(jnp.bfloat16).astype(jnp.float32)
    middle = (weights - coarse).astype(jnp.bfloat16).astype(jnp.float32)
    fine = weights - coarse - middle
    used = [ids.astype(jnp.float32), coarse, middle, fine]
    empty = jnp.zeros((LANES - 4 * ids.shape[0], ids.shape[1]), jnp.float32)
    return jnp.concatenate(used + [empty], axis=0).T.astype(jnp.bfloat16)


def norm_kernel(
    side_ref, residual_ref, near_ref, far_ref, gain_ref, rows_ref, ids_ref, weights_ref, out_ref, sent_ref, kept_ref,
    whole_ref, sending_ref,
):
    side = side_ref[0]
    half_tokens, half, width = sent_ref.shape[0], kept_ref.shape[1], whole_ref.shape[1]
    added = near_ref[...].astype(jnp.float32) + far_ref[...].astype(jnp.float32)
    whole = (residual_ref[...].astype(jnp.float32) + added).astype(jnp.bfloat16)
    whole_ref[...] = whole
    wide = whole.astype(jnp.float32)
    mean_square = jnp.mean(wide * wide, axis=1, keepdims=True)
    normed = (wide * lax.rsqrt(mean_square + epsilon) * gain_ref[...]).astype(jnp.bfloat16)
    sending_ref[:, :width] = normed
    sending_ref[:, width:] = noted(ids_ref[...], weights_ref[...])
    kept_ref[...] = whole_ref[:, pl.ds(pl.multiple_of(side * half, LANES), half)]
    sent_ref[...] = sending_ref[pl.ds(pl.multiple_of(side * half_tokens, half_tokens), half_tokens), :]
    pack(rows_ref[...], normed, out_ref)


def norm_and_pack(side, residual_in, near, far, gain, placed, ids, weights, half, rows):
    tokens, width = residual_in.shape
    return pl.pallas_call(
        norm_kernel,
        out_shape=(shape_of((rows, width)), shape_of((tokens // 2, width + LANES)), shape_of((tokens, half))),
        in_specs=[SMEM] + [VMEM] * 7,
        out_specs=(VMEM, VMEM, VMEM),
        scratch_shapes=[pltpu.VMEM((tokens, width), jnp.bfloat16), pltpu.VMEM((tokens, width + LANES), jnp.bfloat16)],
        compiler_params=pltpu.CompilerParams(vmem_limit_bytes=24 * MIB),
        cost_estimate=cost(2 * rows * tokens * width, 2 * rows * width),
        name="norm_and_pack",
    )(side, residual_in, near, far, gain.reshape(1, width), placed, ids, weights)


def peer_kernel(
    experts, side_rows, base_ref, side_ref, mine_ref, other_ref, out_ref, rows_ref, weights_ref, arrived_ref
):
    side, part = side_ref[0], mine_ref.shape[0]
    top_count = rows_ref.shape[0]
    width = out_ref.shape[1]
    arrived_ref[pl.ds(pl.multiple_of(side * part, part), part), :] = mine_ref[...]
    arrived_ref[pl.ds(pl.multiple_of((1 - side) * part, part), part), :] = other_ref[...]
    notes = arrived_ref[:, width:].astype(jnp.float32).T
    weights_ref[...] = sum([notes[k * top_count : (k + 1) * top_count, :] for k in range(2, 4)], notes[top_count : 2 * top_count, :])
    rows = rows_of(notes[:top_count, :], experts, side_rows, base_ref[0], side)
    rows_ref[...] = rows
    pack(rows, arrived_ref[:, :width], out_ref)


def pack_peer(base, side, mine, other, top_count, experts, side_rows, rows):
    part = mine.shape[0]
    width = mine.shape[1] - LANES
    return pl.pallas_call(
        functools.partial(peer_kernel, experts, side_rows),
        out_shape=(
            shape_of((rows, width)),
            shape_of((top_count, 2 * part), jnp.int32),
            shape_of((top_count, 2 * part), jnp.float32),
        ),
        in_specs=[SMEM, SMEM, VMEM, VMEM],
        out_specs=(VMEM, VMEM, VMEM),
        scratch_shapes=[pltpu.VMEM((2 * part, width + LANES), jnp.bfloat16)],
        compiler_params=pltpu.CompilerParams(vmem_limit_bytes=24 * MIB),
        cost_estimate=cost(4 * rows * part * width, 2 * rows * width),
        name="pack_peer",
    )(base, side, mine, other)


def expert_kernel(x_ref, gate_ref, up_ref, down_ref, gate_too_ref, up_too_ref, down_too_ref, y_ref, hidden_ref):
    rows, width = x_ref.shape
    share = gate_ref.shape[2]
    step = 2 * LANES
    tile = min(rows, 256)
    for at in range(0, rows, tile):
        x = x_ref[at : at + tile, :]
        for k, (gate_part, up_part) in enumerate([(gate_ref, up_ref), (gate_too_ref, up_too_ref)]):
            for i in range(0, share, step):
                gate = jnp.dot(x, gate_part[0, :, i : i + step], preferred_element_type=jnp.float32)
                up = jnp.dot(x, up_part[0, :, i : i + step], preferred_element_type=jnp.float32)
                hidden = gate / (1.0 + jnp.exp(-gate)) * up
                hidden_ref[at : at + tile, k * share + i : k * share + i + step] = hidden.astype(jnp.bfloat16)
        for i in range(0, width, step):
            first = jnp.dot(
                hidden_ref[at : at + tile, :share], down_ref[0, :, i : i + step], preferred_element_type=jnp.float32
            )
            second = jnp.dot(
                hidden_ref[at : at + tile, share:], down_too_ref[0, :, i : i + step], preferred_element_type=jnp.float32
            )
            y_ref[at : at + tile, i : i + step] = (first + second).astype(jnp.bfloat16)


def expert_layer(x, mine, others):
    rows, width = x.shape
    share = mine[0].shape[2]
    return pl.pallas_call(
        expert_kernel,
        out_shape=shape_of((rows, width)),
        in_specs=[VMEM] * 7,
        out_specs=VMEM,
        scratch_shapes=[pltpu.VMEM((rows, 2 * share), jnp.bfloat16)],
        compiler_params=pltpu.CompilerParams(vmem_limit_bytes=24 * MIB),
        cost_estimate=cost(12 * rows * width * share, 12 * width * share, 2 * rows * share),
        name="expert_layer",
    )(x, *mine, *others)


def combine_kernel(side_ref, rows_ref, weights_ref, y_ref, *refs):
    *more_refs, mine_ref, sent_ref, total_ref = refs
    top_count, tokens = rows_ref.shape
    half = mine_ref.shape[1]
    row = iota((y_ref.shape[0], tokens), 0)
    share = jnp.zeros(row.shape, jnp.float32)
    for c in range(top_count):
        share = jnp.where(rows_ref[c : c + 1, :] == row, weights_ref[c : c + 1, :], share)
    coarse = share.astype(jnp.bfloat16)
    fine = (share - coarse.astype(jnp.float32)).astype(jnp.bfloat16)
    y = y_ref[...]
    contract = (((0,), (0,)), ((), ()))
    total_ref[...] = lax.dot_general(coarse, y, contract, preferred_element_type=jnp.float32)
    total_ref[...] += lax.dot_general(fine, y, contract, preferred_element_type=jnp.float32)
    side = side_ref[0]
    mine = total_ref[:, pl.ds(pl.multiple_of(side * half, LANES), half)]
    for more_ref in more_refs:
        mine += more_ref[...].astype(jnp.float32)
    mine_ref[...] = mine
    sent_ref[...] = total_ref[:, pl.ds(pl.multiple_of((1 - side) * half, LANES), half)].astype(jnp.bfloat16)


def combine(side, placed, weights, y, half, more=()):
    tokens = placed.shape[1]
    rows, width = y.shape
    return pl.pallas_call(
        combine_kernel,
        out_shape=(shape_of((tokens, half), jnp.float32), shape_of((tokens, half))),
        in_specs=[SMEM] + [VMEM] * (3 + len(more)),
        out_specs=(VMEM, VMEM),
        scratch_shapes=[pltpu.VMEM((tokens, width), jnp.float32)],
        compiler_params=pltpu.CompilerParams(vmem_limit_bytes=24 * MIB),
        cost_estimate=cost(4 * rows * tokens * width, 2 * rows * width),
        name="combine",
    )(side, placed, weights, y, *more)


def local(
    residual_in,
    query_rows,
    rotated_key_rows,
    value_row_matrix,
    learned_sink_scores,
    w_out,
    norm_gain,
    expert_ids,
    route_weights,
    w_gate,
    w_up,
    w_down,
):
    tok_dev, model_width = residual_in.shape
    seq_count = lax.axis_size("seq")
    experts = w_gate.shape[0] * seq_count
    top_count = expert_ids.shape[1]
    capacity = max(2, 8 * tok_dev // experts)
    sides = lax.axis_size("tp")
    side_rows = capacity // sides
    group = seq_count // 2
    rows = experts // 2 * side_rows
    half = model_width // sides
    at_seq = lax.axis_index("seq").astype(jnp.int32)
    base = jnp.where(at_seq < group, 0, experts // 2).astype(jnp.int32).reshape(1)
    side = lax.axis_index("tp").astype(jnp.int32).reshape(1)
    first = (at_seq == 0).astype(jnp.int32).reshape(1)
    ids, route = expert_ids.T, route_weights.T

    key_values = jnp.concatenate([rotated_key_rows, value_row_matrix], axis=1)
    before = passed_along(key_values, "seq", 1)
    weights = (w_gate, w_up, w_down)
    others = [swapped(weight, "tp") for weight in weights]
    placed = places(base, side, ids, experts, side_rows)
    near = attention(first, learned_sink_scores, query_rows, key_values, before, w_out)
    far = swapped(near, "tp")
    packed, sent, kept = norm_and_pack(
        side, residual_in, near, far, norm_gain, placed, ids, route, half, rows
    )

    def exchanged(block):
        block = block.reshape(group, rows // group, model_width)
        groups = [list(range(group)), list(range(group, seq_count))]
        block = lax.all_to_all(
            block, "seq", split_axis=0, concat_axis=0, axis_index_groups=groups, tiled=True
        )
        return block.reshape(rows, model_width)

    crossed = swapped_halves(sent, "seq")
    arrived = exchanged(packed)
    crossed, arrived, *others = lax.optimization_barrier((crossed, arrived, *others))
    packed_peer, placed_peer, route_peer = pack_peer(
        base, side, crossed, swapped(crossed, "tp"), top_count, experts, side_rows, rows
    )
    arrived_peer = exchanged(packed_peer)
    result = expert_layer(arrived, weights, others)
    result, arrived_peer = lax.optimization_barrier((result, arrived_peer))
    result_peer = expert_layer(arrived_peer, weights, others)

    returned_peer = exchanged(result_peer)
    result, returned_peer = lax.optimization_barrier((result, returned_peer))
    returned = exchanged(result)
    mine_peer, sent_peer = combine(side, placed_peer, route_peer, returned_peer, half)
    summed_peer = (mine_peer + swapped(sent_peer, "tp").astype(jnp.float32)).astype(jnp.bfloat16)
    back = swapped_halves(summed_peer, "seq")
    mine, sent = combine(side, placed, route, returned, half, (kept, back))
    return (mine + swapped(sent, "tp").astype(jnp.float32)).astype(jnp.bfloat16)


def solution(mesh):
    placed = (
        P("seq", None),
        P("seq", "tp"),
        P("seq", "tp"),
        P("seq", "tp"),
        P("tp"),
        P("tp", None),
        P(),
        P("seq", None),
        P("seq", None),
        P("seq", None, "tp"),
        P("seq", None, "tp"),
        P("seq", "tp", None),
    )
    return jax.shard_map(
        local, mesh=mesh, in_specs=placed, out_specs=P("seq", "tp"), check_vma=False
    )
```

```python
import functools

import jax
import jax.numpy as jnp
from jax import lax
from jax.experimental import pallas as pl
from jax.experimental.pallas import tpu as pltpu
from jax.sharding import PartitionSpec as P

HEAD_SIZE = 64
WINDOW_LENGTH = 128
LANES = 128
MIB = 1024 * 1024

neg_large = -1e30
epsilon = 1e-05

VMEM = pl.BlockSpec(memory_space=pltpu.VMEM)
SMEM = pl.BlockSpec(memory_space=pltpu.SMEM)
HBM = pl.BlockSpec(memory_space=pltpu.HBM)


def passed_along(block, axis, distance):
    devices = range(lax.axis_size(axis))
    route = [(i - distance, i) for i in devices if i - distance in devices]
    return lax.ppermute(block, axis, route)


def swapped(block, axis):
    count = lax.axis_size(axis)
    return lax.ppermute(block, axis, [(i, count - 1 - i) for i in range(count)])


def swapped_halves(block, axis):
    count = lax.axis_size(axis)
    return lax.ppermute(block, axis, [(i, (i + count // 2) % count) for i in range(count)])


def shape_of(dims, dtype=jnp.bfloat16):
    return jax.ShapeDtypeStruct(dims, dtype)


def cost(flops, moved, transcendentals=0):
    return pl.CostEstimate(flops=flops, bytes_accessed=moved, transcendentals=transcendentals)


def iota(dims, dimension):
    return lax.broadcasted_iota(jnp.int32, dims, dimension)


def rows_of(ids, experts, side_rows, base, side):
    top_count, tokens = ids.shape
    names = iota((experts, tokens), 0).astype(jnp.float32)
    hits = [ids[c : c + 1, :] == names for c in range(top_count)]
    named = sum([hit.astype(jnp.float32) for hit in hits]).astype(jnp.bfloat16)
    square = (tokens, tokens)
    earlier = (iota(square, 0) < iota(square, 1)).astype(jnp.bfloat16)
    slot = jnp.dot(named, earlier, preferred_element_type=jnp.float32) - (side * side_rows).astype(jnp.float32)
    expert = names - base.astype(jnp.float32)
    here = (slot >= 0.0) & (slot < side_rows) & (expert >= 0.0) & (expert < experts // 2)
    rows = jnp.where(here, expert * side_rows + slot, -1.0)
    lines = [jnp.sum(jnp.where(hit, rows, 0.0), axis=0, keepdims=True) for hit in hits]
    return jnp.concatenate(lines, axis=0).astype(jnp.int32)


def place_kernel(experts, side_rows, base_ref, side_ref, ids_ref, rows_ref):
    rows_ref[...] = rows_of(ids_ref[...].astype(jnp.float32), experts, side_rows, base_ref[0], side_ref[0])


def places(base, side, ids, experts, side_rows):
    top_count, tokens = ids.shape
    return pl.pallas_call(
        functools.partial(place_kernel, experts, side_rows),
        out_shape=shape_of(ids.shape, jnp.int32),
        in_specs=[SMEM, SMEM, VMEM],
        out_specs=VMEM,
        cost_estimate=cost(2 * tokens * tokens * experts, 8 * tokens * top_count),
        name="places",
    )(base, side, ids)


def attention_kernel(first_ref, sink_hbm, q_hbm, kv_ref, before_ref, w_hbm, out_ref, sink_ref, q_ref, w_ref, att_ref, sems):
    tokens, width = q_ref.shape
    kv_heads = kv_ref.shape[1] // (2 * HEAD_SIZE)
    pairs = width // LANES // kv_heads
    moves = [(sink_hbm, sink_ref), (q_hbm, q_ref), (w_hbm, w_ref)]
    *loads, w_load = [pltpu.make_async_copy(source, target, sems.at[i]) for i, (source, target) in enumerate(moves)]
    for load in loads + [w_load]:
        load.start()
    low = iota((tokens, LANES), 1) < HEAD_SIZE

    def doubled(block, head):
        wide = block.astype(jnp.float32)
        turned = pltpu.roll(wide, HEAD_SIZE, 1)
        first, second = (wide, turned) if head == 0 else (turned, wide)
        return [
            jnp.where(low, first, 0.0).astype(jnp.bfloat16),
            jnp.where(low, 0.0, second).astype(jnp.bfloat16),
        ]

    own = iota((tokens, tokens), 1) <= iota((tokens, tokens), 0)
    usable = first_ref[0] == 0
    k, v = kv_ref[:, :LANES], kv_ref[:, LANES:]
    k_before, v_before = before_ref[:, :LANES], before_ref[:, LANES:]
    contract = (((1,), (1,)), ((), ()))
    loaded = False
    for head in range(kv_heads):
        keys = jnp.concatenate(doubled(k, head), axis=0)
        keys_before = jnp.concatenate(doubled(k_before, head), axis=0)
        values = jnp.concatenate(doubled(v, head) + doubled(v_before, head), axis=0)
        if not loaded:
            for load in loads:
                load.wait()
            loaded = True
        for j in range(head * pairs, (head + 1) * pairs):
            q = q_ref[:, j * LANES : (j + 1) * LANES]
            near = lax.dot_general(q, keys, contract, preferred_element_type=jnp.float32)
            far = lax.dot_general(q, keys_before, contract, preferred_element_type=jnp.float32)
            kept_own, kept_before = [], []
            for at in range(2):
                far_part = jnp.where(usable, far[:, at * tokens : (at + 1) * tokens], neg_large)
                part = jnp.where(own, near[:, at * tokens : (at + 1) * tokens], far_part) * HEAD_SIZE**-0.5
                sink = sink_ref[2 * j + at]
                top = jnp.maximum(jnp.max(part, axis=1, keepdims=True), sink)
                terms = jnp.exp(part - top)
                total = jnp.sum(terms, axis=1, keepdims=True) + jnp.exp(sink - top)
                prob = terms * (1.0 / total)
                kept_own.append(jnp.where(own, prob, 0.0).astype(jnp.bfloat16))
                kept_before.append(jnp.where(own, 0.0, prob).astype(jnp.bfloat16))
            probs = jnp.concatenate(kept_own + kept_before, axis=1)
            att_ref[:, j * LANES : (j + 1) * LANES] = jnp.dot(
                probs, values, preferred_element_type=jnp.float32
            ).astype(jnp.bfloat16)
    w_load.wait()
    step = 2 * LANES
    for at in range(0, out_ref.shape[1], step):
        out_ref[:, at : at + step] = jnp.dot(
            att_ref[...], w_ref[:, at : at + step], preferred_element_type=jnp.float32
        ).astype(jnp.bfloat16)


def attention(first, sinks, q, kv, before, w_out):
    tokens = q.shape[0]
    return pl.pallas_call(
        attention_kernel,
        out_shape=shape_of((tokens, w_out.shape[1])),
        in_specs=[SMEM, HBM, HBM, VMEM, VMEM, HBM],
        out_specs=VMEM,
        scratch_shapes=[
            pltpu.SMEM(sinks.shape, jnp.float32),
            pltpu.VMEM(q.shape, jnp.bfloat16),
            pltpu.VMEM(w_out.shape, jnp.bfloat16),
            pltpu.VMEM(q.shape, jnp.bfloat16),
            pltpu.SemaphoreType.DMA((3,)),
        ],
        compiler_params=pltpu.CompilerParams(vmem_limit_bytes=62_500_000),
        cost_estimate=cost(2 * tokens * w_out.size * 2, 2 * w_out.size, tokens * tokens * q.shape[1] // HEAD_SIZE),
        name="attention",
    )(first, sinks, q, kv, before, w_out)


def pack(placed, normed, out_ref):
    rows, tokens = out_ref.shape[0], normed.shape[0]
    row = iota((rows, tokens), 0)
    taken = placed[0:1, :] == row
    for c in range(1, placed.shape[0]):
        taken = taken | (placed[c : c + 1, :] == row)
    taken = jnp.where(taken, 1.0, 0.0).astype(jnp.bfloat16)
    out_ref[...] = jnp.dot(taken, normed, preferred_element_type=jnp.float32).astype(jnp.bfloat16)


def noted(ids, weights):
    coarse = weights.astype(jnp.bfloat16).astype(jnp.float32)
    middle = (weights - coarse).astype(jnp.bfloat16).astype(jnp.float32)
    fine = weights - coarse - middle
    used = [ids.astype(jnp.float32), coarse, middle, fine]
    empty = jnp.zeros((LANES - 4 * ids.shape[0], ids.shape[1]), jnp.float32)
    return jnp.concatenate(used + [empty], axis=0).T.astype(jnp.bfloat16)


def norm_kernel(
    side_ref, residual_ref, near_ref, far_ref, gain_ref, rows_ref, ids_ref, weights_ref, out_ref, sent_ref, kept_ref,
    whole_ref, sending_ref,
):
    side = side_ref[0]
    half_tokens, half, width = sent_ref.shape[0], kept_ref.shape[1], whole_ref.shape[1]
    added = near_ref[...].astype(jnp.float32) + far_ref[...].astype(jnp.float32)
    whole = (residual_ref[...].astype(jnp.float32) + added).astype(jnp.bfloat16)
    whole_ref[...] = whole
    wide = whole.astype(jnp.float32)
    mean_square = jnp.mean(wide * wide, axis=1, keepdims=True)
    normed = (wide * lax.rsqrt(mean_square + epsilon) * gain_ref[...]).astype(jnp.bfloat16)
    sending_ref[:, :width] = normed
    sending_ref[:, width:] = noted(ids_ref[...], weights_ref[...])
    kept_ref[...] = whole_ref[:, pl.ds(pl.multiple_of(side * half, LANES), half)]
    sent_ref[...] = sending_ref[pl.ds(pl.multiple_of(side * half_tokens, half_tokens), half_tokens), :]
    pack(rows_ref[...], normed, out_ref)


def norm_and_pack(side, residual_in, near, far, gain, placed, ids, weights, half, rows):
    tokens, width = residual_in.shape
    return pl.pallas_call(
        norm_kernel,
        out_shape=(shape_of((rows, width)), shape_of((tokens // 2, width + LANES)), shape_of((tokens, half))),
        in_specs=[SMEM] + [VMEM] * 7,
        out_specs=(VMEM, VMEM, VMEM),
        scratch_shapes=[pltpu.VMEM((tokens, width), jnp.bfloat16), pltpu.VMEM((tokens, width + LANES), jnp.bfloat16)],
        compiler_params=pltpu.CompilerParams(vmem_limit_bytes=24 * MIB),
        cost_estimate=cost(2 * rows * tokens * width, 2 * rows * width),
        name="norm_and_pack",
    )(side, residual_in, near, far, gain.reshape(1, width), placed, ids, weights)


def peer_kernel(
    experts, side_rows, base_ref, side_ref, mine_ref, other_ref, out_ref, rows_ref, weights_ref, arrived_ref
):
    side, part = side_ref[0], mine_ref.shape[0]
    top_count = rows_ref.shape[0]
    width = out_ref.shape[1]
    arrived_ref[pl.ds(pl.multiple_of(side * part, part), part), :] = mine_ref[...]
    arrived_ref[pl.ds(pl.multiple_of((1 - side) * part, part), part), :] = other_ref[...]
    notes = arrived_ref[:, width:].astype(jnp.float32).T
    weights_ref[...] = sum([notes[k * top_count : (k + 1) * top_count, :] for k in range(2, 4)], notes[top_count : 2 * top_count, :])
    rows = rows_of(notes[:top_count, :], experts, side_rows, base_ref[0], side)
    rows_ref[...] = rows
    pack(rows, arrived_ref[:, :width], out_ref)


def pack_peer(base, side, mine, other, top_count, experts, side_rows, rows):
    part = mine.shape[0]
    width = mine.shape[1] - LANES
    return pl.pallas_call(
        functools.partial(peer_kernel, experts, side_rows),
        out_shape=(
            shape_of((rows, width)),
            shape_of((top_count, 2 * part), jnp.int32),
            shape_of((top_count, 2 * part), jnp.float32),
        ),
        in_specs=[SMEM, SMEM, VMEM, VMEM],
        out_specs=(VMEM, VMEM, VMEM),
        scratch_shapes=[pltpu.VMEM((2 * part, width + LANES), jnp.bfloat16)],
        compiler_params=pltpu.CompilerParams(vmem_limit_bytes=24 * MIB),
        cost_estimate=cost(4 * rows * part * width, 2 * rows * width),
        name="pack_peer",
    )(base, side, mine, other)


def expert_kernel(
    x_hbm, gate_hbm, up_hbm, down_hbm, gate_too_hbm, up_too_hbm, down_too_hbm, y_hbm, x_ref, y_ref, gate_ref, up_ref,
    down_ref, hidden_ref, total_ref, x_sem, y_sem, gate_sem, up_sem, down_sem,
):
    rows, width = x_ref.shape
    share = gate_hbm.shape[2]
    step = 2 * LANES
    tile = min(rows, 256)

    def loads_of(source, target, sem):
        cut = source.shape[1] // 2
        spans = [pl.ds(k * cut, cut) for k in range(2)]
        return [pltpu.make_async_copy(source.at[0, span], target.at[span], sem.at[k]) for k, span in enumerate(spans)]

    loads = [[pltpu.make_async_copy(x_hbm, x_ref, x_sem)]]
    for k, (gate, up) in enumerate([(gate_hbm, up_hbm), (gate_too_hbm, up_too_hbm)]):
        loads[-1] += loads_of(gate, gate_ref.at[k], gate_sem.at[k]) + loads_of(up, up_ref.at[k], up_sem.at[k])
        loads.append([])
    for k, down in enumerate([down_hbm, down_too_hbm]):
        loads[-1] += loads_of(down, down_ref.at[pl.ds(k * share, share)], down_sem.at[k])
    for load in sum(loads, []):
        load.start()
    for k in range(2):
        for load in loads[k]:
            load.wait()
        for i in range(share // step):
            columns = slice(i * step, (i + 1) * step)
            for at in range(0, rows, tile):
                x = x_ref[at : at + tile, :]
                gate = jnp.dot(x, gate_ref[k, :, columns], preferred_element_type=jnp.float32)
                up = jnp.dot(x, up_ref[k, :, columns], preferred_element_type=jnp.float32)
                hidden = gate * (0.5 + 0.5 * jnp.tanh(0.5 * gate)) * up
                hidden_ref[at : at + tile, k * share + i * step : k * share + (i + 1) * step] = hidden.astype(
                    jnp.bfloat16
                )
    stores = []
    for k in range(2):
        for load in loads[2][2 * k : 2 * k + 2]:
            load.wait()
        for i in range(width // step):
            columns = slice(i * step, (i + 1) * step)
            for at in range(0, rows, tile):
                part = jnp.dot(
                    hidden_ref[at : at + tile, k * share : (k + 1) * share],
                    down_ref[k * share : (k + 1) * share, columns],
                    preferred_element_type=jnp.float32,
                )
                if k == 0:
                    total_ref[at : at + tile, columns] = part
                else:
                    y_ref[at : at + tile, columns] = (total_ref[at : at + tile, columns] + part).astype(jnp.bfloat16)
            if k == 1:
                span = pl.ds(i * step, step)
                stores.append(pltpu.make_async_copy(y_ref.at[:, span], y_hbm.at[:, span], y_sem.at[i]))
                stores[i].start()
    for store in stores:
        store.wait()


def expert_layer(x, mine, others):
    rows, width = x.shape
    share = mine[0].shape[2]
    return pl.pallas_call(
        expert_kernel,
        out_shape=shape_of((rows, width)),
        in_specs=[HBM] * 7,
        out_specs=HBM,
        scratch_shapes=[
            pltpu.VMEM((rows, width), jnp.bfloat16),
            pltpu.VMEM((rows, width), jnp.bfloat16),
            pltpu.VMEM((2, width, share), jnp.bfloat16),
            pltpu.VMEM((2, width, share), jnp.bfloat16),
            pltpu.VMEM((2 * share, width), jnp.bfloat16),
            pltpu.VMEM((rows, 2 * share), jnp.bfloat16),
            pltpu.VMEM((rows, width), jnp.float32),
            pltpu.SemaphoreType.DMA,
            pltpu.SemaphoreType.DMA((width // (2 * LANES),)),
            pltpu.SemaphoreType.DMA((2, 2)),
            pltpu.SemaphoreType.DMA((2, 2)),
            pltpu.SemaphoreType.DMA((2, 2)),
        ],
        compiler_params=pltpu.CompilerParams(vmem_limit_bytes=60 * MIB),
        cost_estimate=cost(12 * rows * width * share, 12 * width * share, 2 * rows * share),
        name="expert_layer",
    )(x, *mine, *others)


def combine_kernel(side_ref, rows_ref, weights_ref, y_ref, *refs):
    *more_refs, mine_ref, sent_ref, total_ref = refs
    top_count, tokens = rows_ref.shape
    half = mine_ref.shape[1]
    row = iota((y_ref.shape[0], tokens), 0)
    share = jnp.zeros(row.shape, jnp.float32)
    for c in range(top_count):
        share = jnp.where(rows_ref[c : c + 1, :] == row, weights_ref[c : c + 1, :], share)
    coarse = share.astype(jnp.bfloat16)
    fine = (share - coarse.astype(jnp.float32)).astype(jnp.bfloat16)
    y = y_ref[...]
    contract = (((0,), (0,)), ((), ()))
    total_ref[...] = lax.dot_general(coarse, y, contract, preferred_element_type=jnp.float32)
    total_ref[...] += lax.dot_general(fine, y, contract, preferred_element_type=jnp.float32)
    side = side_ref[0]
    mine = total_ref[:, pl.ds(pl.multiple_of(side * half, LANES), half)]
    for more_ref in more_refs:
        mine += more_ref[...].astype(jnp.float32)
    mine_ref[...] = mine
    sent_ref[...] = total_ref[:, pl.ds(pl.multiple_of((1 - side) * half, LANES), half)].astype(jnp.bfloat16)


def combine(side, placed, weights, y, half, more=()):
    tokens = placed.shape[1]
    rows, width = y.shape
    return pl.pallas_call(
        combine_kernel,
        out_shape=(shape_of((tokens, half), jnp.float32), shape_of((tokens, half))),
        in_specs=[SMEM] + [VMEM] * (3 + len(more)),
        out_specs=(VMEM, VMEM),
        scratch_shapes=[pltpu.VMEM((tokens, width), jnp.float32)],
        compiler_params=pltpu.CompilerParams(vmem_limit_bytes=24 * MIB),
        cost_estimate=cost(4 * rows * tokens * width, 2 * rows * width),
        name="combine",
    )(side, placed, weights, y, *more)


def local(
    residual_in,
    query_rows,
    rotated_key_rows,
    value_row_matrix,
    learned_sink_scores,
    w_out,
    norm_gain,
    expert_ids,
    route_weights,
    w_gate,
    w_up,
    w_down,
):
    tok_dev, model_width = residual_in.shape
    seq_count = lax.axis_size("seq")
    experts = w_gate.shape[0] * seq_count
    top_count = expert_ids.shape[1]
    capacity = max(2, 8 * tok_dev // experts)
    sides = lax.axis_size("tp")
    side_rows = capacity // sides
    group = seq_count // 2
    rows = experts // 2 * side_rows
    half = model_width // sides
    at_seq = lax.axis_index("seq").astype(jnp.int32)
    base = jnp.where(at_seq < group, 0, experts // 2).astype(jnp.int32).reshape(1)
    side = lax.axis_index("tp").astype(jnp.int32).reshape(1)
    first = (at_seq == 0).astype(jnp.int32).reshape(1)
    ids, route = expert_ids.T, route_weights.T

    key_values = jnp.concatenate([rotated_key_rows, value_row_matrix], axis=1)
    before = passed_along(key_values, "seq", 1)
    weights = (w_gate, w_up, w_down)
    others = [swapped(weight, "tp") for weight in weights]
    placed = places(base, side, ids, experts, side_rows)
    near = attention(first, learned_sink_scores, query_rows, key_values, before, w_out)
    near, *others = lax.optimization_barrier((near, *others))
    far = swapped(near, "tp")
    packed, sent, kept = norm_and_pack(
        side, residual_in, near, far, norm_gain, placed, ids, route, half, rows
    )

    def exchanged(block):
        block = block.reshape(group, rows // group, model_width)
        groups = [list(range(group)), list(range(group, seq_count))]
        block = lax.all_to_all(
            block, "seq", split_axis=0, concat_axis=0, axis_index_groups=groups, tiled=True
        )
        return block.reshape(rows, model_width)

    crossed = swapped_halves(sent, "seq")
    arrived = exchanged(packed)
    packed_peer, placed_peer, route_peer = pack_peer(
        base, side, crossed, swapped(crossed, "tp"), top_count, experts, side_rows, rows
    )
    packed_peer, arrived = lax.optimization_barrier((packed_peer, arrived))
    arrived_peer = exchanged(packed_peer)
    result = expert_layer(arrived, weights, others)
    result_peer = expert_layer(arrived_peer, weights, others)

    returned_peer = exchanged(result_peer)
    result, returned_peer = lax.optimization_barrier((result, returned_peer))
    returned = exchanged(result)
    mine_peer, sent_peer = combine(side, placed_peer, route_peer, returned_peer, half)
    summed_peer = (mine_peer + swapped(sent_peer, "tp").astype(jnp.float32)).astype(jnp.bfloat16)
    back = swapped_halves(summed_peer, "seq")
    mine, sent = combine(side, placed, route, returned, half, (kept, back))
    return (mine + swapped(sent, "tp").astype(jnp.float32)).astype(jnp.bfloat16)


def solution(mesh):
    placed = (
        P("seq", None),
        P("seq", "tp"),
        P("seq", "tp"),
        P("seq", "tp"),
        P("tp"),
        P("tp", None),
        P(),
        P("seq", None),
        P("seq", None),
        P("seq", None, "tp"),
        P("seq", None, "tp"),
        P("seq", "tp", None),
    )
    return jax.shard_map(
        local, mesh=mesh, in_specs=placed, out_specs=P("seq", "tp"), check_vma=False
    )
```

```python
import functools

import jax
import jax.numpy as jnp
from jax import lax
from jax.experimental import pallas as pl
from jax.experimental.pallas import tpu as pltpu
from jax.sharding import PartitionSpec as P

HEAD_SIZE = 64
WINDOW_LENGTH = 128
LANES = 128
MIB = 1024 * 1024
CUTS = 4
AHEAD = 3

neg_large = -1e30
epsilon = 1e-05

VMEM = pl.BlockSpec(memory_space=pltpu.VMEM)
SMEM = pl.BlockSpec(memory_space=pltpu.SMEM)
HBM = pl.BlockSpec(memory_space=pltpu.HBM)


def passed_along(block, axis, distance):
    devices = range(lax.axis_size(axis))
    route = [(i - distance, i) for i in devices if i - distance in devices]
    return lax.ppermute(block, axis, route)


def swapped(block, axis):
    count = lax.axis_size(axis)
    return lax.ppermute(block, axis, [(i, count - 1 - i) for i in range(count)])


def swapped_halves(block, axis):
    count = lax.axis_size(axis)
    return lax.ppermute(block, axis, [(i, (i + count // 2) % count) for i in range(count)])


def shape_of(dims, dtype=jnp.bfloat16):
    return jax.ShapeDtypeStruct(dims, dtype)


def cost(flops, moved, transcendentals=0):
    return pl.CostEstimate(flops=flops, bytes_accessed=moved, transcendentals=transcendentals)


def iota(dims, dimension):
    return lax.broadcasted_iota(jnp.int32, dims, dimension)


def rows_of(ids, experts, side_rows, base, side):
    top_count, tokens = ids.shape
    names = iota((experts, tokens), 0).astype(jnp.float32)
    hits = [ids[c : c + 1, :] == names for c in range(top_count)]
    named = sum([hit.astype(jnp.float32) for hit in hits]).astype(jnp.bfloat16)
    square = (tokens, tokens)
    earlier = (iota(square, 0) < iota(square, 1)).astype(jnp.bfloat16)
    slot = jnp.dot(named, earlier, preferred_element_type=jnp.float32) - (side * side_rows).astype(jnp.float32)
    expert = names - base.astype(jnp.float32)
    here = (slot >= 0.0) & (slot < side_rows) & (expert >= 0.0) & (expert < experts // 2)
    rows = jnp.where(here, expert * side_rows + slot, -1.0)
    lines = [jnp.sum(jnp.where(hit, rows, 0.0), axis=0, keepdims=True) for hit in hits]
    return jnp.concatenate(lines, axis=0).astype(jnp.int32)


def attention_kernel(
    first_ref, sink_hbm, q_hbm, k_hbm, v_hbm, before_ref, w_hbm, out_ref, sink_ref, q_ref, k_ref, v_ref, w_ref,
    att_ref, sems,
):
    tokens, width = q_ref.shape
    kv_heads = k_ref.shape[1] // HEAD_SIZE
    pairs = width // LANES // kv_heads
    moves = [(k_hbm, k_ref), (v_hbm, v_ref), (q_hbm, q_ref), (sink_hbm, sink_ref), (w_hbm, w_ref)]
    *loads, w_load = [pltpu.make_async_copy(source, target, sems.at[i]) for i, (source, target) in enumerate(moves)]
    for load in loads + [w_load]:
        load.start()
    low = iota((tokens, LANES), 1) < HEAD_SIZE

    def doubled(block, head):
        wide = block.astype(jnp.float32)
        turned = pltpu.roll(wide, HEAD_SIZE, 1)
        first, second = (wide, turned) if head == 0 else (turned, wide)
        return [
            jnp.where(low, first, 0.0).astype(jnp.bfloat16),
            jnp.where(low, 0.0, second).astype(jnp.bfloat16),
        ]

    own = iota((tokens, tokens), 1) <= iota((tokens, tokens), 0)
    bias = jnp.where(own, 0.0, jnp.where(first_ref[0] == 0, 0.0, neg_large))
    own_factor = jnp.where(own, 1.0, 0.0).astype(jnp.bfloat16)
    before_factor = jnp.where(own, 0.0, 1.0).astype(jnp.bfloat16)
    head_lanes = jnp.where(low, 1.0, 0.0).astype(jnp.bfloat16), jnp.where(low, 0.0, 1.0).astype(jnp.bfloat16)
    ones = jnp.concatenate(head_lanes, axis=0)
    keys_before = [jnp.concatenate(doubled(before_ref[:, :LANES], head), axis=0) for head in range(kv_heads)]
    values_before = [doubled(before_ref[:, LANES:], head) for head in range(kv_heads)]
    for load in loads:
        load.wait()
    contract = (((1,), (1,)), ((), ()))
    for head in range(kv_heads):
        keys = jnp.concatenate(doubled(k_ref[...], head), axis=0)
        values = jnp.concatenate(doubled(v_ref[...], head) + values_before[head], axis=0)
        for j in range(head * pairs, (head + 1) * pairs):
            q = q_ref[:, j * LANES : (j + 1) * LANES] * jnp.bfloat16(HEAD_SIZE**-0.5)
            near = lax.dot_general(q, keys, contract, preferred_element_type=jnp.float32)
            far = lax.dot_general(q, keys_before[head], contract, preferred_element_type=jnp.float32)
            terms, sinks = [], []
            for at in range(2):
                span = slice(at * tokens, (at + 1) * tokens)
                part = jnp.where(own, near[:, span], far[:, span]) + bias
                sink = sink_ref[2 * j + at]
                top = jnp.maximum(jnp.max(part, axis=1, keepdims=True), sink)
                terms.append(jnp.exp(part - top).astype(jnp.bfloat16))
                sinks.append(jnp.exp(sink - top))
            total = jnp.dot(jnp.concatenate(terms, axis=1), ones, preferred_element_type=jnp.float32)
            total += jnp.where(low, sinks[0], sinks[1])
            kept = [term * own_factor for term in terms] + [term * before_factor for term in terms]
            found = jnp.dot(jnp.concatenate(kept, axis=1), values, preferred_element_type=jnp.float32)
            att_ref[:, j * LANES : (j + 1) * LANES] = (found / total).astype(jnp.bfloat16)
    w_load.wait()
    step = 2 * LANES
    for at in range(0, out_ref.shape[1], step):
        out_ref[:, at : at + step] = jnp.dot(
            att_ref[...], w_ref[:, at : at + step], preferred_element_type=jnp.float32
        ).astype(jnp.bfloat16)


def attention(first, sinks, q, k, v, before, w_out):
    tokens = q.shape[0]
    return pl.pallas_call(
        attention_kernel,
        out_shape=shape_of((tokens, w_out.shape[1])),
        in_specs=[SMEM, HBM, HBM, HBM, HBM, VMEM, HBM],
        out_specs=VMEM,
        scratch_shapes=[
            pltpu.SMEM(sinks.shape, jnp.float32),
            pltpu.VMEM(q.shape, jnp.bfloat16),
            pltpu.VMEM(k.shape, jnp.bfloat16),
            pltpu.VMEM(v.shape, jnp.bfloat16),
            pltpu.VMEM(w_out.shape, jnp.bfloat16),
            pltpu.VMEM(q.shape, jnp.bfloat16),
            pltpu.SemaphoreType.DMA((5,)),
        ],
        compiler_params=pltpu.CompilerParams(vmem_limit_bytes=62_000_000),
        cost_estimate=cost(2 * tokens * w_out.size * 2, 2 * w_out.size, tokens * tokens * q.shape[1] // HEAD_SIZE),
        name="attention",
    )(first, sinks, q, k, v, before, w_out)


def pack(placed, normed, out_ref):
    rows, tokens = out_ref.shape[0], normed.shape[0]
    row = iota((rows, tokens), 0)
    taken = placed[0:1, :] == row
    for c in range(1, placed.shape[0]):
        taken = taken | (placed[c : c + 1, :] == row)
    taken = jnp.where(taken, 1.0, 0.0).astype(jnp.bfloat16)
    out_ref[...] = jnp.dot(taken, normed, preferred_element_type=jnp.float32).astype(jnp.bfloat16)


def noted(ids, weights):
    coarse = weights.astype(jnp.bfloat16).astype(jnp.float32)
    middle = (weights - coarse).astype(jnp.bfloat16).astype(jnp.float32)
    fine = weights - coarse - middle
    used = [ids.astype(jnp.float32), coarse, middle, fine]
    empty = jnp.zeros((LANES - 4 * ids.shape[0], ids.shape[1]), jnp.float32)
    return jnp.concatenate(used + [empty], axis=0).T.astype(jnp.bfloat16)


def norm_kernel(
    experts, side_rows, base_ref, side_ref, residual_ref, near_hbm, far_ref, gain_ref, ids_ref, weights_ref, out_ref,
    sent_ref, kept_ref, rows_ref, near_ref, whole_ref, sending_ref, sem,
):
    load = pltpu.make_async_copy(near_hbm, near_ref, sem)
    load.start()
    side = side_ref[0]
    rows = rows_of(ids_ref[...].astype(jnp.float32), experts, side_rows, base_ref[0], side)
    rows_ref[...] = rows
    half_tokens, half, width = sent_ref.shape[0], kept_ref.shape[1], whole_ref.shape[1]
    load.wait()
    added = near_ref[...].astype(jnp.float32) + far_ref[...].astype(jnp.float32)
    whole = (residual_ref[...].astype(jnp.float32) + added).astype(jnp.bfloat16)
    whole_ref[...] = whole
    wide = whole.astype(jnp.float32)
    mean_square = jnp.mean(wide * wide, axis=1, keepdims=True)
    normed = (wide * lax.rsqrt(mean_square + epsilon) * gain_ref[...]).astype(jnp.bfloat16)
    sending_ref[:, :width] = normed
    sending_ref[:, width:] = noted(ids_ref[...], weights_ref[...])
    kept_ref[...] = whole_ref[:, pl.ds(pl.multiple_of(side * half, LANES), half)]
    sent_ref[...] = sending_ref[pl.ds(pl.multiple_of(side * half_tokens, half_tokens), half_tokens), :]
    pack(rows, normed, out_ref)


def norm_and_pack(base, side, residual_in, near, far, gain, ids, weights, half, experts, side_rows, rows):
    tokens, width = residual_in.shape
    return pl.pallas_call(
        functools.partial(norm_kernel, experts, side_rows),
        out_shape=(
            shape_of((rows, width)),
            shape_of((tokens // 2, width + LANES)),
            shape_of((tokens, half)),
            shape_of(ids.shape, jnp.int32),
        ),
        in_specs=[SMEM, SMEM, VMEM, HBM, VMEM, VMEM, VMEM, VMEM],
        out_specs=(VMEM, VMEM, VMEM, VMEM),
        scratch_shapes=[
            pltpu.VMEM((tokens, width), jnp.bfloat16),
            pltpu.VMEM((tokens, width), jnp.bfloat16),
            pltpu.VMEM((tokens, width + LANES), jnp.bfloat16),
            pltpu.SemaphoreType.DMA,
        ],
        compiler_params=pltpu.CompilerParams(vmem_limit_bytes=24 * MIB),
        cost_estimate=cost(2 * rows * tokens * width, 2 * rows * width),
        name="norm_and_pack",
    )(base, side, residual_in, near, far, gain.reshape(1, width), ids, weights)


def peer_kernel(
    experts, side_rows, base_ref, side_ref, mine_ref, other_ref, out_ref, rows_ref, weights_ref, arrived_ref
):
    side, part = side_ref[0], mine_ref.shape[0]
    top_count = rows_ref.shape[0]
    width = out_ref.shape[1]
    arrived_ref[pl.ds(pl.multiple_of(side * part, part), part), :] = mine_ref[...]
    arrived_ref[pl.ds(pl.multiple_of((1 - side) * part, part), part), :] = other_ref[...]
    notes = arrived_ref[:, width:].astype(jnp.float32).T
    weights_ref[...] = sum([notes[k * top_count : (k + 1) * top_count, :] for k in range(2, 4)], notes[top_count : 2 * top_count, :])
    rows = rows_of(notes[:top_count, :], experts, side_rows, base_ref[0], side)
    rows_ref[...] = rows
    pack(rows, arrived_ref[:, :width], out_ref)


def pack_peer(base, side, mine, other, top_count, experts, side_rows, rows):
    part = mine.shape[0]
    width = mine.shape[1] - LANES
    return pl.pallas_call(
        functools.partial(peer_kernel, experts, side_rows),
        out_shape=(
            shape_of((rows, width)),
            shape_of((top_count, 2 * part), jnp.int32),
            shape_of((top_count, 2 * part), jnp.float32),
        ),
        in_specs=[SMEM, SMEM, VMEM, VMEM],
        out_specs=(VMEM, VMEM, VMEM),
        scratch_shapes=[pltpu.VMEM((2 * part, width + LANES), jnp.bfloat16)],
        compiler_params=pltpu.CompilerParams(vmem_limit_bytes=24 * MIB),
        cost_estimate=cost(4 * rows * part * width, 36 * rows * width),
        name="pack_peer",
    )(base, side, mine, other)


def expert_kernel(
    x_hbm, gate_hbm, up_hbm, down_hbm, gate_too_hbm, up_too_hbm, down_too_hbm, y_hbm, x_ref, y_ref, gate_ref, up_ref,
    down_ref, hidden_ref, gate_sum, up_sum, total_ref, x_sem, y_sem, gate_sem, up_sem, down_sem,
):
    rows, width = x_ref.shape
    share = gate_hbm.shape[2]
    deep, cuts = width // CUTS, share * CUTS // width
    loads = []
    for k, (gate, up) in enumerate([(gate_hbm, up_hbm), (gate_too_hbm, up_too_hbm)]):
        for c in range(CUTS):
            span = pl.ds(c * deep, deep)
            loads.append(
                [
                    pltpu.make_async_copy(gate.at[0, span], gate_ref.at[k, span], gate_sem.at[k, c]),
                    pltpu.make_async_copy(up.at[0, span], up_ref.at[k, span], up_sem.at[k, c]),
                ]
            )
    for k, down in enumerate([down_hbm, down_too_hbm]):
        for c in range(cuts):
            source, target = pl.ds(c * deep, deep), pl.ds(k * share + c * deep, deep)
            loads.append([pltpu.make_async_copy(down.at[0, source], down_ref.at[target], down_sem.at[k, c])])

    def start(number):
        if number < len(loads):
            for load in loads[number]:
                load.start()

    def arrive(number):
        for load in loads[number]:
            load.wait()
        start(number + AHEAD)

    x_load = pltpu.make_async_copy(x_hbm, x_ref, x_sem)
    x_load.start()
    for number in range(AHEAD):
        start(number)
    x_load.wait()
    for k in range(2):
        for c in range(CUTS):
            arrive(k * CUTS + c)
            span = slice(c * deep, (c + 1) * deep)
            x = x_ref[:, span]
            gate = jnp.dot(x, gate_ref[k, span, :], preferred_element_type=jnp.float32)
            up = jnp.dot(x, up_ref[k, span, :], preferred_element_type=jnp.float32)
            if c > 0:
                gate, up = gate_sum[...] + gate, up_sum[...] + up
            if c < CUTS - 1:
                gate_sum[...], up_sum[...] = gate, up
            else:
                hidden = gate * (0.5 + 0.5 * jnp.tanh(0.5 * gate)) * up
                hidden_ref[:, k * share : (k + 1) * share] = hidden.astype(jnp.bfloat16)
    for c in range(2 * cuts - 1):
        arrive(2 * CUTS + c)
        span = slice(c * deep, (c + 1) * deep)
        part = jnp.dot(hidden_ref[:, span], down_ref[span, :], preferred_element_type=jnp.float32)
        total_ref[...] = part if c == 0 else total_ref[...] + part
    arrive(2 * CUTS + 2 * cuts - 1)
    span = slice((2 * cuts - 1) * deep, 2 * cuts * deep)
    step = 2 * LANES
    stores = []
    for i in range(width // step):
        columns = slice(i * step, (i + 1) * step)
        part = jnp.dot(hidden_ref[:, span], down_ref[span, columns], preferred_element_type=jnp.float32)
        y_ref[:, columns] = (total_ref[:, columns] + part).astype(jnp.bfloat16)
        column_span = pl.ds(i * step, step)
        stores.append(pltpu.make_async_copy(y_ref.at[:, column_span], y_hbm.at[:, column_span], y_sem.at[i]))
        stores[i].start()
    for store in stores:
        store.wait()


def expert_layer(x, mine, others):
    rows, width = x.shape
    share = mine[0].shape[2]
    return pl.pallas_call(
        expert_kernel,
        out_shape=shape_of((rows, width)),
        in_specs=[HBM] * 7,
        out_specs=HBM,
        scratch_shapes=[
            pltpu.VMEM((rows, width), jnp.bfloat16),
            pltpu.VMEM((rows, width), jnp.bfloat16),
            pltpu.VMEM((2, width, share), jnp.bfloat16),
            pltpu.VMEM((2, width, share), jnp.bfloat16),
            pltpu.VMEM((2 * share, width), jnp.bfloat16),
            pltpu.VMEM((rows, 2 * share), jnp.bfloat16),
            pltpu.VMEM((rows, share), jnp.float32),
            pltpu.VMEM((rows, share), jnp.float32),
            pltpu.VMEM((rows, width), jnp.float32),
            pltpu.SemaphoreType.DMA,
            pltpu.SemaphoreType.DMA((width // (2 * LANES),)),
            pltpu.SemaphoreType.DMA((2, CUTS)),
            pltpu.SemaphoreType.DMA((2, CUTS)),
            pltpu.SemaphoreType.DMA((2, share * CUTS // width)),
        ],
        compiler_params=pltpu.CompilerParams(vmem_limit_bytes=60 * MIB),
        cost_estimate=cost(12 * rows * width * share, 12 * width * share, 2 * rows * share),
        name="expert_layer",
    )(x, *mine, *others)


def combine_kernel(side_ref, rows_ref, weights_ref, y_ref, *refs):
    *more_refs, mine_ref, sent_ref, total_ref = refs
    top_count, tokens = rows_ref.shape
    half = mine_ref.shape[1]
    row = iota((y_ref.shape[0], tokens), 0)
    share = jnp.zeros(row.shape, jnp.float32)
    for c in range(top_count):
        share = jnp.where(rows_ref[c : c + 1, :] == row, weights_ref[c : c + 1, :], share)
    coarse = share.astype(jnp.bfloat16)
    fine = (share - coarse.astype(jnp.float32)).astype(jnp.bfloat16)
    y = y_ref[...]
    contract = (((0,), (0,)), ((), ()))
    total_ref[...] = lax.dot_general(coarse, y, contract, preferred_element_type=jnp.float32)
    total_ref[...] += lax.dot_general(fine, y, contract, preferred_element_type=jnp.float32)
    side = side_ref[0]
    mine = total_ref[:, pl.ds(pl.multiple_of(side * half, LANES), half)]
    for more_ref in more_refs:
        mine += more_ref[...].astype(jnp.float32)
    mine_ref[...] = mine
    sent_ref[...] = total_ref[:, pl.ds(pl.multiple_of((1 - side) * half, LANES), half)].astype(jnp.bfloat16)


def combine(side, placed, weights, y, half, more=()):
    tokens = placed.shape[1]
    rows, width = y.shape
    return pl.pallas_call(
        combine_kernel,
        out_shape=(shape_of((tokens, half), jnp.float32), shape_of((tokens, half))),
        in_specs=[SMEM] + [VMEM] * (3 + len(more)),
        out_specs=(VMEM, VMEM),
        scratch_shapes=[pltpu.VMEM((tokens, width), jnp.float32)],
        compiler_params=pltpu.CompilerParams(vmem_limit_bytes=24 * MIB),
        cost_estimate=cost(4 * rows * tokens * width, 2 * rows * width),
        name="combine",
    )(side, placed, weights, y, *more)


def local(
    residual_in,
    query_rows,
    rotated_key_rows,
    value_row_matrix,
    learned_sink_scores,
    w_out,
    norm_gain,
    expert_ids,
    route_weights,
    w_gate,
    w_up,
    w_down,
):
    tok_dev, model_width = residual_in.shape
    seq_count = lax.axis_size("seq")
    experts = w_gate.shape[0] * seq_count
    top_count = expert_ids.shape[1]
    capacity = max(2, 8 * tok_dev // experts)
    sides = lax.axis_size("tp")
    side_rows = capacity // sides
    group = seq_count // 2
    rows = experts // 2 * side_rows
    half = model_width // sides
    at_seq = lax.axis_index("seq").astype(jnp.int32)
    base = jnp.where(at_seq < group, 0, experts // 2).astype(jnp.int32).reshape(1)
    side = lax.axis_index("tp").astype(jnp.int32).reshape(1)
    first = (at_seq == 0).astype(jnp.int32).reshape(1)
    ids, route = expert_ids.T, route_weights.T

    key_values = jnp.concatenate([rotated_key_rows, value_row_matrix], axis=1)
    before = passed_along(key_values, "seq", 1)
    weights = (w_gate, w_up, w_down)
    others = [swapped(weight, "tp") for weight in weights]
    near = attention(
        first, learned_sink_scores, query_rows, rotated_key_rows, value_row_matrix, before, w_out
    )
    near, *others = lax.optimization_barrier((near, *others))
    far = swapped(near, "tp")
    packed, sent, kept, placed = norm_and_pack(
        base, side, residual_in, near, far, norm_gain, ids, route, half, experts, side_rows, rows
    )

    def exchanged(block):
        block = block.reshape(group, rows // group, model_width)
        groups = [list(range(group)), list(range(group, seq_count))]
        block = lax.all_to_all(
            block, "seq", split_axis=0, concat_axis=0, axis_index_groups=groups, tiled=True
        )
        return block.reshape(rows, model_width)

    crossed = swapped_halves(sent, "seq")
    arrived = exchanged(packed)
    packed_peer, placed_peer, route_peer = pack_peer(
        base, side, crossed, swapped(crossed, "tp"), top_count, experts, side_rows, rows
    )
    packed_peer, arrived = lax.optimization_barrier((packed_peer, arrived))
    arrived_peer = exchanged(packed_peer)
    result = expert_layer(arrived, weights, others)
    result_peer = expert_layer(arrived_peer, weights, others)

    returned_peer = exchanged(result_peer)
    result, returned_peer = lax.optimization_barrier((result, returned_peer))
    returned = exchanged(result)
    mine_peer, sent_peer = combine(side, placed_peer, route_peer, returned_peer, half)
    summed_peer = (mine_peer + swapped(sent_peer, "tp").astype(jnp.float32)).astype(jnp.bfloat16)
    back = swapped_halves(summed_peer, "seq")
    mine, sent = combine(side, placed, route, returned, half, (kept, back))
    return (mine + swapped(sent, "tp").astype(jnp.float32)).astype(jnp.bfloat16)


def solution(mesh):
    placed = (
        P("seq", None),
        P("seq", "tp"),
        P("seq", "tp"),
        P("seq", "tp"),
        P("tp"),
        P("tp", None),
        P(),
        P("seq", None),
        P("seq", None),
        P("seq", None, "tp"),
        P("seq", None, "tp"),
        P("seq", "tp", None),
    )
    return jax.shard_map(
        local, mesh=mesh, in_specs=placed, out_specs=P("seq", "tp"), check_vma=False
    )
```

```python
import functools

import jax
import jax.numpy as jnp
from jax import lax
from jax.experimental import pallas as pl
from jax.experimental.pallas import tpu as pltpu
from jax.sharding import PartitionSpec as P

HEAD_SIZE = 64
WINDOW_LENGTH = 128
LANES = 128
MIB = 1024 * 1024
CUTS = 4
AHEAD = 3

neg_large = -1e30
epsilon = 1e-05

VMEM = pl.BlockSpec(memory_space=pltpu.VMEM)
SMEM = pl.BlockSpec(memory_space=pltpu.SMEM)
HBM = pl.BlockSpec(memory_space=pltpu.HBM)


def passed_along(block, axis, distance):
    devices = range(lax.axis_size(axis))
    route = [(i - distance, i) for i in devices if i - distance in devices]
    return lax.ppermute(block, axis, route)


def swapped(block, axis):
    count = lax.axis_size(axis)
    return lax.ppermute(block, axis, [(i, count - 1 - i) for i in range(count)])


def swapped_halves(block, axis):
    count = lax.axis_size(axis)
    return lax.ppermute(block, axis, [(i, (i + count // 2) % count) for i in range(count)])


def shape_of(dims, dtype=jnp.bfloat16):
    return jax.ShapeDtypeStruct(dims, dtype)


def cost(flops, moved, transcendentals=0):
    return pl.CostEstimate(flops=flops, bytes_accessed=moved, transcendentals=transcendentals)


def iota(dims, dimension):
    return lax.broadcasted_iota(jnp.int32, dims, dimension)


def rows_of(ids, experts, side_rows, base, side):
    top_count, tokens = ids.shape
    names = iota((experts, tokens), 0).astype(jnp.float32)
    hits = [ids[c : c + 1, :] == names for c in range(top_count)]
    named = sum([hit.astype(jnp.float32) for hit in hits]).astype(jnp.bfloat16)
    square = (tokens, tokens)
    earlier = (iota(square, 0) < iota(square, 1)).astype(jnp.bfloat16)
    slot = jnp.dot(named, earlier, preferred_element_type=jnp.float32) - (side * side_rows).astype(jnp.float32)
    expert = names - base.astype(jnp.float32)
    here = (slot >= 0.0) & (slot < side_rows) & (expert >= 0.0) & (expert < experts // 2)
    rows = jnp.where(here, expert * side_rows + slot, -1.0)
    lines = [jnp.sum(jnp.where(hit, rows, 0.0), axis=0, keepdims=True) for hit in hits]
    return jnp.concatenate(lines, axis=0).astype(jnp.int32)


def attention_kernel(
    first_ref, sink_hbm, q_hbm, k_hbm, v_hbm, before_ref, w_hbm, out_ref, sink_ref, q_ref, k_ref, v_ref, w_ref,
    att_ref, sems,
):
    tokens, width = q_ref.shape
    kv_heads = k_ref.shape[1] // HEAD_SIZE
    pairs = width // LANES // kv_heads
    moves = [(k_hbm, k_ref), (v_hbm, v_ref), (q_hbm, q_ref), (sink_hbm, sink_ref), (w_hbm, w_ref)]
    *loads, w_load = [pltpu.make_async_copy(source, target, sems.at[i]) for i, (source, target) in enumerate(moves)]
    for load in loads + [w_load]:
        load.start()
    low = iota((tokens, LANES), 1) < HEAD_SIZE

    def doubled(block, head):
        wide = block.astype(jnp.float32)
        turned = pltpu.roll(wide, HEAD_SIZE, 1)
        first, second = (wide, turned) if head == 0 else (turned, wide)
        return [
            jnp.where(low, first, 0.0).astype(jnp.bfloat16),
            jnp.where(low, 0.0, second).astype(jnp.bfloat16),
        ]

    own = iota((tokens, tokens), 1) <= iota((tokens, tokens), 0)
    bias = jnp.where(own, 0.0, jnp.where(first_ref[0] == 0, 0.0, neg_large))
    own_factor = jnp.where(own, 1.0, 0.0).astype(jnp.bfloat16)
    before_factor = jnp.where(own, 0.0, 1.0).astype(jnp.bfloat16)
    head_lanes = jnp.where(low, 1.0, 0.0).astype(jnp.bfloat16), jnp.where(low, 0.0, 1.0).astype(jnp.bfloat16)
    ones = jnp.concatenate(head_lanes, axis=0)
    keys_before = [jnp.concatenate(doubled(before_ref[:, :LANES], head), axis=0) for head in range(kv_heads)]
    values_before = [doubled(before_ref[:, LANES:], head) for head in range(kv_heads)]
    for load in loads:
        load.wait()
    contract = (((1,), (1,)), ((), ()))
    for head in range(kv_heads):
        keys = jnp.concatenate(doubled(k_ref[...], head), axis=0)
        values = jnp.concatenate(doubled(v_ref[...], head) + values_before[head], axis=0)
        for j in range(head * pairs, (head + 1) * pairs):
            q = q_ref[:, j * LANES : (j + 1) * LANES] * jnp.bfloat16(HEAD_SIZE**-0.5)
            near = lax.dot_general(q, keys, contract, preferred_element_type=jnp.float32)
            far = lax.dot_general(q, keys_before[head], contract, preferred_element_type=jnp.float32)
            terms, sinks = [], []
            for at in range(2):
                span = slice(at * tokens, (at + 1) * tokens)
                part = jnp.where(own, near[:, span], far[:, span]) + bias
                sink = sink_ref[2 * j + at]
                top = jnp.maximum(jnp.max(part, axis=1, keepdims=True), sink)
                terms.append(jnp.exp(part - top).astype(jnp.bfloat16))
                sinks.append(jnp.exp(sink - top))
            total = jnp.dot(jnp.concatenate(terms, axis=1), ones, preferred_element_type=jnp.float32)
            total += jnp.where(low, sinks[0], sinks[1])
            kept = [term * own_factor for term in terms] + [term * before_factor for term in terms]
            found = jnp.dot(jnp.concatenate(kept, axis=1), values, preferred_element_type=jnp.float32)
            att_ref[:, j * LANES : (j + 1) * LANES] = (found / total).astype(jnp.bfloat16)
    w_load.wait()
    step = 2 * LANES
    for at in range(0, out_ref.shape[1], step):
        out_ref[:, at : at + step] = jnp.dot(
            att_ref[...], w_ref[:, at : at + step], preferred_element_type=jnp.float32
        ).astype(jnp.bfloat16)


def attention(first, sinks, q, k, v, before, w_out):
    tokens = q.shape[0]
    return pl.pallas_call(
        attention_kernel,
        out_shape=shape_of((tokens, w_out.shape[1])),
        in_specs=[SMEM, HBM, HBM, HBM, HBM, VMEM, HBM],
        out_specs=VMEM,
        scratch_shapes=[
            pltpu.SMEM(sinks.shape, jnp.float32),
            pltpu.VMEM(q.shape, jnp.bfloat16),
            pltpu.VMEM(k.shape, jnp.bfloat16),
            pltpu.VMEM(v.shape, jnp.bfloat16),
            pltpu.VMEM(w_out.shape, jnp.bfloat16),
            pltpu.VMEM(q.shape, jnp.bfloat16),
            pltpu.SemaphoreType.DMA((5,)),
        ],
        compiler_params=pltpu.CompilerParams(vmem_limit_bytes=62_000_000),
        cost_estimate=cost(2 * tokens * w_out.size * 2, 2 * w_out.size, tokens * tokens * q.shape[1] // HEAD_SIZE),
        name="attention",
    )(first, sinks, q, k, v, before, w_out)


def pack(placed, normed, out_ref):
    rows, tokens = out_ref.shape[0], normed.shape[0]
    row = iota((rows, tokens), 0)
    taken = placed[0:1, :] == row
    for c in range(1, placed.shape[0]):
        taken = taken | (placed[c : c + 1, :] == row)
    taken = jnp.where(taken, 1.0, 0.0).astype(jnp.bfloat16)
    out_ref[...] = jnp.dot(taken, normed, preferred_element_type=jnp.float32).astype(jnp.bfloat16)


def noted(ids, weights):
    coarse = weights.astype(jnp.bfloat16).astype(jnp.float32)
    middle = (weights - coarse).astype(jnp.bfloat16).astype(jnp.float32)
    fine = weights - coarse - middle
    used = [ids.astype(jnp.float32), coarse, middle, fine]
    empty = jnp.zeros((LANES - 4 * ids.shape[0], ids.shape[1]), jnp.float32)
    return jnp.concatenate(used + [empty], axis=0).T.astype(jnp.bfloat16)


def norm_kernel(
    experts, side_rows, base_ref, side_ref, residual_ref, near_hbm, far_ref, gain_ref, ids_ref, weights_ref, out_ref,
    sent_ref, kept_ref, rows_ref, near_ref, whole_ref, sending_ref, sem,
):
    load = pltpu.make_async_copy(near_hbm, near_ref, sem)
    load.start()
    side = side_ref[0]
    rows = rows_of(ids_ref[...].astype(jnp.float32), experts, side_rows, base_ref[0], side)
    rows_ref[...] = rows
    half_tokens, half, width = sent_ref.shape[0], kept_ref.shape[1], whole_ref.shape[1]
    load.wait()
    added = near_ref[...].astype(jnp.float32) + far_ref[...].astype(jnp.float32)
    whole = (residual_ref[...].astype(jnp.float32) + added).astype(jnp.bfloat16)
    whole_ref[...] = whole
    wide = whole.astype(jnp.float32)
    mean_square = jnp.mean(wide * wide, axis=1, keepdims=True)
    normed = (wide * lax.rsqrt(mean_square + epsilon) * gain_ref[...]).astype(jnp.bfloat16)
    sending_ref[:, :width] = normed
    sending_ref[:, width:] = noted(ids_ref[...], weights_ref[...])
    kept_ref[...] = whole_ref[:, pl.ds(pl.multiple_of(side * half, LANES), half)]
    sent_ref[...] = sending_ref[pl.ds(pl.multiple_of(side * half_tokens, half_tokens), half_tokens), :]
    pack(rows, normed, out_ref)


def norm_and_pack(base, side, residual_in, near, far, gain, ids, weights, half, experts, side_rows, rows):
    tokens, width = residual_in.shape
    return pl.pallas_call(
        functools.partial(norm_kernel, experts, side_rows),
        out_shape=(
            shape_of((rows, width)),
            shape_of((tokens // 2, width + LANES)),
            shape_of((tokens, half)),
            shape_of(ids.shape, jnp.int32),
        ),
        in_specs=[SMEM, SMEM, VMEM, HBM, VMEM, VMEM, VMEM, VMEM],
        out_specs=(VMEM, VMEM, VMEM, VMEM),
        scratch_shapes=[
            pltpu.VMEM((tokens, width), jnp.bfloat16),
            pltpu.VMEM((tokens, width), jnp.bfloat16),
            pltpu.VMEM((tokens, width + LANES), jnp.bfloat16),
            pltpu.SemaphoreType.DMA,
        ],
        compiler_params=pltpu.CompilerParams(vmem_limit_bytes=24 * MIB),
        cost_estimate=cost(2 * rows * tokens * width, 2 * rows * width),
        name="norm_and_pack",
    )(base, side, residual_in, near, far, gain.reshape(1, width), ids, weights)


def peer_kernel(
    experts, side_rows, base_ref, side_ref, mine_ref, other_ref, out_ref, rows_ref, weights_ref, arrived_ref
):
    side, part = side_ref[0], mine_ref.shape[0]
    top_count = rows_ref.shape[0]
    width = out_ref.shape[1]
    arrived_ref[pl.ds(pl.multiple_of(side * part, part), part), :] = mine_ref[...]
    arrived_ref[pl.ds(pl.multiple_of((1 - side) * part, part), part), :] = other_ref[...]
    notes = arrived_ref[:, width:].astype(jnp.float32).T
    weights_ref[...] = sum([notes[k * top_count : (k + 1) * top_count, :] for k in range(2, 4)], notes[top_count : 2 * top_count, :])
    rows = rows_of(notes[:top_count, :], experts, side_rows, base_ref[0], side)
    rows_ref[...] = rows
    pack(rows, arrived_ref[:, :width], out_ref)


def pack_peer(base, side, mine, other, top_count, experts, side_rows, rows):
    part = mine.shape[0]
    width = mine.shape[1] - LANES
    return pl.pallas_call(
        functools.partial(peer_kernel, experts, side_rows),
        out_shape=(
            shape_of((rows, width)),
            shape_of((top_count, 2 * part), jnp.int32),
            shape_of((top_count, 2 * part), jnp.float32),
        ),
        in_specs=[SMEM, SMEM, VMEM, VMEM],
        out_specs=(VMEM, VMEM, VMEM),
        scratch_shapes=[pltpu.VMEM((2 * part, width + LANES), jnp.bfloat16)],
        compiler_params=pltpu.CompilerParams(vmem_limit_bytes=24 * MIB),
        cost_estimate=cost(400 * rows * part * width, 72 * rows * width),
        name="pack_peer",
    )(base, side, mine, other)


def expert_kernel(
    x_hbm, gate_hbm, up_hbm, down_hbm, gate_too_hbm, up_too_hbm, down_too_hbm, y_hbm, x_ref, y_ref, gate_ref, up_ref,
    down_ref, hidden_ref, gate_sum, up_sum, total_ref, x_sem, y_sem, gate_sem, up_sem, down_sem,
):
    rows, width = x_ref.shape
    share = gate_hbm.shape[2]
    deep, cuts = width // CUTS, share * CUTS // width
    loads = []
    for k, (gate, up) in enumerate([(gate_hbm, up_hbm), (gate_too_hbm, up_too_hbm)]):
        for c in range(CUTS):
            span = pl.ds(c * deep, deep)
            loads.append(
                [
                    pltpu.make_async_copy(gate.at[0, span], gate_ref.at[k, span], gate_sem.at[k, c]),
                    pltpu.make_async_copy(up.at[0, span], up_ref.at[k, span], up_sem.at[k, c]),
                ]
            )
    for k, down in enumerate([down_hbm, down_too_hbm]):
        for c in range(cuts):
            source, target = pl.ds(c * deep, deep), pl.ds(k * share + c * deep, deep)
            loads.append([pltpu.make_async_copy(down.at[0, source], down_ref.at[target], down_sem.at[k, c])])

    def start(number):
        if number < len(loads):
            for load in loads[number]:
                load.start()

    def arrive(number):
        for load in loads[number]:
            load.wait()
        start(number + AHEAD)

    x_load = pltpu.make_async_copy(x_hbm, x_ref, x_sem)
    x_load.start()
    for number in range(AHEAD):
        start(number)
    x_load.wait()
    for k in range(2):
        for c in range(CUTS):
            arrive(k * CUTS + c)
            span = slice(c * deep, (c + 1) * deep)
            x = x_ref[:, span]
            gate = jnp.dot(x, gate_ref[k, span, :], preferred_element_type=jnp.float32)
            up = jnp.dot(x, up_ref[k, span, :], preferred_element_type=jnp.float32)
            if c > 0:
                gate, up = gate_sum[...] + gate, up_sum[...] + up
            if c < CUTS - 1:
                gate_sum[...], up_sum[...] = gate, up
            else:
                hidden = gate * (0.5 + 0.5 * jnp.tanh(0.5 * gate)) * up
                hidden_ref[:, k * share : (k + 1) * share] = hidden.astype(jnp.bfloat16)
    for c in range(2 * cuts - 1):
        arrive(2 * CUTS + c)
        span = slice(c * deep, (c + 1) * deep)
        part = jnp.dot(hidden_ref[:, span], down_ref[span, :], preferred_element_type=jnp.float32)
        total_ref[...] = part if c == 0 else total_ref[...] + part
    arrive(2 * CUTS + 2 * cuts - 1)
    span = slice((2 * cuts - 1) * deep, 2 * cuts * deep)
    step = 2 * LANES
    stores = []
    for i in range(width // step):
        columns = slice(i * step, (i + 1) * step)
        part = jnp.dot(hidden_ref[:, span], down_ref[span, columns], preferred_element_type=jnp.float32)
        y_ref[:, columns] = (total_ref[:, columns] + part).astype(jnp.bfloat16)
        column_span = pl.ds(i * step, step)
        stores.append(pltpu.make_async_copy(y_ref.at[:, column_span], y_hbm.at[:, column_span], y_sem.at[i]))
        stores[i].start()
    for store in stores:
        store.wait()


def expert_layer(x, mine, others):
    rows, width = x.shape
    share = mine[0].shape[2]
    return pl.pallas_call(
        expert_kernel,
        out_shape=shape_of((rows, width)),
        in_specs=[HBM] * 7,
        out_specs=HBM,
        scratch_shapes=[
            pltpu.VMEM((rows, width), jnp.bfloat16),
            pltpu.VMEM((rows, width), jnp.bfloat16),
            pltpu.VMEM((2, width, share), jnp.bfloat16),
            pltpu.VMEM((2, width, share), jnp.bfloat16),
            pltpu.VMEM((2 * share, width), jnp.bfloat16),
            pltpu.VMEM((rows, 2 * share), jnp.bfloat16),
            pltpu.VMEM((rows, share), jnp.float32),
            pltpu.VMEM((rows, share), jnp.float32),
            pltpu.VMEM((rows, width), jnp.float32),
            pltpu.SemaphoreType.DMA,
            pltpu.SemaphoreType.DMA((width // (2 * LANES),)),
            pltpu.SemaphoreType.DMA((2, CUTS)),
            pltpu.SemaphoreType.DMA((2, CUTS)),
            pltpu.SemaphoreType.DMA((2, share * CUTS // width)),
        ],
        compiler_params=pltpu.CompilerParams(vmem_limit_bytes=60 * MIB),
        cost_estimate=cost(12 * rows * width * share, 12 * width * share, 2 * rows * share),
        name="expert_layer",
    )(x, *mine, *others)


def combine_kernel(side_ref, rows_ref, weights_ref, y_ref, *refs):
    *more_refs, mine_ref, sent_ref, total_ref = refs
    top_count, tokens = rows_ref.shape
    half = mine_ref.shape[1]
    row = iota((y_ref.shape[0], tokens), 0)
    share = jnp.zeros(row.shape, jnp.float32)
    for c in range(top_count):
        share = jnp.where(rows_ref[c : c + 1, :] == row, weights_ref[c : c + 1, :], share)
    coarse = share.astype(jnp.bfloat16)
    fine = (share - coarse.astype(jnp.float32)).astype(jnp.bfloat16)
    y = y_ref[...]
    contract = (((0,), (0,)), ((), ()))
    total_ref[...] = lax.dot_general(coarse, y, contract, preferred_element_type=jnp.float32)
    total_ref[...] += lax.dot_general(fine, y, contract, preferred_element_type=jnp.float32)
    side = side_ref[0]
    mine = total_ref[:, pl.ds(pl.multiple_of(side * half, LANES), half)]
    for more_ref in more_refs:
        mine += more_ref[...].astype(jnp.float32)
    mine_ref[...] = mine
    sent_ref[...] = total_ref[:, pl.ds(pl.multiple_of((1 - side) * half, LANES), half)].astype(jnp.bfloat16)


def combine(side, placed, weights, y, half, more=()):
    tokens = placed.shape[1]
    rows, width = y.shape
    return pl.pallas_call(
        combine_kernel,
        out_shape=(shape_of((tokens, half), jnp.float32), shape_of((tokens, half))),
        in_specs=[SMEM] + [VMEM] * (3 + len(more)),
        out_specs=(VMEM, VMEM),
        scratch_shapes=[pltpu.VMEM((tokens, width), jnp.float32)],
        compiler_params=pltpu.CompilerParams(vmem_limit_bytes=24 * MIB),
        cost_estimate=cost(4 * rows * tokens * width, 2 * rows * width),
        name="combine",
    )(side, placed, weights, y, *more)


def local(
    residual_in,
    query_rows,
    rotated_key_rows,
    value_row_matrix,
    learned_sink_scores,
    w_out,
    norm_gain,
    expert_ids,
    route_weights,
    w_gate,
    w_up,
    w_down,
):
    tok_dev, model_width = residual_in.shape
    seq_count = lax.axis_size("seq")
    experts = w_gate.shape[0] * seq_count
    top_count = expert_ids.shape[1]
    capacity = max(2, 8 * tok_dev // experts)
    sides = lax.axis_size("tp")
    side_rows = capacity // sides
    group = seq_count // 2
    rows = experts // 2 * side_rows
    half = model_width // sides
    at_seq = lax.axis_index("seq").astype(jnp.int32)
    base = jnp.where(at_seq < group, 0, experts // 2).astype(jnp.int32).reshape(1)
    side = lax.axis_index("tp").astype(jnp.int32).reshape(1)
    first = (at_seq == 0).astype(jnp.int32).reshape(1)
    ids, route = expert_ids.T, route_weights.T

    key_values = jnp.concatenate([rotated_key_rows, value_row_matrix], axis=1)
    before = passed_along(key_values, "seq", 1)
    weights = (w_gate, w_up, w_down)
    others = [swapped(weight, "tp") for weight in weights]
    near = attention(
        first, learned_sink_scores, query_rows, rotated_key_rows, value_row_matrix, before, w_out
    )
    near, *others = lax.optimization_barrier((near, *others))
    far = swapped(near, "tp")
    packed, sent, kept, placed = norm_and_pack(
        base, side, residual_in, near, far, norm_gain, ids, route, half, experts, side_rows, rows
    )

    def exchanged(block):
        block = block.reshape(group, rows // group, model_width)
        groups = [list(range(group)), list(range(group, seq_count))]
        block = lax.all_to_all(
            block, "seq", split_axis=0, concat_axis=0, axis_index_groups=groups, tiled=True
        )
        return block.reshape(rows, model_width)

    crossed = swapped_halves(sent, "seq")
    arrived = exchanged(packed)
    packed_peer, placed_peer, route_peer = pack_peer(
        base, side, crossed, swapped(crossed, "tp"), top_count, experts, side_rows, rows
    )
    packed_peer, arrived = lax.optimization_barrier((packed_peer, arrived))
    arrived_peer = exchanged(packed_peer)
    result = expert_layer(arrived, weights, others)
    result, arrived_peer = lax.optimization_barrier((result, arrived_peer))
    returned = exchanged(result)
    result_peer = expert_layer(arrived_peer, weights, others)
    returned, result_peer = lax.optimization_barrier((returned, result_peer))
    returned_peer = exchanged(result_peer)

    mine, sent = combine(side, placed, route, returned, half, (kept,))
    mine_peer, sent_peer = combine(side, placed_peer, route_peer, returned_peer, half)
    summed_peer = (mine_peer + swapped(sent_peer, "tp").astype(jnp.float32)).astype(jnp.bfloat16)
    back = swapped_halves(summed_peer, "seq").astype(jnp.float32)
    return (mine + swapped(sent, "tp").astype(jnp.float32) + back).astype(jnp.bfloat16)


def solution(mesh):
    placed = (
        P("seq", None),
        P("seq", "tp"),
        P("seq", "tp"),
        P("seq", "tp"),
        P("tp"),
        P("tp", None),
        P(),
        P("seq", None),
        P("seq", None),
        P("seq", None, "tp"),
        P("seq", None, "tp"),
        P("seq", "tp", None),
    )
    return jax.shard_map(
        local, mesh=mesh, in_specs=placed, out_specs=P("seq", "tp"), check_vma=False
    )
```

```python
import functools

import jax
import jax.numpy as jnp
from jax import lax
from jax.experimental import pallas as pl
from jax.experimental.pallas import tpu as pltpu
from jax.sharding import PartitionSpec as P

HEAD_SIZE = 64
WINDOW_LENGTH = 128
LANES = 128
MIB = 1024 * 1024
CUTS = 4
AHEAD = 3

neg_large = -1e30
epsilon = 1e-05

VMEM = pl.BlockSpec(memory_space=pltpu.VMEM)
SMEM = pl.BlockSpec(memory_space=pltpu.SMEM)
HBM = pl.BlockSpec(memory_space=pltpu.HBM)


def passed_along(block, axis, distance):
    devices = range(lax.axis_size(axis))
    route = [(i - distance, i) for i in devices if i - distance in devices]
    return lax.ppermute(block, axis, route)


def swapped(block, axis):
    count = lax.axis_size(axis)
    return lax.ppermute(block, axis, [(i, count - 1 - i) for i in range(count)])


def paired(block, axis):
    half = lax.axis_size(axis) // 2
    pairs = [[i, i + half] for i in range(half)]
    return lax.all_gather(block, axis, axis=0, axis_index_groups=pairs, tiled=True)


def shape_of(dims, dtype=jnp.bfloat16):
    return jax.ShapeDtypeStruct(dims, dtype)


def cost(flops, moved, transcendentals=0):
    return pl.CostEstimate(flops=flops, bytes_accessed=moved, transcendentals=transcendentals)


def iota(dims, dimension):
    return lax.broadcasted_iota(jnp.int32, dims, dimension)


def rows_of(ids, experts, side_rows, base, side):
    top_count, tokens = ids.shape
    names = iota((experts, tokens), 0).astype(jnp.float32)
    hits = [ids[c : c + 1, :] == names for c in range(top_count)]
    named = sum([hit.astype(jnp.float32) for hit in hits]).astype(jnp.bfloat16)
    square = (tokens, tokens)
    earlier = (iota(square, 0) < iota(square, 1)).astype(jnp.bfloat16)
    slot = jnp.dot(named, earlier, preferred_element_type=jnp.float32) - (side * side_rows).astype(jnp.float32)
    expert = names - base.astype(jnp.float32)
    here = (slot >= 0.0) & (slot < side_rows) & (expert >= 0.0) & (expert < experts // 2)
    rows = jnp.where(here, expert * side_rows + slot, -1.0)
    lines = [jnp.sum(jnp.where(hit, rows, 0.0), axis=0, keepdims=True) for hit in hits]
    return jnp.concatenate(lines, axis=0).astype(jnp.int32)


def attention_kernel(
    first_ref, sink_hbm, q_hbm, k_hbm, v_hbm, before_ref, w_hbm, out_ref, sink_ref, q_ref, k_ref, v_ref, w_ref,
    att_ref, sems,
):
    tokens, width = q_ref.shape
    kv_heads = k_ref.shape[1] // HEAD_SIZE
    pairs = width // LANES // kv_heads
    moves = [(k_hbm, k_ref), (v_hbm, v_ref), (q_hbm, q_ref), (sink_hbm, sink_ref), (w_hbm, w_ref)]
    *loads, w_load = [pltpu.make_async_copy(source, target, sems.at[i]) for i, (source, target) in enumerate(moves)]
    for load in loads + [w_load]:
        load.start()
    low = iota((tokens, LANES), 1) < HEAD_SIZE

    def doubled(block, head):
        wide = block.astype(jnp.float32)
        turned = pltpu.roll(wide, HEAD_SIZE, 1)
        first, second = (wide, turned) if head == 0 else (turned, wide)
        return [
            jnp.where(low, first, 0.0).astype(jnp.bfloat16),
            jnp.where(low, 0.0, second).astype(jnp.bfloat16),
        ]

    own = iota((tokens, tokens), 1) <= iota((tokens, tokens), 0)
    bias = jnp.where(own, 0.0, jnp.where(first_ref[0] == 0, 0.0, neg_large))
    own_factor = jnp.where(own, 1.0, 0.0).astype(jnp.bfloat16)
    before_factor = jnp.where(own, 0.0, 1.0).astype(jnp.bfloat16)
    head_lanes = jnp.where(low, 1.0, 0.0).astype(jnp.bfloat16), jnp.where(low, 0.0, 1.0).astype(jnp.bfloat16)
    ones = jnp.concatenate(head_lanes, axis=0)
    keys_before = [jnp.concatenate(doubled(before_ref[:, :LANES], head), axis=0) for head in range(kv_heads)]
    values_before = [doubled(before_ref[:, LANES:], head) for head in range(kv_heads)]
    for load in loads:
        load.wait()
    contract = (((1,), (1,)), ((), ()))
    for head in range(kv_heads):
        keys = jnp.concatenate(doubled(k_ref[...], head), axis=0)
        values = jnp.concatenate(doubled(v_ref[...], head) + values_before[head], axis=0)
        for j in range(head * pairs, (head + 1) * pairs):
            q = q_ref[:, j * LANES : (j + 1) * LANES] * jnp.bfloat16(HEAD_SIZE**-0.5)
            near = lax.dot_general(q, keys, contract, preferred_element_type=jnp.float32)
            far = lax.dot_general(q, keys_before[head], contract, preferred_element_type=jnp.float32)
            terms, sinks = [], []
            for at in range(2):
                span = slice(at * tokens, (at + 1) * tokens)
                part = jnp.where(own, near[:, span], far[:, span]) + bias
                sink = sink_ref[2 * j + at]
                top = jnp.maximum(jnp.max(part, axis=1, keepdims=True), sink)
                terms.append(jnp.exp(part - top).astype(jnp.bfloat16))
                sinks.append(jnp.exp(sink - top))
            total = jnp.dot(jnp.concatenate(terms, axis=1), ones, preferred_element_type=jnp.float32)
            total += jnp.where(low, sinks[0], sinks[1])
            kept = [term * own_factor for term in terms] + [term * before_factor for term in terms]
            found = jnp.dot(jnp.concatenate(kept, axis=1), values, preferred_element_type=jnp.float32)
            att_ref[:, j * LANES : (j + 1) * LANES] = (found / total).astype(jnp.bfloat16)
    w_load.wait()
    step = 2 * LANES
    for at in range(0, out_ref.shape[1], step):
        out_ref[:, at : at + step] = jnp.dot(
            att_ref[...], w_ref[:, at : at + step], preferred_element_type=jnp.float32
        ).astype(jnp.bfloat16)


def attention(first, sinks, q, k, v, before, w_out):
    tokens = q.shape[0]
    return pl.pallas_call(
        attention_kernel,
        out_shape=shape_of((tokens, w_out.shape[1])),
        in_specs=[SMEM, HBM, HBM, HBM, HBM, VMEM, HBM],
        out_specs=VMEM,
        scratch_shapes=[
            pltpu.SMEM(sinks.shape, jnp.float32),
            pltpu.VMEM(q.shape, jnp.bfloat16),
            pltpu.VMEM(k.shape, jnp.bfloat16),
            pltpu.VMEM(v.shape, jnp.bfloat16),
            pltpu.VMEM(w_out.shape, jnp.bfloat16),
            pltpu.VMEM(q.shape, jnp.bfloat16),
            pltpu.SemaphoreType.DMA((5,)),
        ],
        compiler_params=pltpu.CompilerParams(vmem_limit_bytes=62_000_000),
        cost_estimate=cost(2 * tokens * w_out.size * 2, 2 * w_out.size, tokens * tokens * q.shape[1] // HEAD_SIZE),
        name="attention",
    )(first, sinks, q, k, v, before, w_out)


def pack(placed, normed, out_ref):
    rows, tokens = out_ref.shape[0], normed.shape[0]
    row = iota((rows, tokens), 0)
    taken = placed[0:1, :] == row
    for c in range(1, placed.shape[0]):
        taken = taken | (placed[c : c + 1, :] == row)
    taken = jnp.where(taken, 1.0, 0.0).astype(jnp.bfloat16)
    out_ref[...] = jnp.dot(taken, normed, preferred_element_type=jnp.float32).astype(jnp.bfloat16)


def noted(ids, weights):
    coarse = weights.astype(jnp.bfloat16).astype(jnp.float32)
    middle = (weights - coarse).astype(jnp.bfloat16).astype(jnp.float32)
    fine = weights - coarse - middle
    used = [ids.astype(jnp.float32), coarse, middle, fine]
    empty = jnp.zeros((LANES - 4 * ids.shape[0], ids.shape[1]), jnp.float32)
    return jnp.concatenate(used + [empty], axis=0).T.astype(jnp.bfloat16)


def norm_kernel(
    experts, side_rows, base_ref, side_ref, residual_ref, near_hbm, far_ref, gain_ref, ids_ref, weights_ref, out_ref,
    sent_ref, kept_ref, rows_ref, near_ref, whole_ref, sending_ref, sem,
):
    load = pltpu.make_async_copy(near_hbm, near_ref, sem)
    load.start()
    side = side_ref[0]
    rows = rows_of(ids_ref[...].astype(jnp.float32), experts, side_rows, base_ref[0], side)
    rows_ref[...] = rows
    half_tokens, half, width = sent_ref.shape[0], kept_ref.shape[1], whole_ref.shape[1]
    load.wait()
    added = near_ref[...].astype(jnp.float32) + far_ref[...].astype(jnp.float32)
    whole = (residual_ref[...].astype(jnp.float32) + added).astype(jnp.bfloat16)
    whole_ref[...] = whole
    wide = whole.astype(jnp.float32)
    mean_square = jnp.mean(wide * wide, axis=1, keepdims=True)
    normed = (wide * lax.rsqrt(mean_square + epsilon) * gain_ref[...]).astype(jnp.bfloat16)
    sending_ref[:, :width] = normed
    sending_ref[:, width:] = noted(ids_ref[...], weights_ref[...])
    kept_ref[...] = whole_ref[:, pl.ds(pl.multiple_of(side * half, LANES), half)]
    sent_ref[...] = sending_ref[pl.ds(pl.multiple_of(side * half_tokens, half_tokens), half_tokens), :]
    pack(rows, normed, out_ref)


def norm_and_pack(base, side, residual_in, near, far, gain, ids, weights, half, experts, side_rows, rows):
    tokens, width = residual_in.shape
    return pl.pallas_call(
        functools.partial(norm_kernel, experts, side_rows),
        out_shape=(
            shape_of((rows, width)),
            shape_of((tokens // 2, width + LANES)),
            shape_of((tokens, half)),
            shape_of(ids.shape, jnp.int32),
        ),
        in_specs=[SMEM, SMEM, VMEM, HBM, VMEM, VMEM, VMEM, VMEM],
        out_specs=(VMEM, VMEM, VMEM, VMEM),
        scratch_shapes=[
            pltpu.VMEM((tokens, width), jnp.bfloat16),
            pltpu.VMEM((tokens, width), jnp.bfloat16),
            pltpu.VMEM((tokens, width + LANES), jnp.bfloat16),
            pltpu.SemaphoreType.DMA,
        ],
        compiler_params=pltpu.CompilerParams(vmem_limit_bytes=24 * MIB),
        cost_estimate=cost(2 * rows * tokens * width, 2 * rows * width),
        name="norm_and_pack",
    )(base, side, residual_in, near, far, gain.reshape(1, width), ids, weights)


def peer_kernel(
    experts, side_rows, base_ref, side_ref, mine_ref, other_ref, out_ref, rows_ref, weights_ref, arrived_ref
):
    side, part = side_ref[0], mine_ref.shape[0] // 2
    top_count = rows_ref.shape[0]
    width = out_ref.shape[1]
    peer = pl.ds(pl.multiple_of(jnp.where(base_ref[0] == 0, part, 0), part), part)
    arrived_ref[pl.ds(pl.multiple_of(side * part, part), part), :] = mine_ref[peer, :]
    arrived_ref[pl.ds(pl.multiple_of((1 - side) * part, part), part), :] = other_ref[peer, :]
    notes = arrived_ref[:, width:].astype(jnp.float32).T
    weights_ref[...] = sum([notes[k * top_count : (k + 1) * top_count, :] for k in range(2, 4)], notes[top_count : 2 * top_count, :])
    rows = rows_of(notes[:top_count, :], experts, side_rows, base_ref[0], side)
    rows_ref[...] = rows
    pack(rows, arrived_ref[:, :width], out_ref)


def pack_peer(base, side, mine, other, top_count, experts, side_rows, rows):
    part = mine.shape[0] // 2
    width = mine.shape[1] - LANES
    return pl.pallas_call(
        functools.partial(peer_kernel, experts, side_rows),
        out_shape=(
            shape_of((rows, width)),
            shape_of((top_count, 2 * part), jnp.int32),
            shape_of((top_count, 2 * part), jnp.float32),
        ),
        in_specs=[SMEM, SMEM, VMEM, VMEM],
        out_specs=(VMEM, VMEM, VMEM),
        scratch_shapes=[pltpu.VMEM((2 * part, width + LANES), jnp.bfloat16)],
        compiler_params=pltpu.CompilerParams(vmem_limit_bytes=24 * MIB),
        cost_estimate=cost(4 * rows * part * width, 2 * rows * width),
        name="pack_peer",
    )(base, side, mine, other)


def expert_kernel(
    x_hbm, gate_hbm, up_hbm, down_hbm, gate_too_hbm, up_too_hbm, down_too_hbm, y_hbm, x_ref, y_ref, gate_ref, up_ref,
    down_ref, hidden_ref, gate_sum, up_sum, total_ref, x_sem, y_sem, gate_sem, up_sem, down_sem,
):
    rows, width = x_ref.shape
    share = gate_hbm.shape[2]
    deep, cuts = width // CUTS, share * CUTS // width
    loads = []
    for k, (gate, up) in enumerate([(gate_hbm, up_hbm), (gate_too_hbm, up_too_hbm)]):
        for c in range(CUTS):
            span = pl.ds(c * deep, deep)
            loads.append(
                [
                    pltpu.make_async_copy(gate.at[0, span], gate_ref.at[k, span], gate_sem.at[k, c]),
                    pltpu.make_async_copy(up.at[0, span], up_ref.at[k, span], up_sem.at[k, c]),
                ]
            )
    for k, down in enumerate([down_hbm, down_too_hbm]):
        for c in range(cuts):
            source, target = pl.ds(c * deep, deep), pl.ds(k * share + c * deep, deep)
            loads.append([pltpu.make_async_copy(down.at[0, source], down_ref.at[target], down_sem.at[k, c])])

    def start(number):
        if number < len(loads):
            for load in loads[number]:
                load.start()

    def arrive(number):
        for load in loads[number]:
            load.wait()
        start(number + AHEAD)

    x_load = pltpu.make_async_copy(x_hbm, x_ref, x_sem)
    x_load.start()
    for number in range(AHEAD):
        start(number)
    x_load.wait()
    for k in range(2):
        for c in range(CUTS):
            arrive(k * CUTS + c)
            span = slice(c * deep, (c + 1) * deep)
            x = x_ref[:, span]
            gate = jnp.dot(x, gate_ref[k, span, :], preferred_element_type=jnp.float32)
            up = jnp.dot(x, up_ref[k, span, :], preferred_element_type=jnp.float32)
            if c > 0:
                gate, up = gate_sum[...] + gate, up_sum[...] + up
            if c < CUTS - 1:
                gate_sum[...], up_sum[...] = gate, up
            else:
                hidden = gate * (0.5 + 0.5 * jnp.tanh(0.5 * gate)) * up
                hidden_ref[:, k * share : (k + 1) * share] = hidden.astype(jnp.bfloat16)
    for c in range(2 * cuts - 1):
        arrive(2 * CUTS + c)
        span = slice(c * deep, (c + 1) * deep)
        part = jnp.dot(hidden_ref[:, span], down_ref[span, :], preferred_element_type=jnp.float32)
        total_ref[...] = part if c == 0 else total_ref[...] + part
    arrive(2 * CUTS + 2 * cuts - 1)
    span = slice((2 * cuts - 1) * deep, 2 * cuts * deep)
    step = 2 * LANES
    stores = []
    for i in range(width // step):
        columns = slice(i * step, (i + 1) * step)
        part = jnp.dot(hidden_ref[:, span], down_ref[span, columns], preferred_element_type=jnp.float32)
        y_ref[:, columns] = (total_ref[:, columns] + part).astype(jnp.bfloat16)
        column_span = pl.ds(i * step, step)
        stores.append(pltpu.make_async_copy(y_ref.at[:, column_span], y_hbm.at[:, column_span], y_sem.at[i]))
        stores[i].start()
    for store in stores:
        store.wait()


def expert_layer(x, mine, others):
    rows, width = x.shape
    share = mine[0].shape[2]
    return pl.pallas_call(
        expert_kernel,
        out_shape=shape_of((rows, width)),
        in_specs=[HBM] * 7,
        out_specs=HBM,
        scratch_shapes=[
            pltpu.VMEM((rows, width), jnp.bfloat16),
            pltpu.VMEM((rows, width), jnp.bfloat16),
            pltpu.VMEM((2, width, share), jnp.bfloat16),
            pltpu.VMEM((2, width, share), jnp.bfloat16),
            pltpu.VMEM((2 * share, width), jnp.bfloat16),
            pltpu.VMEM((rows, 2 * share), jnp.bfloat16),
            pltpu.VMEM((rows, share), jnp.float32),
            pltpu.VMEM((rows, share), jnp.float32),
            pltpu.VMEM((rows, width), jnp.float32),
            pltpu.SemaphoreType.DMA,
            pltpu.SemaphoreType.DMA((width // (2 * LANES),)),
            pltpu.SemaphoreType.DMA((2, CUTS)),
            pltpu.SemaphoreType.DMA((2, CUTS)),
            pltpu.SemaphoreType.DMA((2, share * CUTS // width)),
        ],
        compiler_params=pltpu.CompilerParams(vmem_limit_bytes=60 * MIB),
        cost_estimate=cost(12 * rows * width * share, 12 * width * share, 2 * rows * share),
        name="expert_layer",
    )(x, *mine, *others)


def combine_kernel(base_ref, side_ref, rows_ref, weights_ref, y_ref, *refs):
    *more_refs, mine_ref, sent_ref, total_ref = refs
    top_count, tokens = rows_ref.shape
    half = mine_ref.shape[1]
    row = iota((y_ref.shape[0], tokens), 0)
    share = jnp.zeros(row.shape, jnp.float32)
    for c in range(top_count):
        share = jnp.where(rows_ref[c : c + 1, :] == row, weights_ref[c : c + 1, :], share)
    coarse = share.astype(jnp.bfloat16)
    fine = (share - coarse.astype(jnp.float32)).astype(jnp.bfloat16)
    y = y_ref[...]
    contract = (((0,), (0,)), ((), ()))
    total_ref[...] = lax.dot_general(coarse, y, contract, preferred_element_type=jnp.float32)
    total_ref[...] += lax.dot_general(fine, y, contract, preferred_element_type=jnp.float32)
    side = side_ref[0]
    mine = total_ref[:, pl.ds(pl.multiple_of(side * half, LANES), half)]
    tokens = mine.shape[0]
    if more_refs:
        kept_ref, back_ref = more_refs
        peer = pl.ds(pl.multiple_of(jnp.where(base_ref[0] == 0, tokens, 0), tokens), tokens)
        mine += kept_ref[...].astype(jnp.float32) + back_ref[peer, :].astype(jnp.float32)
    mine_ref[...] = mine
    sent_ref[...] = total_ref[:, pl.ds(pl.multiple_of((1 - side) * half, LANES), half)].astype(jnp.bfloat16)


def combine(base, side, placed, weights, y, half, more=()):
    tokens = placed.shape[1]
    rows, width = y.shape
    return pl.pallas_call(
        combine_kernel,
        out_shape=(shape_of((tokens, half), jnp.float32), shape_of((tokens, half))),
        in_specs=[SMEM, SMEM] + [VMEM] * (3 + len(more)),
        out_specs=(VMEM, VMEM),
        scratch_shapes=[pltpu.VMEM((tokens, width), jnp.float32)],
        compiler_params=pltpu.CompilerParams(vmem_limit_bytes=24 * MIB),
        cost_estimate=cost(4 * rows * tokens * width, 2 * rows * width),
        name="combine",
    )(base, side, placed, weights, y, *more)


def local(
    residual_in,
    query_rows,
    rotated_key_rows,
    value_row_matrix,
    learned_sink_scores,
    w_out,
    norm_gain,
    expert_ids,
    route_weights,
    w_gate,
    w_up,
    w_down,
):
    tok_dev, model_width = residual_in.shape
    seq_count = lax.axis_size("seq")
    experts = w_gate.shape[0] * seq_count
    top_count = expert_ids.shape[1]
    capacity = max(2, 8 * tok_dev // experts)
    sides = lax.axis_size("tp")
    side_rows = capacity // sides
    group = seq_count // 2
    rows = experts // 2 * side_rows
    half = model_width // sides
    at_seq = lax.axis_index("seq").astype(jnp.int32)
    base = jnp.where(at_seq < group, 0, experts // 2).astype(jnp.int32).reshape(1)
    side = lax.axis_index("tp").astype(jnp.int32).reshape(1)
    first = (at_seq == 0).astype(jnp.int32).reshape(1)
    ids, route = expert_ids.T, route_weights.T

    key_values = jnp.concatenate([rotated_key_rows, value_row_matrix], axis=1)
    before = passed_along(key_values, "seq", 1)
    weights = (w_gate, w_up, w_down)
    others = [swapped(weight, "tp") for weight in weights]
    near = attention(
        first, learned_sink_scores, query_rows, rotated_key_rows, value_row_matrix, before, w_out
    )
    near, *others = lax.optimization_barrier((near, *others))
    far = swapped(near, "tp")
    packed, sent, kept, placed = norm_and_pack(
        base, side, residual_in, near, far, norm_gain, ids, route, half, experts, side_rows, rows
    )

    def exchanged(block):
        block = block.reshape(group, rows // group, model_width)
        groups = [list(range(group)), list(range(group, seq_count))]
        block = lax.all_to_all(
            block, "seq", split_axis=0, concat_axis=0, axis_index_groups=groups, tiled=True
        )
        return block.reshape(rows, model_width)

    crossed = paired(sent, "seq")
    arrived = exchanged(packed)
    packed_peer, placed_peer, route_peer = pack_peer(
        base, side, crossed, swapped(crossed, "tp"), top_count, experts, side_rows, rows
    )
    packed_peer, arrived = lax.optimization_barrier((packed_peer, arrived))
    arrived_peer = exchanged(packed_peer)
    result = expert_layer(arrived, weights, others)
    result_peer = expert_layer(arrived_peer, weights, others)

    returned_peer = exchanged(result_peer)
    result, returned_peer = lax.optimization_barrier((result, returned_peer))
    returned = exchanged(result)
    mine_peer, sent_peer = combine(base, side, placed_peer, route_peer, returned_peer, half)
    summed_peer = (mine_peer + swapped(sent_peer, "tp").astype(jnp.float32)).astype(jnp.bfloat16)
    back = paired(summed_peer, "seq")
    mine, sent = combine(base, side, placed, route, returned, half, (kept, back))
    return (mine + swapped(sent, "tp").astype(jnp.float32)).astype(jnp.bfloat16)


def solution(mesh):
    placed = (
        P("seq", None),
        P("seq", "tp"),
        P("seq", "tp"),
        P("seq", "tp"),
        P("tp"),
        P("tp", None),
        P(),
        P("seq", None),
        P("seq", None),
        P("seq", None, "tp"),
        P("seq", None, "tp"),
        P("seq", "tp", None),
    )
    return jax.shard_map(
        local, mesh=mesh, in_specs=placed, out_specs=P("seq", "tp"), check_vma=False
    )
```

```python
import functools

import jax
import jax.numpy as jnp
from jax import lax
from jax.experimental import pallas as pl
from jax.experimental.pallas import tpu as pltpu
from jax.sharding import PartitionSpec as P

HEAD_SIZE = 64
WINDOW_LENGTH = 128
LANES = 128
MIB = 1024 * 1024
CUTS = 3
DEEP = 256
AHEAD = 3

neg_large = -1e30
epsilon = 1e-05

VMEM = pl.BlockSpec(memory_space=pltpu.VMEM)
SMEM = pl.BlockSpec(memory_space=pltpu.SMEM)
HBM = pl.BlockSpec(memory_space=pltpu.HBM)


def passed_along(block, axis, distance):
    devices = range(lax.axis_size(axis))
    route = [(i - distance, i) for i in devices if i - distance in devices]
    return lax.ppermute(block, axis, route)


def swapped(block, axis):
    count = lax.axis_size(axis)
    return lax.ppermute(block, axis, [(i, count - 1 - i) for i in range(count)])


def swapped_halves(block, axis):
    count = lax.axis_size(axis)
    return lax.ppermute(block, axis, [(i, (i + count // 2) % count) for i in range(count)])


def shape_of(dims, dtype=jnp.bfloat16):
    return jax.ShapeDtypeStruct(dims, dtype)


def cost(flops, moved, transcendentals=0):
    return pl.CostEstimate(flops=flops, bytes_accessed=moved, transcendentals=transcendentals)


def iota(dims, dimension):
    return lax.broadcasted_iota(jnp.int32, dims, dimension)


def rows_of(ids, experts, side_rows, base, side):
    top_count, tokens = ids.shape
    names = iota((experts, tokens), 0).astype(jnp.float32)
    hits = [ids[c : c + 1, :] == names for c in range(top_count)]
    named = sum([hit.astype(jnp.float32) for hit in hits]).astype(jnp.bfloat16)
    square = (tokens, tokens)
    earlier = (iota(square, 0) < iota(square, 1)).astype(jnp.bfloat16)
    slot = jnp.dot(named, earlier, preferred_element_type=jnp.float32) - (side * side_rows).astype(jnp.float32)
    expert = names - base.astype(jnp.float32)
    here = (slot >= 0.0) & (slot < side_rows) & (expert >= 0.0) & (expert < experts // 2)
    rows = jnp.where(here, expert * side_rows + slot, -1.0)
    lines = [jnp.sum(jnp.where(hit, rows, 0.0), axis=0, keepdims=True) for hit in hits]
    return jnp.concatenate(lines, axis=0).astype(jnp.int32)


def attention_kernel(
    first_ref, sink_hbm, q_hbm, k_hbm, v_hbm, before_ref, w_hbm, out_ref, sink_ref, q_ref, k_ref, v_ref, w_ref,
    att_ref, sems,
):
    tokens, width = q_ref.shape
    kv_heads = k_ref.shape[1] // HEAD_SIZE
    pairs = width // LANES // kv_heads
    moves = [(k_hbm, k_ref), (v_hbm, v_ref), (q_hbm, q_ref), (sink_hbm, sink_ref), (w_hbm, w_ref)]
    *loads, w_load = [pltpu.make_async_copy(source, target, sems.at[i]) for i, (source, target) in enumerate(moves)]
    for load in loads + [w_load]:
        load.start()
    low = iota((tokens, LANES), 1) < HEAD_SIZE

    def doubled(block, head):
        wide = block.astype(jnp.float32)
        turned = pltpu.roll(wide, HEAD_SIZE, 1)
        first, second = (wide, turned) if head == 0 else (turned, wide)
        return [
            jnp.where(low, first, 0.0).astype(jnp.bfloat16),
            jnp.where(low, 0.0, second).astype(jnp.bfloat16),
        ]

    own = iota((tokens, tokens), 1) <= iota((tokens, tokens), 0)
    bias = jnp.where(own, 0.0, jnp.where(first_ref[0] == 0, 0.0, neg_large))
    own_factor = jnp.where(own, 1.0, 0.0).astype(jnp.bfloat16)
    before_factor = jnp.where(own, 0.0, 1.0).astype(jnp.bfloat16)
    head_lanes = jnp.where(low, 1.0, 0.0).astype(jnp.bfloat16), jnp.where(low, 0.0, 1.0).astype(jnp.bfloat16)
    ones = jnp.concatenate(head_lanes, axis=0)
    keys_before = [jnp.concatenate(doubled(before_ref[:, :LANES], head), axis=0) for head in range(kv_heads)]
    values_before = [doubled(before_ref[:, LANES:], head) for head in range(kv_heads)]
    for load in loads:
        load.wait()
    contract = (((1,), (1,)), ((), ()))
    for head in range(kv_heads):
        keys = jnp.concatenate(doubled(k_ref[...], head), axis=0)
        values = jnp.concatenate(doubled(v_ref[...], head) + values_before[head], axis=0)
        for j in range(head * pairs, (head + 1) * pairs):
            q = q_ref[:, j * LANES : (j + 1) * LANES] * jnp.bfloat16(HEAD_SIZE**-0.5)
            near = lax.dot_general(q, keys, contract, preferred_element_type=jnp.float32)
            far = lax.dot_general(q, keys_before[head], contract, preferred_element_type=jnp.float32)
            terms, sinks = [], []
            for at in range(2):
                span = slice(at * tokens, (at + 1) * tokens)
                part = jnp.where(own, near[:, span], far[:, span]) + bias
                sink = sink_ref[2 * j + at]
                top = jnp.maximum(jnp.max(part, axis=1, keepdims=True), sink)
                terms.append(jnp.exp(part - top).astype(jnp.bfloat16))
                sinks.append(jnp.exp(sink - top))
            total = jnp.dot(jnp.concatenate(terms, axis=1), ones, preferred_element_type=jnp.float32)
            total += jnp.where(low, sinks[0], sinks[1])
            kept = [term * own_factor for term in terms] + [term * before_factor for term in terms]
            found = jnp.dot(jnp.concatenate(kept, axis=1), values, preferred_element_type=jnp.float32)
            att_ref[:, j * LANES : (j + 1) * LANES] = (found / total).astype(jnp.bfloat16)
    w_load.wait()
    step = 2 * LANES
    for at in range(0, out_ref.shape[1], step):
        out_ref[:, at : at + step] = jnp.dot(
            att_ref[...], w_ref[:, at : at + step], preferred_element_type=jnp.float32
        ).astype(jnp.bfloat16)


def attention(first, sinks, q, k, v, before, w_out):
    tokens = q.shape[0]
    return pl.pallas_call(
        attention_kernel,
        out_shape=shape_of((tokens, w_out.shape[1])),
        in_specs=[SMEM, HBM, HBM, HBM, HBM, VMEM, HBM],
        out_specs=VMEM,
        scratch_shapes=[
            pltpu.SMEM(sinks.shape, jnp.float32),
            pltpu.VMEM(q.shape, jnp.bfloat16),
            pltpu.VMEM(k.shape, jnp.bfloat16),
            pltpu.VMEM(v.shape, jnp.bfloat16),
            pltpu.VMEM(w_out.shape, jnp.bfloat16),
            pltpu.VMEM(q.shape, jnp.bfloat16),
            pltpu.SemaphoreType.DMA((5,)),
        ],
        compiler_params=pltpu.CompilerParams(vmem_limit_bytes=62_000_000),
        cost_estimate=cost(2 * tokens * w_out.size * 2, 2 * w_out.size, tokens * tokens * q.shape[1] // HEAD_SIZE),
        name="attention",
    )(first, sinks, q, k, v, before, w_out)


def pack(placed, normed, out_ref):
    rows, tokens = out_ref.shape[0], normed.shape[0]
    row = iota((rows, tokens), 0)
    taken = placed[0:1, :] == row
    for c in range(1, placed.shape[0]):
        taken = taken | (placed[c : c + 1, :] == row)
    taken = jnp.where(taken, 1.0, 0.0).astype(jnp.bfloat16)
    out_ref[...] = jnp.dot(taken, normed, preferred_element_type=jnp.float32).astype(jnp.bfloat16)


def noted(ids, weights):
    coarse = weights.astype(jnp.bfloat16).astype(jnp.float32)
    middle = (weights - coarse).astype(jnp.bfloat16).astype(jnp.float32)
    fine = weights - coarse - middle
    used = [ids.astype(jnp.float32), coarse, middle, fine]
    empty = jnp.zeros((LANES - 4 * ids.shape[0], ids.shape[1]), jnp.float32)
    return jnp.concatenate(used + [empty], axis=0).T.astype(jnp.bfloat16)


def norm_kernel(
    experts, side_rows, base_ref, side_ref, residual_ref, near_hbm, far_ref, gain_ref, ids_ref, weights_ref, out_ref,
    sent_ref, kept_ref, rows_ref, near_ref, whole_ref, sending_ref, sem,
):
    load = pltpu.make_async_copy(near_hbm, near_ref, sem)
    load.start()
    side = side_ref[0]
    rows = rows_of(ids_ref[...].astype(jnp.float32), experts, side_rows, base_ref[0], side)
    rows_ref[...] = rows
    half_tokens, half, width = sent_ref.shape[0], kept_ref.shape[1], whole_ref.shape[1]
    load.wait()
    added = near_ref[...].astype(jnp.float32) + far_ref[...].astype(jnp.float32)
    whole = (residual_ref[...].astype(jnp.float32) + added).astype(jnp.bfloat16)
    whole_ref[...] = whole
    wide = whole.astype(jnp.float32)
    mean_square = jnp.mean(wide * wide, axis=1, keepdims=True)
    normed = (wide * lax.rsqrt(mean_square + epsilon) * gain_ref[...]).astype(jnp.bfloat16)
    sending_ref[:, :width] = normed
    sending_ref[:, width:] = noted(ids_ref[...], weights_ref[...])
    kept_ref[...] = whole_ref[:, pl.ds(pl.multiple_of(side * half, LANES), half)]
    sent_ref[...] = sending_ref[pl.ds(pl.multiple_of(side * half_tokens, half_tokens), half_tokens), :]
    pack(rows, normed, out_ref)


def norm_and_pack(base, side, residual_in, near, far, gain, ids, weights, half, experts, side_rows, rows):
    tokens, width = residual_in.shape
    return pl.pallas_call(
        functools.partial(norm_kernel, experts, side_rows),
        out_shape=(
            shape_of((rows, width)),
            shape_of((tokens // 2, width + LANES)),
            shape_of((tokens, half)),
            shape_of(ids.shape, jnp.int32),
        ),
        in_specs=[SMEM, SMEM, VMEM, HBM, VMEM, VMEM, VMEM, VMEM],
        out_specs=(VMEM, VMEM, VMEM, VMEM),
        scratch_shapes=[
            pltpu.VMEM((tokens, width), jnp.bfloat16),
            pltpu.VMEM((tokens, width), jnp.bfloat16),
            pltpu.VMEM((tokens, width + LANES), jnp.bfloat16),
            pltpu.SemaphoreType.DMA,
        ],
        compiler_params=pltpu.CompilerParams(vmem_limit_bytes=24 * MIB),
        cost_estimate=cost(2 * rows * tokens * width, 2 * rows * width),
        name="norm_and_pack",
    )(base, side, residual_in, near, far, gain.reshape(1, width), ids, weights)


def peer_kernel(
    experts, side_rows, base_ref, side_ref, mine_ref, other_ref, out_ref, rows_ref, weights_ref, arrived_ref
):
    side, part = side_ref[0], mine_ref.shape[0]
    top_count = rows_ref.shape[0]
    width = out_ref.shape[1]
    arrived_ref[pl.ds(pl.multiple_of(side * part, part), part), :] = mine_ref[...]
    arrived_ref[pl.ds(pl.multiple_of((1 - side) * part, part), part), :] = other_ref[...]
    notes = arrived_ref[:, width:].astype(jnp.float32).T
    weights_ref[...] = sum([notes[k * top_count : (k + 1) * top_count, :] for k in range(2, 4)], notes[top_count : 2 * top_count, :])
    rows = rows_of(notes[:top_count, :], experts, side_rows, base_ref[0], side)
    rows_ref[...] = rows
    pack(rows, arrived_ref[:, :width], out_ref)


def pack_peer(base, side, mine, other, top_count, experts, side_rows, rows):
    part = mine.shape[0]
    width = mine.shape[1] - LANES
    return pl.pallas_call(
        functools.partial(peer_kernel, experts, side_rows),
        out_shape=(
            shape_of((rows, width)),
            shape_of((top_count, 2 * part), jnp.int32),
            shape_of((top_count, 2 * part), jnp.float32),
        ),
        in_specs=[SMEM, SMEM, VMEM, VMEM],
        out_specs=(VMEM, VMEM, VMEM),
        scratch_shapes=[pltpu.VMEM((2 * part, width + LANES), jnp.bfloat16)],
        compiler_params=pltpu.CompilerParams(vmem_limit_bytes=24 * MIB),
        cost_estimate=cost(4 * rows * part * width, 36 * rows * width),
        name="pack_peer",
    )(base, side, mine, other)


def expert_kernel(
    x_hbm, gate_hbm, up_hbm, down_hbm, gate_too_hbm, up_too_hbm, down_too_hbm, y_hbm, x_ref, y_ref, gate_ref, up_ref,
    down_ref, hidden_ref, gate_sum, up_sum, total_ref, x_sem, y_sem, gate_sem, up_sem, down_sem,
):
    rows, width = x_ref.shape
    share = gate_hbm.shape[2]
    deep, cuts = width // CUTS, share // DEEP
    loads = []
    for k, (gate, up) in enumerate([(gate_hbm, up_hbm), (gate_too_hbm, up_too_hbm)]):
        for c in range(CUTS):
            span = pl.ds(c * deep, deep)
            loads.append(
                [
                    pltpu.make_async_copy(gate.at[0, span], gate_ref.at[k, span], gate_sem.at[k, c]),
                    pltpu.make_async_copy(up.at[0, span], up_ref.at[k, span], up_sem.at[k, c]),
                ]
            )
    for k, down in enumerate([down_hbm, down_too_hbm]):
        for c in range(cuts):
            source, target = pl.ds(c * DEEP, DEEP), pl.ds(k * share + c * DEEP, DEEP)
            loads.append([pltpu.make_async_copy(down.at[0, source], down_ref.at[target], down_sem.at[k, c])])

    def start(number):
        if number < len(loads):
            for load in loads[number]:
                load.start()

    def arrive(number):
        for load in loads[number]:
            load.wait()
        start(number + AHEAD)

    x_load = pltpu.make_async_copy(x_hbm, x_ref, x_sem)
    x_load.start()
    for number in range(AHEAD):
        start(number)
    x_load.wait()
    for k in range(2):
        for c in range(CUTS):
            arrive(k * CUTS + c)
            span = slice(c * deep, (c + 1) * deep)
            x = x_ref[:, span]
            gate = jnp.dot(x, gate_ref[k, span, :], preferred_element_type=jnp.float32)
            up = jnp.dot(x, up_ref[k, span, :], preferred_element_type=jnp.float32)
            if c > 0:
                gate, up = gate_sum[...] + gate, up_sum[...] + up
            if c < CUTS - 1:
                gate_sum[...], up_sum[...] = gate, up
            else:
                hidden = gate * (0.5 + 0.5 * jnp.tanh(0.5 * gate)) * up
                hidden_ref[:, k * share : (k + 1) * share] = hidden.astype(jnp.bfloat16)
    for c in range(2 * cuts - 1):
        arrive(2 * CUTS + c)
        span = slice(c * DEEP, (c + 1) * DEEP)
        part = jnp.dot(hidden_ref[:, span], down_ref[span, :], preferred_element_type=jnp.float32)
        total_ref[...] = part if c == 0 else total_ref[...] + part
    arrive(2 * CUTS + 2 * cuts - 1)
    span = slice((2 * cuts - 1) * DEEP, 2 * cuts * DEEP)
    step = 2 * LANES
    stores = []
    for i in range(width // step):
        columns = slice(i * step, (i + 1) * step)
        part = jnp.dot(hidden_ref[:, span], down_ref[span, columns], preferred_element_type=jnp.float32)
        y_ref[:, columns] = (total_ref[:, columns] + part).astype(jnp.bfloat16)
        column_span = pl.ds(i * step, step)
        stores.append(pltpu.make_async_copy(y_ref.at[:, column_span], y_hbm.at[:, column_span], y_sem.at[i]))
        stores[i].start()
    for store in stores:
        store.wait()


def expert_layer(x, mine, others):
    rows, width = x.shape
    share = mine[0].shape[2]
    return pl.pallas_call(
        expert_kernel,
        out_shape=shape_of((rows, width)),
        in_specs=[HBM] * 7,
        out_specs=HBM,
        scratch_shapes=[
            pltpu.VMEM((rows, width), jnp.bfloat16),
            pltpu.VMEM((rows, width), jnp.bfloat16),
            pltpu.VMEM((2, width, share), jnp.bfloat16),
            pltpu.VMEM((2, width, share), jnp.bfloat16),
            pltpu.VMEM((2 * share, width), jnp.bfloat16),
            pltpu.VMEM((rows, 2 * share), jnp.bfloat16),
            pltpu.VMEM((rows, share), jnp.float32),
            pltpu.VMEM((rows, share), jnp.float32),
            pltpu.VMEM((rows, width), jnp.float32),
            pltpu.SemaphoreType.DMA,
            pltpu.SemaphoreType.DMA((width // (2 * LANES),)),
            pltpu.SemaphoreType.DMA((2, CUTS)),
            pltpu.SemaphoreType.DMA((2, CUTS)),
            pltpu.SemaphoreType.DMA((2, share // DEEP)),
        ],
        compiler_params=pltpu.CompilerParams(vmem_limit_bytes=60 * MIB),
        cost_estimate=cost(12 * rows * width * share, 12 * width * share, 2 * rows * share),
        name="expert_layer",
    )(x, *mine, *others)


def combine_kernel(side_ref, rows_ref, weights_ref, y_ref, *refs):
    *more_refs, mine_ref, sent_ref, total_ref = refs
    top_count, tokens = rows_ref.shape
    half = mine_ref.shape[1]
    row = iota((y_ref.shape[0], tokens), 0)
    share = jnp.zeros(row.shape, jnp.float32)
    for c in range(top_count):
        share = jnp.where(rows_ref[c : c + 1, :] == row, weights_ref[c : c + 1, :], share)
    coarse = share.astype(jnp.bfloat16)
    fine = (share - coarse.astype(jnp.float32)).astype(jnp.bfloat16)
    y = y_ref[...]
    contract = (((0,), (0,)), ((), ()))
    total_ref[...] = lax.dot_general(coarse, y, contract, preferred_element_type=jnp.float32)
    total_ref[...] += lax.dot_general(fine, y, contract, preferred_element_type=jnp.float32)
    side = side_ref[0]
    mine = total_ref[:, pl.ds(pl.multiple_of(side * half, LANES), half)]
    for more_ref in more_refs:
        mine += more_ref[...].astype(jnp.float32)
    mine_ref[...] = mine
    sent_ref[...] = total_ref[:, pl.ds(pl.multiple_of((1 - side) * half, LANES), half)].astype(jnp.bfloat16)


def combine(side, placed, weights, y, half, more=()):
    tokens = placed.shape[1]
    rows, width = y.shape
    return pl.pallas_call(
        combine_kernel,
        out_shape=(shape_of((tokens, half), jnp.float32), shape_of((tokens, half))),
        in_specs=[SMEM] + [VMEM] * (3 + len(more)),
        out_specs=(VMEM, VMEM),
        scratch_shapes=[pltpu.VMEM((tokens, width), jnp.float32)],
        compiler_params=pltpu.CompilerParams(vmem_limit_bytes=24 * MIB),
        cost_estimate=cost(4 * rows * tokens * width, 2 * rows * width),
        name="combine",
    )(side, placed, weights, y, *more)


def local(
    residual_in,
    query_rows,
    rotated_key_rows,
    value_row_matrix,
    learned_sink_scores,
    w_out,
    norm_gain,
    expert_ids,
    route_weights,
    w_gate,
    w_up,
    w_down,
):
    tok_dev, model_width = residual_in.shape
    seq_count = lax.axis_size("seq")
    experts = w_gate.shape[0] * seq_count
    top_count = expert_ids.shape[1]
    capacity = max(2, 8 * tok_dev // experts)
    sides = lax.axis_size("tp")
    side_rows = capacity // sides
    group = seq_count // 2
    rows = experts // 2 * side_rows
    half = model_width // sides
    at_seq = lax.axis_index("seq").astype(jnp.int32)
    base = jnp.where(at_seq < group, 0, experts // 2).astype(jnp.int32).reshape(1)
    side = lax.axis_index("tp").astype(jnp.int32).reshape(1)
    first = (at_seq == 0).astype(jnp.int32).reshape(1)
    ids, route = expert_ids.T, route_weights.T

    key_values = jnp.concatenate([rotated_key_rows, value_row_matrix], axis=1)
    before = passed_along(key_values, "seq", 1)
    weights = (w_gate, w_up, w_down)
    others = [swapped(weight, "tp") for weight in weights]
    near = attention(
        first, learned_sink_scores, query_rows, rotated_key_rows, value_row_matrix, before, w_out
    )
    near, *others = lax.optimization_barrier((near, *others))
    far = swapped(near, "tp")
    packed, sent, kept, placed = norm_and_pack(
        base, side, residual_in, near, far, norm_gain, ids, route, half, experts, side_rows, rows
    )

    def exchanged(block):
        block = block.reshape(group, rows // group, model_width)
        groups = [list(range(group)), list(range(group, seq_count))]
        block = lax.all_to_all(
            block, "seq", split_axis=0, concat_axis=0, axis_index_groups=groups, tiled=True
        )
        return block.reshape(rows, model_width)

    crossed = swapped_halves(sent, "seq")
    packed_peer, placed_peer, route_peer = pack_peer(
        base, side, crossed, swapped(crossed, "tp"), top_count, experts, side_rows, rows
    )
    arrived_peer = exchanged(packed_peer)
    arrived_peer, packed = lax.optimization_barrier((arrived_peer, packed))
    arrived = exchanged(packed)
    result_peer = expert_layer(arrived_peer, weights, others)
    result_peer, arrived = lax.optimization_barrier((result_peer, arrived))
    result = expert_layer(arrived, weights, others)

    returned_peer = exchanged(result_peer)
    result, returned_peer = lax.optimization_barrier((result, returned_peer))
    returned = exchanged(result)
    mine_peer, sent_peer = combine(side, placed_peer, route_peer, returned_peer, half)
    summed_peer = (mine_peer + swapped(sent_peer, "tp").astype(jnp.float32)).astype(jnp.bfloat16)
    back = swapped_halves(summed_peer, "seq")
    mine, sent = combine(side, placed, route, returned, half, (kept, back))
    return (mine + swapped(sent, "tp").astype(jnp.float32)).astype(jnp.bfloat16)


def solution(mesh):
    placed = (
        P("seq", None),
        P("seq", "tp"),
        P("seq", "tp"),
        P("seq", "tp"),
        P("tp"),
        P("tp", None),
        P(),
        P("seq", None),
        P("seq", None),
        P("seq", None, "tp"),
        P("seq", None, "tp"),
        P("seq", "tp", None),
    )
    return jax.shard_map(
        local, mesh=mesh, in_specs=placed, out_specs=P("seq", "tp"), check_vma=False
    )
```

```python
import functools

import jax
import jax.numpy as jnp
from jax import lax
from jax.experimental import pallas as pl
from jax.experimental.pallas import tpu as pltpu
from jax.sharding import PartitionSpec as P

HEAD_SIZE = 64
WINDOW_LENGTH = 128
LANES = 128
MIB = 1024 * 1024
CUTS = 3
DEEP = 256
AHEAD = 3

neg_large = -1e30
epsilon = 1e-05

VMEM = pl.BlockSpec(memory_space=pltpu.VMEM)
SMEM = pl.BlockSpec(memory_space=pltpu.SMEM)
HBM = pl.BlockSpec(memory_space=pltpu.HBM)


def passed_along(block, axis, distance):
    devices = range(lax.axis_size(axis))
    route = [(i - distance, i) for i in devices if i - distance in devices]
    return lax.ppermute(block, axis, route)


def swapped(block, axis):
    count = lax.axis_size(axis)
    return lax.ppermute(block, axis, [(i, count - 1 - i) for i in range(count)])


def swapped_halves(block, axis):
    count = lax.axis_size(axis)
    return lax.ppermute(block, axis, [(i, (i + count // 2) % count) for i in range(count)])


def shape_of(dims, dtype=jnp.bfloat16):
    return jax.ShapeDtypeStruct(dims, dtype)


def cost(flops, moved, transcendentals=0):
    return pl.CostEstimate(flops=flops, bytes_accessed=moved, transcendentals=transcendentals)


def iota(dims, dimension):
    return lax.broadcasted_iota(jnp.int32, dims, dimension)


def rows_of(ids, experts, side_rows, base, side):
    top_count, tokens = ids.shape
    names = iota((experts, tokens), 0).astype(jnp.float32)
    hits = [ids[c : c + 1, :] == names for c in range(top_count)]
    named = sum([hit.astype(jnp.float32) for hit in hits]).astype(jnp.bfloat16)
    square = (tokens, tokens)
    earlier = (iota(square, 0) < iota(square, 1)).astype(jnp.bfloat16)
    slot = jnp.dot(named, earlier, preferred_element_type=jnp.float32) - (side * side_rows).astype(jnp.float32)
    expert = names - base.astype(jnp.float32)
    here = (slot >= 0.0) & (slot < side_rows) & (expert >= 0.0) & (expert < experts // 2)
    rows = jnp.where(here, expert * side_rows + slot, -1.0)
    lines = [jnp.sum(jnp.where(hit, rows, 0.0), axis=0, keepdims=True) for hit in hits]
    return jnp.concatenate(lines, axis=0).astype(jnp.int32)


def attention_kernel(
    first_ref, sink_hbm, q_hbm, k_hbm, v_hbm, before_hbm, w_hbm, out_hbm, sink_ref, q_ref, k_ref, v_ref, before_ref,
    w_ref, att_ref, out_ref, sems, out_sems,
):
    tokens, width = q_ref.shape
    kv_heads = k_ref.shape[1] // HEAD_SIZE
    pairs = width // LANES // kv_heads
    moves = [(before_hbm, before_ref), (k_hbm, k_ref), (v_hbm, v_ref), (q_hbm, q_ref)]
    moves += [(sink_hbm, sink_ref), (w_hbm, w_ref)]
    *loads, w_load = [pltpu.make_async_copy(source, target, sems.at[i]) for i, (source, target) in enumerate(moves)]
    for load in loads + [w_load]:
        load.start()
    low = iota((tokens, LANES), 1) < HEAD_SIZE

    def doubled(block, head):
        wide = block.astype(jnp.float32)
        turned = pltpu.roll(wide, HEAD_SIZE, 1)
        first, second = (wide, turned) if head == 0 else (turned, wide)
        return [
            jnp.where(low, first, 0.0).astype(jnp.bfloat16),
            jnp.where(low, 0.0, second).astype(jnp.bfloat16),
        ]

    own = iota((tokens, tokens), 1) <= iota((tokens, tokens), 0)
    bias = jnp.where(own, 0.0, jnp.where(first_ref[0] == 0, 0.0, neg_large))
    own_factor = jnp.where(own, 1.0, 0.0).astype(jnp.bfloat16)
    before_factor = jnp.where(own, 0.0, 1.0).astype(jnp.bfloat16)
    head_lanes = jnp.where(low, 1.0, 0.0).astype(jnp.bfloat16), jnp.where(low, 0.0, 1.0).astype(jnp.bfloat16)
    ones = jnp.concatenate(head_lanes, axis=0)
    for load in loads:
        load.wait()
    keys_before = [jnp.concatenate(doubled(before_ref[:, :LANES], head), axis=0) for head in range(kv_heads)]
    values_before = [doubled(before_ref[:, LANES:], head) for head in range(kv_heads)]
    contract = (((1,), (1,)), ((), ()))
    for head in range(kv_heads):
        keys = jnp.concatenate(doubled(k_ref[...], head), axis=0)
        values = jnp.concatenate(doubled(v_ref[...], head) + values_before[head], axis=0)
        for j in range(head * pairs, (head + 1) * pairs):
            q = q_ref[:, j * LANES : (j + 1) * LANES] * jnp.bfloat16(HEAD_SIZE**-0.5)
            near = lax.dot_general(q, keys, contract, preferred_element_type=jnp.float32)
            far = lax.dot_general(q, keys_before[head], contract, preferred_element_type=jnp.float32)
            terms, sinks = [], []
            for at in range(2):
                span = slice(at * tokens, (at + 1) * tokens)
                part = jnp.where(own, near[:, span], far[:, span]) + bias
                sink = sink_ref[2 * j + at]
                top = jnp.maximum(jnp.max(part, axis=1, keepdims=True), sink)
                terms.append(jnp.exp(part - top).astype(jnp.bfloat16))
                sinks.append(jnp.exp(sink - top))
            total = jnp.dot(jnp.concatenate(terms, axis=1), ones, preferred_element_type=jnp.float32)
            total += jnp.where(low, sinks[0], sinks[1])
            kept = [term * own_factor for term in terms] + [term * before_factor for term in terms]
            found = jnp.dot(jnp.concatenate(kept, axis=1), values, preferred_element_type=jnp.float32)
            att_ref[:, j * LANES : (j + 1) * LANES] = (found / total).astype(jnp.bfloat16)
    w_load.wait()
    step = 2 * LANES
    stores = []
    for at in range(0, out_ref.shape[1], step):
        out_ref[:, at : at + step] = jnp.dot(
            att_ref[...], w_ref[:, at : at + step], preferred_element_type=jnp.float32
        ).astype(jnp.bfloat16)
        span = pl.ds(at, step)
        stores.append(pltpu.make_async_copy(out_ref.at[:, span], out_hbm.at[:, span], out_sems.at[at // step]))
        stores[-1].start()
    for store in stores:
        store.wait()


def attention(first, sinks, q, k, v, before, w_out):
    tokens = q.shape[0]
    return pl.pallas_call(
        attention_kernel,
        out_shape=shape_of((tokens, w_out.shape[1])),
        in_specs=[SMEM, HBM, HBM, HBM, HBM, HBM, HBM],
        out_specs=HBM,
        scratch_shapes=[
            pltpu.SMEM(sinks.shape, jnp.float32),
            pltpu.VMEM(q.shape, jnp.bfloat16),
            pltpu.VMEM(k.shape, jnp.bfloat16),
            pltpu.VMEM(v.shape, jnp.bfloat16),
            pltpu.VMEM(before.shape, jnp.bfloat16),
            pltpu.VMEM(w_out.shape, jnp.bfloat16),
            pltpu.VMEM(q.shape, jnp.bfloat16),
            pltpu.VMEM((tokens, w_out.shape[1]), jnp.bfloat16),
            pltpu.SemaphoreType.DMA((6,)),
            pltpu.SemaphoreType.DMA((w_out.shape[1] // (2 * LANES),)),
        ],
        compiler_params=pltpu.CompilerParams(vmem_limit_bytes=62_000_000),
        cost_estimate=cost(2 * tokens * w_out.size * 2, 2 * w_out.size, tokens * tokens * q.shape[1] // HEAD_SIZE),
        name="attention",
    )(first, sinks, q, k, v, before, w_out)


def pack(placed, normed, out_ref):
    rows, tokens = out_ref.shape[0], normed.shape[0]
    row = iota((rows, tokens), 0)
    taken = placed[0:1, :] == row
    for c in range(1, placed.shape[0]):
        taken = taken | (placed[c : c + 1, :] == row)
    taken = jnp.where(taken, 1.0, 0.0).astype(jnp.bfloat16)
    out_ref[...] = jnp.dot(taken, normed, preferred_element_type=jnp.float32).astype(jnp.bfloat16)


def noted(ids, weights):
    coarse = weights.astype(jnp.bfloat16).astype(jnp.float32)
    middle = (weights - coarse).astype(jnp.bfloat16).astype(jnp.float32)
    fine = weights - coarse - middle
    used = [ids.astype(jnp.float32), coarse, middle, fine]
    empty = jnp.zeros((LANES - 4 * ids.shape[0], ids.shape[1]), jnp.float32)
    return jnp.concatenate(used + [empty], axis=0).T.astype(jnp.bfloat16)


def norm_kernel(
    side_ref, residual_ref, near_ref, far_ref, gain_ref, ids_ref, weights_ref, sending_ref, sent_ref, kept_ref, whole_ref
):
    side = side_ref[0]
    half_tokens, half, width = sent_ref.shape[0], kept_ref.shape[1], whole_ref.shape[1]
    added = near_ref[...].astype(jnp.float32) + far_ref[...].astype(jnp.float32)
    whole = (residual_ref[...].astype(jnp.float32) + added).astype(jnp.bfloat16)
    whole_ref[...] = whole
    wide = whole.astype(jnp.float32)
    mean_square = jnp.mean(wide * wide, axis=1, keepdims=True)
    normed = (wide * lax.rsqrt(mean_square + epsilon) * gain_ref[...]).astype(jnp.bfloat16)
    sending_ref[:, :width] = normed
    sending_ref[:, width:] = noted(ids_ref[...], weights_ref[...])
    kept_ref[...] = whole_ref[:, pl.ds(pl.multiple_of(side * half, LANES), half)]
    sent_ref[...] = sending_ref[pl.ds(pl.multiple_of(side * half_tokens, half_tokens), half_tokens), :]


def norm(side, residual_in, near, far, gain, ids, weights, half):
    tokens, width = residual_in.shape
    return pl.pallas_call(
        norm_kernel,
        out_shape=(
            shape_of((tokens, width + LANES)),
            shape_of((tokens // 2, width + LANES)),
            shape_of((tokens, half)),
        ),
        in_specs=[SMEM] + [VMEM] * 6,
        out_specs=(VMEM, VMEM, VMEM),
        scratch_shapes=[pltpu.VMEM((tokens, width), jnp.bfloat16)],
        compiler_params=pltpu.CompilerParams(vmem_limit_bytes=24 * MIB),
        cost_estimate=cost(8 * tokens * width, 10 * tokens * width),
        name="norm",
    )(side, residual_in, near, far, gain.reshape(1, width), ids, weights)


def pack_kernel(experts, side_rows, base_ref, side_ref, *refs):
    *part_refs, out_ref, rows_ref, weights_ref, arrived_ref = refs
    side, top_count, width = side_ref[0], rows_ref.shape[0], out_ref.shape[1]
    if len(part_refs) == 1:
        arrived_ref = part_refs[0]
    else:
        mine_ref, other_ref = part_refs
        part = mine_ref.shape[0]
        arrived_ref[pl.ds(pl.multiple_of(side * part, part), part), :] = mine_ref[...]
        arrived_ref[pl.ds(pl.multiple_of((1 - side) * part, part), part), :] = other_ref[...]
    notes = arrived_ref[:, width:].astype(jnp.float32).T
    first, second, third = [notes[k * top_count : (k + 1) * top_count, :] for k in range(1, 4)]
    weights_ref[...] = first + second + third
    rows = rows_of(notes[:top_count, :], experts, side_rows, base_ref[0], side)
    rows_ref[...] = rows
    pack(rows, arrived_ref[:, :width], out_ref)


def packed_rows(base, side, parts, top_count, experts, side_rows, rows):
    tokens = sum([part.shape[0] for part in parts])
    width = parts[0].shape[1] - LANES
    return pl.pallas_call(
        functools.partial(pack_kernel, experts, side_rows),
        out_shape=(
            shape_of((rows, width)),
            shape_of((top_count, tokens), jnp.int32),
            shape_of((top_count, tokens), jnp.float32),
        ),
        in_specs=[SMEM, SMEM] + [VMEM] * len(parts),
        out_specs=(VMEM, VMEM, VMEM),
        scratch_shapes=[pltpu.VMEM((tokens, width + LANES), jnp.bfloat16)],
        compiler_params=pltpu.CompilerParams(vmem_limit_bytes=24 * MIB),
        cost_estimate=cost(2 * rows * tokens * width, 2 * rows * width),
        name="packed_rows",
    )(base, side, *parts)


def expert_kernel(
    x_hbm, gate_hbm, up_hbm, down_hbm, gate_too_hbm, up_too_hbm, down_too_hbm, y_hbm, x_ref, y_ref, gate_ref, up_ref,
    down_ref, hidden_ref, gate_sum, up_sum, total_ref, x_sem, y_sem, gate_sem, up_sem, down_sem,
):
    rows, width = x_ref.shape
    share = gate_hbm.shape[2]
    deep, cuts = width // CUTS, share // DEEP
    loads = []
    for k, (gate, up) in enumerate([(gate_hbm, up_hbm), (gate_too_hbm, up_too_hbm)]):
        for c in range(CUTS):
            span = pl.ds(c * deep, deep)
            loads.append(
                [
                    pltpu.make_async_copy(gate.at[0, span], gate_ref.at[k, span], gate_sem.at[k, c]),
                    pltpu.make_async_copy(up.at[0, span], up_ref.at[k, span], up_sem.at[k, c]),
                ]
            )
    for k, down in enumerate([down_hbm, down_too_hbm]):
        for c in range(cuts):
            source, target = pl.ds(c * DEEP, DEEP), pl.ds(k * share + c * DEEP, DEEP)
            loads.append([pltpu.make_async_copy(down.at[0, source], down_ref.at[target], down_sem.at[k, c])])

    def start(number):
        if number < len(loads):
            for load in loads[number]:
                load.start()

    def arrive(number):
        for load in loads[number]:
            load.wait()
        start(number + AHEAD)

    x_load = pltpu.make_async_copy(x_hbm, x_ref, x_sem)
    x_load.start()
    for number in range(AHEAD):
        start(number)
    x_load.wait()
    for k in range(2):
        for c in range(CUTS):
            arrive(k * CUTS + c)
            span = slice(c * deep, (c + 1) * deep)
            x = x_ref[:, span]
            gate = jnp.dot(x, gate_ref[k, span, :], preferred_element_type=jnp.float32)
            up = jnp.dot(x, up_ref[k, span, :], preferred_element_type=jnp.float32)
            if c > 0:
                gate, up = gate_sum[...] + gate, up_sum[...] + up
            if c < CUTS - 1:
                gate_sum[...], up_sum[...] = gate, up
            else:
                hidden = gate * (0.5 + 0.5 * jnp.tanh(0.5 * gate)) * up
                hidden_ref[:, k * share : (k + 1) * share] = hidden.astype(jnp.bfloat16)
    for c in range(2 * cuts - 1):
        arrive(2 * CUTS + c)
        span = slice(c * DEEP, (c + 1) * DEEP)
        part = jnp.dot(hidden_ref[:, span], down_ref[span, :], preferred_element_type=jnp.float32)
        total_ref[...] = part if c == 0 else total_ref[...] + part
    arrive(2 * CUTS + 2 * cuts - 1)
    span = slice((2 * cuts - 1) * DEEP, 2 * cuts * DEEP)
    step = 2 * LANES
    stores = []
    for i in range(width // step):
        columns = slice(i * step, (i + 1) * step)
        part = jnp.dot(hidden_ref[:, span], down_ref[span, columns], preferred_element_type=jnp.float32)
        y_ref[:, columns] = (total_ref[:, columns] + part).astype(jnp.bfloat16)
        column_span = pl.ds(i * step, step)
        stores.append(pltpu.make_async_copy(y_ref.at[:, column_span], y_hbm.at[:, column_span], y_sem.at[i]))
        stores[i].start()
    for store in stores:
        store.wait()


def expert_layer(x, mine, others):
    rows, width = x.shape
    share = mine[0].shape[2]
    return pl.pallas_call(
        expert_kernel,
        out_shape=shape_of((rows, width)),
        in_specs=[HBM] * 7,
        out_specs=HBM,
        scratch_shapes=[
            pltpu.VMEM((rows, width), jnp.bfloat16),
            pltpu.VMEM((rows, width), jnp.bfloat16),
            pltpu.VMEM((2, width, share), jnp.bfloat16),
            pltpu.VMEM((2, width, share), jnp.bfloat16),
            pltpu.VMEM((2 * share, width), jnp.bfloat16),
            pltpu.VMEM((rows, 2 * share), jnp.bfloat16),
            pltpu.VMEM((rows, share), jnp.float32),
            pltpu.VMEM((rows, share), jnp.float32),
            pltpu.VMEM((rows, width), jnp.float32),
            pltpu.SemaphoreType.DMA,
            pltpu.SemaphoreType.DMA((width // (2 * LANES),)),
            pltpu.SemaphoreType.DMA((2, CUTS)),
            pltpu.SemaphoreType.DMA((2, CUTS)),
            pltpu.SemaphoreType.DMA((2, share // DEEP)),
        ],
        compiler_params=pltpu.CompilerParams(vmem_limit_bytes=60 * MIB),
        cost_estimate=cost(12 * rows * width * share, 12 * width * share, 2 * rows * share),
        name="expert_layer",
    )(x, *mine, *others)


def combine_kernel(side_ref, rows_ref, weights_ref, y_ref, *refs):
    *more_refs, mine_ref, sent_ref, total_ref = refs
    top_count, tokens = rows_ref.shape
    half = mine_ref.shape[1]
    row = iota((y_ref.shape[0], tokens), 0)
    share = jnp.zeros(row.shape, jnp.float32)
    for c in range(top_count):
        share = jnp.where(rows_ref[c : c + 1, :] == row, weights_ref[c : c + 1, :], share)
    coarse = share.astype(jnp.bfloat16)
    fine = (share - coarse.astype(jnp.float32)).astype(jnp.bfloat16)
    y = y_ref[...]
    contract = (((0,), (0,)), ((), ()))
    total_ref[...] = lax.dot_general(coarse, y, contract, preferred_element_type=jnp.float32)
    total_ref[...] += lax.dot_general(fine, y, contract, preferred_element_type=jnp.float32)
    side = side_ref[0]
    mine = total_ref[:, pl.ds(pl.multiple_of(side * half, LANES), half)]
    for more_ref in more_refs:
        mine += more_ref[...].astype(jnp.float32)
    mine_ref[...] = mine
    sent_ref[...] = total_ref[:, pl.ds(pl.multiple_of((1 - side) * half, LANES), half)].astype(jnp.bfloat16)


def combine(side, placed, weights, y, half, more=()):
    tokens = placed.shape[1]
    rows, width = y.shape
    return pl.pallas_call(
        combine_kernel,
        out_shape=(shape_of((tokens, half), jnp.float32), shape_of((tokens, half))),
        in_specs=[SMEM] + [VMEM] * (3 + len(more)),
        out_specs=(VMEM, VMEM),
        scratch_shapes=[pltpu.VMEM((tokens, width), jnp.float32)],
        compiler_params=pltpu.CompilerParams(vmem_limit_bytes=24 * MIB),
        cost_estimate=cost(4 * rows * tokens * width, 2 * rows * width),
        name="combine",
    )(side, placed, weights, y, *more)


def local(
    residual_in,
    query_rows,
    rotated_key_rows,
    value_row_matrix,
    learned_sink_scores,
    w_out,
    norm_gain,
    expert_ids,
    route_weights,
    w_gate,
    w_up,
    w_down,
):
    tok_dev, model_width = residual_in.shape
    seq_count = lax.axis_size("seq")
    experts = w_gate.shape[0] * seq_count
    top_count = expert_ids.shape[1]
    capacity = max(2, 8 * tok_dev // experts)
    sides = lax.axis_size("tp")
    side_rows = capacity // sides
    group = seq_count // 2
    rows = experts // 2 * side_rows
    half = model_width // sides
    at_seq = lax.axis_index("seq").astype(jnp.int32)
    base = jnp.where(at_seq < group, 0, experts // 2).astype(jnp.int32).reshape(1)
    side = lax.axis_index("tp").astype(jnp.int32).reshape(1)
    first = (at_seq == 0).astype(jnp.int32).reshape(1)
    ids, route = expert_ids.T, route_weights.T

    before = passed_along(jnp.concatenate([rotated_key_rows, value_row_matrix], axis=1), "seq", 1)
    weights = (w_gate, w_up, w_down)
    others = [swapped(weight, "tp") for weight in weights]
    near = attention(
        first, learned_sink_scores, query_rows, rotated_key_rows, value_row_matrix, before, w_out
    )
    near, *others = lax.optimization_barrier((near, *others))
    far = swapped(near, "tp")
    sending, sent, kept = norm(side, residual_in, near, far, norm_gain, ids, route, half)

    def exchanged(block):
        block = block.reshape(group, rows // group, model_width)
        groups = [list(range(group)), list(range(group, seq_count))]
        block = lax.all_to_all(
            block, "seq", split_axis=0, concat_axis=0, axis_index_groups=groups, tiled=True
        )
        return block.reshape(rows, model_width)

    crossed = swapped_halves(sent, "seq")
    packed, placed, _ = packed_rows(base, side, (sending,), top_count, experts, side_rows, rows)
    crossed, packed = lax.optimization_barrier((crossed, packed))
    packed_peer, placed_peer, route_peer = packed_rows(
        base, side, (crossed, swapped(crossed, "tp")), top_count, experts, side_rows, rows
    )
    arrived_peer = exchanged(packed_peer)
    arrived_peer, packed = lax.optimization_barrier((arrived_peer, packed))
    arrived = exchanged(packed)
    result_peer = expert_layer(arrived_peer, weights, others)
    result_peer, arrived = lax.optimization_barrier((result_peer, arrived))
    result = expert_layer(arrived, weights, others)

    returned_peer = exchanged(result_peer)
    result, returned_peer = lax.optimization_barrier((result, returned_peer))
    returned = exchanged(result)
    mine_peer, sent_peer = combine(side, placed_peer, route_peer, returned_peer, half)
    summed_peer = (mine_peer + swapped(sent_peer, "tp").astype(jnp.float32)).astype(jnp.bfloat16)
    back = swapped_halves(summed_peer, "seq")
    mine, sent = combine(side, placed, route, returned, half, (kept,))
    sent, back = lax.optimization_barrier((sent, back))
    return (mine + swapped(sent, "tp").astype(jnp.float32) + back.astype(jnp.float32)).astype(jnp.bfloat16)


def solution(mesh):
    placed = (
        P("seq", None),
        P("seq", "tp"),
        P("seq", "tp"),
        P("seq", "tp"),
        P("tp"),
        P("tp", None),
        P(),
        P("seq", None),
        P("seq", None),
        P("seq", None, "tp"),
        P("seq", None, "tp"),
        P("seq", "tp", None),
    )
    return jax.shard_map(
        local, mesh=mesh, in_specs=placed, out_specs=P("seq", "tp"), check_vma=False
    )
```

```python
import functools

import jax
import jax.numpy as jnp
from jax import lax
from jax.experimental import pallas as pl
from jax.experimental.pallas import tpu as pltpu
from jax.sharding import PartitionSpec as P

HEAD_SIZE = 64
WINDOW_LENGTH = 128
LANES = 128
MIB = 1024 * 1024
CUTS = 3
DEEP = 256
AHEAD = 3

neg_large = -1e30
epsilon = 1e-05

VMEM = pl.BlockSpec(memory_space=pltpu.VMEM)
SMEM = pl.BlockSpec(memory_space=pltpu.SMEM)
HBM = pl.BlockSpec(memory_space=pltpu.HBM)


def passed_along(block, axis, distance):
    devices = range(lax.axis_size(axis))
    route = [(i - distance, i) for i in devices if i - distance in devices]
    return lax.ppermute(block, axis, route)


def swapped(block, axis):
    count = lax.axis_size(axis)
    return lax.ppermute(block, axis, [(i, count - 1 - i) for i in range(count)])


def swapped_halves(block, axis):
    count = lax.axis_size(axis)
    return lax.ppermute(block, axis, [(i, (i + count // 2) % count) for i in range(count)])


def shape_of(dims, dtype=jnp.bfloat16):
    return jax.ShapeDtypeStruct(dims, dtype)


def cost(flops, moved, transcendentals=0):
    return pl.CostEstimate(flops=flops, bytes_accessed=moved, transcendentals=transcendentals)


def iota(dims, dimension):
    return lax.broadcasted_iota(jnp.int32, dims, dimension)


def rows_of(ids, experts, side_rows, base, side):
    top_count, tokens = ids.shape
    names = iota((experts, tokens), 0).astype(jnp.float32)
    hits = [ids[c : c + 1, :] == names for c in range(top_count)]
    named = sum([hit.astype(jnp.float32) for hit in hits]).astype(jnp.bfloat16)
    square = (tokens, tokens)
    earlier = (iota(square, 0) < iota(square, 1)).astype(jnp.bfloat16)
    slot = jnp.dot(named, earlier, preferred_element_type=jnp.float32) - (side * side_rows).astype(jnp.float32)
    expert = names - base.astype(jnp.float32)
    here = (slot >= 0.0) & (slot < side_rows) & (expert >= 0.0) & (expert < experts // 2)
    rows = jnp.where(here, expert * side_rows + slot, -1.0)
    lines = [jnp.sum(jnp.where(hit, rows, 0.0), axis=0, keepdims=True) for hit in hits]
    return jnp.concatenate(lines, axis=0).astype(jnp.int32)


def attention_kernel(
    first_ref, sink_ref, q_ref, kv_ref, before_ref, w_hbm, out_ref, w_ref, att_ref, sem
):
    tokens, width = q_ref.shape
    kv_heads = kv_ref.shape[1] // (2 * HEAD_SIZE)
    pairs = width // LANES // kv_heads
    w_load = pltpu.make_async_copy(w_hbm, w_ref, sem)
    w_load.start()
    low = iota((tokens, LANES), 1) < HEAD_SIZE

    def doubled(block, head):
        wide = block.astype(jnp.float32)
        turned = pltpu.roll(wide, HEAD_SIZE, 1)
        first, second = (wide, turned) if head == 0 else (turned, wide)
        return [
            jnp.where(low, first, 0.0).astype(jnp.bfloat16),
            jnp.where(low, 0.0, second).astype(jnp.bfloat16),
        ]

    own = iota((tokens, tokens), 1) <= iota((tokens, tokens), 0)
    bias = jnp.where(own, 0.0, jnp.where(first_ref[0] == 0, 0.0, neg_large))
    own_factor = jnp.where(own, 1.0, 0.0).astype(jnp.bfloat16)
    before_factor = jnp.where(own, 0.0, 1.0).astype(jnp.bfloat16)
    head_lanes = jnp.where(low, 1.0, 0.0).astype(jnp.bfloat16), jnp.where(low, 0.0, 1.0).astype(jnp.bfloat16)
    ones = jnp.concatenate(head_lanes, axis=0)
    keys_before = [jnp.concatenate(doubled(before_ref[:, :LANES], head), axis=0) for head in range(kv_heads)]
    values_before = [doubled(before_ref[:, LANES:], head) for head in range(kv_heads)]
    contract = (((1,), (1,)), ((), ()))
    for head in range(kv_heads):
        keys = jnp.concatenate(doubled(kv_ref[:, :LANES], head), axis=0)
        values = jnp.concatenate(doubled(kv_ref[:, LANES:], head) + values_before[head], axis=0)
        for j in range(head * pairs, (head + 1) * pairs):
            q = q_ref[:, j * LANES : (j + 1) * LANES]
            near = lax.dot_general(q, keys, contract, preferred_element_type=jnp.float32)
            far = lax.dot_general(q, keys_before[head], contract, preferred_element_type=jnp.float32)
            terms, sinks = [], []
            for at in range(2):
                span = slice(at * tokens, (at + 1) * tokens)
                part = jnp.where(own, near[:, span], far[:, span]) + bias
                sink = sink_ref[2 * j + at : 2 * j + at + 1, 0:1]
                top = jnp.maximum(jnp.max(part, axis=1, keepdims=True), sink)
                terms.append(jnp.exp(part - top).astype(jnp.bfloat16))
                sinks.append(jnp.exp(sink - top))
            total = jnp.dot(jnp.concatenate(terms, axis=1), ones, preferred_element_type=jnp.float32)
            total += jnp.where(low, sinks[0], sinks[1])
            kept = [term * own_factor for term in terms] + [term * before_factor for term in terms]
            found = jnp.dot(jnp.concatenate(kept, axis=1), values, preferred_element_type=jnp.float32)
            att_ref[:, j * LANES : (j + 1) * LANES] = (found / total).astype(jnp.bfloat16)
    w_load.wait()
    step = 2 * LANES
    for at in range(0, out_ref.shape[1], step):
        out_ref[:, at : at + step] = jnp.dot(
            att_ref[...], w_ref[:, at : at + step], preferred_element_type=jnp.float32
        ).astype(jnp.bfloat16)


def attention(first, sinks, q, key_values, before, w_out):
    tokens = q.shape[0]
    return pl.pallas_call(
        attention_kernel,
        out_shape=shape_of((tokens, w_out.shape[1])),
        in_specs=[SMEM, VMEM, VMEM, VMEM, VMEM, HBM],
        out_specs=VMEM,
        scratch_shapes=[
            pltpu.VMEM(w_out.shape, jnp.bfloat16),
            pltpu.VMEM(q.shape, jnp.bfloat16),
            pltpu.SemaphoreType.DMA,
        ],
        compiler_params=pltpu.CompilerParams(vmem_limit_bytes=54_000_000),
        cost_estimate=cost(2 * tokens * w_out.size * 2, 2 * w_out.size, tokens * tokens * q.shape[1] // HEAD_SIZE),
        name="attention",
    )(first, sinks, q, key_values, before, w_out)


def pack(placed, normed, out_ref):
    rows, tokens = out_ref.shape[0], normed.shape[0]
    row = iota((rows, tokens), 0)
    taken = placed[0:1, :] == row
    for c in range(1, placed.shape[0]):
        taken = taken | (placed[c : c + 1, :] == row)
    taken = jnp.where(taken, 1.0, 0.0).astype(jnp.bfloat16)
    out_ref[...] = jnp.dot(taken, normed, preferred_element_type=jnp.float32).astype(jnp.bfloat16)


def noted(ids, weights):
    coarse = weights.astype(jnp.bfloat16).astype(jnp.float32)
    middle = (weights - coarse).astype(jnp.bfloat16).astype(jnp.float32)
    fine = weights - coarse - middle
    used = [ids.astype(jnp.float32), coarse, middle, fine]
    empty = jnp.zeros((LANES - 4 * ids.shape[0], ids.shape[1]), jnp.float32)
    return jnp.concatenate(used + [empty], axis=0).T.astype(jnp.bfloat16)


def norm_kernel(
    side_ref, residual_ref, near_ref, far_ref, gain_ref, ids_ref, weights_ref, sending_ref, sent_ref, kept_ref, whole_ref
):
    side = side_ref[0]
    half_tokens, half, width = sent_ref.shape[0], kept_ref.shape[1], whole_ref.shape[1]
    added = near_ref[...].astype(jnp.float32) + far_ref[...].astype(jnp.float32)
    whole = (residual_ref[...].astype(jnp.float32) + added).astype(jnp.bfloat16)
    whole_ref[...] = whole
    wide = whole.astype(jnp.float32)
    mean_square = jnp.mean(wide * wide, axis=1, keepdims=True)
    normed = (wide * lax.rsqrt(mean_square + epsilon) * gain_ref[...]).astype(jnp.bfloat16)
    sending_ref[:, :width] = normed
    sending_ref[:, width:] = noted(ids_ref[...], weights_ref[...])
    kept_ref[...] = whole_ref[:, pl.ds(pl.multiple_of(side * half, LANES), half)]
    sent_ref[...] = sending_ref[pl.ds(pl.multiple_of(side * half_tokens, half_tokens), half_tokens), :]


def norm(side, residual_in, near, far, gain, ids, weights, half):
    tokens, width = residual_in.shape
    return pl.pallas_call(
        norm_kernel,
        out_shape=(
            shape_of((tokens, width + LANES)),
            shape_of((tokens // 2, width + LANES)),
            shape_of((tokens, half)),
        ),
        in_specs=[SMEM] + [VMEM] * 6,
        out_specs=(VMEM, VMEM, VMEM),
        scratch_shapes=[pltpu.VMEM((tokens, width), jnp.bfloat16)],
        compiler_params=pltpu.CompilerParams(vmem_limit_bytes=24 * MIB),
        cost_estimate=cost(8 * tokens * width, 10 * tokens * width),
        name="norm",
    )(side, residual_in, near, far, gain.reshape(1, width), ids, weights)


def pack_kernel(experts, side_rows, base_ref, side_ref, *refs):
    *part_refs, out_ref, rows_ref, weights_ref, arrived_ref = refs
    side, top_count, width = side_ref[0], rows_ref.shape[0], out_ref.shape[1]
    if len(part_refs) == 1:
        arrived_ref = part_refs[0]
    else:
        mine_ref, other_ref = part_refs
        part = mine_ref.shape[0]
        arrived_ref[pl.ds(pl.multiple_of(side * part, part), part), :] = mine_ref[...]
        arrived_ref[pl.ds(pl.multiple_of((1 - side) * part, part), part), :] = other_ref[...]
    notes = arrived_ref[:, width:].astype(jnp.float32).T
    first, second, third = [notes[k * top_count : (k + 1) * top_count, :] for k in range(1, 4)]
    weights_ref[...] = first + second + third
    rows = rows_of(notes[:top_count, :], experts, side_rows, base_ref[0], side)
    rows_ref[...] = rows
    pack(rows, arrived_ref[:, :width], out_ref)


def packed_rows(base, side, parts, top_count, experts, side_rows, rows):
    tokens = sum([part.shape[0] for part in parts])
    width = parts[0].shape[1] - LANES
    return pl.pallas_call(
        functools.partial(pack_kernel, experts, side_rows),
        out_shape=(
            shape_of((rows, width)),
            shape_of((top_count, tokens), jnp.int32),
            shape_of((top_count, tokens), jnp.float32),
        ),
        in_specs=[SMEM, SMEM] + [VMEM] * len(parts),
        out_specs=(VMEM, VMEM, VMEM),
        scratch_shapes=[pltpu.VMEM((tokens, width + LANES), jnp.bfloat16)],
        compiler_params=pltpu.CompilerParams(vmem_limit_bytes=24 * MIB),
        cost_estimate=cost(2 * rows * tokens * width, 2 * rows * width),
        name="packed_rows",
    )(base, side, *parts)


def expert_kernel(
    x_hbm, gate_hbm, up_hbm, down_hbm, gate_too_hbm, up_too_hbm, down_too_hbm, y_hbm, x_ref, y_ref, gate_ref, up_ref,
    down_ref, hidden_ref, gate_sum, up_sum, total_ref, x_sem, y_sem, gate_sem, up_sem, down_sem,
):
    rows, width = x_ref.shape
    share = gate_hbm.shape[2]
    deep, cuts = width // CUTS, share // DEEP
    loads = []
    for k, (gate, up) in enumerate([(gate_hbm, up_hbm), (gate_too_hbm, up_too_hbm)]):
        for c in range(CUTS):
            span = pl.ds(c * deep, deep)
            loads.append(
                [
                    pltpu.make_async_copy(gate.at[0, span], gate_ref.at[k, span], gate_sem.at[k, c]),
                    pltpu.make_async_copy(up.at[0, span], up_ref.at[k, span], up_sem.at[k, c]),
                ]
            )
    for k, down in enumerate([down_hbm, down_too_hbm]):
        for c in range(cuts):
            source, target = pl.ds(c * DEEP, DEEP), pl.ds(k * share + c * DEEP, DEEP)
            loads.append([pltpu.make_async_copy(down.at[0, source], down_ref.at[target], down_sem.at[k, c])])

    def start(number):
        if number < len(loads):
            for load in loads[number]:
                load.start()

    def arrive(number):
        for load in loads[number]:
            load.wait()
        start(number + AHEAD)

    x_load = pltpu.make_async_copy(x_hbm, x_ref, x_sem)
    x_load.start()
    for number in range(AHEAD):
        start(number)
    x_load.wait()
    for k in range(2):
        for c in range(CUTS):
            arrive(k * CUTS + c)
            span = slice(c * deep, (c + 1) * deep)
            x = x_ref[:, span]
            gate = jnp.dot(x, gate_ref[k, span, :], preferred_element_type=jnp.float32)
            up = jnp.dot(x, up_ref[k, span, :], preferred_element_type=jnp.float32)
            if c > 0:
                gate, up = gate_sum[...] + gate, up_sum[...] + up
            if c < CUTS - 1:
                gate_sum[...], up_sum[...] = gate, up
            else:
                hidden = gate * (0.5 + 0.5 * jnp.tanh(0.5 * gate)) * up
                hidden_ref[:, k * share : (k + 1) * share] = hidden.astype(jnp.bfloat16)
    for c in range(2 * cuts - 1):
        arrive(2 * CUTS + c)
        span = slice(c * DEEP, (c + 1) * DEEP)
        part = jnp.dot(hidden_ref[:, span], down_ref[span, :], preferred_element_type=jnp.float32)
        total_ref[...] = part if c == 0 else total_ref[...] + part
    arrive(2 * CUTS + 2 * cuts - 1)
    span = slice((2 * cuts - 1) * DEEP, 2 * cuts * DEEP)
    step = 2 * LANES
    stores = []
    for i in range(width // step):
        columns = slice(i * step, (i + 1) * step)
        part = jnp.dot(hidden_ref[:, span], down_ref[span, columns], preferred_element_type=jnp.float32)
        y_ref[:, columns] = (total_ref[:, columns] + part).astype(jnp.bfloat16)
        column_span = pl.ds(i * step, step)
        stores.append(pltpu.make_async_copy(y_ref.at[:, column_span], y_hbm.at[:, column_span], y_sem.at[i]))
        stores[i].start()
    for store in stores:
        store.wait()


def expert_layer(x, mine, others):
    rows, width = x.shape
    share = mine[0].shape[2]
    return pl.pallas_call(
        expert_kernel,
        out_shape=shape_of((rows, width)),
        in_specs=[HBM] * 7,
        out_specs=HBM,
        scratch_shapes=[
            pltpu.VMEM((rows, width), jnp.bfloat16),
            pltpu.VMEM((rows, width), jnp.bfloat16),
            pltpu.VMEM((2, width, share), jnp.bfloat16),
            pltpu.VMEM((2, width, share), jnp.bfloat16),
            pltpu.VMEM((2 * share, width), jnp.bfloat16),
            pltpu.VMEM((rows, 2 * share), jnp.bfloat16),
            pltpu.VMEM((rows, share), jnp.float32),
            pltpu.VMEM((rows, share), jnp.float32),
            pltpu.VMEM((rows, width), jnp.float32),
            pltpu.SemaphoreType.DMA,
            pltpu.SemaphoreType.DMA((width // (2 * LANES),)),
            pltpu.SemaphoreType.DMA((2, CUTS)),
            pltpu.SemaphoreType.DMA((2, CUTS)),
            pltpu.SemaphoreType.DMA((2, share // DEEP)),
        ],
        compiler_params=pltpu.CompilerParams(vmem_limit_bytes=60 * MIB),
        cost_estimate=cost(12 * rows * width * share, 12 * width * share, 2 * rows * share),
        name="expert_layer",
    )(x, *mine, *others)


def combine_kernel(side_ref, rows_ref, weights_ref, y_ref, *refs):
    *more_refs, mine_ref, sent_ref, total_ref = refs
    top_count, tokens = rows_ref.shape
    half = mine_ref.shape[1]
    row = iota((y_ref.shape[0], tokens), 0)
    share = jnp.zeros(row.shape, jnp.float32)
    for c in range(top_count):
        share = jnp.where(rows_ref[c : c + 1, :] == row, weights_ref[c : c + 1, :], share)
    coarse = share.astype(jnp.bfloat16)
    fine = (share - coarse.astype(jnp.float32)).astype(jnp.bfloat16)
    y = y_ref[...]
    contract = (((0,), (0,)), ((), ()))
    total_ref[...] = lax.dot_general(coarse, y, contract, preferred_element_type=jnp.float32)
    total_ref[...] += lax.dot_general(fine, y, contract, preferred_element_type=jnp.float32)
    side = side_ref[0]
    mine = total_ref[:, pl.ds(pl.multiple_of(side * half, LANES), half)]
    for more_ref in more_refs:
        mine += more_ref[...].astype(jnp.float32)
    mine_ref[...] = mine
    sent_ref[...] = total_ref[:, pl.ds(pl.multiple_of((1 - side) * half, LANES), half)].astype(jnp.bfloat16)


def combine(side, placed, weights, y, half, more=()):
    tokens = placed.shape[1]
    rows, width = y.shape
    return pl.pallas_call(
        combine_kernel,
        out_shape=(shape_of((tokens, half), jnp.float32), shape_of((tokens, half))),
        in_specs=[SMEM] + [VMEM] * (3 + len(more)),
        out_specs=(VMEM, VMEM),
        scratch_shapes=[pltpu.VMEM((tokens, width), jnp.float32)],
        compiler_params=pltpu.CompilerParams(vmem_limit_bytes=24 * MIB),
        cost_estimate=cost(4 * rows * tokens * width, 2 * rows * width),
        name="combine",
    )(side, placed, weights, y, *more)


def local(
    residual_in,
    query_rows,
    rotated_key_rows,
    value_row_matrix,
    learned_sink_scores,
    w_out,
    norm_gain,
    expert_ids,
    route_weights,
    w_gate,
    w_up,
    w_down,
):
    tok_dev, model_width = residual_in.shape
    seq_count = lax.axis_size("seq")
    experts = w_gate.shape[0] * seq_count
    top_count = expert_ids.shape[1]
    capacity = max(2, 8 * tok_dev // experts)
    sides = lax.axis_size("tp")
    side_rows = capacity // sides
    group = seq_count // 2
    rows = experts // 2 * side_rows
    half = model_width // sides
    at_seq = lax.axis_index("seq").astype(jnp.int32)
    base = jnp.where(at_seq < group, 0, experts // 2).astype(jnp.int32).reshape(1)
    side = lax.axis_index("tp").astype(jnp.int32).reshape(1)
    first = (at_seq == 0).astype(jnp.int32).reshape(1)
    ids, route = expert_ids.T, route_weights.T

    key_values = lax.optimization_barrier(jnp.concatenate([rotated_key_rows, value_row_matrix], axis=1))
    before = passed_along(key_values, "seq", 1)
    sinks = jnp.broadcast_to(learned_sink_scores[:, None], (learned_sink_scores.shape[0], LANES))
    sinks, queries = lax.optimization_barrier((sinks, query_rows))
    scaled = queries * jnp.bfloat16(HEAD_SIZE**-0.5)
    weights = (w_gate, w_up, w_down)
    others = [swapped(weight, "tp") for weight in weights]
    near = attention(
        first, sinks, scaled, key_values, before, w_out
    )
    near, *others = lax.optimization_barrier((near, *others))
    far = swapped(near, "tp")
    sending, sent, kept = norm(side, residual_in, near, far, norm_gain, ids, route, half)

    def exchanged(block):
        block = block.reshape(group, rows // group, model_width)
        groups = [list(range(group)), list(range(group, seq_count))]
        block = lax.all_to_all(
            block, "seq", split_axis=0, concat_axis=0, axis_index_groups=groups, tiled=True
        )
        return block.reshape(rows, model_width)

    crossed = swapped_halves(sent, "seq")
    packed, placed, _ = packed_rows(base, side, (sending,), top_count, experts, side_rows, rows)
    crossed, packed = lax.optimization_barrier((crossed, packed))
    packed_peer, placed_peer, route_peer = packed_rows(
        base, side, (crossed, swapped(crossed, "tp")), top_count, experts, side_rows, rows
    )
    arrived_peer = exchanged(packed_peer)
    arrived_peer, packed = lax.optimization_barrier((arrived_peer, packed))
    arrived = exchanged(packed)
    result_peer = expert_layer(arrived_peer, weights, others)
    result_peer, arrived = lax.optimization_barrier((result_peer, arrived))
    result = expert_layer(arrived, weights, others)

    returned_peer = exchanged(result_peer)
    result, returned_peer = lax.optimization_barrier((result, returned_peer))
    returned = exchanged(result)
    mine_peer, sent_peer = combine(side, placed_peer, route_peer, returned_peer, half)
    summed_peer = (mine_peer + swapped(sent_peer, "tp").astype(jnp.float32)).astype(jnp.bfloat16)
    back = swapped_halves(summed_peer, "seq")
    mine, sent = combine(side, placed, route, returned, half, (kept,))
    sent, back = lax.optimization_barrier((sent, back))
    return (mine + swapped(sent, "tp").astype(jnp.float32) + back.astype(jnp.float32)).astype(jnp.bfloat16)


def solution(mesh):
    placed = (
        P("seq", None),
        P("seq", "tp"),
        P("seq", "tp"),
        P("seq", "tp"),
        P("tp"),
        P("tp", None),
        P(),
        P("seq", None),
        P("seq", None),
        P("seq", None, "tp"),
        P("seq", None, "tp"),
        P("seq", "tp", None),
    )
    return jax.shard_map(
        local, mesh=mesh, in_specs=placed, out_specs=P("seq", "tp"), check_vma=False
    )
```

```python
import functools

import jax
import jax.numpy as jnp
from jax import lax
from jax.experimental import pallas as pl
from jax.experimental.pallas import tpu as pltpu
from jax.sharding import PartitionSpec as P

HEAD_SIZE = 64
WINDOW_LENGTH = 128
LANES = 128
MIB = 1024 * 1024
CUTS = 3
DEEP = 256
AHEAD = 3

neg_large = -1e30
epsilon = 1e-05

VMEM = pl.BlockSpec(memory_space=pltpu.VMEM)
SMEM = pl.BlockSpec(memory_space=pltpu.SMEM)
HBM = pl.BlockSpec(memory_space=pltpu.HBM)


def passed_along(block, axis, distance):
    devices = range(lax.axis_size(axis))
    route = [(i - distance, i) for i in devices if i - distance in devices]
    return lax.ppermute(block, axis, route)


def swapped(block, axis):
    count = lax.axis_size(axis)
    return lax.ppermute(block, axis, [(i, count - 1 - i) for i in range(count)])


def swapped_halves(block, axis):
    count = lax.axis_size(axis)
    return lax.ppermute(block, axis, [(i, (i + count // 2) % count) for i in range(count)])


def shape_of(dims, dtype=jnp.bfloat16):
    return jax.ShapeDtypeStruct(dims, dtype)


def cost(flops, moved, transcendentals=0):
    return pl.CostEstimate(flops=flops, bytes_accessed=moved, transcendentals=transcendentals)


def iota(dims, dimension):
    return lax.broadcasted_iota(jnp.int32, dims, dimension)


def rows_of(ids, experts, side_rows, base, side):
    top_count, tokens = ids.shape
    names = iota((experts, tokens), 0).astype(jnp.float32)
    hits = [ids[c : c + 1, :] == names for c in range(top_count)]
    named = sum([hit.astype(jnp.float32) for hit in hits]).astype(jnp.bfloat16)
    square = (tokens, tokens)
    earlier = (iota(square, 0) < iota(square, 1)).astype(jnp.bfloat16)
    slot = jnp.dot(named, earlier, preferred_element_type=jnp.float32) - (side * side_rows).astype(jnp.float32)
    expert = names - base.astype(jnp.float32)
    here = (slot >= 0.0) & (slot < side_rows) & (expert >= 0.0) & (expert < experts // 2)
    rows = jnp.where(here, expert * side_rows + slot, -1.0)
    lines = [jnp.sum(jnp.where(hit, rows, 0.0), axis=0, keepdims=True) for hit in hits]
    return jnp.concatenate(lines, axis=0).astype(jnp.int32)


def attention_kernel(
    first_ref, sink_ref, q_ref, kv_ref, before_ref, w_hbm, out_ref, w_ref, att_ref, sum_ref, sem
):
    tokens, width = q_ref.shape
    kv_heads = kv_ref.shape[1] // (2 * HEAD_SIZE)
    pairs = width // LANES // kv_heads
    w_load = pltpu.make_async_copy(w_hbm, w_ref, sem)
    w_load.start()
    low = iota((tokens, LANES), 1) < HEAD_SIZE

    def doubled(block, head):
        wide = block.astype(jnp.float32)
        turned = pltpu.roll(wide, HEAD_SIZE, 1)
        first, second = (wide, turned) if head == 0 else (turned, wide)
        return [
            jnp.where(low, first, 0.0).astype(jnp.bfloat16),
            jnp.where(low, 0.0, second).astype(jnp.bfloat16),
        ]

    own = iota((tokens, tokens), 1) <= iota((tokens, tokens), 0)
    bias = jnp.where(own, 0.0, jnp.where(first_ref[0] == 0, 0.0, neg_large))
    own_factor = jnp.where(own, 1.0, 0.0).astype(jnp.bfloat16)
    before_factor = jnp.where(own, 0.0, 1.0).astype(jnp.bfloat16)
    head_lanes = jnp.where(low, 1.0, 0.0).astype(jnp.bfloat16), jnp.where(low, 0.0, 1.0).astype(jnp.bfloat16)
    ones = jnp.concatenate(head_lanes, axis=0)
    keys_before = [jnp.concatenate(doubled(before_ref[:, :LANES], head), axis=0) for head in range(kv_heads)]
    values_before = [doubled(before_ref[:, LANES:], head) for head in range(kv_heads)]
    contract = (((1,), (1,)), ((), ()))
    for head in range(kv_heads):
        keys = jnp.concatenate(doubled(kv_ref[:, :LANES], head), axis=0)
        values = jnp.concatenate(doubled(kv_ref[:, LANES:], head) + values_before[head], axis=0)
        for j in range(head * pairs, (head + 1) * pairs):
            q = q_ref[:, j * LANES : (j + 1) * LANES]
            near = lax.dot_general(q, keys, contract, preferred_element_type=jnp.float32)
            far = lax.dot_general(q, keys_before[head], contract, preferred_element_type=jnp.float32)
            terms, sinks = [], []
            for at in range(2):
                span = slice(at * tokens, (at + 1) * tokens)
                part = jnp.where(own, near[:, span], far[:, span]) + bias
                sink = sink_ref[2 * j + at : 2 * j + at + 1, :]
                top = jnp.maximum(jnp.max(part, axis=1, keepdims=True), sink)
                terms.append(jnp.exp(part - top).astype(jnp.bfloat16))
                sinks.append(jnp.exp(sink - top))
            total = jnp.dot(jnp.concatenate(terms, axis=1), ones, preferred_element_type=jnp.float32)
            total += jnp.where(low, sinks[0], sinks[1])
            kept = [term * own_factor for term in terms] + [term * before_factor for term in terms]
            found = jnp.dot(jnp.concatenate(kept, axis=1), values, preferred_element_type=jnp.float32)
            att_ref[:, j * LANES : (j + 1) * LANES] = (found / total).astype(jnp.bfloat16)
        if head == 0:
            w_load.wait()
        depth = pairs * LANES
        step = 2 * LANES
        for at in range(0, out_ref.shape[1], step):
            part = jnp.dot(
                att_ref[:, head * depth : (head + 1) * depth],
                w_ref[head * depth : (head + 1) * depth, at : at + step],
                preferred_element_type=jnp.float32,
            )
            if head > 0:
                part += sum_ref[:, at : at + step]
            if head < kv_heads - 1:
                sum_ref[:, at : at + step] = part
            else:
                out_ref[:, at : at + step] = part.astype(jnp.bfloat16)


def attention(first, sinks, q, key_values, before, w_out):
    tokens = q.shape[0]
    return pl.pallas_call(
        attention_kernel,
        out_shape=shape_of((tokens, w_out.shape[1])),
        in_specs=[SMEM, VMEM, VMEM, VMEM, VMEM, HBM],
        out_specs=VMEM,
        scratch_shapes=[
            pltpu.VMEM(w_out.shape, jnp.bfloat16),
            pltpu.VMEM(q.shape, jnp.bfloat16),
            pltpu.VMEM((tokens, w_out.shape[1]), jnp.float32),
            pltpu.SemaphoreType.DMA,
        ],
        compiler_params=pltpu.CompilerParams(vmem_limit_bytes=54_000_000),
        cost_estimate=cost(2 * tokens * w_out.size * 2, 2 * w_out.size, tokens * tokens * q.shape[1] // HEAD_SIZE),
        name="attention",
    )(first, sinks, q, key_values, before, w_out)


def pack(placed, normed, out_ref):
    rows, tokens = out_ref.shape[0], normed.shape[0]
    row = iota((rows, tokens), 0)
    taken = placed[0:1, :] == row
    for c in range(1, placed.shape[0]):
        taken = taken | (placed[c : c + 1, :] == row)
    taken = jnp.where(taken, 1.0, 0.0).astype(jnp.bfloat16)
    out_ref[...] = jnp.dot(taken, normed, preferred_element_type=jnp.float32).astype(jnp.bfloat16)


def norm_kernel(side_ref, residual_ref, near_ref, far_ref, gain_ref, normed_ref, sent_ref, kept_ref, whole_ref):
    side = side_ref[0]
    half_tokens, half = sent_ref.shape[0], kept_ref.shape[1]
    added = near_ref[...].astype(jnp.float32) + far_ref[...].astype(jnp.float32)
    whole = (residual_ref[...].astype(jnp.float32) + added).astype(jnp.bfloat16)
    whole_ref[...] = whole
    wide = whole.astype(jnp.float32)
    mean_square = jnp.mean(wide * wide, axis=1, keepdims=True)
    normed_ref[...] = (wide * lax.rsqrt(mean_square + epsilon) * gain_ref[...]).astype(jnp.bfloat16)
    kept_ref[...] = whole_ref[:, pl.ds(pl.multiple_of(side * half, LANES), half)]
    sent_ref[...] = normed_ref[pl.ds(pl.multiple_of(side * half_tokens, half_tokens), half_tokens), :]


def norm(side, residual_in, near, far, gain, half):
    tokens, width = residual_in.shape
    return pl.pallas_call(
        norm_kernel,
        out_shape=(shape_of((tokens, width)), shape_of((tokens // 2, width)), shape_of((tokens, half))),
        in_specs=[SMEM] + [VMEM] * 4,
        out_specs=(VMEM, VMEM, VMEM),
        scratch_shapes=[pltpu.VMEM((tokens, width), jnp.bfloat16)],
        compiler_params=pltpu.CompilerParams(vmem_limit_bytes=24 * MIB),
        cost_estimate=cost(8 * tokens * width, 10 * tokens * width),
        name="norm",
    )(side, residual_in, near, far, gain.reshape(1, width))


def pack_kernel(experts, side_rows, base_ref, side_ref, notes_ref, *refs):
    *part_refs, out_ref, rows_ref, arrived_ref = refs
    side, top_count = side_ref[0], rows_ref.shape[0]
    if len(part_refs) == 1:
        arrived_ref = part_refs[0]
    else:
        mine_ref, other_ref = part_refs
        part = mine_ref.shape[0]
        arrived_ref[pl.ds(pl.multiple_of(side * part, part), part), :] = mine_ref[...]
        arrived_ref[pl.ds(pl.multiple_of((1 - side) * part, part), part), :] = other_ref[...]
    rows = rows_of(notes_ref[:top_count, :], experts, side_rows, base_ref[0], side)
    rows_ref[...] = rows
    pack(rows, arrived_ref[...], out_ref)


def packed_rows(base, side, notes, parts, experts, side_rows, rows):
    tokens = sum([part.shape[0] for part in parts])
    width = parts[0].shape[1]
    return pl.pallas_call(
        functools.partial(pack_kernel, experts, side_rows),
        out_shape=(shape_of((rows, width)), shape_of((notes.shape[0] // 2, tokens), jnp.int32)),
        in_specs=[SMEM, SMEM, VMEM] + [VMEM] * len(parts),
        out_specs=(VMEM, VMEM),
        scratch_shapes=[pltpu.VMEM((tokens, width), jnp.bfloat16)],
        compiler_params=pltpu.CompilerParams(vmem_limit_bytes=24 * MIB),
        cost_estimate=cost(2 * rows * tokens * width, 2 * rows * width),
        name="packed_rows",
    )(base, side, notes, *parts)


def expert_kernel(
    x_hbm, gate_hbm, up_hbm, down_hbm, gate_too_hbm, up_too_hbm, down_too_hbm, y_hbm, x_ref, y_ref, gate_ref, up_ref,
    down_ref, hidden_ref, gate_sum, up_sum, total_ref, x_sem, y_sem, gate_sem, up_sem, down_sem,
):
    rows, width = x_ref.shape
    share = gate_hbm.shape[2]
    deep, cuts = width // CUTS, share // DEEP
    loads = []
    for k, (gate, up) in enumerate([(gate_hbm, up_hbm), (gate_too_hbm, up_too_hbm)]):
        for c in range(CUTS):
            span = pl.ds(c * deep, deep)
            loads.append(
                [
                    pltpu.make_async_copy(gate.at[0, span], gate_ref.at[k, span], gate_sem.at[k, c]),
                    pltpu.make_async_copy(up.at[0, span], up_ref.at[k, span], up_sem.at[k, c]),
                ]
            )
    for k, down in enumerate([down_hbm, down_too_hbm]):
        for c in range(cuts):
            source, target = pl.ds(c * DEEP, DEEP), pl.ds(k * share + c * DEEP, DEEP)
            loads.append([pltpu.make_async_copy(down.at[0, source], down_ref.at[target], down_sem.at[k, c])])

    def start(number):
        if number < len(loads):
            for load in loads[number]:
                load.start()

    def arrive(number):
        for load in loads[number]:
            load.wait()
        start(number + AHEAD)

    x_load = pltpu.make_async_copy(x_hbm, x_ref, x_sem)
    x_load.start()
    for number in range(AHEAD):
        start(number)
    x_load.wait()
    for k in range(2):
        for c in range(CUTS):
            arrive(k * CUTS + c)
            span = slice(c * deep, (c + 1) * deep)
            x = x_ref[:, span]
            gate = jnp.dot(x, gate_ref[k, span, :], preferred_element_type=jnp.float32)
            up = jnp.dot(x, up_ref[k, span, :], preferred_element_type=jnp.float32)
            if c > 0:
                gate, up = gate_sum[...] + gate, up_sum[...] + up
            if c < CUTS - 1:
                gate_sum[...], up_sum[...] = gate, up
            else:
                hidden = gate * (0.5 + 0.5 * jnp.tanh(0.5 * gate)) * up
                hidden_ref[:, k * share : (k + 1) * share] = hidden.astype(jnp.bfloat16)
    for c in range(2 * cuts - 1):
        arrive(2 * CUTS + c)
        span = slice(c * DEEP, (c + 1) * DEEP)
        part = jnp.dot(hidden_ref[:, span], down_ref[span, :], preferred_element_type=jnp.float32)
        total_ref[...] = part if c == 0 else total_ref[...] + part
    arrive(2 * CUTS + 2 * cuts - 1)
    span = slice((2 * cuts - 1) * DEEP, 2 * cuts * DEEP)
    step = 2 * LANES
    stores = []
    for i in range(width // step):
        columns = slice(i * step, (i + 1) * step)
        part = jnp.dot(hidden_ref[:, span], down_ref[span, columns], preferred_element_type=jnp.float32)
        y_ref[:, columns] = (total_ref[:, columns] + part).astype(jnp.bfloat16)
        column_span = pl.ds(i * step, step)
        stores.append(pltpu.make_async_copy(y_ref.at[:, column_span], y_hbm.at[:, column_span], y_sem.at[i]))
        stores[i].start()
    for store in stores:
        store.wait()


def expert_layer(x, mine, others):
    rows, width = x.shape
    share = mine[0].shape[2]
    return pl.pallas_call(
        expert_kernel,
        out_shape=shape_of((rows, width)),
        in_specs=[HBM] * 7,
        out_specs=HBM,
        scratch_shapes=[
            pltpu.VMEM((rows, width), jnp.bfloat16),
            pltpu.VMEM((rows, width), jnp.bfloat16),
            pltpu.VMEM((2, width, share), jnp.bfloat16),
            pltpu.VMEM((2, width, share), jnp.bfloat16),
            pltpu.VMEM((2 * share, width), jnp.bfloat16),
            pltpu.VMEM((rows, 2 * share), jnp.bfloat16),
            pltpu.VMEM((rows, share), jnp.float32),
            pltpu.VMEM((rows, share), jnp.float32),
            pltpu.VMEM((rows, width), jnp.float32),
            pltpu.SemaphoreType.DMA,
            pltpu.SemaphoreType.DMA((width // (2 * LANES),)),
            pltpu.SemaphoreType.DMA((2, CUTS)),
            pltpu.SemaphoreType.DMA((2, CUTS)),
            pltpu.SemaphoreType.DMA((2, share // DEEP)),
        ],
        compiler_params=pltpu.CompilerParams(vmem_limit_bytes=60 * MIB),
        cost_estimate=cost(12 * rows * width * share, 12 * width * share, 2 * rows * share),
        name="expert_layer",
    )(x, *mine, *others)


def combine_kernel(side_ref, rows_ref, weights_ref, y_ref, *refs):
    *more_refs, mine_ref, sent_ref, total_ref = refs
    top_count, tokens = rows_ref.shape
    half = mine_ref.shape[1]
    row = iota((y_ref.shape[0], tokens), 0)
    share = jnp.zeros(row.shape, jnp.float32)
    for c in range(top_count):
        share = jnp.where(rows_ref[c : c + 1, :] == row, weights_ref[top_count + c : top_count + c + 1, :], share)
    coarse = share.astype(jnp.bfloat16)
    fine = (share - coarse.astype(jnp.float32)).astype(jnp.bfloat16)
    y = y_ref[...]
    contract = (((0,), (0,)), ((), ()))
    total_ref[...] = lax.dot_general(coarse, y, contract, preferred_element_type=jnp.float32)
    total_ref[...] += lax.dot_general(fine, y, contract, preferred_element_type=jnp.float32)
    side = side_ref[0]
    mine = total_ref[:, pl.ds(pl.multiple_of(side * half, LANES), half)]
    for more_ref in more_refs:
        mine += more_ref[...].astype(jnp.float32)
    mine_ref[...] = mine
    sent_ref[...] = total_ref[:, pl.ds(pl.multiple_of((1 - side) * half, LANES), half)].astype(jnp.bfloat16)


def combine(side, placed, weights, y, half, more=()):
    tokens = placed.shape[1]
    rows, width = y.shape
    return pl.pallas_call(
        combine_kernel,
        out_shape=(shape_of((tokens, half), jnp.float32), shape_of((tokens, half))),
        in_specs=[SMEM] + [VMEM] * (3 + len(more)),
        out_specs=(VMEM, VMEM),
        scratch_shapes=[pltpu.VMEM((tokens, width), jnp.float32)],
        compiler_params=pltpu.CompilerParams(vmem_limit_bytes=24 * MIB),
        cost_estimate=cost(4 * rows * tokens * width, 2 * rows * width),
        name="combine",
    )(side, placed, weights, y, *more)


def local(
    residual_in,
    query_rows,
    rotated_key_rows,
    value_row_matrix,
    learned_sink_scores,
    w_out,
    norm_gain,
    expert_ids,
    route_weights,
    w_gate,
    w_up,
    w_down,
):
    tok_dev, model_width = residual_in.shape
    seq_count = lax.axis_size("seq")
    experts = w_gate.shape[0] * seq_count
    capacity = max(2, 8 * tok_dev // experts)
    sides = lax.axis_size("tp")
    side_rows = capacity // sides
    group = seq_count // 2
    rows = experts // 2 * side_rows
    half = model_width // sides
    at_seq = lax.axis_index("seq").astype(jnp.int32)
    base = jnp.where(at_seq < group, 0, experts // 2).astype(jnp.int32).reshape(1)
    side = lax.axis_index("tp").astype(jnp.int32).reshape(1)
    first = (at_seq == 0).astype(jnp.int32).reshape(1)
    key_values = lax.optimization_barrier(jnp.concatenate([rotated_key_rows, value_row_matrix], axis=1))
    before = passed_along(key_values, "seq", 1)
    sinks = jnp.broadcast_to(learned_sink_scores[:, None], (learned_sink_scores.shape[0], LANES))
    sinks, queries = lax.optimization_barrier((sinks, query_rows))
    scaled = queries * jnp.bfloat16(HEAD_SIZE**-0.5)
    weights = (w_gate, w_up, w_down)
    others = [swapped(weight, "tp") for weight in weights]
    near = attention(
        first, sinks, scaled, key_values, before, w_out
    )
    near, *others = lax.optimization_barrier((near, *others))
    far = swapped(near, "tp")
    normed, sent, kept = norm(side, residual_in, near, far, norm_gain, half)

    def exchanged(block):
        block = block.reshape(group, rows // group, model_width)
        groups = [list(range(group)), list(range(group, seq_count))]
        block = lax.all_to_all(
            block, "seq", split_axis=0, concat_axis=0, axis_index_groups=groups, tiled=True
        )
        return block.reshape(rows, model_width)

    notes = jnp.concatenate([expert_ids.T.astype(jnp.float32), route_weights.T], axis=0)
    crossed = swapped_halves(sent, "seq")
    notes_peer = swapped_halves(notes, "seq")
    packed, placed = packed_rows(base, side, notes, (normed,), experts, side_rows, rows)
    crossed, notes_peer, packed = lax.optimization_barrier((crossed, notes_peer, packed))
    packed_peer, placed_peer = packed_rows(
        base, side, notes_peer, (crossed, swapped(crossed, "tp")), experts, side_rows, rows
    )
    arrived_peer = exchanged(packed_peer)
    arrived_peer, packed = lax.optimization_barrier((arrived_peer, packed))
    arrived = exchanged(packed)
    result_peer = expert_layer(arrived_peer, weights, others)
    result_peer, arrived = lax.optimization_barrier((result_peer, arrived))
    result = expert_layer(arrived, weights, others)

    returned_peer = exchanged(result_peer)
    result, returned_peer = lax.optimization_barrier((result, returned_peer))
    returned = exchanged(result)
    mine_peer, sent_peer = combine(side, placed_peer, notes_peer, returned_peer, half)
    summed_peer = (mine_peer + swapped(sent_peer, "tp").astype(jnp.float32)).astype(jnp.bfloat16)
    back = swapped_halves(summed_peer, "seq")
    mine, sent = combine(side, placed, notes, returned, half, (kept,))
    sent, back = lax.optimization_barrier((sent, back))
    return (mine + swapped(sent, "tp").astype(jnp.float32) + back.astype(jnp.float32)).astype(jnp.bfloat16)


def solution(mesh):
    placed = (
        P("seq", None),
        P("seq", "tp"),
        P("seq", "tp"),
        P("seq", "tp"),
        P("tp"),
        P("tp", None),
        P(),
        P("seq", None),
        P("seq", None),
        P("seq", None, "tp"),
        P("seq", None, "tp"),
        P("seq", "tp", None),
    )
    return jax.shard_map(
        local, mesh=mesh, in_specs=placed, out_specs=P("seq", "tp"), check_vma=False
    )
```

```python
import functools

import jax
import jax.numpy as jnp
from jax import lax
from jax.experimental import pallas as pl
from jax.experimental.pallas import tpu as pltpu
from jax.sharding import PartitionSpec as P

HEAD_SIZE = 64
WINDOW_LENGTH = 128
LANES = 128
MIB = 1024 * 1024
CUTS = 3
DEEP = 256
AHEAD = 3

neg_large = -1e30
epsilon = 1e-05

VMEM = pl.BlockSpec(memory_space=pltpu.VMEM)
SMEM = pl.BlockSpec(memory_space=pltpu.SMEM)
HBM = pl.BlockSpec(memory_space=pltpu.HBM)


def passed_along(block, axis, distance):
    devices = range(lax.axis_size(axis))
    route = [(i - distance, i) for i in devices if i - distance in devices]
    return lax.ppermute(block, axis, route)


def swapped(block, axis):
    count = lax.axis_size(axis)
    return lax.ppermute(block, axis, [(i, count - 1 - i) for i in range(count)])


def swapped_halves(block, axis):
    count = lax.axis_size(axis)
    return lax.ppermute(block, axis, [(i, (i + count // 2) % count) for i in range(count)])


def shape_of(dims, dtype=jnp.bfloat16):
    return jax.ShapeDtypeStruct(dims, dtype)


def cost(flops, moved, transcendentals=0):
    return pl.CostEstimate(flops=flops, bytes_accessed=moved, transcendentals=transcendentals)


def iota(dims, dimension):
    return lax.broadcasted_iota(jnp.int32, dims, dimension)


def rows_of(ids, experts, side_rows, base, side):
    top_count, tokens = ids.shape
    names = iota((experts, tokens), 0).astype(jnp.float32)
    hits = [ids[c : c + 1, :] == names for c in range(top_count)]
    named = sum([hit.astype(jnp.float32) for hit in hits]).astype(jnp.bfloat16)
    square = (tokens, tokens)
    earlier = (iota(square, 0) < iota(square, 1)).astype(jnp.bfloat16)
    slot = jnp.dot(named, earlier, preferred_element_type=jnp.float32) - (side * side_rows).astype(jnp.float32)
    expert = names - base.astype(jnp.float32)
    here = (slot >= 0.0) & (slot < side_rows) & (expert >= 0.0) & (expert < experts // 2)
    rows = jnp.where(here, expert * side_rows + slot, -1.0)
    lines = [jnp.sum(jnp.where(hit, rows, 0.0), axis=0, keepdims=True) for hit in hits]
    return jnp.concatenate(lines, axis=0).astype(jnp.int32)


def attention_kernel(
    first_ref, sink_ref, q_ref, kv_ref, before_ref, w_hbm, out_ref, w_ref, att_ref, sum_ref, sem
):
    tokens, width = q_ref.shape
    kv_heads = kv_ref.shape[1] // (2 * HEAD_SIZE)
    pairs = width // LANES // kv_heads
    w_load = pltpu.make_async_copy(w_hbm, w_ref, sem)
    w_load.start()
    low = iota((tokens, LANES), 1) < HEAD_SIZE

    def doubled(block, head):
        wide = block.astype(jnp.float32)
        turned = pltpu.roll(wide, HEAD_SIZE, 1)
        first, second = (wide, turned) if head == 0 else (turned, wide)
        return [
            jnp.where(low, first, 0.0).astype(jnp.bfloat16),
            jnp.where(low, 0.0, second).astype(jnp.bfloat16),
        ]

    own = iota((tokens, tokens), 1) <= iota((tokens, tokens), 0)
    bias = jnp.where(own, 0.0, jnp.where(first_ref[0] == 0, 0.0, neg_large))
    own_factor = jnp.where(own, 1.0, 0.0).astype(jnp.bfloat16)
    before_factor = jnp.where(own, 0.0, 1.0).astype(jnp.bfloat16)
    head_lanes = jnp.where(low, 1.0, 0.0).astype(jnp.bfloat16), jnp.where(low, 0.0, 1.0).astype(jnp.bfloat16)
    ones = jnp.concatenate(head_lanes, axis=0)
    keys_before = [jnp.concatenate(doubled(before_ref[:, :LANES], head), axis=0) for head in range(kv_heads)]
    values_before = [doubled(before_ref[:, LANES:], head) for head in range(kv_heads)]
    contract = (((1,), (1,)), ((), ()))
    for head in range(kv_heads):
        keys = jnp.concatenate(doubled(kv_ref[:, :LANES], head), axis=0)
        values = jnp.concatenate(doubled(kv_ref[:, LANES:], head) + values_before[head], axis=0)
        for j in range(head * pairs, (head + 1) * pairs):
            q = q_ref[:, j * LANES : (j + 1) * LANES]
            near = lax.dot_general(q, keys, contract, preferred_element_type=jnp.float32)
            far = lax.dot_general(q, keys_before[head], contract, preferred_element_type=jnp.float32)
            terms, sinks = [], []
            for at in range(2):
                span = slice(at * tokens, (at + 1) * tokens)
                part = jnp.where(own, near[:, span], far[:, span]) + bias
                sink = sink_ref[2 * j + at : 2 * j + at + 1, :]
                top = jnp.maximum(jnp.max(part, axis=1, keepdims=True), sink)
                terms.append(jnp.exp(part - top).astype(jnp.bfloat16))
                sinks.append(jnp.exp(sink - top))
            total = jnp.dot(jnp.concatenate(terms, axis=1), ones, preferred_element_type=jnp.float32)
            total += jnp.where(low, sinks[0], sinks[1])
            kept = [term * own_factor for term in terms] + [term * before_factor for term in terms]
            found = jnp.dot(jnp.concatenate(kept, axis=1), values, preferred_element_type=jnp.float32)
            att_ref[:, j * LANES : (j + 1) * LANES] = (found / total).astype(jnp.bfloat16)
        if head == 0:
            w_load.wait()
        depth = pairs * LANES
        step = 2 * LANES
        for at in range(0, out_ref.shape[1], step):
            part = jnp.dot(
                att_ref[:, head * depth : (head + 1) * depth],
                w_ref[head * depth : (head + 1) * depth, at : at + step],
                preferred_element_type=jnp.float32,
            )
            if head > 0:
                part += sum_ref[:, at : at + step]
            if head < kv_heads - 1:
                sum_ref[:, at : at + step] = part
            else:
                out_ref[:, at : at + step] = part.astype(jnp.bfloat16)


def attention(first, sinks, q, key_values, before, w_out):
    tokens = q.shape[0]
    return pl.pallas_call(
        attention_kernel,
        out_shape=shape_of((tokens, w_out.shape[1])),
        in_specs=[SMEM, VMEM, VMEM, VMEM, VMEM, HBM],
        out_specs=VMEM,
        scratch_shapes=[
            pltpu.VMEM(w_out.shape, jnp.bfloat16),
            pltpu.VMEM(q.shape, jnp.bfloat16),
            pltpu.VMEM((tokens, w_out.shape[1]), jnp.float32),
            pltpu.SemaphoreType.DMA,
        ],
        compiler_params=pltpu.CompilerParams(vmem_limit_bytes=54_000_000),
        cost_estimate=cost(2 * tokens * w_out.size * 2, 2 * w_out.size, tokens * tokens * q.shape[1] // HEAD_SIZE),
        name="attention",
    )(first, sinks, q, key_values, before, w_out)


def pack(placed, normed, out_ref):
    rows, tokens = out_ref.shape[0], normed.shape[0]
    row = iota((rows, tokens), 0)
    taken = placed[0:1, :] == row
    for c in range(1, placed.shape[0]):
        taken = taken | (placed[c : c + 1, :] == row)
    taken = jnp.where(taken, 1.0, 0.0).astype(jnp.bfloat16)
    out_ref[...] = jnp.dot(taken, normed, preferred_element_type=jnp.float32).astype(jnp.bfloat16)


def norm_kernel(side_ref, residual_ref, near_ref, far_ref, gain_ref, normed_ref, sent_ref, kept_ref, whole_ref):
    side = side_ref[0]
    half_tokens, half = sent_ref.shape[0], kept_ref.shape[1]
    added = near_ref[...].astype(jnp.float32) + far_ref[...].astype(jnp.float32)
    whole = (residual_ref[...].astype(jnp.float32) + added).astype(jnp.bfloat16)
    whole_ref[...] = whole
    wide = whole.astype(jnp.float32)
    mean_square = jnp.mean(wide * wide, axis=1, keepdims=True)
    normed_ref[...] = (wide * lax.rsqrt(mean_square + epsilon) * gain_ref[...]).astype(jnp.bfloat16)
    kept_ref[...] = whole_ref[:, pl.ds(pl.multiple_of(side * half, LANES), half)]
    sent_ref[...] = normed_ref[pl.ds(pl.multiple_of(side * half_tokens, half_tokens), half_tokens), :]


def norm(side, residual_in, near, far, gain, half):
    tokens, width = residual_in.shape
    return pl.pallas_call(
        norm_kernel,
        out_shape=(shape_of((tokens, width)), shape_of((tokens // 2, width)), shape_of((tokens, half))),
        in_specs=[SMEM] + [VMEM] * 4,
        out_specs=(VMEM, VMEM, VMEM),
        scratch_shapes=[pltpu.VMEM((tokens, width), jnp.bfloat16)],
        compiler_params=pltpu.CompilerParams(vmem_limit_bytes=24 * MIB),
        cost_estimate=cost(8 * tokens * width, 10 * tokens * width),
        name="norm",
    )(side, residual_in, near, far, gain.reshape(1, width))


def pack_kernel(experts, side_rows, base_ref, side_ref, notes_ref, *refs):
    *part_refs, out_ref, rows_ref, arrived_ref = refs
    side, top_count = side_ref[0], rows_ref.shape[0]
    if len(part_refs) == 1:
        arrived_ref = part_refs[0]
    else:
        mine_ref, other_ref = part_refs
        part = mine_ref.shape[0]
        arrived_ref[pl.ds(pl.multiple_of(side * part, part), part), :] = mine_ref[...]
        arrived_ref[pl.ds(pl.multiple_of((1 - side) * part, part), part), :] = other_ref[...]
    rows = rows_of(notes_ref[:top_count, :], experts, side_rows, base_ref[0], side)
    rows_ref[...] = rows
    pack(rows, arrived_ref[...], out_ref)


def packed_rows(base, side, notes, parts, experts, side_rows, rows):
    tokens = sum([part.shape[0] for part in parts])
    width = parts[0].shape[1]
    return pl.pallas_call(
        functools.partial(pack_kernel, experts, side_rows),
        out_shape=(shape_of((rows, width)), shape_of((notes.shape[0] // 2, tokens), jnp.int32)),
        in_specs=[SMEM, SMEM, VMEM] + [VMEM] * len(parts),
        out_specs=(VMEM, VMEM),
        scratch_shapes=[pltpu.VMEM((tokens, width), jnp.bfloat16)],
        compiler_params=pltpu.CompilerParams(vmem_limit_bytes=24 * MIB),
        cost_estimate=cost(2 * rows * tokens * width, 2 * rows * width),
        name="packed_rows",
    )(base, side, notes, *parts)


def expert_kernel(
    x_hbm, gate_hbm, up_hbm, down_hbm, gate_too_hbm, up_too_hbm, down_too_hbm, y_hbm, x_ref, y_ref, gate_ref, up_ref,
    down_ref, hidden_ref, gate_sum, up_sum, total_ref, x_sem, y_sem, gate_sem, up_sem, down_sem,
):
    rows, width = x_ref.shape
    share = gate_hbm.shape[2]
    deep, cuts = width // CUTS, share // DEEP
    loads = []
    for k, (gate, up) in enumerate([(gate_hbm, up_hbm), (gate_too_hbm, up_too_hbm)]):
        for c in range(CUTS):
            span = pl.ds(c * deep, deep)
            loads.append(
                [
                    pltpu.make_async_copy(gate.at[0, span], gate_ref.at[k, span], gate_sem.at[k, c]),
                    pltpu.make_async_copy(up.at[0, span], up_ref.at[k, span], up_sem.at[k, c]),
                ]
            )
    for k, down in enumerate([down_hbm, down_too_hbm]):
        for c in range(cuts):
            source, target = pl.ds(c * DEEP, DEEP), pl.ds(k * share + c * DEEP, DEEP)
            loads.append([pltpu.make_async_copy(down.at[0, source], down_ref.at[target], down_sem.at[k, c])])

    def start(number):
        if number < len(loads):
            for load in loads[number]:
                load.start()

    def arrive(number):
        for load in loads[number]:
            load.wait()
        start(number + AHEAD)

    x_load = pltpu.make_async_copy(x_hbm, x_ref, x_sem)
    x_load.start()
    for number in range(AHEAD):
        start(number)
    x_load.wait()
    for k in range(2):
        for c in range(CUTS):
            arrive(k * CUTS + c)
            span = slice(c * deep, (c + 1) * deep)
            x = x_ref[:, span]
            gate = jnp.dot(x, gate_ref[k, span, :], preferred_element_type=jnp.float32)
            up = jnp.dot(x, up_ref[k, span, :], preferred_element_type=jnp.float32)
            if c > 0:
                gate, up = gate_sum[...] + gate, up_sum[...] + up
            if c < CUTS - 1:
                gate_sum[...], up_sum[...] = gate, up
            else:
                hidden = gate * (0.5 + 0.5 * jnp.tanh(0.5 * gate)) * up
                hidden_ref[:, k * share : (k + 1) * share] = hidden.astype(jnp.bfloat16)
    for c in range(2 * cuts - 1):
        arrive(2 * CUTS + c)
        span = slice(c * DEEP, (c + 1) * DEEP)
        part = jnp.dot(hidden_ref[:, span], down_ref[span, :], preferred_element_type=jnp.float32)
        total_ref[...] = part if c == 0 else total_ref[...] + part
    arrive(2 * CUTS + 2 * cuts - 1)
    span = slice((2 * cuts - 1) * DEEP, 2 * cuts * DEEP)
    step = 2 * LANES
    stores = []
    for i in range(width // step):
        columns = slice(i * step, (i + 1) * step)
        part = jnp.dot(hidden_ref[:, span], down_ref[span, columns], preferred_element_type=jnp.float32)
        y_ref[:, columns] = (total_ref[:, columns] + part).astype(jnp.bfloat16)
        column_span = pl.ds(i * step, step)
        stores.append(pltpu.make_async_copy(y_ref.at[:, column_span], y_hbm.at[:, column_span], y_sem.at[i]))
        stores[i].start()
    for store in stores:
        store.wait()


def expert_layer(x, mine, others):
    rows, width = x.shape
    share = mine[0].shape[2]
    return pl.pallas_call(
        expert_kernel,
        out_shape=shape_of((rows, width)),
        in_specs=[HBM] * 7,
        out_specs=HBM,
        scratch_shapes=[
            pltpu.VMEM((rows, width), jnp.bfloat16),
            pltpu.VMEM((rows, width), jnp.bfloat16),
            pltpu.VMEM((2, width, share), jnp.bfloat16),
            pltpu.VMEM((2, width, share), jnp.bfloat16),
            pltpu.VMEM((2 * share, width), jnp.bfloat16),
            pltpu.VMEM((rows, 2 * share), jnp.bfloat16),
            pltpu.VMEM((rows, share), jnp.float32),
            pltpu.VMEM((rows, share), jnp.float32),
            pltpu.VMEM((rows, width), jnp.float32),
            pltpu.SemaphoreType.DMA,
            pltpu.SemaphoreType.DMA((width // (2 * LANES),)),
            pltpu.SemaphoreType.DMA((2, CUTS)),
            pltpu.SemaphoreType.DMA((2, CUTS)),
            pltpu.SemaphoreType.DMA((2, share // DEEP)),
        ],
        compiler_params=pltpu.CompilerParams(vmem_limit_bytes=60 * MIB),
        cost_estimate=cost(12 * rows * width * share, 12 * width * share, 2 * rows * share),
        name="expert_layer",
    )(x, *mine, *others)


def combine_kernel(side_ref, rows_ref, weights_ref, y_ref, *refs):
    *more_refs, mine_ref, sent_ref, total_ref = refs
    top_count, tokens = rows_ref.shape
    half = mine_ref.shape[1]
    row = iota((y_ref.shape[0], tokens), 0)
    share = jnp.zeros(row.shape, jnp.float32)
    for c in range(top_count):
        share = jnp.where(rows_ref[c : c + 1, :] == row, weights_ref[top_count + c : top_count + c + 1, :], share)
    coarse = share.astype(jnp.bfloat16)
    fine = (share - coarse.astype(jnp.float32)).astype(jnp.bfloat16)
    y = y_ref[...]
    contract = (((0,), (0,)), ((), ()))
    total_ref[...] = lax.dot_general(coarse, y, contract, preferred_element_type=jnp.float32)
    total_ref[...] += lax.dot_general(fine, y, contract, preferred_element_type=jnp.float32)
    side = side_ref[0]
    mine = total_ref[:, pl.ds(pl.multiple_of(side * half, LANES), half)]
    for more_ref in more_refs:
        mine += more_ref[...].astype(jnp.float32)
    mine_ref[...] = mine
    sent_ref[...] = total_ref[:, pl.ds(pl.multiple_of((1 - side) * half, LANES), half)].astype(jnp.bfloat16)


def combine(side, placed, weights, y, half, more=()):
    tokens = placed.shape[1]
    rows, width = y.shape
    return pl.pallas_call(
        combine_kernel,
        out_shape=(shape_of((tokens, half), jnp.float32), shape_of((tokens, half))),
        in_specs=[SMEM] + [VMEM] * (3 + len(more)),
        out_specs=(VMEM, VMEM),
        scratch_shapes=[pltpu.VMEM((tokens, width), jnp.float32)],
        compiler_params=pltpu.CompilerParams(vmem_limit_bytes=24 * MIB),
        cost_estimate=cost(4 * rows * tokens * width, 2 * rows * width),
        name="combine",
    )(side, placed, weights, y, *more)


def local(
    residual_in,
    query_rows,
    rotated_key_rows,
    value_row_matrix,
    learned_sink_scores,
    w_out,
    norm_gain,
    expert_ids,
    route_weights,
    w_gate,
    w_up,
    w_down,
):
    tok_dev, model_width = residual_in.shape
    seq_count = lax.axis_size("seq")
    experts = w_gate.shape[0] * seq_count
    capacity = max(2, 8 * tok_dev // experts)
    sides = lax.axis_size("tp")
    side_rows = capacity // sides
    group = seq_count // 2
    rows = experts // 2 * side_rows
    half = model_width // sides
    at_seq = lax.axis_index("seq").astype(jnp.int32)
    base = jnp.where(at_seq < group, 0, experts // 2).astype(jnp.int32).reshape(1)
    side = lax.axis_index("tp").astype(jnp.int32).reshape(1)
    first = (at_seq == 0).astype(jnp.int32).reshape(1)
    key_values = lax.optimization_barrier(jnp.concatenate([rotated_key_rows, value_row_matrix], axis=1))
    before = passed_along(key_values, "seq", 1)
    sinks = jnp.broadcast_to(learned_sink_scores[:, None], (learned_sink_scores.shape[0], LANES))
    sinks, queries = lax.optimization_barrier((sinks, query_rows))
    scaled = queries * jnp.bfloat16(HEAD_SIZE**-0.5)
    weights = (w_gate, w_up, w_down)
    others = [swapped(weight, "tp") for weight in weights]
    near = attention(
        first, sinks, scaled, key_values, before, w_out
    )
    far = swapped(near, "tp")
    normed, sent, kept = norm(side, residual_in, near, far, norm_gain, half)

    def exchanged(block):
        block = block.reshape(group, rows // group, model_width)
        groups = [list(range(group)), list(range(group, seq_count))]
        block = lax.all_to_all(
            block, "seq", split_axis=0, concat_axis=0, axis_index_groups=groups, tiled=True
        )
        return block.reshape(rows, model_width)

    notes = jnp.concatenate([expert_ids.T.astype(jnp.float32), route_weights.T], axis=0)
    crossed = swapped_halves(sent, "seq")
    notes_peer = swapped_halves(notes, "seq")
    packed, placed = packed_rows(base, side, notes, (normed,), experts, side_rows, rows)
    crossed, notes_peer, packed = lax.optimization_barrier((crossed, notes_peer, packed))
    packed_peer, placed_peer = packed_rows(
        base, side, notes_peer, (crossed, swapped(crossed, "tp")), experts, side_rows, rows
    )
    arrived_peer = exchanged(packed_peer)
    arrived_peer, packed, *others = lax.optimization_barrier((arrived_peer, packed, *others))
    arrived = exchanged(packed)
    result_peer = expert_layer(arrived_peer, weights, others)
    result_peer, arrived = lax.optimization_barrier((result_peer, arrived))
    result = expert_layer(arrived, weights, others)

    returned_peer = exchanged(result_peer)
    result, returned_peer = lax.optimization_barrier((result, returned_peer))
    returned = exchanged(result)
    mine_peer, sent_peer = combine(side, placed_peer, notes_peer, returned_peer, half)
    summed_peer = (mine_peer + swapped(sent_peer, "tp").astype(jnp.float32)).astype(jnp.bfloat16)
    back = swapped_halves(summed_peer, "seq")
    mine, sent = combine(side, placed, notes, returned, half, (kept,))
    sent, back = lax.optimization_barrier((sent, back))
    return (mine + swapped(sent, "tp").astype(jnp.float32) + back.astype(jnp.float32)).astype(jnp.bfloat16)


def solution(mesh):
    placed = (
        P("seq", None),
        P("seq", "tp"),
        P("seq", "tp"),
        P("seq", "tp"),
        P("tp"),
        P("tp", None),
        P(),
        P("seq", None),
        P("seq", None),
        P("seq", None, "tp"),
        P("seq", None, "tp"),
        P("seq", "tp", None),
    )
    return jax.shard_map(
        local, mesh=mesh, in_specs=placed, out_specs=P("seq", "tp"), check_vma=False
    )
```

```python
import functools

import jax
import jax.numpy as jnp
from jax import lax
from jax.experimental import pallas as pl
from jax.experimental.pallas import tpu as pltpu
from jax.sharding import PartitionSpec as P

HEAD_SIZE = 64
WINDOW_LENGTH = 128
LANES = 128
MIB = 1024 * 1024
CUTS = 3
DEEP = 256
AHEAD = 3

neg_large = -1e30
epsilon = 1e-05

VMEM = pl.BlockSpec(memory_space=pltpu.VMEM)
SMEM = pl.BlockSpec(memory_space=pltpu.SMEM)
HBM = pl.BlockSpec(memory_space=pltpu.HBM)


def passed_along(block, axis, distance):
    devices = range(lax.axis_size(axis))
    route = [(i - distance, i) for i in devices if i - distance in devices]
    return lax.ppermute(block, axis, route)


def swapped(block, axis):
    count = lax.axis_size(axis)
    return lax.ppermute(block, axis, [(i, count - 1 - i) for i in range(count)])


def swapped_halves(block, axis):
    count = lax.axis_size(axis)
    return lax.ppermute(block, axis, [(i, (i + count // 2) % count) for i in range(count)])


def shape_of(dims, dtype=jnp.bfloat16):
    return jax.ShapeDtypeStruct(dims, dtype)


def cost(flops, moved, transcendentals=0):
    return pl.CostEstimate(flops=flops, bytes_accessed=moved, transcendentals=transcendentals)


def iota(dims, dimension):
    return lax.broadcasted_iota(jnp.int32, dims, dimension)


def rows_of(ids, experts, side_rows, base, side):
    top_count, tokens = ids.shape
    names = iota((experts, tokens), 0).astype(jnp.float32)
    hits = [ids[c : c + 1, :] == names for c in range(top_count)]
    named = sum([hit.astype(jnp.float32) for hit in hits]).astype(jnp.bfloat16)
    square = (tokens, tokens)
    earlier = (iota(square, 0) < iota(square, 1)).astype(jnp.bfloat16)
    slot = jnp.dot(named, earlier, preferred_element_type=jnp.float32) - (side * side_rows).astype(jnp.float32)
    expert = names - base.astype(jnp.float32)
    here = (slot >= 0.0) & (slot < side_rows) & (expert >= 0.0) & (expert < experts // 2)
    rows = jnp.where(here, expert * side_rows + slot, -1.0)
    lines = [jnp.sum(jnp.where(hit, rows, 0.0), axis=0, keepdims=True) for hit in hits]
    return jnp.concatenate(lines, axis=0).astype(jnp.int32)


def attention_kernel(
    first_ref, sink_ref, q_ref, kv_ref, before_ref, w_hbm, out_ref, w_ref, att_ref, sum_ref, sem
):
    tokens, width = q_ref.shape
    kv_heads = kv_ref.shape[1] // (2 * HEAD_SIZE)
    pairs = width // LANES // kv_heads
    w_load = pltpu.make_async_copy(w_hbm, w_ref, sem)
    w_load.start()
    low = iota((tokens, LANES), 1) < HEAD_SIZE

    def doubled(block, head):
        wide = block.astype(jnp.float32)
        turned = pltpu.roll(wide, HEAD_SIZE, 1)
        first, second = (wide, turned) if head == 0 else (turned, wide)
        return [
            jnp.where(low, first, 0.0).astype(jnp.bfloat16),
            jnp.where(low, 0.0, second).astype(jnp.bfloat16),
        ]

    own = iota((tokens, tokens), 1) <= iota((tokens, tokens), 0)
    bias = jnp.where(own, 0.0, jnp.where(first_ref[0] == 0, 0.0, neg_large))
    own_factor = jnp.where(own, 1.0, 0.0).astype(jnp.bfloat16)
    before_factor = jnp.where(own, 0.0, 1.0).astype(jnp.bfloat16)
    head_lanes = jnp.where(low, 1.0, 0.0).astype(jnp.bfloat16), jnp.where(low, 0.0, 1.0).astype(jnp.bfloat16)
    ones = jnp.concatenate(head_lanes, axis=0)
    keys_before = [jnp.concatenate(doubled(before_ref[:, :LANES], head), axis=0) for head in range(kv_heads)]
    values_before = [doubled(before_ref[:, LANES:], head) for head in range(kv_heads)]
    contract = (((1,), (1,)), ((), ()))
    for head in range(kv_heads):
        keys = jnp.concatenate(doubled(kv_ref[:, :LANES], head), axis=0)
        values = jnp.concatenate(doubled(kv_ref[:, LANES:], head) + values_before[head], axis=0)
        for j in range(head * pairs, (head + 1) * pairs):
            q = q_ref[:, j * LANES : (j + 1) * LANES]
            near = lax.dot_general(q, keys, contract, preferred_element_type=jnp.float32)
            far = lax.dot_general(q, keys_before[head], contract, preferred_element_type=jnp.float32)
            terms, sinks = [], []
            for at in range(2):
                span = slice(at * tokens, (at + 1) * tokens)
                part = jnp.where(own, near[:, span], far[:, span]) + bias
                sink = sink_ref[2 * j + at : 2 * j + at + 1, :]
                top = jnp.maximum(jnp.max(part, axis=1, keepdims=True), sink)
                terms.append(jnp.exp(part - top).astype(jnp.bfloat16))
                sinks.append(jnp.exp(sink - top))
            total = jnp.dot(jnp.concatenate(terms, axis=1), ones, preferred_element_type=jnp.float32)
            total += jnp.where(low, sinks[0], sinks[1])
            kept = [term * own_factor for term in terms] + [term * before_factor for term in terms]
            found = jnp.dot(jnp.concatenate(kept, axis=1), values, preferred_element_type=jnp.float32)
            att_ref[:, j * LANES : (j + 1) * LANES] = (found / total).astype(jnp.bfloat16)
        if head == 0:
            w_load.wait()
        depth = pairs * LANES
        step = 2 * LANES
        for at in range(0, out_ref.shape[1], step):
            part = jnp.dot(
                att_ref[:, head * depth : (head + 1) * depth],
                w_ref[head * depth : (head + 1) * depth, at : at + step],
                preferred_element_type=jnp.float32,
            )
            if head > 0:
                part += sum_ref[:, at : at + step]
            if head < kv_heads - 1:
                sum_ref[:, at : at + step] = part
            else:
                out_ref[:, at : at + step] = part.astype(jnp.bfloat16)


def attention(first, sinks, q, key_values, before, w_out):
    tokens = q.shape[0]
    return pl.pallas_call(
        attention_kernel,
        out_shape=shape_of((tokens, w_out.shape[1])),
        in_specs=[SMEM, VMEM, VMEM, VMEM, VMEM, HBM],
        out_specs=VMEM,
        scratch_shapes=[
            pltpu.VMEM(w_out.shape, jnp.bfloat16),
            pltpu.VMEM(q.shape, jnp.bfloat16),
            pltpu.VMEM((tokens, w_out.shape[1]), jnp.float32),
            pltpu.SemaphoreType.DMA,
        ],
        compiler_params=pltpu.CompilerParams(vmem_limit_bytes=54_000_000),
        cost_estimate=cost(2 * tokens * w_out.size * 2, 2 * w_out.size, tokens * tokens * q.shape[1] // HEAD_SIZE),
        name="attention",
    )(first, sinks, q, key_values, before, w_out)


def pack(placed, normed, out_ref):
    rows, tokens = out_ref.shape[0], normed.shape[0]
    row = iota((rows, tokens), 0)
    taken = placed[0:1, :] == row
    for c in range(1, placed.shape[0]):
        taken = taken | (placed[c : c + 1, :] == row)
    taken = jnp.where(taken, 1.0, 0.0).astype(jnp.bfloat16)
    out_ref[...] = jnp.dot(taken, normed, preferred_element_type=jnp.float32).astype(jnp.bfloat16)


def norm_kernel(side_ref, residual_ref, near_ref, far_ref, gain_ref, normed_ref, sent_ref, kept_ref, whole_ref):
    side = side_ref[0]
    half_tokens, half = sent_ref.shape[0], kept_ref.shape[1]
    added = near_ref[...].astype(jnp.float32) + far_ref[...].astype(jnp.float32)
    whole = (residual_ref[...].astype(jnp.float32) + added).astype(jnp.bfloat16)
    whole_ref[...] = whole
    wide = whole.astype(jnp.float32)
    mean_square = jnp.mean(wide * wide, axis=1, keepdims=True)
    normed_ref[...] = (wide * lax.rsqrt(mean_square + epsilon) * gain_ref[...]).astype(jnp.bfloat16)
    kept_ref[...] = whole_ref[:, pl.ds(pl.multiple_of(side * half, LANES), half)]
    sent_ref[...] = normed_ref[pl.ds(pl.multiple_of(side * half_tokens, half_tokens), half_tokens), :]


def norm(side, residual_in, near, far, gain, half):
    tokens, width = residual_in.shape
    return pl.pallas_call(
        norm_kernel,
        out_shape=(shape_of((tokens, width)), shape_of((tokens // 2, width)), shape_of((tokens, half))),
        in_specs=[SMEM] + [VMEM] * 4,
        out_specs=(VMEM, VMEM, VMEM),
        scratch_shapes=[pltpu.VMEM((tokens, width), jnp.bfloat16)],
        compiler_params=pltpu.CompilerParams(vmem_limit_bytes=24 * MIB),
        cost_estimate=cost(8 * tokens * width, 10 * tokens * width),
        name="norm",
    )(side, residual_in, near, far, gain.reshape(1, width))


def pack_kernel(experts, side_rows, base_ref, side_ref, notes_ref, *refs):
    *part_refs, out_ref, rows_ref, arrived_ref = refs
    side, top_count = side_ref[0], rows_ref.shape[0]
    if len(part_refs) == 1:
        arrived_ref = part_refs[0]
    else:
        mine_ref, other_ref = part_refs
        part = mine_ref.shape[0]
        arrived_ref[pl.ds(pl.multiple_of(side * part, part), part), :] = mine_ref[...]
        arrived_ref[pl.ds(pl.multiple_of((1 - side) * part, part), part), :] = other_ref[...]
    rows = rows_of(notes_ref[:top_count, :], experts, side_rows, base_ref[0], side)
    rows_ref[...] = rows
    pack(rows, arrived_ref[...], out_ref)


def packed_rows(base, side, notes, parts, experts, side_rows, rows):
    tokens = sum([part.shape[0] for part in parts])
    width = parts[0].shape[1]
    return pl.pallas_call(
        functools.partial(pack_kernel, experts, side_rows),
        out_shape=(shape_of((rows, width)), shape_of((notes.shape[0] // 2, tokens), jnp.int32)),
        in_specs=[SMEM, SMEM, VMEM] + [VMEM] * len(parts),
        out_specs=(VMEM, VMEM),
        scratch_shapes=[pltpu.VMEM((tokens, width), jnp.bfloat16)],
        compiler_params=pltpu.CompilerParams(vmem_limit_bytes=24 * MIB),
        cost_estimate=cost(2 * rows * tokens * width, 2 * rows * width),
        name="packed_rows",
    )(base, side, notes, *parts)


def expert_kernel(
    x_hbm, gate_hbm, up_hbm, down_hbm, gate_too_hbm, up_too_hbm, down_too_hbm, y_hbm, x_ref, y_ref, gate_ref, up_ref,
    down_ref, hidden_ref, gate_sum, up_sum, total_ref, x_sem, y_sem, gate_sem, up_sem, down_sem,
):
    rows, width = x_ref.shape
    share = gate_hbm.shape[2]
    deep, cuts = width // CUTS, share // DEEP
    loads = []
    for k, (gate, up) in enumerate([(gate_hbm, up_hbm), (gate_too_hbm, up_too_hbm)]):
        for c in range(CUTS):
            span = pl.ds(c * deep, deep)
            loads.append(
                [
                    pltpu.make_async_copy(gate.at[0, span], gate_ref.at[k, span], gate_sem.at[k, c]),
                    pltpu.make_async_copy(up.at[0, span], up_ref.at[k, span], up_sem.at[k, c]),
                ]
            )
    for k, down in enumerate([down_hbm, down_too_hbm]):
        for c in range(cuts):
            source, target = pl.ds(c * DEEP, DEEP), pl.ds(k * share + c * DEEP, DEEP)
            loads.append([pltpu.make_async_copy(down.at[0, source], down_ref.at[target], down_sem.at[k, c])])

    def start(number):
        if number < len(loads):
            for load in loads[number]:
                load.start()

    def arrive(number):
        for load in loads[number]:
            load.wait()
        start(number + AHEAD)

    x_load = pltpu.make_async_copy(x_hbm, x_ref, x_sem)
    x_load.start()
    for number in range(AHEAD):
        start(number)
    x_load.wait()
    for k in range(2):
        for c in range(CUTS):
            arrive(k * CUTS + c)
            span = slice(c * deep, (c + 1) * deep)
            x = x_ref[:, span]
            gate = jnp.dot(x, gate_ref[k, span, :], preferred_element_type=jnp.float32)
            up = jnp.dot(x, up_ref[k, span, :], preferred_element_type=jnp.float32)
            if c > 0:
                gate, up = gate_sum[...] + gate, up_sum[...] + up
            if c < CUTS - 1:
                gate_sum[...], up_sum[...] = gate, up
            else:
                hidden = gate * (0.5 + 0.5 * jnp.tanh(0.5 * gate)) * up
                hidden_ref[:, k * share : (k + 1) * share] = hidden.astype(jnp.bfloat16)
    for c in range(2 * cuts - 1):
        arrive(2 * CUTS + c)
        span = slice(c * DEEP, (c + 1) * DEEP)
        part = jnp.dot(hidden_ref[:, span], down_ref[span, :], preferred_element_type=jnp.float32)
        total_ref[...] = part if c == 0 else total_ref[...] + part
    arrive(2 * CUTS + 2 * cuts - 1)
    span = slice((2 * cuts - 1) * DEEP, 2 * cuts * DEEP)
    step = 2 * LANES
    stores = []
    for i in range(width // step):
        columns = slice(i * step, (i + 1) * step)
        part = jnp.dot(hidden_ref[:, span], down_ref[span, columns], preferred_element_type=jnp.float32)
        y_ref[:, columns] = (total_ref[:, columns] + part).astype(jnp.bfloat16)
        column_span = pl.ds(i * step, step)
        stores.append(pltpu.make_async_copy(y_ref.at[:, column_span], y_hbm.at[:, column_span], y_sem.at[i]))
        stores[i].start()
    for store in stores:
        store.wait()


def expert_layer(x, mine, others):
    rows, width = x.shape
    share = mine[0].shape[2]
    return pl.pallas_call(
        expert_kernel,
        out_shape=shape_of((rows, width)),
        in_specs=[HBM] * 7,
        out_specs=HBM,
        scratch_shapes=[
            pltpu.VMEM((rows, width), jnp.bfloat16),
            pltpu.VMEM((rows, width), jnp.bfloat16),
            pltpu.VMEM((2, width, share), jnp.bfloat16),
            pltpu.VMEM((2, width, share), jnp.bfloat16),
            pltpu.VMEM((2 * share, width), jnp.bfloat16),
            pltpu.VMEM((rows, 2 * share), jnp.bfloat16),
            pltpu.VMEM((rows, share), jnp.float32),
            pltpu.VMEM((rows, share), jnp.float32),
            pltpu.VMEM((rows, width), jnp.float32),
            pltpu.SemaphoreType.DMA,
            pltpu.SemaphoreType.DMA((width // (2 * LANES),)),
            pltpu.SemaphoreType.DMA((2, CUTS)),
            pltpu.SemaphoreType.DMA((2, CUTS)),
            pltpu.SemaphoreType.DMA((2, share // DEEP)),
        ],
        compiler_params=pltpu.CompilerParams(vmem_limit_bytes=60 * MIB),
        cost_estimate=cost(12 * rows * width * share, 12 * width * share, 2 * rows * share),
        name="expert_layer",
    )(x, *mine, *others)


def combine_kernel(side_ref, rows_ref, weights_ref, y_ref, *refs):
    *more_refs, mine_ref, sent_ref, total_ref = refs
    top_count, tokens = rows_ref.shape
    half = mine_ref.shape[1]
    row = iota((y_ref.shape[0], tokens), 0)
    share = jnp.zeros(row.shape, jnp.float32)
    for c in range(top_count):
        share = jnp.where(rows_ref[c : c + 1, :] == row, weights_ref[top_count + c : top_count + c + 1, :], share)
    coarse = share.astype(jnp.bfloat16)
    fine = (share - coarse.astype(jnp.float32)).astype(jnp.bfloat16)
    y = y_ref[...]
    contract = (((0,), (0,)), ((), ()))
    total_ref[...] = lax.dot_general(coarse, y, contract, preferred_element_type=jnp.float32)
    total_ref[...] += lax.dot_general(fine, y, contract, preferred_element_type=jnp.float32)
    side = side_ref[0]
    mine = total_ref[:, pl.ds(pl.multiple_of(side * half, LANES), half)]
    for more_ref in more_refs:
        mine += more_ref[...].astype(jnp.float32)
    mine_ref[...] = mine
    sent_ref[...] = total_ref[:, pl.ds(pl.multiple_of((1 - side) * half, LANES), half)].astype(jnp.bfloat16)


def combine(side, placed, weights, y, half, more=()):
    tokens = placed.shape[1]
    rows, width = y.shape
    return pl.pallas_call(
        combine_kernel,
        out_shape=(shape_of((tokens, half), jnp.float32), shape_of((tokens, half))),
        in_specs=[SMEM] + [VMEM] * (3 + len(more)),
        out_specs=(VMEM, VMEM),
        scratch_shapes=[pltpu.VMEM((tokens, width), jnp.float32)],
        compiler_params=pltpu.CompilerParams(vmem_limit_bytes=24 * MIB),
        cost_estimate=cost(4 * rows * tokens * width, 2 * rows * width),
        name="combine",
    )(side, placed, weights, y, *more)


def local(
    residual_in,
    query_rows,
    rotated_key_rows,
    value_row_matrix,
    learned_sink_scores,
    w_out,
    norm_gain,
    expert_ids,
    route_weights,
    w_gate,
    w_up,
    w_down,
):
    tok_dev, model_width = residual_in.shape
    seq_count = lax.axis_size("seq")
    experts = w_gate.shape[0] * seq_count
    capacity = max(2, 8 * tok_dev // experts)
    sides = lax.axis_size("tp")
    side_rows = capacity // sides
    group = seq_count // 2
    rows = experts // 2 * side_rows
    half = model_width // sides
    at_seq = lax.axis_index("seq").astype(jnp.int32)
    base = jnp.where(at_seq < group, 0, experts // 2).astype(jnp.int32).reshape(1)
    side = lax.axis_index("tp").astype(jnp.int32).reshape(1)
    first = (at_seq == 0).astype(jnp.int32).reshape(1)
    key_values = lax.optimization_barrier(jnp.concatenate([rotated_key_rows, value_row_matrix], axis=1))
    before = passed_along(key_values, "seq", 1)
    sinks = jnp.broadcast_to(learned_sink_scores[:, None], (learned_sink_scores.shape[0], LANES))
    sinks, queries = lax.optimization_barrier((sinks, query_rows))
    scaled = queries * jnp.bfloat16(HEAD_SIZE**-0.5)
    weights = (w_gate, w_up, w_down)
    others = [swapped(weight, "tp") for weight in weights[:2]]
    near = attention(
        first, sinks, scaled, key_values, before, w_out
    )
    far = swapped(near, "tp")
    normed, sent, kept = norm(side, residual_in, near, far, norm_gain, half)

    def exchanged(block):
        block = block.reshape(group, rows // group, model_width)
        groups = [list(range(group)), list(range(group, seq_count))]
        block = lax.all_to_all(
            block, "seq", split_axis=0, concat_axis=0, axis_index_groups=groups, tiled=True
        )
        return block.reshape(rows, model_width)

    notes = jnp.concatenate([expert_ids.T.astype(jnp.float32), route_weights.T], axis=0)
    crossed = swapped_halves(sent, "seq")
    notes_peer = swapped_halves(notes, "seq")
    packed, placed = packed_rows(base, side, notes, (normed,), experts, side_rows, rows)
    packed, late = lax.optimization_barrier((packed, w_down))
    others.append(swapped(late, "tp"))
    crossed, notes_peer, packed = lax.optimization_barrier((crossed, notes_peer, packed))
    packed_peer, placed_peer = packed_rows(
        base, side, notes_peer, (crossed, swapped(crossed, "tp")), experts, side_rows, rows
    )
    arrived_peer = exchanged(packed_peer)
    arrived_peer, packed, *others = lax.optimization_barrier((arrived_peer, packed, *others))
    arrived = exchanged(packed)
    result_peer = expert_layer(arrived_peer, weights, others)
    result_peer, arrived = lax.optimization_barrier((result_peer, arrived))
    result = expert_layer(arrived, weights, others)

    returned_peer = exchanged(result_peer)
    result, returned_peer = lax.optimization_barrier((result, returned_peer))
    returned = exchanged(result)
    mine_peer, sent_peer = combine(side, placed_peer, notes_peer, returned_peer, half)
    summed_peer = (mine_peer + swapped(sent_peer, "tp").astype(jnp.float32)).astype(jnp.bfloat16)
    back = swapped_halves(summed_peer, "seq")
    mine, sent = combine(side, placed, notes, returned, half, (kept,))
    sent, back = lax.optimization_barrier((sent, back))
    return (mine + swapped(sent, "tp").astype(jnp.float32) + back.astype(jnp.float32)).astype(jnp.bfloat16)


def solution(mesh):
    placed = (
        P("seq", None),
        P("seq", "tp"),
        P("seq", "tp"),
        P("seq", "tp"),
        P("tp"),
        P("tp", None),
        P(),
        P("seq", None),
        P("seq", None),
        P("seq", None, "tp"),
        P("seq", None, "tp"),
        P("seq", "tp", None),
    )
    return jax.shard_map(
        local, mesh=mesh, in_specs=placed, out_specs=P("seq", "tp"), check_vma=False
    )
```

```python
import functools

import jax
import jax.numpy as jnp
from jax import lax
from jax.experimental import pallas as pl
from jax.experimental.pallas import tpu as pltpu
from jax.sharding import PartitionSpec as P

HEAD_SIZE = 64
WINDOW_LENGTH = 128
LANES = 128
MIB = 1024 * 1024
CUTS = 3
DEEP = 256
AHEAD = 3

neg_large = -1e30
epsilon = 1e-05

VMEM = pl.BlockSpec(memory_space=pltpu.VMEM)
SMEM = pl.BlockSpec(memory_space=pltpu.SMEM)
HBM = pl.BlockSpec(memory_space=pltpu.HBM)


def passed_along(block, axis, distance):
    devices = range(lax.axis_size(axis))
    route = [(i - distance, i) for i in devices if i - distance in devices]
    return lax.ppermute(block, axis, route)


def swapped(block, axis):
    count = lax.axis_size(axis)
    return lax.ppermute(block, axis, [(i, count - 1 - i) for i in range(count)])


def swapped_halves(block, axis):
    count = lax.axis_size(axis)
    return lax.ppermute(block, axis, [(i, (i + count // 2) % count) for i in range(count)])


def shape_of(dims, dtype=jnp.bfloat16):
    return jax.ShapeDtypeStruct(dims, dtype)


def cost(flops, moved, transcendentals=0):
    return pl.CostEstimate(flops=flops, bytes_accessed=moved, transcendentals=transcendentals)


def iota(dims, dimension):
    return lax.broadcasted_iota(jnp.int32, dims, dimension)


def rows_of(ids, experts, side_rows, base, side):
    top_count, tokens = ids.shape
    names = iota((experts, tokens), 0).astype(jnp.float32)
    hits = [ids[c : c + 1, :] == names for c in range(top_count)]
    named = sum([hit.astype(jnp.float32) for hit in hits]).astype(jnp.bfloat16)
    square = (tokens, tokens)
    earlier = (iota(square, 0) < iota(square, 1)).astype(jnp.bfloat16)
    slot = jnp.dot(named, earlier, preferred_element_type=jnp.float32) - (side * side_rows).astype(jnp.float32)
    expert = names - base.astype(jnp.float32)
    here = (slot >= 0.0) & (slot < side_rows) & (expert >= 0.0) & (expert < experts // 2)
    rows = jnp.where(here, expert * side_rows + slot, -1.0)
    lines = [jnp.sum(jnp.where(hit, rows, 0.0), axis=0, keepdims=True) for hit in hits]
    return jnp.concatenate(lines, axis=0).astype(jnp.int32)


def attention_kernel(
    first_ref, sink_ref, q_ref, kv_ref, before_ref, w_hbm, out_ref, w_ref, att_ref, sum_ref, sem
):
    tokens, width = q_ref.shape
    kv_heads = kv_ref.shape[1] // (2 * HEAD_SIZE)
    pairs = width // LANES // kv_heads
    w_load = pltpu.make_async_copy(w_hbm, w_ref, sem)
    w_load.start()
    low = iota((tokens, LANES), 1) < HEAD_SIZE

    def doubled(block, head):
        wide = block.astype(jnp.float32)
        turned = pltpu.roll(wide, HEAD_SIZE, 1)
        first, second = (wide, turned) if head == 0 else (turned, wide)
        return [
            jnp.where(low, first, 0.0).astype(jnp.bfloat16),
            jnp.where(low, 0.0, second).astype(jnp.bfloat16),
        ]

    own = iota((tokens, tokens), 1) <= iota((tokens, tokens), 0)
    bias = jnp.where(own, 0.0, jnp.where(first_ref[0] == 0, 0.0, neg_large))
    own_factor = jnp.where(own, 1.0, 0.0).astype(jnp.bfloat16)
    before_factor = jnp.where(own, 0.0, 1.0).astype(jnp.bfloat16)
    head_lanes = jnp.where(low, 1.0, 0.0).astype(jnp.bfloat16), jnp.where(low, 0.0, 1.0).astype(jnp.bfloat16)
    ones = jnp.concatenate(head_lanes, axis=0)
    keys_before = [jnp.concatenate(doubled(before_ref[:, :LANES], head), axis=0) for head in range(kv_heads)]
    values_before = [doubled(before_ref[:, LANES:], head) for head in range(kv_heads)]
    contract = (((1,), (1,)), ((), ()))
    for head in range(kv_heads):
        keys = jnp.concatenate(doubled(kv_ref[:, :LANES], head), axis=0)
        values = jnp.concatenate(doubled(kv_ref[:, LANES:], head) + values_before[head], axis=0)
        for j in range(head * pairs, (head + 1) * pairs):
            q = q_ref[:, j * LANES : (j + 1) * LANES]
            near = lax.dot_general(q, keys, contract, preferred_element_type=jnp.float32)
            far = lax.dot_general(q, keys_before[head], contract, preferred_element_type=jnp.float32)
            terms, sinks = [], []
            for at in range(2):
                span = slice(at * tokens, (at + 1) * tokens)
                part = jnp.where(own, near[:, span], far[:, span]) + bias
                sink = sink_ref[2 * j + at : 2 * j + at + 1, :]
                top = jnp.maximum(jnp.max(part, axis=1, keepdims=True), sink)
                terms.append(jnp.exp(part - top).astype(jnp.bfloat16))
                sinks.append(jnp.exp(sink - top))
            total = jnp.dot(jnp.concatenate(terms, axis=1), ones, preferred_element_type=jnp.float32)
            total += jnp.where(low, sinks[0], sinks[1])
            kept = [term * own_factor for term in terms] + [term * before_factor for term in terms]
            found = jnp.dot(jnp.concatenate(kept, axis=1), values, preferred_element_type=jnp.float32)
            att_ref[:, j * LANES : (j + 1) * LANES] = (found / total).astype(jnp.bfloat16)
        if head == 0:
            w_load.wait()
        depth = pairs * LANES
        step = 2 * LANES
        for at in range(0, out_ref.shape[1], step):
            part = jnp.dot(
                att_ref[:, head * depth : (head + 1) * depth],
                w_ref[head * depth : (head + 1) * depth, at : at + step],
                preferred_element_type=jnp.float32,
            )
            if head > 0:
                part += sum_ref[:, at : at + step]
            if head < kv_heads - 1:
                sum_ref[:, at : at + step] = part
            else:
                out_ref[:, at : at + step] = part.astype(jnp.bfloat16)


def attention(first, sinks, q, key_values, before, w_out):
    tokens = q.shape[0]
    return pl.pallas_call(
        attention_kernel,
        out_shape=shape_of((tokens, w_out.shape[1])),
        in_specs=[SMEM, VMEM, VMEM, VMEM, VMEM, HBM],
        out_specs=VMEM,
        scratch_shapes=[
            pltpu.VMEM(w_out.shape, jnp.bfloat16),
            pltpu.VMEM(q.shape, jnp.bfloat16),
            pltpu.VMEM((tokens, w_out.shape[1]), jnp.float32),
            pltpu.SemaphoreType.DMA,
        ],
        compiler_params=pltpu.CompilerParams(vmem_limit_bytes=54_000_000),
        cost_estimate=cost(2 * tokens * w_out.size * 2, 2 * w_out.size, tokens * tokens * q.shape[1] // HEAD_SIZE),
        name="attention",
    )(first, sinks, q, key_values, before, w_out)


def pack(placed, normed, out_ref):
    rows, tokens = out_ref.shape[0], normed.shape[0]
    row = iota((rows, tokens), 0)
    taken = placed[0:1, :] == row
    for c in range(1, placed.shape[0]):
        taken = taken | (placed[c : c + 1, :] == row)
    taken = jnp.where(taken, 1.0, 0.0).astype(jnp.bfloat16)
    out_ref[...] = jnp.dot(taken, normed, preferred_element_type=jnp.float32).astype(jnp.bfloat16)


def norm_kernel(side_ref, residual_ref, near_ref, far_ref, gain_ref, normed_ref, sent_ref, kept_ref, whole_ref):
    side = side_ref[0]
    half_tokens, half = sent_ref.shape[0], kept_ref.shape[1]
    added = near_ref[...].astype(jnp.float32) + far_ref[...].astype(jnp.float32)
    whole = (residual_ref[...].astype(jnp.float32) + added).astype(jnp.bfloat16)
    whole_ref[...] = whole
    wide = whole.astype(jnp.float32)
    mean_square = jnp.mean(wide * wide, axis=1, keepdims=True)
    normed_ref[...] = (wide * lax.rsqrt(mean_square + epsilon) * gain_ref[...]).astype(jnp.bfloat16)
    kept_ref[...] = whole_ref[:, pl.ds(pl.multiple_of(side * half, LANES), half)]
    sent_ref[...] = normed_ref[pl.ds(pl.multiple_of(side * half_tokens, half_tokens), half_tokens), :]


def norm(side, residual_in, near, far, gain, half):
    tokens, width = residual_in.shape
    return pl.pallas_call(
        norm_kernel,
        out_shape=(shape_of((tokens, width)), shape_of((tokens // 2, width)), shape_of((tokens, half))),
        in_specs=[SMEM] + [VMEM] * 4,
        out_specs=(VMEM, VMEM, VMEM),
        scratch_shapes=[pltpu.VMEM((tokens, width), jnp.bfloat16)],
        compiler_params=pltpu.CompilerParams(vmem_limit_bytes=24 * MIB),
        cost_estimate=cost(8 * tokens * width, 10 * tokens * width),
        name="norm",
    )(side, residual_in, near, far, gain.reshape(1, width))


def pack_kernel(experts, side_rows, base_ref, side_ref, notes_ref, *refs):
    *part_refs, out_ref, rows_ref, arrived_ref = refs
    side, top_count = side_ref[0], rows_ref.shape[0]
    if len(part_refs) == 1:
        arrived_ref = part_refs[0]
    else:
        mine_ref, other_ref = part_refs
        part = mine_ref.shape[0]
        arrived_ref[pl.ds(pl.multiple_of(side * part, part), part), :] = mine_ref[...]
        arrived_ref[pl.ds(pl.multiple_of((1 - side) * part, part), part), :] = other_ref[...]
    rows = rows_of(notes_ref[:top_count, :], experts, side_rows, base_ref[0], side)
    rows_ref[...] = rows
    pack(rows, arrived_ref[...], out_ref)


def packed_rows(base, side, notes, parts, experts, side_rows, rows):
    tokens = sum([part.shape[0] for part in parts])
    width = parts[0].shape[1]
    return pl.pallas_call(
        functools.partial(pack_kernel, experts, side_rows),
        out_shape=(shape_of((rows, width)), shape_of((notes.shape[0] // 2, tokens), jnp.int32)),
        in_specs=[SMEM, SMEM, VMEM] + [VMEM] * len(parts),
        out_specs=(VMEM, VMEM),
        scratch_shapes=[pltpu.VMEM((tokens, width), jnp.bfloat16)],
        compiler_params=pltpu.CompilerParams(vmem_limit_bytes=24 * MIB),
        cost_estimate=cost(2 * rows * tokens * width, 2 * rows * width),
        name="packed_rows",
    )(base, side, notes, *parts)


def expert_kernel(
    x_hbm, gate_hbm, up_hbm, down_hbm, gate_too_hbm, up_too_hbm, down_too_hbm, y_hbm, x_ref, y_ref, gate_ref, up_ref,
    down_ref, hidden_ref, gate_sum, up_sum, total_ref, x_sem, y_sem, gate_sem, up_sem, down_sem,
):
    rows, width = x_ref.shape
    share = gate_hbm.shape[2]
    deep, cuts = width // CUTS, share // DEEP
    loads = []
    for k, (gate, up) in enumerate([(gate_hbm, up_hbm), (gate_too_hbm, up_too_hbm)]):
        for c in range(CUTS):
            span = pl.ds(c * deep, deep)
            loads.append(
                [
                    pltpu.make_async_copy(gate.at[0, span], gate_ref.at[k, span], gate_sem.at[k, c]),
                    pltpu.make_async_copy(up.at[0, span], up_ref.at[k, span], up_sem.at[k, c]),
                ]
            )
    for k, down in enumerate([down_hbm, down_too_hbm]):
        for c in range(cuts):
            source, target = pl.ds(c * DEEP, DEEP), pl.ds(k * share + c * DEEP, DEEP)
            loads.append([pltpu.make_async_copy(down.at[0, source], down_ref.at[target], down_sem.at[k, c])])

    def start(number):
        if number < len(loads):
            for load in loads[number]:
                load.start()

    def arrive(number):
        for load in loads[number]:
            load.wait()
        start(number + AHEAD)

    x_load = pltpu.make_async_copy(x_hbm, x_ref, x_sem)
    x_load.start()
    for number in range(AHEAD):
        start(number)
    x_load.wait()
    for k in range(2):
        for c in range(CUTS):
            arrive(k * CUTS + c)
            span = slice(c * deep, (c + 1) * deep)
            x = x_ref[:, span]
            gate = jnp.dot(x, gate_ref[k, span, :], preferred_element_type=jnp.float32)
            up = jnp.dot(x, up_ref[k, span, :], preferred_element_type=jnp.float32)
            if c > 0:
                gate, up = gate_sum[...] + gate, up_sum[...] + up
            if c < CUTS - 1:
                gate_sum[...], up_sum[...] = gate, up
            else:
                hidden = gate * (0.5 + 0.5 * jnp.tanh(0.5 * gate)) * up
                hidden_ref[:, k * share : (k + 1) * share] = hidden.astype(jnp.bfloat16)
    for c in range(2 * cuts - 1):
        arrive(2 * CUTS + c)
        span = slice(c * DEEP, (c + 1) * DEEP)
        part = jnp.dot(hidden_ref[:, span], down_ref[span, :], preferred_element_type=jnp.float32)
        total_ref[...] = part if c == 0 else total_ref[...] + part
    arrive(2 * CUTS + 2 * cuts - 1)
    span = slice((2 * cuts - 1) * DEEP, 2 * cuts * DEEP)
    step = 2 * LANES
    stores = []
    for i in range(width // step):
        columns = slice(i * step, (i + 1) * step)
        part = jnp.dot(hidden_ref[:, span], down_ref[span, columns], preferred_element_type=jnp.float32)
        y_ref[:, columns] = (total_ref[:, columns] + part).astype(jnp.bfloat16)
        column_span = pl.ds(i * step, step)
        stores.append(pltpu.make_async_copy(y_ref.at[:, column_span], y_hbm.at[:, column_span], y_sem.at[i]))
        stores[i].start()
    for store in stores:
        store.wait()


def expert_layer(x, mine, others):
    rows, width = x.shape
    share = mine[0].shape[2]
    return pl.pallas_call(
        expert_kernel,
        out_shape=shape_of((rows, width)),
        in_specs=[HBM] * 7,
        out_specs=HBM,
        scratch_shapes=[
            pltpu.VMEM((rows, width), jnp.bfloat16),
            pltpu.VMEM((rows, width), jnp.bfloat16),
            pltpu.VMEM((2, width, share), jnp.bfloat16),
            pltpu.VMEM((2, width, share), jnp.bfloat16),
            pltpu.VMEM((2 * share, width), jnp.bfloat16),
            pltpu.VMEM((rows, 2 * share), jnp.bfloat16),
            pltpu.VMEM((rows, share), jnp.float32),
            pltpu.VMEM((rows, share), jnp.float32),
            pltpu.VMEM((rows, width), jnp.float32),
            pltpu.SemaphoreType.DMA,
            pltpu.SemaphoreType.DMA((width // (2 * LANES),)),
            pltpu.SemaphoreType.DMA((2, CUTS)),
            pltpu.SemaphoreType.DMA((2, CUTS)),
            pltpu.SemaphoreType.DMA((2, share // DEEP)),
        ],
        compiler_params=pltpu.CompilerParams(vmem_limit_bytes=60 * MIB),
        cost_estimate=cost(12 * rows * width * share, 12 * width * share, 2 * rows * share),
        name="expert_layer",
    )(x, *mine, *others)


def combine_kernel(side_ref, rows_ref, weights_ref, y_ref, *refs):
    *more_refs, mine_ref, sent_ref, total_ref = refs
    top_count, tokens = rows_ref.shape
    half = mine_ref.shape[1]
    row = iota((y_ref.shape[0], tokens), 0)
    share = jnp.zeros(row.shape, jnp.float32)
    for c in range(top_count):
        share = jnp.where(rows_ref[c : c + 1, :] == row, weights_ref[top_count + c : top_count + c + 1, :], share)
    coarse = share.astype(jnp.bfloat16)
    fine = (share - coarse.astype(jnp.float32)).astype(jnp.bfloat16)
    y = y_ref[...]
    contract = (((0,), (0,)), ((), ()))
    total_ref[...] = lax.dot_general(coarse, y, contract, preferred_element_type=jnp.float32)
    total_ref[...] += lax.dot_general(fine, y, contract, preferred_element_type=jnp.float32)
    side = side_ref[0]
    mine = total_ref[:, pl.ds(pl.multiple_of(side * half, LANES), half)]
    for more_ref in more_refs:
        mine += more_ref[...].astype(jnp.float32)
    mine_ref[...] = mine
    sent_ref[...] = total_ref[:, pl.ds(pl.multiple_of((1 - side) * half, LANES), half)].astype(jnp.bfloat16)


def combine(side, placed, weights, y, half, more=()):
    tokens = placed.shape[1]
    rows, width = y.shape
    return pl.pallas_call(
        combine_kernel,
        out_shape=(shape_of((tokens, half), jnp.float32), shape_of((tokens, half))),
        in_specs=[SMEM] + [VMEM] * (3 + len(more)),
        out_specs=(VMEM, VMEM),
        scratch_shapes=[pltpu.VMEM((tokens, width), jnp.float32)],
        compiler_params=pltpu.CompilerParams(vmem_limit_bytes=24 * MIB),
        cost_estimate=cost(4 * rows * tokens * width, 2 * rows * width),
        name="combine",
    )(side, placed, weights, y, *more)


def local(
    residual_in,
    query_rows,
    rotated_key_rows,
    value_row_matrix,
    learned_sink_scores,
    w_out,
    norm_gain,
    expert_ids,
    route_weights,
    w_gate,
    w_up,
    w_down,
):
    tok_dev, model_width = residual_in.shape
    seq_count = lax.axis_size("seq")
    experts = w_gate.shape[0] * seq_count
    capacity = max(2, 8 * tok_dev // experts)
    sides = lax.axis_size("tp")
    side_rows = capacity // sides
    group = seq_count // 2
    rows = experts // 2 * side_rows
    half = model_width // sides
    at_seq = lax.axis_index("seq").astype(jnp.int32)
    base = jnp.where(at_seq < group, 0, experts // 2).astype(jnp.int32).reshape(1)
    side = lax.axis_index("tp").astype(jnp.int32).reshape(1)
    first = (at_seq == 0).astype(jnp.int32).reshape(1)
    key_values = lax.optimization_barrier(jnp.concatenate([rotated_key_rows, value_row_matrix], axis=1))
    before = passed_along(key_values, "seq", 1)
    sinks = jnp.broadcast_to(learned_sink_scores[:, None], (learned_sink_scores.shape[0], LANES))
    sinks, queries = lax.optimization_barrier((sinks, query_rows))
    scaled = queries * jnp.bfloat16(HEAD_SIZE**-0.5)
    weights = (w_gate, w_up, w_down)
    others = [swapped(weight, "tp") for weight in weights[:2]]
    near = attention(
        first, sinks, scaled, key_values, before, w_out
    )
    far, late = lax.optimization_barrier((swapped(near, "tp"), w_down))
    others.append(swapped(late, "tp"))
    normed, sent, kept = norm(side, residual_in, near, far, norm_gain, half)

    def exchanged(block):
        block = block.reshape(group, rows // group, model_width)
        groups = [list(range(group)), list(range(group, seq_count))]
        block = lax.all_to_all(
            block, "seq", split_axis=0, concat_axis=0, axis_index_groups=groups, tiled=True
        )
        return block.reshape(rows, model_width)

    notes = jnp.concatenate([expert_ids.T.astype(jnp.float32), route_weights.T], axis=0)
    crossed = swapped_halves(sent, "seq")
    notes_peer = swapped_halves(notes, "seq")
    packed, placed = packed_rows(base, side, notes, (normed,), experts, side_rows, rows)
    crossed, notes_peer, packed = lax.optimization_barrier((crossed, notes_peer, packed))
    packed_peer, placed_peer = packed_rows(
        base, side, notes_peer, (crossed, swapped(crossed, "tp")), experts, side_rows, rows
    )
    arrived_peer = exchanged(packed_peer)
    arrived_peer, packed, *others = lax.optimization_barrier((arrived_peer, packed, *others))
    arrived = exchanged(packed)
    result_peer = expert_layer(arrived_peer, weights, others)
    result_peer, arrived = lax.optimization_barrier((result_peer, arrived))
    result = expert_layer(arrived, weights, others)

    returned_peer = exchanged(result_peer)
    result, returned_peer = lax.optimization_barrier((result, returned_peer))
    returned = exchanged(result)
    mine_peer, sent_peer = combine(side, placed_peer, notes_peer, returned_peer, half)
    summed_peer = (mine_peer + swapped(sent_peer, "tp").astype(jnp.float32)).astype(jnp.bfloat16)
    back = swapped_halves(summed_peer, "seq")
    mine, sent = combine(side, placed, notes, returned, half, (kept,))
    sent, back = lax.optimization_barrier((sent, back))
    return (mine + swapped(sent, "tp").astype(jnp.float32) + back.astype(jnp.float32)).astype(jnp.bfloat16)


def solution(mesh):
    placed = (
        P("seq", None),
        P("seq", "tp"),
        P("seq", "tp"),
        P("seq", "tp"),
        P("tp"),
        P("tp", None),
        P(),
        P("seq", None),
        P("seq", None),
        P("seq", None, "tp"),
        P("seq", None, "tp"),
        P("seq", "tp", None),
    )
    return jax.shard_map(
        local, mesh=mesh, in_specs=placed, out_specs=P("seq", "tp"), check_vma=False
    )
```

```python
import functools

import jax
import jax.numpy as jnp
from jax import lax
from jax.experimental import pallas as pl
from jax.experimental.pallas import tpu as pltpu
from jax.sharding import PartitionSpec as P

HEAD_SIZE = 64
WINDOW_LENGTH = 128
LANES = 128
MIB = 1024 * 1024
CUTS = 3
AHEAD = 3

neg_large = -1e30
epsilon = 1e-05

VMEM = pl.BlockSpec(memory_space=pltpu.VMEM)
SMEM = pl.BlockSpec(memory_space=pltpu.SMEM)
HBM = pl.BlockSpec(memory_space=pltpu.HBM)


def passed_along(block, axis, distance):
    devices = range(lax.axis_size(axis))
    route = [(i - distance, i) for i in devices if i - distance in devices]
    return lax.ppermute(block, axis, route)


def swapped(block, axis):
    count = lax.axis_size(axis)
    return lax.ppermute(block, axis, [(i, count - 1 - i) for i in range(count)])


def swapped_halves(block, axis):
    count = lax.axis_size(axis)
    return lax.ppermute(block, axis, [(i, (i + count // 2) % count) for i in range(count)])


def shape_of(dims, dtype=jnp.bfloat16):
    return jax.ShapeDtypeStruct(dims, dtype)


def cost(flops, moved, transcendentals=0):
    return pl.CostEstimate(flops=flops, bytes_accessed=moved, transcendentals=transcendentals)


def iota(dims, dimension):
    return lax.broadcasted_iota(jnp.int32, dims, dimension)


def rows_of(ids, experts, side_rows, base, side):
    top_count, tokens = ids.shape
    names = iota((experts, tokens), 0).astype(jnp.float32)
    hits = [ids[c : c + 1, :] == names for c in range(top_count)]
    named = sum([hit.astype(jnp.float32) for hit in hits]).astype(jnp.bfloat16)
    square = (tokens, tokens)
    earlier = (iota(square, 0) < iota(square, 1)).astype(jnp.bfloat16)
    slot = jnp.dot(named, earlier, preferred_element_type=jnp.float32)
    turned = slot - (side * side_rows).astype(jnp.float32)
    turned = jnp.where(turned < 0.0, turned + 2.0 * side_rows, turned)
    expert = names - base.astype(jnp.float32)
    here = (expert >= 0.0) & (expert < experts // 2)
    sent = jnp.where(here & (turned < side_rows), expert * side_rows + turned, -1.0)
    back = jnp.where(here, expert * (2 * side_rows) + turned, -1.0)

    def picked(rows):
        lines = [jnp.sum(jnp.where(hit, rows, 0.0), axis=0, keepdims=True) for hit in hits]
        return jnp.concatenate(lines, axis=0).astype(jnp.int32)

    return picked(sent), picked(back)


def attention_kernel(
    first_ref, sink_ref, q_ref, kv_ref, before_ref, w_hbm, out_ref, w_ref, att_ref, sum_ref, sem
):
    tokens, width = q_ref.shape
    kv_heads = kv_ref.shape[1] // (2 * HEAD_SIZE)
    pairs = width // LANES // kv_heads
    w_load = pltpu.make_async_copy(w_hbm, w_ref, sem)
    w_load.start()
    low = iota((tokens, LANES), 1) < HEAD_SIZE

    def doubled(block, head):
        wide = block.astype(jnp.float32)
        turned = pltpu.roll(wide, HEAD_SIZE, 1)
        first, second = (wide, turned) if head == 0 else (turned, wide)
        return [
            jnp.where(low, first, 0.0).astype(jnp.bfloat16),
            jnp.where(low, 0.0, second).astype(jnp.bfloat16),
        ]

    own = iota((tokens, tokens), 1) <= iota((tokens, tokens), 0)
    bias = jnp.where(own, 0.0, jnp.where(first_ref[0] == 0, 0.0, neg_large))
    own_factor = jnp.where(own, 1.0, 0.0).astype(jnp.bfloat16)
    before_factor = jnp.where(own, 0.0, 1.0).astype(jnp.bfloat16)
    head_lanes = jnp.where(low, 1.0, 0.0).astype(jnp.bfloat16), jnp.where(low, 0.0, 1.0).astype(jnp.bfloat16)
    ones = jnp.concatenate(head_lanes, axis=0)
    keys_before = [jnp.concatenate(doubled(before_ref[:, :LANES], head), axis=0) for head in range(kv_heads)]
    values_before = [doubled(before_ref[:, LANES:], head) for head in range(kv_heads)]
    contract = (((1,), (1,)), ((), ()))
    for head in range(kv_heads):
        keys = jnp.concatenate(doubled(kv_ref[:, :LANES], head), axis=0)
        values = jnp.concatenate(doubled(kv_ref[:, LANES:], head) + values_before[head], axis=0)
        for j in range(head * pairs, (head + 1) * pairs):
            q = q_ref[:, j * LANES : (j + 1) * LANES]
            near = lax.dot_general(q, keys, contract, preferred_element_type=jnp.float32)
            far = lax.dot_general(q, keys_before[head], contract, preferred_element_type=jnp.float32)
            terms, sinks = [], []
            for at in range(2):
                span = slice(at * tokens, (at + 1) * tokens)
                part = jnp.where(own, near[:, span], far[:, span]) + bias
                sink = sink_ref[2 * j + at : 2 * j + at + 1, :]
                top = jnp.maximum(jnp.max(part, axis=1, keepdims=True), sink)
                terms.append(jnp.exp(part - top).astype(jnp.bfloat16))
                sinks.append(jnp.exp(sink - top))
            total = jnp.dot(jnp.concatenate(terms, axis=1), ones, preferred_element_type=jnp.float32)
            total += jnp.where(low, sinks[0], sinks[1])
            kept = [term * own_factor for term in terms] + [term * before_factor for term in terms]
            found = jnp.dot(jnp.concatenate(kept, axis=1), values, preferred_element_type=jnp.float32)
            att_ref[:, j * LANES : (j + 1) * LANES] = (found / total).astype(jnp.bfloat16)
        if head == 0:
            w_load.wait()
        depth = pairs * LANES
        step = 2 * LANES
        for at in range(0, out_ref.shape[1], step):
            part = jnp.dot(
                att_ref[:, head * depth : (head + 1) * depth],
                w_ref[head * depth : (head + 1) * depth, at : at + step],
                preferred_element_type=jnp.float32,
            )
            if head > 0:
                part += sum_ref[:, at : at + step]
            if head < kv_heads - 1:
                sum_ref[:, at : at + step] = part
            else:
                out_ref[:, at : at + step] = part.astype(jnp.bfloat16)


def attention(first, sinks, q, key_values, before, w_out):
    tokens = q.shape[0]
    return pl.pallas_call(
        attention_kernel,
        out_shape=shape_of((tokens, w_out.shape[1])),
        in_specs=[SMEM, VMEM, VMEM, VMEM, VMEM, HBM],
        out_specs=VMEM,
        scratch_shapes=[
            pltpu.VMEM(w_out.shape, jnp.bfloat16),
            pltpu.VMEM(q.shape, jnp.bfloat16),
            pltpu.VMEM((tokens, w_out.shape[1]), jnp.float32),
            pltpu.SemaphoreType.DMA,
        ],
        compiler_params=pltpu.CompilerParams(vmem_limit_bytes=54_000_000),
        cost_estimate=cost(2 * tokens * w_out.size * 2, 2 * w_out.size, tokens * tokens * q.shape[1] // HEAD_SIZE),
        name="attention",
    )(first, sinks, q, key_values, before, w_out)


def pack(placed, normed, out_ref):
    rows, tokens = out_ref.shape[0], normed.shape[0]
    row = iota((rows, tokens), 0)
    taken = placed[0:1, :] == row
    for c in range(1, placed.shape[0]):
        taken = taken | (placed[c : c + 1, :] == row)
    taken = jnp.where(taken, 1.0, 0.0).astype(jnp.bfloat16)
    out_ref[...] = jnp.dot(taken, normed, preferred_element_type=jnp.float32).astype(jnp.bfloat16)


def norm_kernel(side_ref, residual_ref, near_ref, far_ref, gain_ref, normed_ref, sent_ref, kept_ref, whole_ref):
    side = side_ref[0]
    half_tokens, half = sent_ref.shape[0], kept_ref.shape[1]
    added = near_ref[...].astype(jnp.float32) + far_ref[...].astype(jnp.float32)
    whole = (residual_ref[...].astype(jnp.float32) + added).astype(jnp.bfloat16)
    whole_ref[...] = whole
    wide = whole.astype(jnp.float32)
    mean_square = jnp.mean(wide * wide, axis=1, keepdims=True)
    normed_ref[...] = (wide * lax.rsqrt(mean_square + epsilon) * gain_ref[...]).astype(jnp.bfloat16)
    kept_ref[...] = whole_ref[:, pl.ds(pl.multiple_of(side * half, LANES), half)]
    sent_ref[...] = normed_ref[pl.ds(pl.multiple_of(side * half_tokens, half_tokens), half_tokens), :]


def norm(side, residual_in, near, far, gain, half):
    tokens, width = residual_in.shape
    return pl.pallas_call(
        norm_kernel,
        out_shape=(shape_of((tokens, width)), shape_of((tokens // 2, width)), shape_of((tokens, half))),
        in_specs=[SMEM] + [VMEM] * 4,
        out_specs=(VMEM, VMEM, VMEM),
        scratch_shapes=[pltpu.VMEM((tokens, width), jnp.bfloat16)],
        compiler_params=pltpu.CompilerParams(vmem_limit_bytes=24 * MIB),
        cost_estimate=cost(8 * tokens * width, 10 * tokens * width),
        name="norm",
    )(side, residual_in, near, far, gain.reshape(1, width))


def pack_kernel(experts, side_rows, base_ref, side_ref, notes_ref, *refs):
    *part_refs, out_ref, rows_ref, arrived_ref = refs
    side, top_count = side_ref[0], rows_ref.shape[0]
    if len(part_refs) == 1:
        arrived_ref = part_refs[0]
    else:
        mine_ref, other_ref = part_refs
        part = mine_ref.shape[0]
        arrived_ref[pl.ds(pl.multiple_of(side * part, part), part), :] = mine_ref[...]
        arrived_ref[pl.ds(pl.multiple_of((1 - side) * part, part), part), :] = other_ref[...]
    rows, rows_ref[...] = rows_of(notes_ref[:top_count, :], experts, side_rows, base_ref[0], side)
    pack(rows, arrived_ref[...], out_ref)


def packed_rows(base, side, notes, parts, experts, side_rows, rows):
    tokens = sum([part.shape[0] for part in parts])
    width = parts[0].shape[1]
    return pl.pallas_call(
        functools.partial(pack_kernel, experts, side_rows),
        out_shape=(shape_of((rows, width)), shape_of((notes.shape[0] // 2, tokens), jnp.int32)),
        in_specs=[SMEM, SMEM, VMEM] + [VMEM] * len(parts),
        out_specs=(VMEM, VMEM),
        scratch_shapes=[pltpu.VMEM((tokens, width), jnp.bfloat16)],
        compiler_params=pltpu.CompilerParams(vmem_limit_bytes=24 * MIB),
        cost_estimate=cost(2 * rows * tokens * width, 2 * rows * width),
        name="packed_rows",
    )(base, side, notes, *parts)


def hidden_kernel(
    x_hbm, gate_hbm, up_hbm, gate_too_hbm, up_too_hbm, out_hbm, x_ref, gate_ref, up_ref, hidden_ref, gate_sum, up_sum,
    x_sem, out_sem, gate_sem, up_sem,
):
    rows, width = x_ref.shape
    share = gate_hbm.shape[2]
    deep = width // CUTS
    loads = []
    for k, (gate, up) in enumerate([(gate_hbm, up_hbm), (gate_too_hbm, up_too_hbm)]):
        for c in range(CUTS):
            span = pl.ds(c * deep, deep)
            loads.append(
                [
                    pltpu.make_async_copy(gate.at[0, span], gate_ref.at[k, span], gate_sem.at[k, c]),
                    pltpu.make_async_copy(up.at[0, span], up_ref.at[k, span], up_sem.at[k, c]),
                ]
            )

    def start(number):
        if number < len(loads):
            for load in loads[number]:
                load.start()

    x_load = pltpu.make_async_copy(x_hbm, x_ref, x_sem)
    x_load.start()
    for number in range(AHEAD):
        start(number)
    x_load.wait()
    stores = []
    for k in range(2):
        for c in range(CUTS):
            for load in loads[k * CUTS + c]:
                load.wait()
            start(k * CUTS + c + AHEAD)
            span = slice(c * deep, (c + 1) * deep)
            x = x_ref[:, span]
            gate = jnp.dot(x, gate_ref[k, span, :], preferred_element_type=jnp.float32)
            up = jnp.dot(x, up_ref[k, span, :], preferred_element_type=jnp.float32)
            if c > 0:
                gate, up = gate_sum[...] + gate, up_sum[...] + up
            if c < CUTS - 1:
                gate_sum[...], up_sum[...] = gate, up
            else:
                hidden = gate * (0.5 + 0.5 * jnp.tanh(0.5 * gate)) * up
                hidden_ref[:, k * share : (k + 1) * share] = hidden.astype(jnp.bfloat16)
        columns = pl.ds(k * share, share)
        stores.append(pltpu.make_async_copy(hidden_ref.at[:, columns], out_hbm.at[:, columns], out_sem.at[k]))
        stores[k].start()
    for store in stores:
        store.wait()


def hidden_rows(x, mine, others):
    rows, width = x.shape
    share = mine[0].shape[2]
    return pl.pallas_call(
        hidden_kernel,
        out_shape=shape_of((rows, 2 * share)),
        in_specs=[HBM] * 5,
        out_specs=HBM,
        scratch_shapes=[
            pltpu.VMEM((rows, width), jnp.bfloat16),
            pltpu.VMEM((2, width, share), jnp.bfloat16),
            pltpu.VMEM((2, width, share), jnp.bfloat16),
            pltpu.VMEM((rows, 2 * share), jnp.bfloat16),
            pltpu.VMEM((rows, share), jnp.float32),
            pltpu.VMEM((rows, share), jnp.float32),
            pltpu.SemaphoreType.DMA,
            pltpu.SemaphoreType.DMA((2,)),
            pltpu.SemaphoreType.DMA((2, CUTS)),
            pltpu.SemaphoreType.DMA((2, CUTS)),
        ],
        compiler_params=pltpu.CompilerParams(vmem_limit_bytes=60 * MIB),
        cost_estimate=cost(8 * rows * width * share, 8 * width * share, 2 * rows * share),
        name="hidden_rows",
    )(x, *mine[:2], *others[:2])


def down_kernel(
    blocks, side_ref, mine_hbm, theirs_hbm, down_hbm, down_too_hbm, out_ref, mine_ref, theirs_ref, down_ref,
    down_too_ref, sems,
):
    rows, half = mine_ref.shape[0], out_ref.shape[1]
    share = down_hbm.shape[1]
    columns = pl.ds(pl.multiple_of(side_ref[0] * half, LANES), half)
    moves = [(mine_hbm, mine_ref), (down_hbm.at[0, :, columns], down_ref)]
    moves += [(down_too_hbm.at[0, :, columns], down_too_ref), (theirs_hbm, theirs_ref)]
    loads = [pltpu.make_async_copy(source, target, sems.at[i]) for i, (source, target) in enumerate(moves)]
    for load in loads:
        load.start()
    for load in loads[:3]:
        load.wait()
    per = rows // blocks
    for number, (ref, first, second) in enumerate(
        [(mine_ref, down_ref, down_too_ref), (theirs_ref, down_too_ref, down_ref)]
    ):
        if number == 1:
            loads[3].wait()
        y = jnp.dot(ref[:, :share], first[...], preferred_element_type=jnp.float32)
        y += jnp.dot(ref[:, share:], second[...], preferred_element_type=jnp.float32)
        y = y.astype(jnp.bfloat16)
        for block in range(blocks):
            at = (2 * block + number) * per
            out_ref[at : at + per, :] = y[block * per : (block + 1) * per]


def down_rows(side, mine, theirs, down, down_too, side_rows):
    rows, hidden_width = mine.shape
    share, width = down.shape[1:]
    half = width // 2
    group = rows // side_rows
    blocks = group if side_rows % 16 == 0 else 1
    out = pl.pallas_call(
        functools.partial(down_kernel, blocks),
        out_shape=shape_of((2 * rows, half)),
        in_specs=[SMEM] + [HBM] * 4,
        out_specs=VMEM,
        scratch_shapes=[
            pltpu.VMEM((rows, hidden_width), jnp.bfloat16),
            pltpu.VMEM((rows, hidden_width), jnp.bfloat16),
            pltpu.VMEM((share, half), jnp.bfloat16),
            pltpu.VMEM((share, half), jnp.bfloat16),
            pltpu.SemaphoreType.DMA((4,)),
        ],
        compiler_params=pltpu.CompilerParams(vmem_limit_bytes=60 * MIB),
        cost_estimate=cost(4 * rows * hidden_width * half, 4 * rows * width),
        name="down_rows",
    )(side, mine, theirs, down, down_too)
    if blocks == 1:
        out = out.reshape(2, group, side_rows, half).transpose(1, 0, 2, 3)
    return out.reshape(group, 2 * side_rows, half)


def combine_kernel(rows_ref, notes_ref, y_ref, *refs):
    *more_refs, out_ref = refs
    top_count, tokens = rows_ref.shape
    row = iota((y_ref.shape[0], tokens), 0)
    share = jnp.zeros(row.shape, jnp.float32)
    for c in range(top_count):
        share = jnp.where(rows_ref[c : c + 1, :] == row, notes_ref[top_count + c : top_count + c + 1, :], share)
    coarse = share.astype(jnp.bfloat16)
    fine = (share - coarse.astype(jnp.float32)).astype(jnp.bfloat16)
    y = y_ref[...]
    contract = (((0,), (0,)), ((), ()))
    total = lax.dot_general(coarse, y, contract, preferred_element_type=jnp.float32)
    total += lax.dot_general(fine, y, contract, preferred_element_type=jnp.float32)
    for more_ref in more_refs:
        total += more_ref[...].astype(jnp.float32)
    out_ref[...] = total.astype(jnp.bfloat16)


def combine(placed, notes, y, more=()):
    tokens = placed.shape[1]
    rows, half = y.shape
    return pl.pallas_call(
        combine_kernel,
        out_shape=shape_of((tokens, half)),
        in_specs=[VMEM] * (3 + len(more)),
        out_specs=VMEM,
        compiler_params=pltpu.CompilerParams(vmem_limit_bytes=24 * MIB),
        cost_estimate=cost(4 * rows * tokens * half, 2 * rows * half),
        name="combine",
    )(placed, notes, y, *more)


def local(
    residual_in,
    query_rows,
    rotated_key_rows,
    value_row_matrix,
    learned_sink_scores,
    w_out,
    norm_gain,
    expert_ids,
    route_weights,
    w_gate,
    w_up,
    w_down,
):
    tok_dev, model_width = residual_in.shape
    seq_count = lax.axis_size("seq")
    experts = w_gate.shape[0] * seq_count
    capacity = max(2, 8 * tok_dev // experts)
    sides = lax.axis_size("tp")
    side_rows = capacity // sides
    group = seq_count // 2
    rows = experts // 2 * side_rows
    half = model_width // sides
    at_seq = lax.axis_index("seq").astype(jnp.int32)
    base = jnp.where(at_seq < group, 0, experts // 2).astype(jnp.int32).reshape(1)
    side = lax.axis_index("tp").astype(jnp.int32).reshape(1)
    first = (at_seq == 0).astype(jnp.int32).reshape(1)
    key_values = lax.optimization_barrier(jnp.concatenate([rotated_key_rows, value_row_matrix], axis=1))
    before = passed_along(key_values, "seq", 1)
    sinks = jnp.broadcast_to(learned_sink_scores[:, None], (learned_sink_scores.shape[0], LANES))
    sinks, queries = lax.optimization_barrier((sinks, query_rows))
    scaled = queries * jnp.bfloat16(HEAD_SIZE**-0.5)
    weights = (w_gate, w_up, w_down)
    others = [swapped(weight, "tp") for weight in weights[:2]]
    near = attention(
        first, sinks, scaled, key_values, before, w_out
    )
    far, late = lax.optimization_barrier((swapped(near, "tp"), w_down))
    others.append(swapped(late, "tp"))
    normed, sent, kept = norm(side, residual_in, near, far, norm_gain, half)

    def exchanged(block):
        groups = [list(range(group)), list(range(group, seq_count))]
        return lax.all_to_all(
            block, "seq", split_axis=0, concat_axis=0, axis_index_groups=groups, tiled=True
        )

    def expert_layer(arrived):
        hidden = hidden_rows(arrived.reshape(rows, model_width), weights, others)
        return down_rows(side, hidden, swapped(hidden, "tp"), w_down, others[2], side_rows)

    notes = jnp.concatenate([expert_ids.T.astype(jnp.float32), route_weights.T], axis=0)
    crossed = swapped_halves(sent, "seq")
    notes_peer = swapped_halves(notes, "seq")
    packed, placed = packed_rows(base, side, notes, (normed,), experts, side_rows, rows)
    crossed, notes_peer, packed = lax.optimization_barrier((crossed, notes_peer, packed))
    packed_peer, placed_peer = packed_rows(
        base, side, notes_peer, (crossed, swapped(crossed, "tp")), experts, side_rows, rows
    )
    arrived_peer = exchanged(packed_peer.reshape(group, side_rows, model_width))
    arrived_peer, packed, *others = lax.optimization_barrier((arrived_peer, packed, *others))
    arrived = exchanged(packed.reshape(group, side_rows, model_width))
    result_peer = expert_layer(arrived_peer)
    result_peer, arrived = lax.optimization_barrier((result_peer, arrived))
    result = expert_layer(arrived)

    returned_peer = exchanged(result_peer)
    result, returned_peer = lax.optimization_barrier((result, returned_peer))
    returned = exchanged(result)
    summed_peer = combine(placed_peer, notes_peer, returned_peer.reshape(2 * rows, half))
    back = swapped_halves(summed_peer, "seq")
    return combine(placed, notes, returned.reshape(2 * rows, half), (kept, back))


def solution(mesh):
    placed = (
        P("seq", None),
        P("seq", "tp"),
        P("seq", "tp"),
        P("seq", "tp"),
        P("tp"),
        P("tp", None),
        P(),
        P("seq", None),
        P("seq", None),
        P("seq", None, "tp"),
        P("seq", None, "tp"),
        P("seq", "tp", None),
    )
    return jax.shard_map(
        local, mesh=mesh, in_specs=placed, out_specs=P("seq", "tp"), check_vma=False
    )
```

```python
import functools

import jax
import jax.numpy as jnp
from jax import lax
from jax.experimental import pallas as pl
from jax.experimental.pallas import tpu as pltpu
from jax.sharding import PartitionSpec as P

HEAD_SIZE = 64
WINDOW_LENGTH = 128
LANES = 128
MIB = 1024 * 1024
CUTS = 3
DEEP = 256
AHEAD = 3

neg_large = -1e30
epsilon = 1e-05

VMEM = pl.BlockSpec(memory_space=pltpu.VMEM)
SMEM = pl.BlockSpec(memory_space=pltpu.SMEM)
HBM = pl.BlockSpec(memory_space=pltpu.HBM)


def passed_along(block, axis, distance):
    devices = range(lax.axis_size(axis))
    route = [(i - distance, i) for i in devices if i - distance in devices]
    return lax.ppermute(block, axis, route)


def swapped(block, axis):
    count = lax.axis_size(axis)
    return lax.ppermute(block, axis, [(i, count - 1 - i) for i in range(count)])


def swapped_halves(block, axis):
    count = lax.axis_size(axis)
    return lax.ppermute(block, axis, [(i, (i + count // 2) % count) for i in range(count)])


def shape_of(dims, dtype=jnp.bfloat16):
    return jax.ShapeDtypeStruct(dims, dtype)


def cost(flops, moved, transcendentals=0):
    return pl.CostEstimate(flops=flops, bytes_accessed=moved, transcendentals=transcendentals)


def iota(dims, dimension):
    return lax.broadcasted_iota(jnp.int32, dims, dimension)


def rows_of(ids, experts, side_rows, base, side):
    top_count, tokens = ids.shape
    names = iota((experts, tokens), 0).astype(jnp.float32)
    hits = [ids[c : c + 1, :] == names for c in range(top_count)]
    named = sum([hit.astype(jnp.float32) for hit in hits]).astype(jnp.bfloat16)
    square = (tokens, tokens)
    earlier = (iota(square, 0) < iota(square, 1)).astype(jnp.bfloat16)
    slot = jnp.dot(named, earlier, preferred_element_type=jnp.float32) - (side * side_rows).astype(jnp.float32)
    expert = names - base.astype(jnp.float32)
    here = (slot >= 0.0) & (slot < side_rows) & (expert >= 0.0) & (expert < experts // 2)
    rows = jnp.where(here, expert * side_rows + slot, -1.0)
    lines = [jnp.sum(jnp.where(hit, rows, 0.0), axis=0, keepdims=True) for hit in hits]
    return jnp.concatenate(lines, axis=0).astype(jnp.int32)


def attention_kernel(
    first_ref, sink_ref, q_ref, kv_ref, before_ref, w_hbm, out_ref, w_ref, att_ref, sum_ref, sem
):
    tokens, width = q_ref.shape
    kv_heads = kv_ref.shape[1] // (2 * HEAD_SIZE)
    pairs = width // LANES // kv_heads
    w_load = pltpu.make_async_copy(w_hbm, w_ref, sem)
    w_load.start()
    low = iota((tokens, LANES), 1) < HEAD_SIZE

    def doubled(block, head):
        wide = block.astype(jnp.float32)
        turned = pltpu.roll(wide, HEAD_SIZE, 1)
        first, second = (wide, turned) if head == 0 else (turned, wide)
        return [
            jnp.where(low, first, 0.0).astype(jnp.bfloat16),
            jnp.where(low, 0.0, second).astype(jnp.bfloat16),
        ]

    own = iota((tokens, tokens), 1) <= iota((tokens, tokens), 0)
    bias = jnp.where(own, 0.0, jnp.where(first_ref[0] == 0, 0.0, neg_large))
    own_factor = jnp.where(own, 1.0, 0.0).astype(jnp.bfloat16)
    before_factor = jnp.where(own, 0.0, 1.0).astype(jnp.bfloat16)
    head_lanes = jnp.where(low, 1.0, 0.0).astype(jnp.bfloat16), jnp.where(low, 0.0, 1.0).astype(jnp.bfloat16)
    ones = jnp.concatenate(head_lanes * 2, axis=0)
    keys_before = [jnp.concatenate(doubled(before_ref[:, :LANES], head), axis=0) for head in range(kv_heads)]
    values_before = [doubled(before_ref[:, LANES:], head) for head in range(kv_heads)]
    contract = (((1,), (1,)), ((), ()))
    for head in range(kv_heads):
        keys = jnp.concatenate(doubled(kv_ref[:, :LANES], head), axis=0)
        values = jnp.concatenate(doubled(kv_ref[:, LANES:], head) + values_before[head], axis=0)
        values = jnp.concatenate([values, ones], axis=1)
        for j in range(head * pairs, (head + 1) * pairs):
            q = q_ref[:, j * LANES : (j + 1) * LANES]
            near = lax.dot_general(q, keys, contract, preferred_element_type=jnp.float32)
            far = lax.dot_general(q, keys_before[head], contract, preferred_element_type=jnp.float32)
            terms, sinks = [], []
            for at in range(2):
                span = slice(at * tokens, (at + 1) * tokens)
                part = jnp.where(own, near[:, span], far[:, span]) + bias
                sink = sink_ref[2 * j + at : 2 * j + at + 1, :]
                top = jnp.maximum(jnp.max(part, axis=1, keepdims=True), sink)
                terms.append(jnp.exp(part - top).astype(jnp.bfloat16))
                sinks.append(jnp.exp(sink - top))
            kept = [term * own_factor for term in terms] + [term * before_factor for term in terms]
            found = jnp.dot(jnp.concatenate(kept, axis=1), values, preferred_element_type=jnp.float32)
            total = found[:, LANES:] + jnp.where(low, sinks[0], sinks[1])
            att_ref[:, j * LANES : (j + 1) * LANES] = (found[:, :LANES] / total).astype(jnp.bfloat16)
        if head == 0:
            w_load.wait()
        depth = pairs * LANES
        step = 2 * LANES
        for at in range(0, out_ref.shape[1], step):
            part = jnp.dot(
                att_ref[:, head * depth : (head + 1) * depth],
                w_ref[head * depth : (head + 1) * depth, at : at + step],
                preferred_element_type=jnp.float32,
            )
            if head > 0:
                part += sum_ref[:, at : at + step]
            if head < kv_heads - 1:
                sum_ref[:, at : at + step] = part
            else:
                out_ref[:, at : at + step] = part.astype(jnp.bfloat16)


def attention(first, sinks, q, key_values, before, w_out):
    tokens = q.shape[0]
    return pl.pallas_call(
        attention_kernel,
        out_shape=shape_of((tokens, w_out.shape[1])),
        in_specs=[SMEM, VMEM, VMEM, VMEM, VMEM, HBM],
        out_specs=VMEM,
        scratch_shapes=[
            pltpu.VMEM(w_out.shape, jnp.bfloat16),
            pltpu.VMEM(q.shape, jnp.bfloat16),
            pltpu.VMEM((tokens, w_out.shape[1]), jnp.float32),
            pltpu.SemaphoreType.DMA,
        ],
        compiler_params=pltpu.CompilerParams(vmem_limit_bytes=54_000_000),
        cost_estimate=cost(2 * tokens * w_out.size * 2, 2 * w_out.size, tokens * tokens * q.shape[1] // HEAD_SIZE),
        name="attention",
    )(first, sinks, q, key_values, before, w_out)


def pack(placed, normed, out_ref):
    rows, tokens = out_ref.shape[0], normed.shape[0]
    row = iota((rows, tokens), 0)
    taken = placed[0:1, :] == row
    for c in range(1, placed.shape[0]):
        taken = taken | (placed[c : c + 1, :] == row)
    taken = jnp.where(taken, 1.0, 0.0).astype(jnp.bfloat16)
    out_ref[...] = jnp.dot(taken, normed, preferred_element_type=jnp.float32).astype(jnp.bfloat16)


def norm_kernel(side_ref, residual_ref, near_ref, far_ref, gain_ref, normed_ref, sent_ref, kept_ref, whole_ref):
    side = side_ref[0]
    half_tokens, half = sent_ref.shape[0], kept_ref.shape[1]
    added = near_ref[...].astype(jnp.float32) + far_ref[...].astype(jnp.float32)
    whole = (residual_ref[...].astype(jnp.float32) + added).astype(jnp.bfloat16)
    whole_ref[...] = whole
    wide = whole.astype(jnp.float32)
    mean_square = jnp.mean(wide * wide, axis=1, keepdims=True)
    normed_ref[...] = (wide * lax.rsqrt(mean_square + epsilon) * gain_ref[...]).astype(jnp.bfloat16)
    kept_ref[...] = whole_ref[:, pl.ds(pl.multiple_of(side * half, LANES), half)]
    sent_ref[...] = normed_ref[pl.ds(pl.multiple_of(side * half_tokens, half_tokens), half_tokens), :]


def norm(side, residual_in, near, far, gain, half):
    tokens, width = residual_in.shape
    return pl.pallas_call(
        norm_kernel,
        out_shape=(shape_of((tokens, width)), shape_of((tokens // 2, width)), shape_of((tokens, half))),
        in_specs=[SMEM] + [VMEM] * 4,
        out_specs=(VMEM, VMEM, VMEM),
        scratch_shapes=[pltpu.VMEM((tokens, width), jnp.bfloat16)],
        compiler_params=pltpu.CompilerParams(vmem_limit_bytes=24 * MIB),
        cost_estimate=cost(8 * tokens * width, 10 * tokens * width),
        name="norm",
    )(side, residual_in, near, far, gain.reshape(1, width))


def pack_kernel(experts, side_rows, base_ref, side_ref, notes_ref, *refs):
    *part_refs, out_ref, rows_ref, arrived_ref = refs
    side, top_count = side_ref[0], rows_ref.shape[0]
    if len(part_refs) == 1:
        arrived_ref = part_refs[0]
    else:
        mine_ref, other_ref = part_refs
        part = mine_ref.shape[0]
        arrived_ref[pl.ds(pl.multiple_of(side * part, part), part), :] = mine_ref[...]
        arrived_ref[pl.ds(pl.multiple_of((1 - side) * part, part), part), :] = other_ref[...]
    rows = rows_of(notes_ref[:top_count, :], experts, side_rows, base_ref[0], side)
    rows_ref[...] = rows
    pack(rows, arrived_ref[...], out_ref)


def packed_rows(base, side, notes, parts, experts, side_rows, rows):
    tokens = sum([part.shape[0] for part in parts])
    width = parts[0].shape[1]
    return pl.pallas_call(
        functools.partial(pack_kernel, experts, side_rows),
        out_shape=(shape_of((rows, width)), shape_of((notes.shape[0] // 2, tokens), jnp.int32)),
        in_specs=[SMEM, SMEM, VMEM] + [VMEM] * len(parts),
        out_specs=(VMEM, VMEM),
        scratch_shapes=[pltpu.VMEM((tokens, width), jnp.bfloat16)],
        compiler_params=pltpu.CompilerParams(vmem_limit_bytes=24 * MIB),
        cost_estimate=cost(2 * rows * tokens * width, 2 * rows * width),
        name="packed_rows",
    )(base, side, notes, *parts)


def expert_kernel(
    x_hbm, gate_hbm, up_hbm, down_hbm, gate_too_hbm, up_too_hbm, down_too_hbm, y_hbm, x_ref, y_ref, gate_ref, up_ref,
    down_ref, hidden_ref, gate_sum, up_sum, total_ref, x_sem, y_sem, gate_sem, up_sem, down_sem,
):
    rows, width = x_ref.shape
    share = gate_hbm.shape[2]
    deep, cuts = width // CUTS, share // DEEP
    loads = []
    for k, (gate, up) in enumerate([(gate_hbm, up_hbm), (gate_too_hbm, up_too_hbm)]):
        for c in range(CUTS):
            span = pl.ds(c * deep, deep)
            loads.append(
                [
                    pltpu.make_async_copy(gate.at[0, span], gate_ref.at[k, span], gate_sem.at[k, c]),
                    pltpu.make_async_copy(up.at[0, span], up_ref.at[k, span], up_sem.at[k, c]),
                ]
            )
    for k, down in enumerate([down_hbm, down_too_hbm]):
        for c in range(cuts):
            source, target = pl.ds(c * DEEP, DEEP), pl.ds(k * share + c * DEEP, DEEP)
            loads.append([pltpu.make_async_copy(down.at[0, source], down_ref.at[target], down_sem.at[k, c])])

    def start(number):
        if number < len(loads):
            for load in loads[number]:
                load.start()

    def arrive(number):
        for load in loads[number]:
            load.wait()
        start(number + AHEAD)

    x_load = pltpu.make_async_copy(x_hbm, x_ref, x_sem)
    x_load.start()
    for number in range(AHEAD):
        start(number)
    x_load.wait()
    for k in range(2):
        for c in range(CUTS):
            arrive(k * CUTS + c)
            span = slice(c * deep, (c + 1) * deep)
            x = x_ref[:, span]
            gate = jnp.dot(x, gate_ref[k, span, :], preferred_element_type=jnp.float32)
            up = jnp.dot(x, up_ref[k, span, :], preferred_element_type=jnp.float32)
            if c > 0:
                gate, up = gate_sum[...] + gate, up_sum[...] + up
            if c < CUTS - 1:
                gate_sum[...], up_sum[...] = gate, up
            else:
                hidden = gate * (0.5 + 0.5 * jnp.tanh(0.5 * gate)) * up
                hidden_ref[:, k * share : (k + 1) * share] = hidden.astype(jnp.bfloat16)
    for c in range(2 * cuts - 1):
        arrive(2 * CUTS + c)
        span = slice(c * DEEP, (c + 1) * DEEP)
        part = jnp.dot(hidden_ref[:, span], down_ref[span, :], preferred_element_type=jnp.float32)
        total_ref[...] = part if c == 0 else total_ref[...] + part
    arrive(2 * CUTS + 2 * cuts - 1)
    span = slice((2 * cuts - 1) * DEEP, 2 * cuts * DEEP)
    step = 2 * LANES
    stores = []
    for i in range(width // step):
        columns = slice(i * step, (i + 1) * step)
        part = jnp.dot(hidden_ref[:, span], down_ref[span, columns], preferred_element_type=jnp.float32)
        y_ref[:, columns] = (total_ref[:, columns] + part).astype(jnp.bfloat16)
        column_span = pl.ds(i * step, step)
        stores.append(pltpu.make_async_copy(y_ref.at[:, column_span], y_hbm.at[:, column_span], y_sem.at[i]))
        stores[i].start()
    for store in stores:
        store.wait()


def expert_layer(x, mine, others):
    rows, width = x.shape
    share = mine[0].shape[2]
    return pl.pallas_call(
        expert_kernel,
        out_shape=shape_of((rows, width)),
        in_specs=[HBM] * 7,
        out_specs=HBM,
        scratch_shapes=[
            pltpu.VMEM((rows, width), jnp.bfloat16),
            pltpu.VMEM((rows, width), jnp.bfloat16),
            pltpu.VMEM((2, width, share), jnp.bfloat16),
            pltpu.VMEM((2, width, share), jnp.bfloat16),
            pltpu.VMEM((2 * share, width), jnp.bfloat16),
            pltpu.VMEM((rows, 2 * share), jnp.bfloat16),
            pltpu.VMEM((rows, share), jnp.float32),
            pltpu.VMEM((rows, share), jnp.float32),
            pltpu.VMEM((rows, width), jnp.float32),
            pltpu.SemaphoreType.DMA,
            pltpu.SemaphoreType.DMA((width // (2 * LANES),)),
            pltpu.SemaphoreType.DMA((2, CUTS)),
            pltpu.SemaphoreType.DMA((2, CUTS)),
            pltpu.SemaphoreType.DMA((2, share // DEEP)),
        ],
        compiler_params=pltpu.CompilerParams(vmem_limit_bytes=60 * MIB),
        cost_estimate=cost(12 * rows * width * share, 12 * width * share, 2 * rows * share),
        name="expert_layer",
    )(x, *mine, *others)


def combine_kernel(side_ref, rows_ref, weights_ref, y_ref, *refs):
    *more_refs, mine_ref, sent_ref, total_ref = refs
    top_count, tokens = rows_ref.shape
    half = mine_ref.shape[1]
    row = iota((y_ref.shape[0], tokens), 0)
    share = jnp.zeros(row.shape, jnp.float32)
    for c in range(top_count):
        share = jnp.where(rows_ref[c : c + 1, :] == row, weights_ref[top_count + c : top_count + c + 1, :], share)
    coarse = share.astype(jnp.bfloat16)
    fine = (share - coarse.astype(jnp.float32)).astype(jnp.bfloat16)
    y = y_ref[...]
    contract = (((0,), (0,)), ((), ()))
    total_ref[...] = lax.dot_general(coarse, y, contract, preferred_element_type=jnp.float32)
    total_ref[...] += lax.dot_general(fine, y, contract, preferred_element_type=jnp.float32)
    side = side_ref[0]
    mine = total_ref[:, pl.ds(pl.multiple_of(side * half, LANES), half)]
    for more_ref in more_refs:
        mine += more_ref[...].astype(jnp.float32)
    mine_ref[...] = mine
    sent_ref[...] = total_ref[:, pl.ds(pl.multiple_of((1 - side) * half, LANES), half)].astype(jnp.bfloat16)


def combine(side, placed, weights, y, half, more=()):
    tokens = placed.shape[1]
    rows, width = y.shape
    return pl.pallas_call(
        combine_kernel,
        out_shape=(shape_of((tokens, half), jnp.float32), shape_of((tokens, half))),
        in_specs=[SMEM] + [VMEM] * (3 + len(more)),
        out_specs=(VMEM, VMEM),
        scratch_shapes=[pltpu.VMEM((tokens, width), jnp.float32)],
        compiler_params=pltpu.CompilerParams(vmem_limit_bytes=24 * MIB),
        cost_estimate=cost(4 * rows * tokens * width, 2 * rows * width),
        name="combine",
    )(side, placed, weights, y, *more)


def local(
    residual_in,
    query_rows,
    rotated_key_rows,
    value_row_matrix,
    learned_sink_scores,
    w_out,
    norm_gain,
    expert_ids,
    route_weights,
    w_gate,
    w_up,
    w_down,
):
    tok_dev, model_width = residual_in.shape
    seq_count = lax.axis_size("seq")
    experts = w_gate.shape[0] * seq_count
    capacity = max(2, 8 * tok_dev // experts)
    sides = lax.axis_size("tp")
    side_rows = capacity // sides
    group = seq_count // 2
    rows = experts // 2 * side_rows
    half = model_width // sides
    at_seq = lax.axis_index("seq").astype(jnp.int32)
    base = jnp.where(at_seq < group, 0, experts // 2).astype(jnp.int32).reshape(1)
    side = lax.axis_index("tp").astype(jnp.int32).reshape(1)
    first = (at_seq == 0).astype(jnp.int32).reshape(1)
    key_values = lax.optimization_barrier(jnp.concatenate([rotated_key_rows, value_row_matrix], axis=1))
    before = passed_along(key_values, "seq", 1)
    sinks = jnp.broadcast_to(learned_sink_scores[:, None], (learned_sink_scores.shape[0], LANES))
    sinks, queries = lax.optimization_barrier((sinks, query_rows))
    scaled = queries * jnp.bfloat16(HEAD_SIZE**-0.5)
    weights = (w_gate, w_up, w_down)
    others = [swapped(weight, "tp") for weight in weights[:2]]
    near = attention(
        first, sinks, scaled, key_values, before, w_out
    )
    far, late = lax.optimization_barrier((swapped(near, "tp"), w_down))
    others.append(swapped(late, "tp"))
    normed, sent, kept = norm(side, residual_in, near, far, norm_gain, half)

    def exchanged(block):
        block = block.reshape(group, rows // group, model_width)
        groups = [list(range(group)), list(range(group, seq_count))]
        block = lax.all_to_all(
            block, "seq", split_axis=0, concat_axis=0, axis_index_groups=groups, tiled=True
        )
        return block.reshape(rows, model_width)

    notes = jnp.concatenate([expert_ids.T.astype(jnp.float32), route_weights.T], axis=0)
    crossed = swapped_halves(sent, "seq")
    notes_peer = swapped_halves(notes, "seq")
    packed, placed = packed_rows(base, side, notes, (normed,), experts, side_rows, rows)
    crossed, notes_peer, packed = lax.optimization_barrier((crossed, notes_peer, packed))
    packed_peer, placed_peer = packed_rows(
        base, side, notes_peer, (crossed, swapped(crossed, "tp")), experts, side_rows, rows
    )
    arrived_peer = exchanged(packed_peer)
    arrived_peer, packed, *others = lax.optimization_barrier((arrived_peer, packed, *others))
    arrived = exchanged(packed)
    result_peer = expert_layer(arrived_peer, weights, others)
    result_peer, arrived = lax.optimization_barrier((result_peer, arrived))
    result = expert_layer(arrived, weights, others)

    returned_peer = exchanged(result_peer)
    result, returned_peer = lax.optimization_barrier((result, returned_peer))
    returned = exchanged(result)
    mine_peer, sent_peer = combine(side, placed_peer, notes_peer, returned_peer, half)
    summed_peer = (mine_peer + swapped(sent_peer, "tp").astype(jnp.float32)).astype(jnp.bfloat16)
    back = swapped_halves(summed_peer, "seq")
    mine, sent = combine(side, placed, notes, returned, half, (kept,))
    sent, back = lax.optimization_barrier((sent, back))
    return (mine + swapped(sent, "tp").astype(jnp.float32) + back.astype(jnp.float32)).astype(jnp.bfloat16)


def solution(mesh):
    placed = (
        P("seq", None),
        P("seq", "tp"),
        P("seq", "tp"),
        P("seq", "tp"),
        P("tp"),
        P("tp", None),
        P(),
        P("seq", None),
        P("seq", None),
        P("seq", None, "tp"),
        P("seq", None, "tp"),
        P("seq", "tp", None),
    )
    return jax.shard_map(
        local, mesh=mesh, in_specs=placed, out_specs=P("seq", "tp"), check_vma=False
    )
```

```python
import functools

import jax
import jax.numpy as jnp
from jax import lax
from jax.experimental import pallas as pl
from jax.experimental.pallas import tpu as pltpu
from jax.sharding import PartitionSpec as P

HEAD_SIZE = 64
WINDOW_LENGTH = 128
LANES = 128
MIB = 1024 * 1024
CUTS = 3
DEEP = 256
AHEAD = 3

epsilon = 1e-05

VMEM = pl.BlockSpec(memory_space=pltpu.VMEM)
SMEM = pl.BlockSpec(memory_space=pltpu.SMEM)
HBM = pl.BlockSpec(memory_space=pltpu.HBM)


def passed_along(block, axis, distance):
    devices = range(lax.axis_size(axis))
    route = [(i - distance, i) for i in devices if i - distance in devices]
    return lax.ppermute(block, axis, route)


def swapped(block, axis):
    count = lax.axis_size(axis)
    return lax.ppermute(block, axis, [(i, count - 1 - i) for i in range(count)])


def swapped_halves(block, axis):
    count = lax.axis_size(axis)
    return lax.ppermute(block, axis, [(i, (i + count // 2) % count) for i in range(count)])


def shape_of(dims, dtype=jnp.bfloat16):
    return jax.ShapeDtypeStruct(dims, dtype)


def cost(flops, moved, transcendentals=0):
    return pl.CostEstimate(flops=flops, bytes_accessed=moved, transcendentals=transcendentals)


def iota(dims, dimension):
    return lax.broadcasted_iota(jnp.int32, dims, dimension)


def rows_of(ids, experts, side_rows, base, side):
    top_count, tokens = ids.shape
    names = iota((experts, tokens), 0).astype(jnp.float32)
    hits = [ids[c : c + 1, :] == names for c in range(top_count)]
    named = sum([hit.astype(jnp.float32) for hit in hits]).astype(jnp.bfloat16)
    square = (tokens, tokens)
    earlier = (iota(square, 0) < iota(square, 1)).astype(jnp.bfloat16)
    slot = jnp.dot(named, earlier, preferred_element_type=jnp.float32) - (side * side_rows).astype(jnp.float32)
    expert = names - base.astype(jnp.float32)
    here = (slot >= 0.0) & (slot < side_rows) & (expert >= 0.0) & (expert < experts // 2)
    rows = jnp.where(here, expert * side_rows + slot, -1.0)
    lines = [jnp.sum(jnp.where(hit, rows, 0.0), axis=0, keepdims=True) for hit in hits]
    return jnp.concatenate(lines, axis=0).astype(jnp.int32)


def attention_kernel(
    first_ref, sink_ref, q_ref, kv_ref, before_ref, w_hbm, out_ref, w_ref, att_ref, sum_ref, sems
):
    tokens, width = q_ref.shape
    kv_heads = kv_ref.shape[1] // (2 * HEAD_SIZE)
    pairs = width // LANES // kv_heads
    depth = pairs * LANES
    spans = [pl.ds(head * depth, depth) for head in range(kv_heads)]
    w_loads = [pltpu.make_async_copy(w_hbm.at[span], w_ref.at[span], sems.at[i]) for i, span in enumerate(spans)]
    for load in w_loads:
        load.start()
    low = iota((tokens, LANES), 1) < HEAD_SIZE

    def doubled(block, head):
        wide = block.astype(jnp.float32)
        turned = pltpu.roll(wide, HEAD_SIZE, 1)
        first, second = (wide, turned) if head == 0 else (turned, wide)
        return [
            jnp.where(low, first, 0.0).astype(jnp.bfloat16),
            jnp.where(low, 0.0, second).astype(jnp.bfloat16),
        ]

    own = iota((tokens, tokens), 1) <= iota((tokens, tokens), 0)
    usable = jnp.where(first_ref[0] == 0, 1.0, 0.0)
    own_factor = jnp.where(own, 1.0, 0.0).astype(jnp.bfloat16)
    before_factor = jnp.where(own, 0.0, usable).astype(jnp.bfloat16)
    head_lanes = jnp.where(low, 1.0, 0.0).astype(jnp.bfloat16), jnp.where(low, 0.0, 1.0).astype(jnp.bfloat16)
    ones = jnp.concatenate(head_lanes * 2, axis=0)
    keys_before = [jnp.concatenate(doubled(before_ref[:, :LANES], head), axis=0) for head in range(kv_heads)]
    values_before = [doubled(before_ref[:, LANES:], head) for head in range(kv_heads)]
    contract = (((1,), (1,)), ((), ()))
    for head in range(kv_heads):
        keys = jnp.concatenate(doubled(kv_ref[:, :LANES], head), axis=0)
        values = jnp.concatenate(doubled(kv_ref[:, LANES:], head) + values_before[head], axis=0)
        values = jnp.concatenate([values, ones], axis=1)
        for j in range(head * pairs, (head + 1) * pairs):
            q = q_ref[:, j * LANES : (j + 1) * LANES]
            near = lax.dot_general(q, keys, contract, preferred_element_type=jnp.float32)
            far = lax.dot_general(q, keys_before[head], contract, preferred_element_type=jnp.float32)
            terms, sinks = [], []
            for at in range(2):
                span = slice(at * tokens, (at + 1) * tokens)
                part = jnp.where(own, near[:, span], far[:, span])
                sink = sink_ref[2 * j + at : 2 * j + at + 1, :]
                top = jnp.maximum(jnp.max(part, axis=1, keepdims=True), sink)
                terms.append(jnp.exp(part - top).astype(jnp.bfloat16))
                sinks.append(jnp.exp(sink - top))
            kept = [term * own_factor for term in terms] + [term * before_factor for term in terms]
            found = jnp.dot(jnp.concatenate(kept, axis=1), values, preferred_element_type=jnp.float32)
            total = found[:, LANES:] + jnp.where(low, sinks[0], sinks[1])
            att_ref[:, j * LANES : (j + 1) * LANES] = (found[:, :LANES] / total).astype(jnp.bfloat16)
        w_loads[head].wait()
        step = 2 * LANES
        for at in range(0, out_ref.shape[1], step):
            part = jnp.dot(
                att_ref[:, head * depth : (head + 1) * depth],
                w_ref[head * depth : (head + 1) * depth, at : at + step],
                preferred_element_type=jnp.float32,
            )
            if head > 0:
                part += sum_ref[:, at : at + step]
            if head < kv_heads - 1:
                sum_ref[:, at : at + step] = part
            else:
                out_ref[:, at : at + step] = part.astype(jnp.bfloat16)


def attention(first, sinks, q, key_values, before, w_out):
    tokens = q.shape[0]
    return pl.pallas_call(
        attention_kernel,
        out_shape=shape_of((tokens, w_out.shape[1])),
        in_specs=[SMEM, VMEM, VMEM, VMEM, VMEM, HBM],
        out_specs=VMEM,
        scratch_shapes=[
            pltpu.VMEM(w_out.shape, jnp.bfloat16),
            pltpu.VMEM(q.shape, jnp.bfloat16),
            pltpu.VMEM((tokens, w_out.shape[1]), jnp.float32),
            pltpu.SemaphoreType.DMA((key_values.shape[1] // (2 * HEAD_SIZE),)),
        ],
        compiler_params=pltpu.CompilerParams(vmem_limit_bytes=54_000_000),
        cost_estimate=cost(2 * tokens * w_out.size * 2, 2 * w_out.size, tokens * tokens * q.shape[1] // HEAD_SIZE),
        name="attention",
    )(first, sinks, q, key_values, before, w_out)


def pack(placed, normed, out_ref):
    rows, tokens = out_ref.shape[0], normed.shape[0]
    row = iota((rows, tokens), 0)
    taken = placed[0:1, :] == row
    for c in range(1, placed.shape[0]):
        taken = taken | (placed[c : c + 1, :] == row)
    taken = jnp.where(taken, 1.0, 0.0).astype(jnp.bfloat16)
    out_ref[...] = jnp.dot(taken, normed, preferred_element_type=jnp.float32).astype(jnp.bfloat16)


def norm_kernel(side_ref, residual_ref, near_ref, far_ref, gain_ref, normed_ref, sent_ref, kept_ref, whole_ref):
    side = side_ref[0]
    half_tokens, half = sent_ref.shape[0], kept_ref.shape[1]
    added = near_ref[...].astype(jnp.float32) + far_ref[...].astype(jnp.float32)
    whole = (residual_ref[...].astype(jnp.float32) + added).astype(jnp.bfloat16)
    whole_ref[...] = whole
    wide = whole.astype(jnp.float32)
    mean_square = jnp.mean(wide * wide, axis=1, keepdims=True)
    normed_ref[...] = (wide * lax.rsqrt(mean_square + epsilon) * gain_ref[...]).astype(jnp.bfloat16)
    kept_ref[...] = whole_ref[:, pl.ds(pl.multiple_of(side * half, LANES), half)]
    sent_ref[...] = normed_ref[pl.ds(pl.multiple_of(side * half_tokens, half_tokens), half_tokens), :]


def norm(side, residual_in, near, far, gain, half):
    tokens, width = residual_in.shape
    return pl.pallas_call(
        norm_kernel,
        out_shape=(shape_of((tokens, width)), shape_of((tokens // 2, width)), shape_of((tokens, half))),
        in_specs=[SMEM] + [VMEM] * 4,
        out_specs=(VMEM, VMEM, VMEM),
        scratch_shapes=[pltpu.VMEM((tokens, width), jnp.bfloat16)],
        compiler_params=pltpu.CompilerParams(vmem_limit_bytes=24 * MIB),
        cost_estimate=cost(8 * tokens * width, 10 * tokens * width),
        name="norm",
    )(side, residual_in, near, far, gain.reshape(1, width))


def pack_kernel(experts, side_rows, base_ref, side_ref, notes_ref, *refs):
    *part_refs, out_ref, rows_ref, arrived_ref = refs
    side, top_count = side_ref[0], rows_ref.shape[0]
    if len(part_refs) == 1:
        arrived_ref = part_refs[0]
    else:
        mine_ref, other_ref = part_refs
        part = mine_ref.shape[0]
        arrived_ref[pl.ds(pl.multiple_of(side * part, part), part), :] = mine_ref[...]
        arrived_ref[pl.ds(pl.multiple_of((1 - side) * part, part), part), :] = other_ref[...]
    rows = rows_of(notes_ref[:top_count, :], experts, side_rows, base_ref[0], side)
    rows_ref[...] = rows
    pack(rows, arrived_ref[...], out_ref)


def packed_rows(base, side, notes, parts, experts, side_rows, rows):
    tokens = sum([part.shape[0] for part in parts])
    width = parts[0].shape[1]
    return pl.pallas_call(
        functools.partial(pack_kernel, experts, side_rows),
        out_shape=(shape_of((rows, width)), shape_of((notes.shape[0] // 2, tokens), jnp.int32)),
        in_specs=[SMEM, SMEM, VMEM] + [VMEM] * len(parts),
        out_specs=(VMEM, VMEM),
        scratch_shapes=[pltpu.VMEM((tokens, width), jnp.bfloat16)],
        compiler_params=pltpu.CompilerParams(vmem_limit_bytes=24 * MIB),
        cost_estimate=cost(2 * rows * tokens * width, 2 * rows * width),
        name="packed_rows",
    )(base, side, notes, *parts)


def expert_kernel(
    x_hbm, gate_hbm, up_hbm, down_hbm, gate_too_hbm, up_too_hbm, down_too_hbm, y_hbm, x_ref, y_ref, gate_ref, up_ref,
    down_ref, hidden_ref, gate_sum, up_sum, total_ref, x_sem, y_sem, gate_sem, up_sem, down_sem,
):
    rows, width = x_ref.shape
    share = gate_hbm.shape[2]
    deep, cuts = width // CUTS, share // DEEP
    loads = []
    for k, (gate, up) in enumerate([(gate_hbm, up_hbm), (gate_too_hbm, up_too_hbm)]):
        for c in range(CUTS):
            span = pl.ds(c * deep, deep)
            loads.append(
                [
                    pltpu.make_async_copy(gate.at[0, span], gate_ref.at[k, span], gate_sem.at[k, c]),
                    pltpu.make_async_copy(up.at[0, span], up_ref.at[k, span], up_sem.at[k, c]),
                ]
            )
    for k, down in enumerate([down_hbm, down_too_hbm]):
        for c in range(cuts):
            source, target = pl.ds(c * DEEP, DEEP), pl.ds(k * share + c * DEEP, DEEP)
            loads.append([pltpu.make_async_copy(down.at[0, source], down_ref.at[target], down_sem.at[k, c])])

    def start(number):
        if number < len(loads):
            for load in loads[number]:
                load.start()

    def arrive(number):
        for load in loads[number]:
            load.wait()
        start(number + AHEAD)

    x_load = pltpu.make_async_copy(x_hbm, x_ref, x_sem)
    x_load.start()
    for number in range(AHEAD):
        start(number)
    x_load.wait()
    for k in range(2):
        for c in range(CUTS):
            arrive(k * CUTS + c)
            span = slice(c * deep, (c + 1) * deep)
            x = x_ref[:, span]
            gate = jnp.dot(x, gate_ref[k, span, :], preferred_element_type=jnp.float32)
            up = jnp.dot(x, up_ref[k, span, :], preferred_element_type=jnp.float32)
            if c > 0:
                gate, up = gate_sum[...] + gate, up_sum[...] + up
            if c < CUTS - 1:
                gate_sum[...], up_sum[...] = gate, up
            else:
                hidden = gate * (0.5 + 0.5 * jnp.tanh(0.5 * gate)) * up
                hidden_ref[:, k * share : (k + 1) * share] = hidden.astype(jnp.bfloat16)
    for c in range(2 * cuts - 1):
        arrive(2 * CUTS + c)
        span = slice(c * DEEP, (c + 1) * DEEP)
        part = jnp.dot(hidden_ref[:, span], down_ref[span, :], preferred_element_type=jnp.float32)
        total_ref[...] = part if c == 0 else total_ref[...] + part
    arrive(2 * CUTS + 2 * cuts - 1)
    span = slice((2 * cuts - 1) * DEEP, 2 * cuts * DEEP)
    step = 2 * LANES
    stores = []
    for i in range(width // step):
        columns = slice(i * step, (i + 1) * step)
        part = jnp.dot(hidden_ref[:, span], down_ref[span, columns], preferred_element_type=jnp.float32)
        y_ref[:, columns] = (total_ref[:, columns] + part).astype(jnp.bfloat16)
        column_span = pl.ds(i * step, step)
        stores.append(pltpu.make_async_copy(y_ref.at[:, column_span], y_hbm.at[:, column_span], y_sem.at[i]))
        stores[i].start()
    for store in stores:
        store.wait()


def expert_layer(x, mine, others):
    rows, width = x.shape
    share = mine[0].shape[2]
    return pl.pallas_call(
        expert_kernel,
        out_shape=shape_of((rows, width)),
        in_specs=[HBM] * 7,
        out_specs=HBM,
        scratch_shapes=[
            pltpu.VMEM((rows, width), jnp.bfloat16),
            pltpu.VMEM((rows, width), jnp.bfloat16),
            pltpu.VMEM((2, width, share), jnp.bfloat16),
            pltpu.VMEM((2, width, share), jnp.bfloat16),
            pltpu.VMEM((2 * share, width), jnp.bfloat16),
            pltpu.VMEM((rows, 2 * share), jnp.bfloat16),
            pltpu.VMEM((rows, share), jnp.float32),
            pltpu.VMEM((rows, share), jnp.float32),
            pltpu.VMEM((rows, width), jnp.float32),
            pltpu.SemaphoreType.DMA,
            pltpu.SemaphoreType.DMA((width // (2 * LANES),)),
            pltpu.SemaphoreType.DMA((2, CUTS)),
            pltpu.SemaphoreType.DMA((2, CUTS)),
            pltpu.SemaphoreType.DMA((2, share // DEEP)),
        ],
        compiler_params=pltpu.CompilerParams(vmem_limit_bytes=60 * MIB),
        cost_estimate=cost(12 * rows * width * share, 12 * width * share, 2 * rows * share),
        name="expert_layer",
    )(x, *mine, *others)


def combine_kernel(side_ref, rows_ref, weights_ref, y_ref, *refs):
    *more_refs, mine_ref, sent_ref, total_ref = refs
    top_count, tokens = rows_ref.shape
    half = mine_ref.shape[1]
    row = iota((y_ref.shape[0], tokens), 0)
    share = jnp.zeros(row.shape, jnp.float32)
    for c in range(top_count):
        share = jnp.where(rows_ref[c : c + 1, :] == row, weights_ref[top_count + c : top_count + c + 1, :], share)
    coarse = share.astype(jnp.bfloat16)
    fine = (share - coarse.astype(jnp.float32)).astype(jnp.bfloat16)
    y = y_ref[...]
    contract = (((0,), (0,)), ((), ()))
    total_ref[...] = lax.dot_general(coarse, y, contract, preferred_element_type=jnp.float32)
    total_ref[...] += lax.dot_general(fine, y, contract, preferred_element_type=jnp.float32)
    side = side_ref[0]
    mine = total_ref[:, pl.ds(pl.multiple_of(side * half, LANES), half)]
    for more_ref in more_refs:
        mine += more_ref[...].astype(jnp.float32)
    mine_ref[...] = mine
    sent_ref[...] = total_ref[:, pl.ds(pl.multiple_of((1 - side) * half, LANES), half)].astype(jnp.bfloat16)


def combine(side, placed, weights, y, half, more=()):
    tokens = placed.shape[1]
    rows, width = y.shape
    return pl.pallas_call(
        combine_kernel,
        out_shape=(shape_of((tokens, half), jnp.float32), shape_of((tokens, half))),
        in_specs=[SMEM] + [VMEM] * (3 + len(more)),
        out_specs=(VMEM, VMEM),
        scratch_shapes=[pltpu.VMEM((tokens, width), jnp.float32)],
        compiler_params=pltpu.CompilerParams(vmem_limit_bytes=24 * MIB),
        cost_estimate=cost(4 * rows * tokens * width, 2 * rows * width),
        name="combine",
    )(side, placed, weights, y, *more)


def local(
    residual_in,
    query_rows,
    rotated_key_rows,
    value_row_matrix,
    learned_sink_scores,
    w_out,
    norm_gain,
    expert_ids,
    route_weights,
    w_gate,
    w_up,
    w_down,
):
    tok_dev, model_width = residual_in.shape
    seq_count = lax.axis_size("seq")
    experts = w_gate.shape[0] * seq_count
    capacity = max(2, 8 * tok_dev // experts)
    sides = lax.axis_size("tp")
    side_rows = capacity // sides
    group = seq_count // 2
    rows = experts // 2 * side_rows
    half = model_width // sides
    at_seq = lax.axis_index("seq").astype(jnp.int32)
    base = jnp.where(at_seq < group, 0, experts // 2).astype(jnp.int32).reshape(1)
    side = lax.axis_index("tp").astype(jnp.int32).reshape(1)
    first = (at_seq == 0).astype(jnp.int32).reshape(1)
    key_values = lax.optimization_barrier(jnp.concatenate([rotated_key_rows, value_row_matrix], axis=1))
    before = passed_along(key_values, "seq", 1)
    sinks = jnp.broadcast_to(learned_sink_scores[:, None], (learned_sink_scores.shape[0], LANES))
    sinks, queries = lax.optimization_barrier((sinks, query_rows))
    scaled = queries * jnp.bfloat16(HEAD_SIZE**-0.5)
    weights = (w_gate, w_up, w_down)
    others = [swapped(weight, "tp") for weight in weights[:2]]
    near = attention(
        first, sinks, scaled, key_values, before, w_out
    )
    far, late = lax.optimization_barrier((swapped(near, "tp"), w_down))
    others.append(swapped(late, "tp"))
    normed, sent, kept = norm(side, residual_in, near, far, norm_gain, half)

    def exchanged(block):
        block = block.reshape(group, rows // group, model_width)
        groups = [list(range(group)), list(range(group, seq_count))]
        block = lax.all_to_all(
            block, "seq", split_axis=0, concat_axis=0, axis_index_groups=groups, tiled=True
        )
        return block.reshape(rows, model_width)

    notes = jnp.concatenate([expert_ids.T.astype(jnp.float32), route_weights.T], axis=0)
    crossed = swapped_halves(sent, "seq")
    notes_peer = swapped_halves(notes, "seq")
    packed, placed = packed_rows(base, side, notes, (normed,), experts, side_rows, rows)
    crossed, notes_peer, packed = lax.optimization_barrier((crossed, notes_peer, packed))
    packed_peer, placed_peer = packed_rows(
        base, side, notes_peer, (crossed, swapped(crossed, "tp")), experts, side_rows, rows
    )
    arrived_peer = exchanged(packed_peer)
    arrived_peer, packed, *others = lax.optimization_barrier((arrived_peer, packed, *others))
    arrived = exchanged(packed)
    result_peer = expert_layer(arrived_peer, weights, others)
    result_peer, arrived = lax.optimization_barrier((result_peer, arrived))
    result = expert_layer(arrived, weights, others)

    returned_peer = exchanged(result_peer)
    result, returned_peer = lax.optimization_barrier((result, returned_peer))
    returned = exchanged(result)
    mine_peer, sent_peer = combine(side, placed_peer, notes_peer, returned_peer, half)
    summed_peer = (mine_peer + swapped(sent_peer, "tp").astype(jnp.float32)).astype(jnp.bfloat16)
    back = swapped_halves(summed_peer, "seq")
    mine, sent = combine(side, placed, notes, returned, half, (kept,))
    sent, back = lax.optimization_barrier((sent, back))
    return (mine + swapped(sent, "tp").astype(jnp.float32) + back.astype(jnp.float32)).astype(jnp.bfloat16)


def solution(mesh):
    placed = (
        P("seq", None),
        P("seq", "tp"),
        P("seq", "tp"),
        P("seq", "tp"),
        P("tp"),
        P("tp", None),
        P(),
        P("seq", None),
        P("seq", None),
        P("seq", None, "tp"),
        P("seq", None, "tp"),
        P("seq", "tp", None),
    )
    return jax.shard_map(
        local, mesh=mesh, in_specs=placed, out_specs=P("seq", "tp"), check_vma=False
    )
```

```python
import functools

import jax
import jax.numpy as jnp
from jax import lax
from jax.experimental import pallas as pl
from jax.experimental.pallas import tpu as pltpu
from jax.sharding import PartitionSpec as P

HEAD_SIZE = 64
WINDOW_LENGTH = 128
LANES = 128
MIB = 1024 * 1024
CUTS = 3
DEEP = 256
AHEAD = 3

epsilon = 1e-05

VMEM = pl.BlockSpec(memory_space=pltpu.VMEM)
SMEM = pl.BlockSpec(memory_space=pltpu.SMEM)
HBM = pl.BlockSpec(memory_space=pltpu.HBM)


def passed_along(block, axis, distance):
    devices = range(lax.axis_size(axis))
    route = [(i - distance, i) for i in devices if i - distance in devices]
    return lax.ppermute(block, axis, route)


def swapped(block, axis):
    count = lax.axis_size(axis)
    return lax.ppermute(block, axis, [(i, count - 1 - i) for i in range(count)])


def swapped_halves(block, axis):
    count = lax.axis_size(axis)
    return lax.ppermute(block, axis, [(i, (i + count // 2) % count) for i in range(count)])


def shape_of(dims, dtype=jnp.bfloat16):
    return jax.ShapeDtypeStruct(dims, dtype)


def cost(flops, moved, transcendentals=0):
    return pl.CostEstimate(flops=flops, bytes_accessed=moved, transcendentals=transcendentals)


def iota(dims, dimension):
    return lax.broadcasted_iota(jnp.int32, dims, dimension)


def rows_of(ids, experts, side_rows, base, side):
    top_count, tokens = ids.shape
    names = iota((experts, tokens), 0).astype(jnp.float32)
    hits = [ids[c : c + 1, :] == names for c in range(top_count)]
    named = sum([hit.astype(jnp.float32) for hit in hits]).astype(jnp.bfloat16)
    square = (tokens, tokens)
    earlier = (iota(square, 0) < iota(square, 1)).astype(jnp.bfloat16)
    slot = jnp.dot(named, earlier, preferred_element_type=jnp.float32) - (side * side_rows).astype(jnp.float32)
    expert = names - base.astype(jnp.float32)
    here = (slot >= 0.0) & (slot < side_rows) & (expert >= 0.0) & (expert < experts // 2)
    rows = jnp.where(here, expert * side_rows + slot, -1.0)
    lines = [jnp.sum(jnp.where(hit, rows, 0.0), axis=0, keepdims=True) for hit in hits]
    return jnp.concatenate(lines, axis=0).astype(jnp.int32)


def attention_kernel(
    first_ref, sink_ref, q_ref, kv_ref, before_ref, w_hbm, out_ref, w_ref, att_ref, sum_ref, sems
):
    tokens, width = q_ref.shape
    kv_heads = kv_ref.shape[1] // HEAD_SIZE
    pairs = width // LANES // kv_heads
    depth = pairs * LANES
    spans = [pl.ds(head * depth, depth) for head in range(kv_heads)]
    w_loads = [pltpu.make_async_copy(w_hbm.at[span], w_ref.at[span], sems.at[i]) for i, span in enumerate(spans)]
    for load in w_loads:
        load.start()
    low = iota((tokens, LANES), 1) < HEAD_SIZE

    def doubled(block, head):
        wide = block.astype(jnp.float32)
        turned = pltpu.roll(wide, HEAD_SIZE, 1)
        first, second = (wide, turned) if head == 0 else (turned, wide)
        return [
            jnp.where(low, first, 0.0).astype(jnp.bfloat16),
            jnp.where(low, 0.0, second).astype(jnp.bfloat16),
        ]

    own = iota((tokens, tokens), 1) <= iota((tokens, tokens), 0)
    usable = jnp.where(first_ref[0] == 0, 1.0, 0.0)
    own_factor = jnp.where(own, 1.0, 0.0).astype(jnp.bfloat16)
    before_factor = jnp.where(own, 0.0, usable).astype(jnp.bfloat16)
    head_lanes = jnp.where(low, 1.0, 0.0).astype(jnp.bfloat16), jnp.where(low, 0.0, 1.0).astype(jnp.bfloat16)
    ones = jnp.concatenate(head_lanes * 2, axis=0)
    keys_before = [jnp.concatenate(doubled(before_ref[:tokens, :], head), axis=0) for head in range(kv_heads)]
    values_before = [doubled(before_ref[tokens:, :], head) for head in range(kv_heads)]
    contract = (((1,), (1,)), ((), ()))
    for head in range(kv_heads):
        keys = jnp.concatenate(doubled(kv_ref[:tokens, :], head), axis=0)
        values = jnp.concatenate(doubled(kv_ref[tokens:, :], head) + values_before[head], axis=0)
        values = jnp.concatenate([values, ones], axis=1)
        for j in range(head * pairs, (head + 1) * pairs):
            q = q_ref[:, j * LANES : (j + 1) * LANES]
            near = lax.dot_general(q, keys, contract, preferred_element_type=jnp.float32)
            far = lax.dot_general(q, keys_before[head], contract, preferred_element_type=jnp.float32)
            terms, sinks = [], []
            for at in range(2):
                span = slice(at * tokens, (at + 1) * tokens)
                part = jnp.where(own, near[:, span], far[:, span])
                sink = sink_ref[2 * j + at : 2 * j + at + 1, :]
                top = jnp.maximum(jnp.max(part, axis=1, keepdims=True), sink)
                terms.append(jnp.exp(part - top).astype(jnp.bfloat16))
                sinks.append(jnp.exp(sink - top))
            kept = [term * own_factor for term in terms] + [term * before_factor for term in terms]
            found = jnp.dot(jnp.concatenate(kept, axis=1), values, preferred_element_type=jnp.float32)
            total = found[:, LANES:] + jnp.where(low, sinks[0], sinks[1])
            att_ref[:, j * LANES : (j + 1) * LANES] = (found[:, :LANES] / total).astype(jnp.bfloat16)
        w_loads[head].wait()
        step = 2 * LANES
        for at in range(0, out_ref.shape[1], step):
            part = jnp.dot(
                att_ref[:, head * depth : (head + 1) * depth],
                w_ref[head * depth : (head + 1) * depth, at : at + step],
                preferred_element_type=jnp.float32,
            )
            if head > 0:
                part += sum_ref[:, at : at + step]
            if head < kv_heads - 1:
                sum_ref[:, at : at + step] = part
            else:
                out_ref[:, at : at + step] = part.astype(jnp.bfloat16)


def attention(first, sinks, q, key_values, before, w_out):
    tokens = q.shape[0]
    return pl.pallas_call(
        attention_kernel,
        out_shape=shape_of((tokens, w_out.shape[1])),
        in_specs=[SMEM, VMEM, VMEM, VMEM, VMEM, HBM],
        out_specs=VMEM,
        scratch_shapes=[
            pltpu.VMEM(w_out.shape, jnp.bfloat16),
            pltpu.VMEM(q.shape, jnp.bfloat16),
            pltpu.VMEM((tokens, w_out.shape[1]), jnp.float32),
            pltpu.SemaphoreType.DMA((key_values.shape[1] // HEAD_SIZE,)),
        ],
        compiler_params=pltpu.CompilerParams(vmem_limit_bytes=54_000_000),
        cost_estimate=cost(2 * tokens * w_out.size * 2, 2 * w_out.size, tokens * tokens * q.shape[1] // HEAD_SIZE),
        name="attention",
    )(first, sinks, q, key_values, before, w_out)


def pack(placed, normed, out_ref):
    rows, tokens = out_ref.shape[0], normed.shape[0]
    row = iota((rows, tokens), 0)
    taken = placed[0:1, :] == row
    for c in range(1, placed.shape[0]):
        taken = taken | (placed[c : c + 1, :] == row)
    taken = jnp.where(taken, 1.0, 0.0).astype(jnp.bfloat16)
    out_ref[...] = jnp.dot(taken, normed, preferred_element_type=jnp.float32).astype(jnp.bfloat16)


def norm_kernel(side_ref, residual_ref, near_ref, far_ref, gain_ref, normed_ref, sent_ref, kept_ref, whole_ref):
    side = side_ref[0]
    half_tokens, half = sent_ref.shape[0], kept_ref.shape[1]
    added = near_ref[...].astype(jnp.float32) + far_ref[...].astype(jnp.float32)
    whole = (residual_ref[...].astype(jnp.float32) + added).astype(jnp.bfloat16)
    whole_ref[...] = whole
    wide = whole.astype(jnp.float32)
    mean_square = jnp.mean(wide * wide, axis=1, keepdims=True)
    normed_ref[...] = (wide * lax.rsqrt(mean_square + epsilon) * gain_ref[...]).astype(jnp.bfloat16)
    kept_ref[...] = whole_ref[:, pl.ds(pl.multiple_of(side * half, LANES), half)]
    sent_ref[...] = normed_ref[pl.ds(pl.multiple_of(side * half_tokens, half_tokens), half_tokens), :]


def norm(side, residual_in, near, far, gain, half):
    tokens, width = residual_in.shape
    return pl.pallas_call(
        norm_kernel,
        out_shape=(shape_of((tokens, width)), shape_of((tokens // 2, width)), shape_of((tokens, half))),
        in_specs=[SMEM] + [VMEM] * 4,
        out_specs=(VMEM, VMEM, VMEM),
        scratch_shapes=[pltpu.VMEM((tokens, width), jnp.bfloat16)],
        compiler_params=pltpu.CompilerParams(vmem_limit_bytes=24 * MIB),
        cost_estimate=cost(8 * tokens * width, 10 * tokens * width),
        name="norm",
    )(side, residual_in, near, far, gain.reshape(1, width))


def pack_kernel(experts, side_rows, base_ref, side_ref, notes_ref, *refs):
    *part_refs, out_ref, rows_ref, arrived_ref = refs
    side, top_count = side_ref[0], rows_ref.shape[0]
    if len(part_refs) == 1:
        arrived_ref = part_refs[0]
    else:
        mine_ref, other_ref = part_refs
        part = mine_ref.shape[0]
        arrived_ref[pl.ds(pl.multiple_of(side * part, part), part), :] = mine_ref[...]
        arrived_ref[pl.ds(pl.multiple_of((1 - side) * part, part), part), :] = other_ref[...]
    rows = rows_of(notes_ref[:top_count, :], experts, side_rows, base_ref[0], side)
    rows_ref[...] = rows
    pack(rows, arrived_ref[...], out_ref)


def packed_rows(base, side, notes, parts, experts, side_rows, rows):
    tokens = sum([part.shape[0] for part in parts])
    width = parts[0].shape[1]
    return pl.pallas_call(
        functools.partial(pack_kernel, experts, side_rows),
        out_shape=(shape_of((rows, width)), shape_of((notes.shape[0] // 2, tokens), jnp.int32)),
        in_specs=[SMEM, SMEM, VMEM] + [VMEM] * len(parts),
        out_specs=(VMEM, VMEM),
        scratch_shapes=[pltpu.VMEM((tokens, width), jnp.bfloat16)],
        compiler_params=pltpu.CompilerParams(vmem_limit_bytes=24 * MIB),
        cost_estimate=cost(2 * rows * tokens * width, 2 * rows * width),
        name="packed_rows",
    )(base, side, notes, *parts)


def expert_kernel(
    x_hbm, gate_hbm, up_hbm, down_hbm, gate_too_hbm, up_too_hbm, down_too_hbm, y_hbm, x_ref, y_ref, gate_ref, up_ref,
    down_ref, hidden_ref, gate_sum, up_sum, total_ref, x_sem, y_sem, gate_sem, up_sem, down_sem,
):
    rows, width = x_ref.shape
    share = gate_hbm.shape[2]
    deep, cuts = width // CUTS, share // DEEP
    loads = []
    for k, (gate, up) in enumerate([(gate_hbm, up_hbm), (gate_too_hbm, up_too_hbm)]):
        for c in range(CUTS):
            span = pl.ds(c * deep, deep)
            loads.append(
                [
                    pltpu.make_async_copy(gate.at[0, span], gate_ref.at[k, span], gate_sem.at[k, c]),
                    pltpu.make_async_copy(up.at[0, span], up_ref.at[k, span], up_sem.at[k, c]),
                ]
            )
    for k, down in enumerate([down_hbm, down_too_hbm]):
        for c in range(cuts):
            source, target = pl.ds(c * DEEP, DEEP), pl.ds(k * share + c * DEEP, DEEP)
            loads.append([pltpu.make_async_copy(down.at[0, source], down_ref.at[target], down_sem.at[k, c])])

    def start(number):
        if number < len(loads):
            for load in loads[number]:
                load.start()

    def arrive(number):
        for load in loads[number]:
            load.wait()
        start(number + AHEAD)

    x_load = pltpu.make_async_copy(x_hbm, x_ref, x_sem)
    x_load.start()
    for number in range(AHEAD):
        start(number)
    x_load.wait()
    for k in range(2):
        for c in range(CUTS):
            arrive(k * CUTS + c)
            span = slice(c * deep, (c + 1) * deep)
            x = x_ref[:, span]
            gate = jnp.dot(x, gate_ref[k, span, :], preferred_element_type=jnp.float32)
            up = jnp.dot(x, up_ref[k, span, :], preferred_element_type=jnp.float32)
            if c > 0:
                gate, up = gate_sum[...] + gate, up_sum[...] + up
            if c < CUTS - 1:
                gate_sum[...], up_sum[...] = gate, up
            else:
                hidden = gate * (0.5 + 0.5 * jnp.tanh(0.5 * gate)) * up
                hidden_ref[:, k * share : (k + 1) * share] = hidden.astype(jnp.bfloat16)
    for c in range(2 * cuts - 1):
        arrive(2 * CUTS + c)
        span = slice(c * DEEP, (c + 1) * DEEP)
        part = jnp.dot(hidden_ref[:, span], down_ref[span, :], preferred_element_type=jnp.float32)
        total_ref[...] = part if c == 0 else total_ref[...] + part
    arrive(2 * CUTS + 2 * cuts - 1)
    span = slice((2 * cuts - 1) * DEEP, 2 * cuts * DEEP)
    step = 2 * LANES
    stores = []
    for i in range(width // step):
        columns = slice(i * step, (i + 1) * step)
        part = jnp.dot(hidden_ref[:, span], down_ref[span, columns], preferred_element_type=jnp.float32)
        y_ref[:, columns] = (total_ref[:, columns] + part).astype(jnp.bfloat16)
        column_span = pl.ds(i * step, step)
        stores.append(pltpu.make_async_copy(y_ref.at[:, column_span], y_hbm.at[:, column_span], y_sem.at[i]))
        stores[i].start()
    for store in stores:
        store.wait()


def expert_layer(x, mine, others):
    rows, width = x.shape
    share = mine[0].shape[2]
    return pl.pallas_call(
        expert_kernel,
        out_shape=shape_of((rows, width)),
        in_specs=[HBM] * 7,
        out_specs=HBM,
        scratch_shapes=[
            pltpu.VMEM((rows, width), jnp.bfloat16),
            pltpu.VMEM((rows, width), jnp.bfloat16),
            pltpu.VMEM((2, width, share), jnp.bfloat16),
            pltpu.VMEM((2, width, share), jnp.bfloat16),
            pltpu.VMEM((2 * share, width), jnp.bfloat16),
            pltpu.VMEM((rows, 2 * share), jnp.bfloat16),
            pltpu.VMEM((rows, share), jnp.float32),
            pltpu.VMEM((rows, share), jnp.float32),
            pltpu.VMEM((rows, width), jnp.float32),
            pltpu.SemaphoreType.DMA,
            pltpu.SemaphoreType.DMA((width // (2 * LANES),)),
            pltpu.SemaphoreType.DMA((2, CUTS)),
            pltpu.SemaphoreType.DMA((2, CUTS)),
            pltpu.SemaphoreType.DMA((2, share // DEEP)),
        ],
        compiler_params=pltpu.CompilerParams(vmem_limit_bytes=60 * MIB),
        cost_estimate=cost(12 * rows * width * share, 12 * width * share, 2 * rows * share),
        name="expert_layer",
    )(x, *mine, *others)


def combine_kernel(side_ref, rows_ref, weights_ref, y_ref, *refs):
    *more_refs, mine_ref, sent_ref, total_ref = refs
    top_count, tokens = rows_ref.shape
    half = mine_ref.shape[1]
    row = iota((y_ref.shape[0], tokens), 0)
    share = jnp.zeros(row.shape, jnp.float32)
    for c in range(top_count):
        share = jnp.where(rows_ref[c : c + 1, :] == row, weights_ref[top_count + c : top_count + c + 1, :], share)
    coarse = share.astype(jnp.bfloat16)
    fine = (share - coarse.astype(jnp.float32)).astype(jnp.bfloat16)
    y = y_ref[...]
    contract = (((0,), (0,)), ((), ()))
    total_ref[...] = lax.dot_general(coarse, y, contract, preferred_element_type=jnp.float32)
    total_ref[...] += lax.dot_general(fine, y, contract, preferred_element_type=jnp.float32)
    side = side_ref[0]
    mine = total_ref[:, pl.ds(pl.multiple_of(side * half, LANES), half)]
    for more_ref in more_refs:
        mine += more_ref[...].astype(jnp.float32)
    mine_ref[...] = mine
    sent_ref[...] = total_ref[:, pl.ds(pl.multiple_of((1 - side) * half, LANES), half)].astype(jnp.bfloat16)


def combine(side, placed, weights, y, half, more=()):
    tokens = placed.shape[1]
    rows, width = y.shape
    return pl.pallas_call(
        combine_kernel,
        out_shape=(shape_of((tokens, half), jnp.float32), shape_of((tokens, half))),
        in_specs=[SMEM] + [VMEM] * (3 + len(more)),
        out_specs=(VMEM, VMEM),
        scratch_shapes=[pltpu.VMEM((tokens, width), jnp.float32)],
        compiler_params=pltpu.CompilerParams(vmem_limit_bytes=24 * MIB),
        cost_estimate=cost(4 * rows * tokens * width, 2 * rows * width),
        name="combine",
    )(side, placed, weights, y, *more)


def local(
    residual_in,
    query_rows,
    rotated_key_rows,
    value_row_matrix,
    learned_sink_scores,
    w_out,
    norm_gain,
    expert_ids,
    route_weights,
    w_gate,
    w_up,
    w_down,
):
    tok_dev, model_width = residual_in.shape
    seq_count = lax.axis_size("seq")
    experts = w_gate.shape[0] * seq_count
    capacity = max(2, 8 * tok_dev // experts)
    sides = lax.axis_size("tp")
    side_rows = capacity // sides
    group = seq_count // 2
    rows = experts // 2 * side_rows
    half = model_width // sides
    at_seq = lax.axis_index("seq").astype(jnp.int32)
    base = jnp.where(at_seq < group, 0, experts // 2).astype(jnp.int32).reshape(1)
    side = lax.axis_index("tp").astype(jnp.int32).reshape(1)
    first = (at_seq == 0).astype(jnp.int32).reshape(1)
    key_values = lax.optimization_barrier(jnp.concatenate([rotated_key_rows, value_row_matrix], axis=0))
    before = passed_along(key_values, "seq", 1)
    sinks = jnp.broadcast_to(learned_sink_scores[:, None], (learned_sink_scores.shape[0], LANES))
    sinks, queries = lax.optimization_barrier((sinks, query_rows))
    scaled = queries * jnp.bfloat16(HEAD_SIZE**-0.5)
    weights = (w_gate, w_up, w_down)
    others = [swapped(weight, "tp") for weight in weights[:2]]
    near = attention(
        first, sinks, scaled, key_values, before, w_out
    )
    far, late = lax.optimization_barrier((swapped(near, "tp"), w_down))
    others.append(swapped(late, "tp"))
    normed, sent, kept = norm(side, residual_in, near, far, norm_gain, half)

    def exchanged(block):
        block = block.reshape(group, rows // group, model_width)
        groups = [list(range(group)), list(range(group, seq_count))]
        block = lax.all_to_all(
            block, "seq", split_axis=0, concat_axis=0, axis_index_groups=groups, tiled=True
        )
        return block.reshape(rows, model_width)

    notes = jnp.concatenate([expert_ids.T.astype(jnp.float32), route_weights.T], axis=0)
    crossed = swapped_halves(sent, "seq")
    notes_peer = swapped_halves(notes, "seq")
    packed, placed = packed_rows(base, side, notes, (normed,), experts, side_rows, rows)
    crossed, notes_peer, packed = lax.optimization_barrier((crossed, notes_peer, packed))
    packed_peer, placed_peer = packed_rows(
        base, side, notes_peer, (crossed, swapped(crossed, "tp")), experts, side_rows, rows
    )
    arrived_peer = exchanged(packed_peer)
    arrived_peer, packed, *others = lax.optimization_barrier((arrived_peer, packed, *others))
    arrived = exchanged(packed)
    result_peer = expert_layer(arrived_peer, weights, others)
    result_peer, arrived = lax.optimization_barrier((result_peer, arrived))
    result = expert_layer(arrived, weights, others)

    returned_peer = exchanged(result_peer)
    result, returned_peer = lax.optimization_barrier((result, returned_peer))
    returned = exchanged(result)
    mine_peer, sent_peer = combine(side, placed_peer, notes_peer, returned_peer, half)
    summed_peer = (mine_peer + swapped(sent_peer, "tp").astype(jnp.float32)).astype(jnp.bfloat16)
    back = swapped_halves(summed_peer, "seq")
    mine, sent = combine(side, placed, notes, returned, half, (kept,))
    sent, back = lax.optimization_barrier((sent, back))
    return (mine + swapped(sent, "tp").astype(jnp.float32) + back.astype(jnp.float32)).astype(jnp.bfloat16)


def solution(mesh):
    placed = (
        P("seq", None),
        P("seq", "tp"),
        P("seq", "tp"),
        P("seq", "tp"),
        P("tp"),
        P("tp", None),
        P(),
        P("seq", None),
        P("seq", None),
        P("seq", None, "tp"),
        P("seq", None, "tp"),
        P("seq", "tp", None),
    )
    return jax.shard_map(
        local, mesh=mesh, in_specs=placed, out_specs=P("seq", "tp"), check_vma=False
    )
```

```python
import functools

import jax
import jax.numpy as jnp
from jax import lax
from jax.experimental import pallas as pl
from jax.experimental.pallas import tpu as pltpu
from jax.sharding import PartitionSpec as P

HEAD_SIZE = 64
WINDOW_LENGTH = 128
LANES = 128
MIB = 1024 * 1024
CUTS = 3
DEEP = 256
AHEAD = 3

epsilon = 1e-05

VMEM = pl.BlockSpec(memory_space=pltpu.VMEM)
SMEM = pl.BlockSpec(memory_space=pltpu.SMEM)
HBM = pl.BlockSpec(memory_space=pltpu.HBM)


def passed_along(block, axis, distance):
    devices = range(lax.axis_size(axis))
    route = [(i - distance, i) for i in devices if i - distance in devices]
    return lax.ppermute(block, axis, route)


def swapped(block, axis):
    count = lax.axis_size(axis)
    return lax.ppermute(block, axis, [(i, count - 1 - i) for i in range(count)])


def swapped_halves(block, axis):
    count = lax.axis_size(axis)
    return lax.ppermute(block, axis, [(i, (i + count // 2) % count) for i in range(count)])


def shape_of(dims, dtype=jnp.bfloat16):
    return jax.ShapeDtypeStruct(dims, dtype)


def cost(flops, moved, transcendentals=0):
    return pl.CostEstimate(flops=flops, bytes_accessed=moved, transcendentals=transcendentals)


def iota(dims, dimension):
    return lax.broadcasted_iota(jnp.int32, dims, dimension)


def rows_of(ids, experts, side_rows, base, side):
    top_count, tokens = ids.shape
    names = iota((experts, tokens), 0).astype(jnp.float32)
    hits = [ids[c : c + 1, :] == names for c in range(top_count)]
    named = sum([hit.astype(jnp.float32) for hit in hits]).astype(jnp.bfloat16)
    square = (tokens, tokens)
    earlier = (iota(square, 0) < iota(square, 1)).astype(jnp.bfloat16)
    slot = jnp.dot(named, earlier, preferred_element_type=jnp.float32) - (side * side_rows).astype(jnp.float32)
    expert = names - base.astype(jnp.float32)
    here = (slot >= 0.0) & (slot < side_rows) & (expert >= 0.0) & (expert < experts // 2)
    rows = jnp.where(here, expert * side_rows + slot, -1.0)
    lines = [jnp.sum(jnp.where(hit, rows, 0.0), axis=0, keepdims=True) for hit in hits]
    return jnp.concatenate(lines, axis=0).astype(jnp.int32)


def attention_kernel(
    first_ref, sink_ref, q_ref, kv_ref, before_ref, w_hbm, out_ref, w_ref, att_ref, sum_ref, sems
):
    tokens, width = q_ref.shape
    kv_heads = kv_ref.shape[1] // (2 * HEAD_SIZE)
    pairs = width // LANES // kv_heads
    depth = pairs * LANES
    spans = [pl.ds(head * depth, depth) for head in range(kv_heads)]
    w_loads = [pltpu.make_async_copy(w_hbm.at[span], w_ref.at[span], sems.at[i]) for i, span in enumerate(spans)]
    for load in w_loads:
        load.start()
    low = iota((tokens, LANES), 1) < HEAD_SIZE

    def doubled(block, head):
        wide = block.astype(jnp.float32)
        turned = pltpu.roll(wide, HEAD_SIZE, 1)
        first, second = (wide, turned) if head == 0 else (turned, wide)
        return [
            jnp.where(low, first, 0.0).astype(jnp.bfloat16),
            jnp.where(low, 0.0, second).astype(jnp.bfloat16),
        ]

    own = iota((tokens, tokens), 1) <= iota((tokens, tokens), 0)
    usable = jnp.where(first_ref[0] == 0, 1.0, 0.0)
    own_factor = jnp.where(own, 1.0, 0.0).astype(jnp.bfloat16)
    before_factor = jnp.where(own, 0.0, usable).astype(jnp.bfloat16)
    head_lanes = jnp.where(low, 1.0, 0.0).astype(jnp.bfloat16), jnp.where(low, 0.0, 1.0).astype(jnp.bfloat16)
    ones = jnp.concatenate(head_lanes * 2, axis=0)
    keys_before = [jnp.concatenate(doubled(before_ref[:, :LANES], head), axis=0) for head in range(kv_heads)]
    values_before = [doubled(before_ref[:, LANES:], head) for head in range(kv_heads)]
    contract = (((1,), (1,)), ((), ()))
    for head in range(kv_heads):
        keys = jnp.concatenate(doubled(kv_ref[:, :LANES], head) + [keys_before[head]], axis=0)
        values = jnp.concatenate(doubled(kv_ref[:, LANES:], head) + values_before[head], axis=0)
        values = jnp.concatenate([values, ones], axis=1)
        for j in range(head * pairs, (head + 1) * pairs):
            q = q_ref[:, j * LANES : (j + 1) * LANES]
            scores = lax.dot_general(q, keys, contract, preferred_element_type=jnp.float32)
            near, far = scores[:, : 2 * tokens], scores[:, 2 * tokens :]
            terms, sinks = [], []
            for at in range(2):
                span = slice(at * tokens, (at + 1) * tokens)
                part = jnp.where(own, near[:, span], far[:, span])
                sink = sink_ref[2 * j + at : 2 * j + at + 1, :]
                top = jnp.maximum(jnp.max(part, axis=1, keepdims=True), sink)
                terms.append(jnp.exp(part - top).astype(jnp.bfloat16))
                sinks.append(jnp.exp(sink - top))
            kept = [term * own_factor for term in terms] + [term * before_factor for term in terms]
            found = jnp.dot(jnp.concatenate(kept, axis=1), values, preferred_element_type=jnp.float32)
            total = found[:, LANES:] + jnp.where(low, sinks[0], sinks[1])
            att_ref[:, j * LANES : (j + 1) * LANES] = (found[:, :LANES] / total).astype(jnp.bfloat16)
        w_loads[head].wait()
        step = 2 * LANES
        for at in range(0, out_ref.shape[1], step):
            part = jnp.dot(
                att_ref[:, head * depth : (head + 1) * depth],
                w_ref[head * depth : (head + 1) * depth, at : at + step],
                preferred_element_type=jnp.float32,
            )
            if head > 0:
                part += sum_ref[:, at : at + step]
            if head < kv_heads - 1:
                sum_ref[:, at : at + step] = part
            else:
                out_ref[:, at : at + step] = part.astype(jnp.bfloat16)


def attention(first, sinks, q, key_values, before, w_out):
    tokens = q.shape[0]
    return pl.pallas_call(
        attention_kernel,
        out_shape=shape_of((tokens, w_out.shape[1])),
        in_specs=[SMEM, VMEM, VMEM, VMEM, VMEM, HBM],
        out_specs=VMEM,
        scratch_shapes=[
            pltpu.VMEM(w_out.shape, jnp.bfloat16),
            pltpu.VMEM(q.shape, jnp.bfloat16),
            pltpu.VMEM((tokens, w_out.shape[1]), jnp.float32),
            pltpu.SemaphoreType.DMA((key_values.shape[1] // (2 * HEAD_SIZE),)),
        ],
        compiler_params=pltpu.CompilerParams(vmem_limit_bytes=54_000_000),
        cost_estimate=cost(2 * tokens * w_out.size * 2, 2 * w_out.size, tokens * tokens * q.shape[1] // HEAD_SIZE),
        name="attention",
    )(first, sinks, q, key_values, before, w_out)


def pack(placed, normed, out_ref):
    rows, tokens = out_ref.shape[0], normed.shape[0]
    row = iota((rows, tokens), 0)
    taken = placed[0:1, :] == row
    for c in range(1, placed.shape[0]):
        taken = taken | (placed[c : c + 1, :] == row)
    taken = jnp.where(taken, 1.0, 0.0).astype(jnp.bfloat16)
    out_ref[...] = jnp.dot(taken, normed, preferred_element_type=jnp.float32).astype(jnp.bfloat16)


def norm_kernel(side_ref, residual_ref, near_ref, far_ref, gain_ref, normed_ref, sent_ref, kept_ref, whole_ref):
    side = side_ref[0]
    half_tokens, half = sent_ref.shape[0], kept_ref.shape[1]
    added = near_ref[...].astype(jnp.float32) + far_ref[...].astype(jnp.float32)
    whole = (residual_ref[...].astype(jnp.float32) + added).astype(jnp.bfloat16)
    whole_ref[...] = whole
    wide = whole.astype(jnp.float32)
    mean_square = jnp.mean(wide * wide, axis=1, keepdims=True)
    normed_ref[...] = (wide * lax.rsqrt(mean_square + epsilon) * gain_ref[...]).astype(jnp.bfloat16)
    kept_ref[...] = whole_ref[:, pl.ds(pl.multiple_of(side * half, LANES), half)]
    sent_ref[...] = normed_ref[pl.ds(pl.multiple_of(side * half_tokens, half_tokens), half_tokens), :]


def norm(side, residual_in, near, far, gain, half):
    tokens, width = residual_in.shape
    return pl.pallas_call(
        norm_kernel,
        out_shape=(shape_of((tokens, width)), shape_of((tokens // 2, width)), shape_of((tokens, half))),
        in_specs=[SMEM] + [VMEM] * 4,
        out_specs=(VMEM, VMEM, VMEM),
        scratch_shapes=[pltpu.VMEM((tokens, width), jnp.bfloat16)],
        compiler_params=pltpu.CompilerParams(vmem_limit_bytes=24 * MIB),
        cost_estimate=cost(8 * tokens * width, 10 * tokens * width),
        name="norm",
    )(side, residual_in, near, far, gain.reshape(1, width))


def pack_kernel(experts, side_rows, base_ref, side_ref, notes_ref, *refs):
    *part_refs, out_ref, rows_ref, arrived_ref = refs
    side, top_count = side_ref[0], rows_ref.shape[0]
    if len(part_refs) == 1:
        arrived_ref = part_refs[0]
    else:
        mine_ref, other_ref = part_refs
        part = mine_ref.shape[0]
        arrived_ref[pl.ds(pl.multiple_of(side * part, part), part), :] = mine_ref[...]
        arrived_ref[pl.ds(pl.multiple_of((1 - side) * part, part), part), :] = other_ref[...]
    rows = rows_of(notes_ref[:top_count, :], experts, side_rows, base_ref[0], side)
    rows_ref[...] = rows
    pack(rows, arrived_ref[...], out_ref)


def packed_rows(base, side, notes, parts, experts, side_rows, rows):
    tokens = sum([part.shape[0] for part in parts])
    width = parts[0].shape[1]
    return pl.pallas_call(
        functools.partial(pack_kernel, experts, side_rows),
        out_shape=(shape_of((rows, width)), shape_of((notes.shape[0] // 2, tokens), jnp.int32)),
        in_specs=[SMEM, SMEM, VMEM] + [VMEM] * len(parts),
        out_specs=(VMEM, VMEM),
        scratch_shapes=[pltpu.VMEM((tokens, width), jnp.bfloat16)],
        compiler_params=pltpu.CompilerParams(vmem_limit_bytes=24 * MIB),
        cost_estimate=cost(2 * rows * tokens * width, 2 * rows * width),
        name="packed_rows",
    )(base, side, notes, *parts)


def expert_kernel(
    x_hbm, gate_hbm, up_hbm, down_hbm, gate_too_hbm, up_too_hbm, down_too_hbm, y_hbm, x_ref, y_ref, gate_ref, up_ref,
    down_ref, hidden_ref, gate_sum, up_sum, total_ref, x_sem, y_sem, gate_sem, up_sem, down_sem,
):
    rows, width = x_ref.shape
    share = gate_hbm.shape[2]
    deep, cuts = width // CUTS, share // DEEP
    loads = []
    for k, (gate, up) in enumerate([(gate_hbm, up_hbm), (gate_too_hbm, up_too_hbm)]):
        for c in range(CUTS):
            span = pl.ds(c * deep, deep)
            loads.append(
                [
                    pltpu.make_async_copy(gate.at[0, span], gate_ref.at[k, span], gate_sem.at[k, c]),
                    pltpu.make_async_copy(up.at[0, span], up_ref.at[k, span], up_sem.at[k, c]),
                ]
            )
    for k, down in enumerate([down_hbm, down_too_hbm]):
        for c in range(cuts):
            source, target = pl.ds(c * DEEP, DEEP), pl.ds(k * share + c * DEEP, DEEP)
            loads.append([pltpu.make_async_copy(down.at[0, source], down_ref.at[target], down_sem.at[k, c])])

    def start(number):
        if number < len(loads):
            for load in loads[number]:
                load.start()

    def arrive(number):
        for load in loads[number]:
            load.wait()
        start(number + AHEAD)

    x_load = pltpu.make_async_copy(x_hbm, x_ref, x_sem)
    x_load.start()
    for number in range(AHEAD):
        start(number)
    x_load.wait()
    for k in range(2):
        for c in range(CUTS):
            arrive(k * CUTS + c)
            span = slice(c * deep, (c + 1) * deep)
            x = x_ref[:, span]
            gate = jnp.dot(x, gate_ref[k, span, :], preferred_element_type=jnp.float32)
            up = jnp.dot(x, up_ref[k, span, :], preferred_element_type=jnp.float32)
            if c > 0:
                gate, up = gate_sum[...] + gate, up_sum[...] + up
            if c < CUTS - 1:
                gate_sum[...], up_sum[...] = gate, up
            else:
                hidden = gate * (0.5 + 0.5 * jnp.tanh(0.5 * gate)) * up
                hidden_ref[:, k * share : (k + 1) * share] = hidden.astype(jnp.bfloat16)
    for c in range(2 * cuts - 1):
        arrive(2 * CUTS + c)
        span = slice(c * DEEP, (c + 1) * DEEP)
        part = jnp.dot(hidden_ref[:, span], down_ref[span, :], preferred_element_type=jnp.float32)
        total_ref[...] = part if c == 0 else total_ref[...] + part
    arrive(2 * CUTS + 2 * cuts - 1)
    span = slice((2 * cuts - 1) * DEEP, 2 * cuts * DEEP)
    step = 2 * LANES
    stores = []
    for i in range(width // step):
        columns = slice(i * step, (i + 1) * step)
        part = jnp.dot(hidden_ref[:, span], down_ref[span, columns], preferred_element_type=jnp.float32)
        y_ref[:, columns] = (total_ref[:, columns] + part).astype(jnp.bfloat16)
        column_span = pl.ds(i * step, step)
        stores.append(pltpu.make_async_copy(y_ref.at[:, column_span], y_hbm.at[:, column_span], y_sem.at[i]))
        stores[i].start()
    for store in stores:
        store.wait()


def expert_layer(x, mine, others):
    rows, width = x.shape
    share = mine[0].shape[2]
    return pl.pallas_call(
        expert_kernel,
        out_shape=shape_of((rows, width)),
        in_specs=[HBM] * 7,
        out_specs=HBM,
        scratch_shapes=[
            pltpu.VMEM((rows, width), jnp.bfloat16),
            pltpu.VMEM((rows, width), jnp.bfloat16),
            pltpu.VMEM((2, width, share), jnp.bfloat16),
            pltpu.VMEM((2, width, share), jnp.bfloat16),
            pltpu.VMEM((2 * share, width), jnp.bfloat16),
            pltpu.VMEM((rows, 2 * share), jnp.bfloat16),
            pltpu.VMEM((rows, share), jnp.float32),
            pltpu.VMEM((rows, share), jnp.float32),
            pltpu.VMEM((rows, width), jnp.float32),
            pltpu.SemaphoreType.DMA,
            pltpu.SemaphoreType.DMA((width // (2 * LANES),)),
            pltpu.SemaphoreType.DMA((2, CUTS)),
            pltpu.SemaphoreType.DMA((2, CUTS)),
            pltpu.SemaphoreType.DMA((2, share // DEEP)),
        ],
        compiler_params=pltpu.CompilerParams(vmem_limit_bytes=60 * MIB),
        cost_estimate=cost(12 * rows * width * share, 12 * width * share, 2 * rows * share),
        name="expert_layer",
    )(x, *mine, *others)


def combine_kernel(side_ref, rows_ref, weights_ref, y_ref, *refs):
    *more_refs, mine_ref, sent_ref, total_ref = refs
    top_count, tokens = rows_ref.shape
    half = mine_ref.shape[1]
    row = iota((y_ref.shape[0], tokens), 0)
    share = jnp.zeros(row.shape, jnp.float32)
    for c in range(top_count):
        share = jnp.where(rows_ref[c : c + 1, :] == row, weights_ref[top_count + c : top_count + c + 1, :], share)
    coarse = share.astype(jnp.bfloat16)
    fine = (share - coarse.astype(jnp.float32)).astype(jnp.bfloat16)
    y = y_ref[...]
    contract = (((0,), (0,)), ((), ()))
    total_ref[...] = lax.dot_general(coarse, y, contract, preferred_element_type=jnp.float32)
    total_ref[...] += lax.dot_general(fine, y, contract, preferred_element_type=jnp.float32)
    side = side_ref[0]
    mine = total_ref[:, pl.ds(pl.multiple_of(side * half, LANES), half)]
    for more_ref in more_refs:
        mine += more_ref[...].astype(jnp.float32)
    mine_ref[...] = mine
    sent_ref[...] = total_ref[:, pl.ds(pl.multiple_of((1 - side) * half, LANES), half)].astype(jnp.bfloat16)


def combine(side, placed, weights, y, half, more=()):
    tokens = placed.shape[1]
    rows, width = y.shape
    return pl.pallas_call(
        combine_kernel,
        out_shape=(shape_of((tokens, half), jnp.float32), shape_of((tokens, half))),
        in_specs=[SMEM] + [VMEM] * (3 + len(more)),
        out_specs=(VMEM, VMEM),
        scratch_shapes=[pltpu.VMEM((tokens, width), jnp.float32)],
        compiler_params=pltpu.CompilerParams(vmem_limit_bytes=24 * MIB),
        cost_estimate=cost(4 * rows * tokens * width, 2 * rows * width),
        name="combine",
    )(side, placed, weights, y, *more)


def local(
    residual_in,
    query_rows,
    rotated_key_rows,
    value_row_matrix,
    learned_sink_scores,
    w_out,
    norm_gain,
    expert_ids,
    route_weights,
    w_gate,
    w_up,
    w_down,
):
    tok_dev, model_width = residual_in.shape
    seq_count = lax.axis_size("seq")
    experts = w_gate.shape[0] * seq_count
    capacity = max(2, 8 * tok_dev // experts)
    sides = lax.axis_size("tp")
    side_rows = capacity // sides
    group = seq_count // 2
    rows = experts // 2 * side_rows
    half = model_width // sides
    at_seq = lax.axis_index("seq").astype(jnp.int32)
    base = jnp.where(at_seq < group, 0, experts // 2).astype(jnp.int32).reshape(1)
    side = lax.axis_index("tp").astype(jnp.int32).reshape(1)
    first = (at_seq == 0).astype(jnp.int32).reshape(1)
    key_values = lax.optimization_barrier(jnp.concatenate([rotated_key_rows, value_row_matrix], axis=1))
    before = passed_along(key_values, "seq", 1)
    sinks = jnp.broadcast_to(learned_sink_scores[:, None], (learned_sink_scores.shape[0], LANES))
    sinks, queries = lax.optimization_barrier((sinks, query_rows))
    scaled = queries * jnp.bfloat16(HEAD_SIZE**-0.5)
    weights = (w_gate, w_up, w_down)
    others = [swapped(weight, "tp") for weight in weights[:2]]
    near = attention(
        first, sinks, scaled, key_values, before, w_out
    )
    far, late = lax.optimization_barrier((swapped(near, "tp"), w_down))
    others.append(swapped(late, "tp"))
    normed, sent, kept = norm(side, residual_in, near, far, norm_gain, half)

    def exchanged(block):
        block = block.reshape(group, rows // group, model_width)
        groups = [list(range(group)), list(range(group, seq_count))]
        block = lax.all_to_all(
            block, "seq", split_axis=0, concat_axis=0, axis_index_groups=groups, tiled=True
        )
        return block.reshape(rows, model_width)

    notes = jnp.concatenate([expert_ids.T.astype(jnp.float32), route_weights.T], axis=0)
    crossed = swapped_halves(sent, "seq")
    notes_peer = swapped_halves(notes, "seq")
    packed, placed = packed_rows(base, side, notes, (normed,), experts, side_rows, rows)
    crossed, notes_peer, packed = lax.optimization_barrier((crossed, notes_peer, packed))
    packed_peer, placed_peer = packed_rows(
        base, side, notes_peer, (crossed, swapped(crossed, "tp")), experts, side_rows, rows
    )
    arrived_peer = exchanged(packed_peer)
    arrived_peer, packed, *others = lax.optimization_barrier((arrived_peer, packed, *others))
    arrived = exchanged(packed)
    result_peer = expert_layer(arrived_peer, weights, others)
    result_peer, arrived = lax.optimization_barrier((result_peer, arrived))
    result = expert_layer(arrived, weights, others)

    returned_peer = exchanged(result_peer)
    result, returned_peer = lax.optimization_barrier((result, returned_peer))
    returned = exchanged(result)
    mine_peer, sent_peer = combine(side, placed_peer, notes_peer, returned_peer, half)
    summed_peer = (mine_peer + swapped(sent_peer, "tp").astype(jnp.float32)).astype(jnp.bfloat16)
    back = swapped_halves(summed_peer, "seq")
    mine, sent = combine(side, placed, notes, returned, half, (kept,))
    sent, back = lax.optimization_barrier((sent, back))
    return (mine + swapped(sent, "tp").astype(jnp.float32) + back.astype(jnp.float32)).astype(jnp.bfloat16)


def solution(mesh):
    placed = (
        P("seq", None),
        P("seq", "tp"),
        P("seq", "tp"),
        P("seq", "tp"),
        P("tp"),
        P("tp", None),
        P(),
        P("seq", None),
        P("seq", None),
        P("seq", None, "tp"),
        P("seq", None, "tp"),
        P("seq", "tp", None),
    )
    return jax.shard_map(
        local, mesh=mesh, in_specs=placed, out_specs=P("seq", "tp"), check_vma=False
    )
```

```python
import functools

import jax
import jax.numpy as jnp
from jax import lax
from jax.experimental import pallas as pl
from jax.experimental.pallas import tpu as pltpu
from jax.sharding import PartitionSpec as P

HEAD_SIZE = 64
WINDOW_LENGTH = 128
LANES = 128
MIB = 1024 * 1024
CUTS = 3
DEEP = 256
AHEAD = 3

epsilon = 1e-05

VMEM = pl.BlockSpec(memory_space=pltpu.VMEM)
SMEM = pl.BlockSpec(memory_space=pltpu.SMEM)
HBM = pl.BlockSpec(memory_space=pltpu.HBM)


def passed_along(block, axis, distance):
    devices = range(lax.axis_size(axis))
    route = [(i - distance, i) for i in devices if i - distance in devices]
    return lax.ppermute(block, axis, route)


def swapped(block, axis):
    count = lax.axis_size(axis)
    return lax.ppermute(block, axis, [(i, count - 1 - i) for i in range(count)])


def swapped_halves(block, axis):
    count = lax.axis_size(axis)
    return lax.ppermute(block, axis, [(i, (i + count // 2) % count) for i in range(count)])


def shape_of(dims, dtype=jnp.bfloat16):
    return jax.ShapeDtypeStruct(dims, dtype)


def cost(flops, moved, transcendentals=0):
    return pl.CostEstimate(flops=flops, bytes_accessed=moved, transcendentals=transcendentals)


def iota(dims, dimension):
    return lax.broadcasted_iota(jnp.int32, dims, dimension)


def rows_of(ids, experts, side_rows, base, side):
    top_count, tokens = ids.shape
    names = iota((experts, tokens), 0).astype(jnp.float32)
    hits = [ids[c : c + 1, :] == names for c in range(top_count)]
    named = sum([hit.astype(jnp.float32) for hit in hits]).astype(jnp.bfloat16)
    square = (tokens, tokens)
    earlier = (iota(square, 0) < iota(square, 1)).astype(jnp.bfloat16)
    slot = jnp.dot(named, earlier, preferred_element_type=jnp.float32) - (side * side_rows).astype(jnp.float32)
    expert = names - base.astype(jnp.float32)
    here = (slot >= 0.0) & (slot < side_rows) & (expert >= 0.0) & (expert < experts // 2)
    rows = jnp.where(here, expert * side_rows + slot, -1.0)
    lines = [jnp.sum(jnp.where(hit, rows, 0.0), axis=0, keepdims=True) for hit in hits]
    return jnp.concatenate(lines, axis=0).astype(jnp.int32)


def attention_kernel(
    first_ref, sink_ref, q_ref, kv_ref, before_ref, w_hbm, out_ref, w_ref, att_ref, sum_ref, sems
):
    tokens, width = q_ref.shape
    kv_heads = kv_ref.shape[1] // (2 * HEAD_SIZE)
    pairs = width // LANES // kv_heads
    depth = pairs * LANES
    spans = [pl.ds(head * depth, depth) for head in range(kv_heads)]
    w_loads = [pltpu.make_async_copy(w_hbm.at[span], w_ref.at[span], sems.at[i]) for i, span in enumerate(spans)]
    for load in w_loads:
        load.start()
    low = iota((tokens, LANES), 1) < HEAD_SIZE

    def doubled(block, head):
        wide = block.astype(jnp.float32)
        turned = pltpu.roll(wide, HEAD_SIZE, 1)
        first, second = (wide, turned) if head == 0 else (turned, wide)
        return [
            jnp.where(low, first, 0.0).astype(jnp.bfloat16),
            jnp.where(low, 0.0, second).astype(jnp.bfloat16),
        ]

    own = iota((tokens, tokens), 1) <= iota((tokens, tokens), 0)
    usable = jnp.where(first_ref[0] == 0, 1.0, 0.0)
    own_factor = jnp.where(own, 1.0, 0.0).astype(jnp.bfloat16)
    before_factor = jnp.where(own, 0.0, usable).astype(jnp.bfloat16)
    head_lanes = jnp.where(low, 1.0, 0.0).astype(jnp.bfloat16), jnp.where(low, 0.0, 1.0).astype(jnp.bfloat16)
    ones = jnp.concatenate(head_lanes * 2, axis=0)
    keys_before = [jnp.concatenate(doubled(before_ref[:, :LANES], head), axis=0) for head in range(kv_heads)]
    values_before = [doubled(before_ref[:, LANES:], head) for head in range(kv_heads)]
    contract = (((1,), (1,)), ((), ()))
    for head in range(kv_heads):
        keys = jnp.concatenate(doubled(kv_ref[:, :LANES], head), axis=0)
        values = jnp.concatenate(doubled(kv_ref[:, LANES:], head) + values_before[head], axis=0)
        values = jnp.concatenate([values, ones], axis=1)
        for j in range(head * pairs, (head + 1) * pairs):
            q = q_ref[:, j * LANES : (j + 1) * LANES]
            near = lax.dot_general(q, keys, contract, preferred_element_type=jnp.float32)
            far = lax.dot_general(q, keys_before[head], contract, preferred_element_type=jnp.float32)
            terms, sinks = [], []
            for at in range(2):
                span = slice(at * tokens, (at + 1) * tokens)
                part = jnp.where(own, near[:, span], far[:, span])
                sink = sink_ref[2 * j + at : 2 * j + at + 1, :]
                top = jnp.maximum(jnp.max(part, axis=1, keepdims=True), sink)
                terms.append(jnp.exp(part - top).astype(jnp.bfloat16))
                sinks.append(jnp.exp(sink - top))
            kept = [term * own_factor for term in terms] + [term * before_factor for term in terms]
            found = jnp.dot(jnp.concatenate(kept, axis=1), values, preferred_element_type=jnp.float32)
            total = found[:, LANES:] + jnp.where(low, sinks[0], sinks[1])
            att_ref[:, j * LANES : (j + 1) * LANES] = (found[:, :LANES] / total).astype(jnp.bfloat16)
        w_loads[head].wait()
        step = 2 * LANES
        for at in range(0, out_ref.shape[1], step):
            part = jnp.dot(
                att_ref[:, head * depth : (head + 1) * depth],
                w_ref[head * depth : (head + 1) * depth, at : at + step],
                preferred_element_type=jnp.float32,
            )
            if head > 0:
                part += sum_ref[:, at : at + step]
            if head < kv_heads - 1:
                sum_ref[:, at : at + step] = part
            else:
                out_ref[:, at : at + step] = part.astype(jnp.bfloat16)


def attention(first, sinks, q, key_values, before, w_out):
    tokens = q.shape[0]
    return pl.pallas_call(
        attention_kernel,
        out_shape=shape_of((tokens, w_out.shape[1])),
        in_specs=[SMEM, VMEM, VMEM, VMEM, VMEM, HBM],
        out_specs=VMEM,
        scratch_shapes=[
            pltpu.VMEM(w_out.shape, jnp.bfloat16),
            pltpu.VMEM(q.shape, jnp.bfloat16),
            pltpu.VMEM((tokens, w_out.shape[1]), jnp.float32),
            pltpu.SemaphoreType.DMA((key_values.shape[1] // (2 * HEAD_SIZE),)),
        ],
        compiler_params=pltpu.CompilerParams(vmem_limit_bytes=54_000_000),
        cost_estimate=cost(2 * tokens * w_out.size * 2, 2 * w_out.size, tokens * tokens * q.shape[1] // HEAD_SIZE),
        name="attention",
    )(first, sinks, q, key_values, before, w_out)


def pack(placed, normed, out_ref):
    rows, tokens = out_ref.shape[0], normed.shape[0]
    row = iota((rows, tokens), 0)
    taken = placed[0:1, :] == row
    for c in range(1, placed.shape[0]):
        taken = taken | (placed[c : c + 1, :] == row)
    taken = jnp.where(taken, 1.0, 0.0).astype(jnp.bfloat16)
    out_ref[...] = jnp.dot(taken, normed, preferred_element_type=jnp.float32).astype(jnp.bfloat16)


def norm_kernel(side_ref, residual_ref, near_ref, far_ref, gain_ref, normed_ref, sent_ref, kept_ref, whole_ref):
    side = side_ref[0]
    half_tokens, half = sent_ref.shape[0], kept_ref.shape[1]
    added = near_ref[...].astype(jnp.float32) + far_ref[...].astype(jnp.float32)
    whole = (residual_ref[...].astype(jnp.float32) + added).astype(jnp.bfloat16)
    whole_ref[...] = whole
    wide = whole.astype(jnp.float32)
    mean_square = jnp.mean(wide * wide, axis=1, keepdims=True)
    normed_ref[...] = (wide * lax.rsqrt(mean_square + epsilon) * gain_ref[...]).astype(jnp.bfloat16)
    kept_ref[...] = whole_ref[:, pl.ds(pl.multiple_of(side * half, LANES), half)]
    sent_ref[...] = normed_ref[pl.ds(pl.multiple_of(side * half_tokens, half_tokens), half_tokens), :]


def norm(side, residual_in, near, far, gain, half):
    tokens, width = residual_in.shape
    return pl.pallas_call(
        norm_kernel,
        out_shape=(shape_of((tokens, width)), shape_of((tokens // 2, width)), shape_of((tokens, half))),
        in_specs=[SMEM] + [VMEM] * 4,
        out_specs=(VMEM, VMEM, VMEM),
        scratch_shapes=[pltpu.VMEM((tokens, width), jnp.bfloat16)],
        compiler_params=pltpu.CompilerParams(vmem_limit_bytes=24 * MIB),
        cost_estimate=cost(8 * tokens * width, 10 * tokens * width),
        name="norm",
    )(side, residual_in, near, far, gain.reshape(1, width))


def pack_kernel(experts, side_rows, base_ref, side_ref, notes_ref, *refs):
    *part_refs, out_ref, rows_ref, arrived_ref = refs
    side, top_count = side_ref[0], rows_ref.shape[0]
    if len(part_refs) == 1:
        arrived_ref = part_refs[0]
    else:
        mine_ref, other_ref = part_refs
        part = mine_ref.shape[0]
        arrived_ref[pl.ds(pl.multiple_of(side * part, part), part), :] = mine_ref[...]
        arrived_ref[pl.ds(pl.multiple_of((1 - side) * part, part), part), :] = other_ref[...]
    rows = rows_of(notes_ref[:top_count, :], experts, side_rows, base_ref[0], side)
    rows_ref[...] = rows
    pack(rows, arrived_ref[...], out_ref)


def packed_rows(base, side, notes, parts, experts, side_rows, rows):
    tokens = sum([part.shape[0] for part in parts])
    width = parts[0].shape[1]
    return pl.pallas_call(
        functools.partial(pack_kernel, experts, side_rows),
        out_shape=(shape_of((rows, width)), shape_of((notes.shape[0] // 2, tokens), jnp.int32)),
        in_specs=[SMEM, SMEM, VMEM] + [VMEM] * len(parts),
        out_specs=(VMEM, VMEM),
        scratch_shapes=[pltpu.VMEM((tokens, width), jnp.bfloat16)],
        compiler_params=pltpu.CompilerParams(vmem_limit_bytes=24 * MIB),
        cost_estimate=cost(2 * rows * tokens * width, 2 * rows * width),
        name="packed_rows",
    )(base, side, notes, *parts)


def expert_kernel(
    x_hbm, gate_hbm, up_hbm, down_hbm, gate_too_hbm, up_too_hbm, down_too_hbm, y_hbm, x_ref, y_ref, gate_ref, up_ref,
    down_ref, hidden_ref, gate_sum, up_sum, total_ref, x_sem, y_sem, gate_sem, up_sem, down_sem,
):
    rows, width = x_ref.shape
    share = gate_hbm.shape[2]
    deep, cuts = width // CUTS, share // DEEP
    loads = []
    for k, (gate, up) in enumerate([(gate_hbm, up_hbm), (gate_too_hbm, up_too_hbm)]):
        for c in range(CUTS):
            span = pl.ds(c * deep, deep)
            loads.append(
                [
                    pltpu.make_async_copy(gate.at[0, span], gate_ref.at[k, span], gate_sem.at[k, c]),
                    pltpu.make_async_copy(up.at[0, span], up_ref.at[k, span], up_sem.at[k, c]),
                ]
            )
    for k, down in enumerate([down_hbm, down_too_hbm]):
        for c in range(cuts):
            source, target = pl.ds(c * DEEP, DEEP), pl.ds(k * share + c * DEEP, DEEP)
            loads.append([pltpu.make_async_copy(down.at[0, source], down_ref.at[target], down_sem.at[k, c])])

    def start(number):
        if number < len(loads):
            for load in loads[number]:
                load.start()

    def arrive(number):
        for load in loads[number]:
            load.wait()
        start(number + AHEAD)

    x_load = pltpu.make_async_copy(x_hbm, x_ref, x_sem)
    x_load.start()
    for number in range(AHEAD):
        start(number)
    x_load.wait()
    for k in range(2):
        for c in range(CUTS):
            arrive(k * CUTS + c)
            span = slice(c * deep, (c + 1) * deep)
            x = x_ref[:, span]
            gate = jnp.dot(x, gate_ref[k, span, :], preferred_element_type=jnp.float32)
            up = jnp.dot(x, up_ref[k, span, :], preferred_element_type=jnp.float32)
            if c > 0:
                gate, up = gate_sum[...] + gate, up_sum[...] + up
            if c < CUTS - 1:
                gate_sum[...], up_sum[...] = gate, up
            else:
                hidden = gate * (0.5 + 0.5 * jnp.tanh(0.5 * gate)) * up
                hidden_ref[:, k * share : (k + 1) * share] = hidden.astype(jnp.bfloat16)
    for c in range(2 * cuts - 1):
        arrive(2 * CUTS + c)
        span = slice(c * DEEP, (c + 1) * DEEP)
        part = jnp.dot(hidden_ref[:, span], down_ref[span, :], preferred_element_type=jnp.float32)
        total_ref[...] = part if c == 0 else total_ref[...] + part
    arrive(2 * CUTS + 2 * cuts - 1)
    span = slice((2 * cuts - 1) * DEEP, 2 * cuts * DEEP)
    step = 2 * LANES
    stores = []
    for i in range(width // step):
        columns = slice(i * step, (i + 1) * step)
        part = jnp.dot(hidden_ref[:, span], down_ref[span, columns], preferred_element_type=jnp.float32)
        y_ref[:, columns] = (total_ref[:, columns] + part).astype(jnp.bfloat16)
        column_span = pl.ds(i * step, step)
        stores.append(pltpu.make_async_copy(y_ref.at[:, column_span], y_hbm.at[:, column_span], y_sem.at[i]))
        stores[i].start()
    for store in stores:
        store.wait()


def expert_layer(x, mine, others):
    rows, width = x.shape
    share = mine[0].shape[2]
    return pl.pallas_call(
        expert_kernel,
        out_shape=shape_of((rows, width)),
        in_specs=[HBM] * 7,
        out_specs=HBM,
        scratch_shapes=[
            pltpu.VMEM((rows, width), jnp.bfloat16),
            pltpu.VMEM((rows, width), jnp.bfloat16),
            pltpu.VMEM((2, width, share), jnp.bfloat16),
            pltpu.VMEM((2, width, share), jnp.bfloat16),
            pltpu.VMEM((2 * share, width), jnp.bfloat16),
            pltpu.VMEM((rows, 2 * share), jnp.bfloat16),
            pltpu.VMEM((rows, share), jnp.float32),
            pltpu.VMEM((rows, share), jnp.float32),
            pltpu.VMEM((rows, width), jnp.float32),
            pltpu.SemaphoreType.DMA,
            pltpu.SemaphoreType.DMA((width // (2 * LANES),)),
            pltpu.SemaphoreType.DMA((2, CUTS)),
            pltpu.SemaphoreType.DMA((2, CUTS)),
            pltpu.SemaphoreType.DMA((2, share // DEEP)),
        ],
        compiler_params=pltpu.CompilerParams(vmem_limit_bytes=60 * MIB),
        cost_estimate=cost(12 * rows * width * share, 12 * width * share, 2 * rows * share),
        name="expert_layer",
    )(x, *mine, *others)


def combine_kernel(side_ref, rows_ref, weights_ref, y_ref, *refs):
    *more_refs, mine_ref, sent_ref, total_ref = refs
    top_count, tokens = rows_ref.shape
    half = mine_ref.shape[1]
    row = iota((y_ref.shape[0], tokens), 0)
    share = jnp.zeros(row.shape, jnp.float32)
    for c in range(top_count):
        share = jnp.where(rows_ref[c : c + 1, :] == row, weights_ref[top_count + c : top_count + c + 1, :], share)
    coarse = share.astype(jnp.bfloat16)
    fine = (share - coarse.astype(jnp.float32)).astype(jnp.bfloat16)
    y = y_ref[...]
    contract = (((0,), (0,)), ((), ()))
    total_ref[...] = lax.dot_general(coarse, y, contract, preferred_element_type=jnp.float32)
    total_ref[...] += lax.dot_general(fine, y, contract, preferred_element_type=jnp.float32)
    side = side_ref[0]
    mine = total_ref[:, pl.ds(pl.multiple_of(side * half, LANES), half)]
    for more_ref in more_refs:
        mine += more_ref[...].astype(jnp.float32)
    mine_ref[...] = mine
    sent_ref[...] = total_ref[:, pl.ds(pl.multiple_of((1 - side) * half, LANES), half)].astype(jnp.bfloat16)


def combine(side, placed, weights, y, half, more=()):
    tokens = placed.shape[1]
    rows, width = y.shape
    return pl.pallas_call(
        combine_kernel,
        out_shape=(shape_of((tokens, half), jnp.float32), shape_of((tokens, half))),
        in_specs=[SMEM] + [VMEM] * (3 + len(more)),
        out_specs=(VMEM, VMEM),
        scratch_shapes=[pltpu.VMEM((tokens, width), jnp.float32)],
        compiler_params=pltpu.CompilerParams(vmem_limit_bytes=24 * MIB),
        cost_estimate=cost(4 * rows * tokens * width, 2 * rows * width),
        name="combine",
    )(side, placed, weights, y, *more)


def local(
    residual_in,
    query_rows,
    rotated_key_rows,
    value_row_matrix,
    learned_sink_scores,
    w_out,
    norm_gain,
    expert_ids,
    route_weights,
    w_gate,
    w_up,
    w_down,
):
    tok_dev, model_width = residual_in.shape
    seq_count = lax.axis_size("seq")
    experts = w_gate.shape[0] * seq_count
    capacity = max(2, 8 * tok_dev // experts)
    sides = lax.axis_size("tp")
    side_rows = capacity // sides
    group = seq_count // 2
    rows = experts // 2 * side_rows
    half = model_width // sides
    at_seq = lax.axis_index("seq").astype(jnp.int32)
    base = jnp.where(at_seq < group, 0, experts // 2).astype(jnp.int32).reshape(1)
    side = lax.axis_index("tp").astype(jnp.int32).reshape(1)
    first = (at_seq == 0).astype(jnp.int32).reshape(1)
    key_values = lax.optimization_barrier(jnp.concatenate([rotated_key_rows, value_row_matrix], axis=1))
    before = passed_along(key_values, "seq", 1)
    sinks = jnp.broadcast_to(learned_sink_scores[:, None], (learned_sink_scores.shape[0], LANES))
    sinks, queries = lax.optimization_barrier((sinks, query_rows))
    scaled = queries * jnp.bfloat16(HEAD_SIZE**-0.5)
    weights = (w_gate, w_up, w_down)
    others = [swapped(weight, "tp") for weight in weights[:2]]
    near = attention(
        first, sinks, scaled, key_values, before, w_out
    )
    far, late = lax.optimization_barrier((swapped(near, "tp"), w_down))
    others.append(swapped(late, "tp"))
    normed, sent, kept = norm(side, residual_in, near, far, norm_gain, half)

    def exchanged(block):
        block = block.reshape(group, rows // group, model_width)
        groups = [list(range(group)), list(range(group, seq_count))]
        block = lax.all_to_all(
            block, "seq", split_axis=0, concat_axis=0, axis_index_groups=groups, tiled=True
        )
        return block.reshape(rows, model_width)

    notes = jnp.concatenate([expert_ids.T.astype(jnp.float32), route_weights.T], axis=0)
    crossed = swapped_halves(sent, "seq")
    notes_peer = swapped_halves(notes, "seq")
    packed, placed = packed_rows(base, side, notes, (normed,), experts, side_rows, rows)
    crossed, notes_peer, packed = lax.optimization_barrier((crossed, notes_peer, packed))
    packed_peer, placed_peer = packed_rows(
        base, side, notes_peer, (crossed, swapped(crossed, "tp")), experts, side_rows, rows
    )
    arrived_peer = exchanged(packed_peer)
    arrived_peer, packed, *others = lax.optimization_barrier((arrived_peer, packed, *others))
    arrived = exchanged(packed)
    result_peer = expert_layer(arrived_peer, weights, others)
    result_peer, arrived = lax.optimization_barrier((result_peer, arrived))
    result = expert_layer(arrived, weights, others)

    returned_peer = exchanged(result_peer)
    result, returned_peer = lax.optimization_barrier((result, returned_peer))
    returned = exchanged(result)
    mine_peer, sent_peer = combine(side, placed_peer, notes_peer, returned_peer, half)
    summed_peer = (mine_peer + swapped(sent_peer, "tp").astype(jnp.float32)).astype(jnp.bfloat16)
    back = swapped_halves(summed_peer, "seq")
    mine, sent = combine(side, placed, notes, returned, half, (kept,))
    return (mine + swapped(sent, "tp").astype(jnp.float32) + back.astype(jnp.float32)).astype(jnp.bfloat16)


def solution(mesh):
    placed = (
        P("seq", None),
        P("seq", "tp"),
        P("seq", "tp"),
        P("seq", "tp"),
        P("tp"),
        P("tp", None),
        P(),
        P("seq", None),
        P("seq", None),
        P("seq", None, "tp"),
        P("seq", None, "tp"),
        P("seq", "tp", None),
    )
    return jax.shard_map(
        local, mesh=mesh, in_specs=placed, out_specs=P("seq", "tp"), check_vma=False
    )
```
